32 devices in a mesh: band: 16 (over z, y, x), lev: 2 (over core).
Axes of the slice: x: 2, y: 2, z: 4, core: 2. Of those that a mesh axis runs over, the one named last changes fastest.
Arguments:
- spectra: bfloat16 [2, 64, 320, 641], P(None, 'lev', 'band'), may hold values from -0.15625 to 0.15625
- legendre: bfloat16 [8, 16, 320, 641], P('lev', None, 'band'), may hold values from -0.25 to 0.25
- pairing: int32 [320], P('band'), may hold values from 0 to 319, each once
- eta_shift: bfloat16 [16, 128, 2816], P('lev', 'band'), may hold values from -4 to 4
- cells: int32 [3, 16, 128, 2816], P(None, 'lev', 'band'), may hold values from -1 to 2815, as said below
Outputs:
- advected: bfloat16 [2, 16, 128, 2816], P(None, 'lev', 'band')
- displacement: float32 [2, 16, 128, 2816], P(None, 'lev', 'band')
The draws below stay inside these ranges and needn't reach their ends.
Inputs may be any that keep to these rules, and one draw needn't show every extreme that they name: cells[0] is the arrival row or the row before it, cells[1] the arrival longitude or the one before it (cyclically), cells[2] the arrival level or the one before it.
All inputs are finite; a program needn't handle non-finite values.
Results may differ from the reference program's by a relative error of at most 0.0076.
Values may be sent and summed in bfloat16 or wider, within the bound.
No kernel may reach another device: no remote copies, remote signals or barrier semaphores. Data moves between devices by JAX's collectives and lax.ppermute only.
A program may use at most 192 MiB of HBM per device.

```python
import math
import jax
import jax.numpy as jnp
from jax import lax

M = 640
NLON = 2816
LEV = 16
ITERS = 2
LAT_DEV = 8
LAT = 128
PAIRS = 320
N_BAND = 16


def draw_cells(key, part):
    key = jax.random.fold_in(key, 7)
    key_row, key_lon, key_level = jax.random.split(key, 3)
    grid_shape = (LEV, LAT, NLON)
    row_cells = lax.broadcasted_iota(jnp.int32, grid_shape, 1) - jax.random.randint(key_row, grid_shape, 0, 2)
    lon_cells = (lax.broadcasted_iota(jnp.int32, grid_shape, 2) - jax.random.randint(key_lon, grid_shape, 0, 2)) % NLON
    level_cells = lax.broadcasted_iota(jnp.int32, grid_shape, 0) - jax.random.randint(key_level, grid_shape, 0, 2)
    return jnp.stack([row_cells, lon_cells, level_cells]).astype(jnp.int32)


def levels(key, shape, shards, least, top_value):
    def one(dim, parts):
        heights = jax.random.uniform(jax.random.fold_in(jax.random.fold_in(key, 6), dim), (parts,), jnp.float32, least / len(shards), top_value / len(shards))
        return jnp.repeat(jnp.exp(heights), shape[dim] // parts).reshape((-1,) + (1,) * (len(shape) - dim - 1))

    gain = one(*shards[0])
    for cut in shards[1:]:
        gain = gain * one(*cut)
    return gain


def bell_draw(rng, shape, scale, limit, cuts=(), kind=jnp.bfloat16):
    drawn = jax.random.normal(rng, shape, jnp.float32) * scale
    if len(cuts) > 0:
        drawn = levels(rng, shape, cuts, -0.22, 0.18) * drawn
    return jnp.clip(drawn, min=-limit, max=limit).astype(kind)


def setup_inputs(seed: int = 0) -> dict:
    key_list = jax.random.split(jax.random.key(seed), 6)
    spectra = bell_draw(key_list[0], (2, 4 * LEV, PAIRS, M + 1), ((2 * M) ** -0.5), 0.15625, ((1, 2), (2, 16)))
    legendre = bell_draw(key_list[1], (LAT_DEV, N_BAND, PAIRS, M + 1), (M + 1) ** -0.5, 0.25, ((0, 2), (2, 16)))
    pairing = jax.random.permutation(key_list[2], PAIRS).astype(jnp.int32)
    eta_shift = bell_draw(key_list[3], (LEV, LAT, NLON), 0.6, 4.0, ((0, 2), (1, 16)))
    cells = draw_cells(jax.random.fold_in(key_list[5], 71), 0)
    return {"spectra": spectra, "legendre": legendre, "pairing": pairing, "eta_shift": eta_shift, "cells": cells}


COURANT = 0.8


def cubic_weights(fraction):
    return (-fraction * (fraction - 1.0) * (fraction - 2.0) / 6.0,
            (fraction + 1.0) * (fraction - 1.0) * (fraction - 2.0) / 2.0,
            -(fraction + 1.0) * fraction * (fraction - 2.0) / 2.0,
            (fraction + 1.0) * fraction * (fraction - 1.0) / 6.0)


def tap_weights(shift, offset):
    fraction = jnp.clip(-shift - offset.astype(jnp.float32), -0.5, 1.5)
    first, second, third, fourth = cubic_weights(fraction)
    nothing = jnp.zeros_like(fraction)
    at_arrival = offset == 0
    return (jnp.where(at_arrival, nothing, first), jnp.where(at_arrival, first, second),
            jnp.where(at_arrival, second, third), jnp.where(at_arrival, third, fourth),
            jnp.where(at_arrival, fourth, nothing))


def rolled_copies(padded):
    return [jnp.roll(padded, 2 - lon_step, axis=3) for lon_step in range(5)]


def interpolate(copies, field_ids, level_taps, row_taps, lon_taps):
    level_count = level_taps[0].shape[0]
    row_count = level_taps[0].shape[1]
    totals = [jnp.zeros(level_taps[0].shape, jnp.float32) for field_id in field_ids]
    for level_step in range(5):
        for row_step in range(5):
            outer = level_taps[level_step] * row_taps[row_step]
            for position in range(len(field_ids)):
                inner = jnp.zeros(outer.shape, jnp.float32)
                for lon_step in range(5):
                    block = copies[lon_step][level_step:level_step + level_count, field_ids[position],
                                             row_step:row_step + row_count, :]
                    inner = inner + lon_taps[lon_step] * block.astype(jnp.float32)
                totals[position] = totals[position] + outer * inner
    return totals


def departure(fields, wind_copies, tracer_copies, wind_ids, tracer_ids, eta_shift,
              row_offset, lon_offset, level_offset):
    east = fields[:, 0].astype(jnp.float32)
    north = fields[:, 1].astype(jnp.float32)
    level_taps = tap_weights(eta_shift.astype(jnp.float32), level_offset)
    shift_row = COURANT * north
    shift_lon = COURANT * east
    for sweep in range(ITERS):
        row_taps = tap_weights(shift_row, row_offset)
        lon_taps = tap_weights(shift_lon, lon_offset)
        east_found, north_found = interpolate(wind_copies, wind_ids, level_taps, row_taps, lon_taps)
        shift_row = 0.5 * COURANT * (north + north_found)
        shift_lon = 0.5 * COURANT * (east + east_found)
    row_taps = tap_weights(shift_row, row_offset)
    lon_taps = tap_weights(shift_lon, lon_offset)
    heat, moisture = interpolate(tracer_copies, tracer_ids, level_taps, row_taps, lon_taps)
    return jnp.stack([heat, moisture]).astype(jnp.bfloat16), jnp.stack([shift_row, shift_lon])


def split_halves(spectra, pairing):
    width = spectra.shape[-1]
    columns = lax.broadcasted_iota(jnp.int32, (pairing.shape[0], width), 1)
    first_part = columns < (width - 1 - pairing)[:, None]
    nothing = jnp.zeros((), spectra.dtype)
    return jnp.stack([jnp.where(first_part, spectra, nothing), jnp.where(first_part, nothing, spectra)])


def synthesis(pair_ids, lon_ids, lon_total):
    orders = jnp.stack([pair_ids, M - 1 - pair_ids])
    phase = ((orders[:, :, None] * lon_ids[None, None, :]) % lon_total).astype(jnp.float32) * (2.0 * math.pi / lon_total)
    weight = jnp.where(orders == 0, 1.0, 2.0).astype(jnp.float32)[:, :, None]
    return jnp.stack([weight * jnp.cos(phase), -weight * jnp.sin(phase)]).astype(jnp.bfloat16)


def reference(spectra, legendre, pairing, eta_shift, cells):
    table = jnp.transpose(legendre, (1, 0, 2, 3)).reshape(LAT, PAIRS, M + 1)
    halves = split_halves(spectra, pairing)
    coefficients = halves.reshape(16 * LEV, PAIRS, M + 1)

    def one_pair(pair_slot):
        rows_here = lax.dynamic_index_in_dim(table, pair_slot, 1, keepdims=False)
        columns_here = lax.dynamic_index_in_dim(coefficients, pair_slot, 1, keepdims=False)
        return jnp.dot(rows_here, columns_here.T, preferred_element_type=jnp.float32).astype(jnp.bfloat16)

    sums = lax.map(one_pair, jnp.arange(PAIRS, dtype=jnp.int32))
    sums = sums.reshape(PAIRS, LAT, 2, 2, 4 * LEV)
    basis = synthesis(pairing, jnp.arange(NLON, dtype=jnp.int32), NLON)
    grid = jnp.einsum('plhcf,chpj->flj', sums.astype(jnp.float32), basis.astype(jnp.float32)).astype(jnp.bfloat16)
    fields = grid.reshape(LEV, 4, LAT, NLON)
    padded = jnp.pad(fields, ((2, 2), (0, 0), (2, 2), (0, 0)))
    copies = rolled_copies(padded)
    grid_shape = (LEV, LAT, NLON)
    level_ids = lax.broadcasted_iota(jnp.int32, grid_shape, 0)
    row_ids = lax.broadcasted_iota(jnp.int32, grid_shape, 1)
    lon_ids = lax.broadcasted_iota(jnp.int32, grid_shape, 2)
    row_offset = cells[0] - row_ids
    lon_offset = (cells[1] - lon_ids + 2) % NLON - 2
    level_offset = cells[2] - level_ids
    return departure(fields, copies, copies, (0, 1), (2, 3), eta_shift, row_offset, lon_offset, level_offset)
```

```python
import functools
import math

import jax
import jax.numpy as jnp
from jax import lax
from jax.experimental import pallas as pl
from jax.experimental.pallas import tpu as pltpu
from jax.sharding import PartitionSpec as P

M = 640
ITERS = 2


COURANT = 0.8


HALO = 2
LANES = 128


def slot_weights(place, here, low, high, sixth):
    z = jnp.minimum(jnp.maximum(place, low), high)
    square = z * z
    less = square - 1.0
    outer = less * z * sixth
    triple = 3.0 * outer
    half = 0.5 * z
    half_square = 0.5 * square
    return (
        half_square - half - jnp.where(here, outer, triple),
        triple - less,
        half_square + half - jnp.where(here, triple, outer),
        outer,
    )


def bounds(here):
    return (
        jnp.where(here, -0.5, -1.5),
        jnp.where(here, 1.5, 0.5),
        jnp.where(here, 1.0 / 6.0, -1.0 / 6.0),
    )


def weighted(weights, values):
    return (weights[0] * values[0] + weights[1] * values[1]) + (
        weights[2] * values[2] + weights[3] * values[3]
    )


def shifted_lanes(before, here, after, lane):
    return (
        jnp.where(lane < 2, pltpu.roll(before, 2, 1), pltpu.roll(here, 2, 1)),
        jnp.where(lane < 1, pltpu.roll(before, 1, 1), pltpu.roll(here, 1, 1)),
        here,
        jnp.where(lane < LANES - 1, pltpu.roll(here, LANES - 1, 1), pltpu.roll(after, LANES - 1, 1)),
        jnp.where(lane < LANES - 2, pltpu.roll(here, LANES - 2, 1), pltpu.roll(after, LANES - 2, 1)),
    )


def fill(chunk, chunk_total, center_ref, edge_ref, scratch):
    slabs, field_count, rows, _ = center_ref.shape
    before = jnp.where(chunk == 0, chunk_total - 1, chunk - 1)
    after = jnp.where(chunk == chunk_total - 1, 0, chunk + 1)
    starts = [pl.multiple_of(c * LANES, LANES) for c in (before, chunk, after)]
    lane = lax.broadcasted_iota(jnp.int32, (rows, LANES), 1)
    edge_lane = lax.broadcasted_iota(jnp.int32, (2 * HALO, LANES), 1)

    def slab_step(slab, carry):
        for field in range(field_count):
            blocks = [center_ref[slab, field, :, pl.ds(s, LANES)] for s in starts]
            for step, moved in enumerate(shifted_lanes(*blocks, lane)):
                scratch[field, slab, step, rows : 2 * rows, :] = moved
            edges = [edge_ref[slab, field, :, pl.ds(s, LANES)] for s in starts]
            for step, moved in enumerate(shifted_lanes(*edges, edge_lane)):
                scratch[field, slab, step, rows - 2 * HALO : rows, :] = moved
                scratch[field, slab, step, 2 * rows : 2 * rows + 2 * HALO, :] = moved
        return carry

    lax.fori_loop(0, slabs, slab_step, 0)


def level_sums(scratch, field, k, zero, rows, weights, level_here, row_here, lon_here):
    def load(a, b, c):
        return scratch[field, k + HALO + a, c + HALO, pl.ds(zero + (rows + b), rows), :]

    def slab_slots(a):
        out = {}
        for c in (-1, 0, 1):
            for b in (-1, 0, 1):
                out[b, c] = load(a, b, c)
            out[2, c] = jnp.where(row_here, load(a, 2, c), load(a, -2, c))
        for b in (-1, 0, 1):
            out[b, 2] = jnp.where(lon_here, load(a, b, 2), load(a, b, -2))
        out[2, 2] = jnp.where(
            row_here,
            jnp.where(lon_here, load(a, 2, 2), load(a, 2, -2)),
            jnp.where(lon_here, load(a, -2, 2), load(a, -2, -2)),
        )
        return out

    slabs = [slab_slots(a) for a in (-1, 0, 1, 2, -2)]
    return {
        key: weighted(
            weights,
            (
                slabs[0][key],
                slabs[1][key],
                slabs[2][key],
                jnp.where(level_here, slabs[3][key], slabs[4][key]),
            ),
        )
        for key in slabs[0]
    }


def across(sums, row_weights, lon_weights):
    slots = (-1, 0, 1, 2)
    return weighted(
        lon_weights, [weighted(row_weights, [sums[b, c] for b in slots]) for c in slots]
    )


def at_arrival(base_ref, cells_ref, k, chunk, lanes):
    shape = cells_ref.shape[2:3] + (LANES,)
    level_here = cells_ref[2, k, :, lanes] == base_ref[0] + k
    row_here = cells_ref[0, k, :, lanes] == base_ref[1] + lax.broadcasted_iota(jnp.int32, shape, 0)
    lon_here = cells_ref[1, k, :, lanes] == chunk * LANES + lax.broadcasted_iota(
        jnp.int32, shape, 1
    )
    return level_here, row_here, lon_here


def wind_kernel(chunk_total, base_ref, center_ref, edge_ref, eta_ref, cells_ref, out_ref, scratch):
    levels, rows, width = eta_ref.shape
    zero = base_ref[2]

    def chunk_step(part, carry):
        chunk = pl.program_id(0) * (width // LANES) + part
        lanes = pl.ds(pl.multiple_of(part * LANES, LANES), LANES)
        fill(chunk, chunk_total, center_ref, edge_ref, scratch)

        def level_step(k, inner):
            level_here, row_here, lon_here = at_arrival(base_ref, cells_ref, k, chunk, lanes)
            weights = slot_weights(
                -eta_ref[k, :, lanes].astype(jnp.float32), level_here, *bounds(level_here)
            )
            sums = [
                level_sums(
                    scratch, field, k, zero, rows, weights, level_here, row_here, lon_here
                )
                for field in range(2)
            ]
            east = scratch[0, k + HALO, HALO, rows : 2 * rows, :]
            north = scratch[1, k + HALO, HALO, rows : 2 * rows, :]
            row_bounds, lon_bounds = bounds(row_here), bounds(lon_here)
            shift_row = COURANT * north
            shift_lon = COURANT * east
            for sweep in range(ITERS):
                row_weights = slot_weights(-shift_row, row_here, *row_bounds)
                lon_weights = slot_weights(-shift_lon, lon_here, *lon_bounds)
                east_found = across(sums[0], row_weights, lon_weights)
                north_found = across(sums[1], row_weights, lon_weights)
                shift_row = 0.5 * COURANT * (north + north_found)
                shift_lon = 0.5 * COURANT * (east + east_found)
            out_ref[0, k, :, lanes] = shift_row
            out_ref[1, k, :, lanes] = shift_lon
            return inner

        lax.fori_loop(0, levels, level_step, 0)
        return carry

    lax.fori_loop(0, width // LANES, chunk_step, 0)


def tracer_kernel(
    chunk_total, base_ref, center_ref, edge_ref, eta_ref, cells_ref, shift_ref, out_ref, scratch
):
    levels, rows, width = eta_ref.shape
    zero = base_ref[2]

    def chunk_step(part, carry):
        chunk = pl.program_id(0) * (width // LANES) + part
        lanes = pl.ds(pl.multiple_of(part * LANES, LANES), LANES)
        fill(chunk, chunk_total, center_ref, edge_ref, scratch)

        def level_step(k, inner):
            level_here, row_here, lon_here = at_arrival(base_ref, cells_ref, k, chunk, lanes)
            weights = slot_weights(
                -eta_ref[k, :, lanes].astype(jnp.float32), level_here, *bounds(level_here)
            )
            row_weights = slot_weights(-shift_ref[0, k, :, lanes], row_here, *bounds(row_here))
            lon_weights = slot_weights(-shift_ref[1, k, :, lanes], lon_here, *bounds(lon_here))
            for field in range(2):
                sums = level_sums(
                    scratch, field, k, zero, rows, weights, level_here, row_here, lon_here
                )
                found = across(sums, row_weights, lon_weights)
                out_ref[field, k, :, lanes] = found.astype(out_ref.dtype)
            return inner

        lax.fori_loop(0, levels, level_step, 0)
        return carry

    lax.fori_loop(0, width // LANES, chunk_step, 0)


def interpolation_call(kernel, base, center, edge, eta_shift, cells, extra, out_dtype):
    levels, rows, lon_total = eta_shift.shape
    chunk_total = lon_total // LANES
    parts = 2 if chunk_total % 2 == 0 else 1
    width = lon_total // parts
    whole = lambda array: pl.BlockSpec(array.shape, lambda i: (0,) * array.ndim)
    pair = pl.BlockSpec((2, levels, rows, width), lambda i: (0, 0, 0, i))
    points = levels * rows * lon_total
    return pl.pallas_call(
        functools.partial(kernel, chunk_total),
        grid=(parts,),
        out_shape=jax.ShapeDtypeStruct((2, levels, rows, lon_total), out_dtype),
        in_specs=[
            pl.BlockSpec(memory_space=pltpu.SMEM),
            whole(center),
            whole(edge),
            pl.BlockSpec((levels, rows, width), lambda i: (0, 0, i)),
            pl.BlockSpec((3, levels, rows, width), lambda i: (0, 0, 0, i)),
        ]
        + [pair] * len(extra),
        out_specs=pair,
        scratch_shapes=[pltpu.VMEM((2, levels + 2 * HALO, 5, 3 * rows, LANES), jnp.float32)],
        compiler_params=pltpu.CompilerParams(vmem_limit_bytes=48 * 1024 * 1024),
        cost_estimate=pl.CostEstimate(
            flops=points * 500, bytes_accessed=points * 40, transcendentals=0
        ),
    )(base, center, edge, eta_shift, cells, *extra)

def row_edges(fields):
    size = lax.axis_size("band")
    up = [(i, (i + 1) % size) for i in range(size - 1)]
    down = [(j, i) for i, j in up]
    rows = fields.shape[2]
    before = lax.ppermute(fields[:, :, rows - HALO :], "band", up)
    after = lax.ppermute(fields[:, :, :HALO], "band", down)
    return jnp.concatenate([after, before], axis=2)


def level_edges(array):
    size, count = (lax.axis_size("lev"), array.shape[0])
    last, first = (array[count - HALO :], array[:HALO])
    if size == 2:
        at_top = lax.axis_index("lev") == 0
        found = lax.ppermute(jnp.where(at_top, last, first), "lev", [(0, 1), (1, 0)])
        nothing = jnp.zeros_like(found)
        return jnp.where(at_top, nothing, found), jnp.where(at_top, found, nothing)
    up = [(i, i + 1) for i in range(size - 1)]
    down = [(j, i) for i, j in up]
    return lax.ppermute(last, "lev", up), lax.ppermute(first, "lev", down)


def with_edges(fields):
    rows = fields.shape[2]
    edge = row_edges(fields)
    before, after = level_edges(jnp.concatenate([fields, edge], axis=2))
    center = jnp.concatenate([before[:, :, :rows], fields, after[:, :, :rows]], axis=0)
    edge = jnp.concatenate([before[:, :, rows:], edge, after[:, :, rows:]], axis=0)
    return center.astype(jnp.float32), edge.astype(jnp.float32)


def split_halves(spectra, pairing):
    width = spectra.shape[-1]
    columns = lax.broadcasted_iota(jnp.int32, (pairing.shape[0], width), 1)
    first_part = columns < (width - 1 - pairing)[:, None]
    nothing = jnp.zeros((), spectra.dtype)
    return jnp.stack(
        [jnp.where(first_part, spectra, nothing), jnp.where(first_part, nothing, spectra)]
    )


def synthesis(pair_ids, lon_ids, lon_total):
    orders = jnp.stack([pair_ids, M - 1 - pair_ids])
    phase = (orders[:, :, None] * lon_ids[None, None, :] % lon_total).astype(jnp.float32) * (
        2.0 * math.pi / lon_total
    )
    weight = jnp.where(orders == 0, 1.0, 2.0).astype(jnp.float32)[:, :, None]
    return jnp.stack([weight * jnp.cos(phase), -weight * jnp.sin(phase)]).astype(jnp.bfloat16)


def legendre_rows(table, halves):
    return jnp.einsum(
        "scpk,hrfpk->cpsfhr", table, halves, preferred_element_type=jnp.float32
    ).astype(jnp.bfloat16)


def per_device(spectra, legendre, pairing, eta_shift, cells):
    grid_shape = eta_shift.shape
    row_count = grid_shape[1]
    halves = split_halves(spectra, pairing)
    result = legendre_rows(lax.all_gather(legendre, "lev", axis=0, tiled=True), halves)
    local_sums = result.reshape(result.shape[0], result.shape[1], -1)
    spectral = lax.all_to_all(local_sums, "band", split_axis=0, concat_axis=1, tiled=True)
    all_pairs = lax.all_gather(pairing, "band", axis=0, tiled=True)
    field_count = 4 * grid_shape[0]
    spectral = spectral.reshape(all_pairs.shape[0], row_count, field_count, 2, 2)
    lon_total = grid_shape[2]
    lon_half = lon_total // 2
    pieces = []
    for lon_part in range(2):
        lon_block = lon_part * lon_half + jnp.arange(lon_half, dtype=jnp.int32)
        basis = synthesis(all_pairs, lon_block, lon_total)
        pieces.append(
            jnp.einsum(
                "psfhr,rhpj->fsj", spectral, basis, preferred_element_type=jnp.float32
            ).astype(jnp.bfloat16)
        )
    grid = jnp.concatenate(pieces, axis=2)
    fields = grid.reshape(grid_shape[0], 4, grid_shape[1], lon_total)
    base = jnp.stack(
        [
            lax.axis_index("lev") * grid_shape[0],
            lax.axis_index("band") * grid_shape[1],
            jnp.int32(0),
        ]
    ).astype(jnp.int32)
    winds = with_edges(fields[:, :2])
    tracers = with_edges(fields[:, 2:])
    displacement = interpolation_call(
        wind_kernel, base, *winds, eta_shift, cells, (), jnp.float32
    )
    advected = interpolation_call(
        tracer_kernel, base, *tracers, eta_shift, cells, (displacement,), jnp.bfloat16
    )
    return advected, displacement


def solution(mesh):
    return jax.shard_map(
        per_device,
        mesh=mesh,
        in_specs=(
            P(None, "lev", "band", None),
            P("lev", None, "band", None),
            P("band"),
            P("lev", "band", None),
            P(None, "lev", "band", None),
        ),
        out_specs=(P(None, "lev", "band", None), P(None, "lev", "band", None)),
        check_vma=False,
    )
```

```python
import functools
import math

import jax
import jax.numpy as jnp
from jax import lax
from jax.experimental import pallas as pl
from jax.experimental.pallas import tpu as pltpu
from jax.sharding import PartitionSpec as P

M = 640
ITERS = 2


COURANT = 0.8


HALO = 2
LANES = 128


def slot_weights(place, here, low, high, sixth):
    z = jnp.minimum(jnp.maximum(place, low), high)
    square = z * z
    less = square - 1.0
    outer = less * z * sixth
    triple = 3.0 * outer
    half = 0.5 * z
    half_square = 0.5 * square
    return (
        half_square - half - jnp.where(here, outer, triple),
        triple - less,
        half_square + half - jnp.where(here, triple, outer),
        outer,
    )


def bounds(here):
    return (
        jnp.where(here, -0.5, -1.5),
        jnp.where(here, 1.5, 0.5),
        jnp.where(here, 1.0 / 6.0, -1.0 / 6.0),
    )


def weighted(weights, values):
    return (weights[0] * values[0] + weights[1] * values[1]) + (
        weights[2] * values[2] + weights[3] * values[3]
    )


def shifted_lanes(before, here, after, lane):
    return (
        jnp.where(lane < 2, pltpu.roll(before, 2, 1), pltpu.roll(here, 2, 1)),
        jnp.where(lane < 1, pltpu.roll(before, 1, 1), pltpu.roll(here, 1, 1)),
        here,
        jnp.where(lane < LANES - 1, pltpu.roll(here, LANES - 1, 1), pltpu.roll(after, LANES - 1, 1)),
        jnp.where(lane < LANES - 2, pltpu.roll(here, LANES - 2, 1), pltpu.roll(after, LANES - 2, 1)),
    )


def fill(chunk, chunk_total, center_ref, edge_ref, scratch):
    slabs, field_count, rows, _ = center_ref.shape
    before = jnp.where(chunk == 0, chunk_total - 1, chunk - 1)
    after = jnp.where(chunk == chunk_total - 1, 0, chunk + 1)
    starts = [pl.multiple_of(c * LANES, LANES) for c in (before, chunk, after)]
    lane = lax.broadcasted_iota(jnp.int32, (rows, LANES), 1)
    edge_lane = lax.broadcasted_iota(jnp.int32, (2 * HALO, LANES), 1)
    tall = 3 * rows

    def slab_step(slab, carry):
        first = pl.multiple_of(slab * (5 * tall), 8)
        for field in range(field_count):
            blocks = [center_ref[slab, field, :, pl.ds(s, LANES)] for s in starts]
            for step, moved in enumerate(shifted_lanes(*blocks, lane)):
                scratch[field, pl.ds(first + (step * tall + rows), rows), :] = moved
            edges = [edge_ref[slab, field, :, pl.ds(s, LANES)] for s in starts]
            for step, moved in enumerate(shifted_lanes(*edges, edge_lane)):
                top = first + (step * tall + rows - 2 * HALO)
                scratch[field, pl.ds(top, 2 * HALO), :] = moved
                scratch[field, pl.ds(first + (step * tall + 2 * rows), 2 * HALO), :] = moved
        return carry

    lax.fori_loop(0, slabs, slab_step, 0)


def level_sum(scratch, field, base, rows, slot, weights, level_here, row_here, lon_here):
    tall = 3 * rows

    def load(a, b, c):
        offset = ((a + HALO) * 5 + c + HALO) * tall + rows + b
        return scratch[field, pl.ds(base + offset, rows), :]

    def pick_lon(a, b):
        if slot[1] == 2:
            return jnp.where(lon_here, load(a, b, 2), load(a, b, -2))
        return load(a, b, slot[1])

    def pick(a):
        if slot[0] == 2:
            return jnp.where(row_here, pick_lon(a, 2), pick_lon(a, -2))
        return pick_lon(a, slot[0])

    total = weights[0] * pick(-1) + weights[1] * pick(0)
    total = total + weights[2] * pick(1)
    return total + weights[3] * jnp.where(level_here, pick(2), pick(-2))


SLOTS = (-1, 0, 1, 2)


def across(sums, row_weights, lon_weights):
    return weighted(
        lon_weights, [weighted(row_weights, [sums(b, c) for b in SLOTS]) for c in SLOTS]
    )


def at_arrival(base_ref, cells_ref, k, chunk, lanes):
    shape = cells_ref.shape[2:3] + (LANES,)
    level_here = cells_ref[2, k, :, lanes] == base_ref[0] + k
    row_here = cells_ref[0, k, :, lanes] == base_ref[1] + lax.broadcasted_iota(jnp.int32, shape, 0)
    lon_here = cells_ref[1, k, :, lanes] == chunk * LANES + lax.broadcasted_iota(
        jnp.int32, shape, 1
    )
    return level_here, row_here, lon_here


def wind_kernel(chunk_total, base_ref, center_ref, edge_ref, eta_ref, cells_ref, out_ref, scratch):
    levels, rows, width = eta_ref.shape

    def chunk_step(part, carry):
        chunk = pl.program_id(0) * (width // LANES) + part
        lanes = pl.ds(pl.multiple_of(part * LANES, LANES), LANES)
        fill(chunk, chunk_total, center_ref, edge_ref, scratch)

        def level_step(k, inner):
            level_here, row_here, lon_here = at_arrival(base_ref, cells_ref, k, chunk, lanes)
            weights = slot_weights(
                -eta_ref[k, :, lanes].astype(jnp.float32), level_here, *bounds(level_here)
            )
            base = k * (15 * rows)
            sums = [
                {
                    (b, c): level_sum(
                        scratch, field, base, rows, (b, c), weights, level_here, row_here, lon_here
                    )
                    for c in SLOTS
                    for b in SLOTS
                }
                for field in range(2)
            ]
            middle = (HALO * 5 + HALO) * 3 * rows + rows
            east = scratch[0, pl.ds(base + middle, rows), :]
            north = scratch[1, pl.ds(base + middle, rows), :]
            row_bounds, lon_bounds = bounds(row_here), bounds(lon_here)
            shift_row = COURANT * north
            shift_lon = COURANT * east
            for sweep in range(ITERS):
                row_weights = slot_weights(-shift_row, row_here, *row_bounds)
                lon_weights = slot_weights(-shift_lon, lon_here, *lon_bounds)
                east_found = across(lambda b, c: sums[0][b, c], row_weights, lon_weights)
                north_found = across(lambda b, c: sums[1][b, c], row_weights, lon_weights)
                shift_row = 0.5 * COURANT * (north + north_found)
                shift_lon = 0.5 * COURANT * (east + east_found)
            out_ref[0, k, :, lanes] = shift_row
            out_ref[1, k, :, lanes] = shift_lon
            return inner

        lax.fori_loop(0, levels, level_step, 0)
        return carry

    lax.fori_loop(0, width // LANES, chunk_step, 0)


def tracer_kernel(
    chunk_total, base_ref, center_ref, edge_ref, eta_ref, cells_ref, shift_ref, out_ref, scratch
):
    levels, rows, width = eta_ref.shape

    def chunk_step(part, carry):
        chunk = pl.program_id(0) * (width // LANES) + part
        lanes = pl.ds(pl.multiple_of(part * LANES, LANES), LANES)
        fill(chunk, chunk_total, center_ref, edge_ref, scratch)

        def level_step(k, inner):
            level_here, row_here, lon_here = at_arrival(base_ref, cells_ref, k, chunk, lanes)
            weights = slot_weights(
                -eta_ref[k, :, lanes].astype(jnp.float32), level_here, *bounds(level_here)
            )
            row_weights = slot_weights(-shift_ref[0, k, :, lanes], row_here, *bounds(row_here))
            lon_weights = slot_weights(-shift_ref[1, k, :, lanes], lon_here, *bounds(lon_here))
            base = k * (15 * rows)
            for field in range(2):

                def sums(b, c, field=field):
                    return level_sum(
                        scratch, field, base, rows, (b, c), weights, level_here, row_here, lon_here
                    )

                found = across(sums, row_weights, lon_weights)
                out_ref[field, k, :, lanes] = found.astype(out_ref.dtype)
            return inner

        lax.fori_loop(0, levels, level_step, 0)
        return carry

    lax.fori_loop(0, width // LANES, chunk_step, 0)


def interpolation_call(kernel, base, center, edge, eta_shift, cells, extra, out_dtype):
    levels, rows, lon_total = eta_shift.shape
    chunk_total = lon_total // LANES
    parts = 2 if chunk_total % 2 == 0 else 1
    width = lon_total // parts
    whole = lambda array: pl.BlockSpec(array.shape, lambda i: (0,) * array.ndim)
    pair = pl.BlockSpec((2, levels, rows, width), lambda i: (0, 0, 0, i))
    points = levels * rows * lon_total
    return pl.pallas_call(
        functools.partial(kernel, chunk_total),
        grid=(parts,),
        out_shape=jax.ShapeDtypeStruct((2, levels, rows, lon_total), out_dtype),
        in_specs=[
            pl.BlockSpec(memory_space=pltpu.SMEM),
            whole(center),
            whole(edge),
            pl.BlockSpec((levels, rows, width), lambda i: (0, 0, i)),
            pl.BlockSpec((3, levels, rows, width), lambda i: (0, 0, 0, i)),
        ]
        + [pair] * len(extra),
        out_specs=pair,
        scratch_shapes=[pltpu.VMEM((2, (levels + 2 * HALO) * 15 * rows, LANES), jnp.float32)],
        compiler_params=pltpu.CompilerParams(vmem_limit_bytes=48 * 1024 * 1024),
        cost_estimate=pl.CostEstimate(
            flops=points * 500, bytes_accessed=points * 40, transcendentals=0
        ),
    )(base, center, edge, eta_shift, cells, *extra)

def row_edges(fields):
    size = lax.axis_size("band")
    up = [(i, (i + 1) % size) for i in range(size - 1)]
    down = [(j, i) for i, j in up]
    rows = fields.shape[2]
    before = lax.ppermute(fields[:, :, rows - HALO :], "band", up)
    after = lax.ppermute(fields[:, :, :HALO], "band", down)
    return jnp.concatenate([after, before], axis=2)


def level_edges(array):
    size, count = (lax.axis_size("lev"), array.shape[0])
    last, first = (array[count - HALO :], array[:HALO])
    if size == 2:
        at_top = lax.axis_index("lev") == 0
        found = lax.ppermute(jnp.where(at_top, last, first), "lev", [(0, 1), (1, 0)])
        nothing = jnp.zeros_like(found)
        return jnp.where(at_top, nothing, found), jnp.where(at_top, found, nothing)
    up = [(i, i + 1) for i in range(size - 1)]
    down = [(j, i) for i, j in up]
    return lax.ppermute(last, "lev", up), lax.ppermute(first, "lev", down)


def with_edges(fields):
    rows = fields.shape[2]
    edge = row_edges(fields)
    before, after = level_edges(jnp.concatenate([fields, edge], axis=2))
    center = jnp.concatenate([before[:, :, :rows], fields, after[:, :, :rows]], axis=0)
    edge = jnp.concatenate([before[:, :, rows:], edge, after[:, :, rows:]], axis=0)
    return center.astype(jnp.float32), edge.astype(jnp.float32)


def split_halves(spectra, pairing):
    width = spectra.shape[-1]
    columns = lax.broadcasted_iota(jnp.int32, (pairing.shape[0], width), 1)
    first_part = columns < (width - 1 - pairing)[:, None]
    nothing = jnp.zeros((), spectra.dtype)
    return jnp.stack(
        [jnp.where(first_part, spectra, nothing), jnp.where(first_part, nothing, spectra)]
    )


def synthesis(pair_ids, lon_ids, lon_total):
    orders = jnp.stack([pair_ids, M - 1 - pair_ids])
    phase = (orders[:, :, None] * lon_ids[None, None, :] % lon_total).astype(jnp.float32) * (
        2.0 * math.pi / lon_total
    )
    weight = jnp.where(orders == 0, 1.0, 2.0).astype(jnp.float32)[:, :, None]
    return jnp.stack([weight * jnp.cos(phase), -weight * jnp.sin(phase)]).astype(jnp.bfloat16)


def legendre_rows(table, halves):
    return jnp.einsum(
        "scpk,hrfpk->cpsfhr", table, halves, preferred_element_type=jnp.float32
    ).astype(jnp.bfloat16)


def per_device(spectra, legendre, pairing, eta_shift, cells):
    grid_shape = eta_shift.shape
    row_count = grid_shape[1]
    halves = split_halves(spectra, pairing)
    result = legendre_rows(lax.all_gather(legendre, "lev", axis=0, tiled=True), halves)
    local_sums = result.reshape(result.shape[0], result.shape[1], -1)
    spectral = lax.all_to_all(local_sums, "band", split_axis=0, concat_axis=1, tiled=True)
    all_pairs = lax.all_gather(pairing, "band", axis=0, tiled=True)
    field_count = 4 * grid_shape[0]
    spectral = spectral.reshape(all_pairs.shape[0], row_count, field_count, 2, 2)
    lon_total = grid_shape[2]
    lon_half = lon_total // 2
    pieces = []
    for lon_part in range(2):
        lon_block = lon_part * lon_half + jnp.arange(lon_half, dtype=jnp.int32)
        basis = synthesis(all_pairs, lon_block, lon_total)
        pieces.append(
            jnp.einsum(
                "psfhr,rhpj->fsj", spectral, basis, preferred_element_type=jnp.float32
            ).astype(jnp.bfloat16)
        )
    grid = jnp.concatenate(pieces, axis=2)
    fields = grid.reshape(grid_shape[0], 4, grid_shape[1], lon_total)
    base = jnp.stack(
        [
            lax.axis_index("lev") * grid_shape[0],
            lax.axis_index("band") * grid_shape[1],
        ]
    ).astype(jnp.int32)
    winds = with_edges(fields[:, :2])
    tracers = with_edges(fields[:, 2:])
    displacement = interpolation_call(
        wind_kernel, base, *winds, eta_shift, cells, (), jnp.float32
    )
    advected = interpolation_call(
        tracer_kernel, base, *tracers, eta_shift, cells, (displacement,), jnp.bfloat16
    )
    return advected, displacement


def solution(mesh):
    return jax.shard_map(
        per_device,
        mesh=mesh,
        in_specs=(
            P(None, "lev", "band", None),
            P("lev", None, "band", None),
            P("band"),
            P("lev", "band", None),
            P(None, "lev", "band", None),
        ),
        out_specs=(P(None, "lev", "band", None), P(None, "lev", "band", None)),
        check_vma=False,
    )
```

```python
import functools
import math

import jax
import jax.numpy as jnp
import numpy as np
from jax import lax
from jax.experimental import pallas as pl
from jax.experimental.pallas import tpu as pltpu
from jax.sharding import PartitionSpec as P

ITERS = 2


COURANT = 0.8
HALO = 2
LANES = 128
ROWS = 8
SLOTS = (-1, 0, 1, 2)


def slot_weights(place, here, low, high, sixth):
    z = jnp.minimum(jnp.maximum(place, low), high)
    square = z * z
    less = square - 1.0
    outer = less * z * sixth
    triple = 3.0 * outer
    half = 0.5 * z
    half_square = 0.5 * square
    return (
        half_square - half - jnp.where(here, outer, triple),
        triple - less,
        half_square + half - jnp.where(here, triple, outer),
        outer,
    )


def bounds(here):
    return (
        jnp.where(here, -0.5, -1.5),
        jnp.where(here, 1.5, 0.5),
        jnp.where(here, 1.0 / 6.0, -1.0 / 6.0),
    )


def weighted(weights, values):
    return (weights[0] * values[0] + weights[1] * values[1]) + (
        weights[2] * values[2] + weights[3] * values[3]
    )


def shifted_lanes(before, here, after, lane):
    return (
        jnp.where(lane < 2, pltpu.roll(before, 2, 1), pltpu.roll(here, 2, 1)),
        jnp.where(lane < 1, pltpu.roll(before, 1, 1), pltpu.roll(here, 1, 1)),
        here,
        jnp.where(lane < LANES - 1, pltpu.roll(here, LANES - 1, 1), pltpu.roll(after, LANES - 1, 1)),
        jnp.where(lane < LANES - 2, pltpu.roll(here, LANES - 2, 1), pltpu.roll(after, LANES - 2, 1)),
    )


def fill(slab, chunk, chunk_total, center_ref, edge_ref, scratch):
    field_count, _, rows, _ = center_ref.shape
    before = jnp.where(chunk == 0, chunk_total - 1, chunk - 1)
    after = jnp.where(chunk == chunk_total - 1, 0, chunk + 1)
    starts = [pl.multiple_of(c * LANES, LANES) for c in (before, chunk, after)]
    lane = lax.broadcasted_iota(jnp.int32, (rows, LANES), 1)
    edge_lane = lax.broadcasted_iota(jnp.int32, (2 * HALO, LANES), 1)
    tall = 3 * rows
    first = pl.multiple_of(slab * (5 * tall), 8)
    for field in range(field_count):
        blocks = [center_ref[field, slab, :, pl.ds(s, LANES)] for s in starts]
        for step, moved in enumerate(shifted_lanes(*blocks, lane)):
            scratch[field, pl.ds(first + (step * tall + rows), rows), :] = moved
        edges = [edge_ref[field, slab, :, pl.ds(s, LANES)] for s in starts]
        for step, moved in enumerate(shifted_lanes(*edges, edge_lane)):
            top = first + (step * tall + rows - 2 * HALO)
            scratch[field, pl.ds(top, 2 * HALO), :] = moved
            scratch[field, pl.ds(first + (step * tall + 2 * rows), 2 * HALO), :] = moved


def level_sums(scratch, field, base, rows, slot, points):
    tall = 3 * rows
    loaded = {}

    def load(a, b, c):
        if (a, b, c) not in loaded:
            offset = ((a + HALO) * 5 + c + HALO) * tall + rows + b
            loaded[a, b, c] = scratch[field, pl.ds(base + offset, rows), :]
        return loaded[a, b, c]

    def one(step, weights, level_here, row_here, lon_here):
        def pick_lon(a, b):
            if slot[1] == 2:
                return jnp.where(lon_here, load(a + step, b, 2), load(a + step, b, -2))
            return load(a + step, b, slot[1])

        def pick(a):
            if slot[0] == 2:
                return jnp.where(row_here, pick_lon(a, 2), pick_lon(a, -2))
            return pick_lon(a, slot[0])

        total = weights[0] * pick(-1) + weights[1] * pick(0)
        total = total + weights[2] * pick(1)
        return total + weights[3] * jnp.where(level_here, pick(2), pick(-2))

    return [one(step, *point) for step, point in enumerate(points)]


def across(sums, row_weights, lon_weights):
    return weighted(
        lon_weights, [weighted(row_weights, [sums[b, c] for b in SLOTS]) for c in SLOTS]
    )


def arrival(base_ref, eta_ref, cells_ref, k, chunk, lanes):
    shape = (cells_ref.shape[2], LANES)
    level_here = cells_ref[2, k, :, lanes] == base_ref[0] + k
    row_here = cells_ref[0, k, :, lanes] == base_ref[1] + lax.broadcasted_iota(jnp.int32, shape, 0)
    lon_here = cells_ref[1, k, :, lanes] == chunk * LANES + lax.broadcasted_iota(
        jnp.int32, shape, 1
    )
    weights = slot_weights(
        -eta_ref[k, :, lanes].astype(jnp.float32), level_here, *bounds(level_here)
    )
    return weights, level_here, row_here, lon_here


def wind_levels(base, lanes, k, points, scratch, out_ref):
    rows = out_ref.shape[2]
    for step, point in enumerate(points):
        here = base + step * (15 * rows)
        sums = [
            {
                (b, c): level_sums(scratch, field, here, rows, (b, c), [point])[0]
                for c in SLOTS
                for b in SLOTS
            }
            for field in range(2)
        ]
        middle = (HALO * 5 + HALO) * 3 * rows + rows
        east = scratch[0, pl.ds(here + middle, rows), :]
        north = scratch[1, pl.ds(here + middle, rows), :]
        _, _, row_here, lon_here = point
        row_bounds, lon_bounds = bounds(row_here), bounds(lon_here)
        shift_row = COURANT * north
        shift_lon = COURANT * east
        for sweep in range(ITERS):
            row_weights = slot_weights(-shift_row, row_here, *row_bounds)
            lon_weights = slot_weights(-shift_lon, lon_here, *lon_bounds)
            east_found = across(sums[0], row_weights, lon_weights)
            north_found = across(sums[1], row_weights, lon_weights)
            shift_row = 0.5 * COURANT * (north + north_found)
            shift_lon = 0.5 * COURANT * (east + east_found)
        out_ref[0, k + step, :, lanes] = shift_row
        out_ref[1, k + step, :, lanes] = shift_lon


def tracer_levels(shift_ref, base, lanes, k, points, scratch, out_ref):
    rows = out_ref.shape[2]
    row_weights = []
    lon_weights = []
    for step, (_, _, row_here, lon_here) in enumerate(points):
        row_weights.append(
            slot_weights(-shift_ref[0, k + step, :, lanes], row_here, *bounds(row_here))
        )
        lon_weights.append(
            slot_weights(-shift_ref[1, k + step, :, lanes], lon_here, *bounds(lon_here))
        )
    for field in range(2):
        totals = [None] * len(points)
        for c, lon_slot in enumerate(SLOTS):
            columns = [None] * len(points)
            for b, row_slot in enumerate(SLOTS):
                found = level_sums(scratch, field, base, rows, (row_slot, lon_slot), points)
                for step, value in enumerate(found):
                    term = row_weights[step][b] * value
                    columns[step] = term if b == 0 else columns[step] + term
            for step, column in enumerate(columns):
                term = lon_weights[step][c] * column
                totals[step] = term if c == 0 else totals[step] + term
        for step, total in enumerate(totals):
            out_ref[field, k + step, :, lanes] = total.astype(out_ref.dtype)


def interpolation_kernel(
    levels_body, base_ref, center_ref, edge_ref, eta_ref, cells_ref, *others
):
    extra, (out_ref, even_scratch, odd_scratch) = others[:-3], others[-3:]
    levels, rows, lon_total = eta_ref.shape
    chunk_total = lon_total // LANES
    slabs = levels + 2 * HALO
    together = 2 if levels % 2 == 0 and slabs % (levels // 2) == 0 else 1
    steps = levels // together
    per_step = -(-slabs // steps)
    source = (center_ref, edge_ref)

    def first_fill(slab, carry):
        fill(slab, 0, chunk_total, *source, even_scratch)
        return carry

    lax.fori_loop(0, slabs, first_fill, 0)

    def one_chunk(chunk, scratch, other):
        lanes = pl.ds(pl.multiple_of(chunk * LANES, LANES), LANES)
        following = jnp.where(chunk == chunk_total - 1, 0, chunk + 1)

        def level_step(step, carry):
            k = step * together
            for n in range(per_step):
                slab = jnp.minimum(step * per_step + n, slabs - 1)
                fill(slab, following, chunk_total, *source, other)
            points = [
                arrival(base_ref, eta_ref, cells_ref, k + n, chunk, lanes) for n in range(together)
            ]
            levels_body(*extra, k * (15 * rows), lanes, k, points, scratch, out_ref)
            return carry

        lax.fori_loop(0, steps, level_step, 0)

    def chunk_pair(pair, carry):
        one_chunk(2 * pair, even_scratch, odd_scratch)
        one_chunk(2 * pair + 1, odd_scratch, even_scratch)
        return carry

    lax.fori_loop(0, chunk_total // 2, chunk_pair, 0)


def interpolation_call(levels_body, base, center, edge, eta_shift, cells, extra, out_dtype):
    levels, rows, lon_total = eta_shift.shape
    points = levels * rows * lon_total
    scratch = pltpu.VMEM((2, (levels + 2 * HALO) * 15 * rows, LANES), jnp.float32)
    in_vmem = pl.BlockSpec(memory_space=pltpu.VMEM)
    return pl.pallas_call(
        functools.partial(interpolation_kernel, levels_body),
        out_shape=jax.ShapeDtypeStruct((2, levels, rows, lon_total), out_dtype),
        in_specs=[pl.BlockSpec(memory_space=pltpu.SMEM)] + [in_vmem] * (4 + len(extra)),
        out_specs=in_vmem,
        scratch_shapes=[scratch, scratch],
        compiler_params=pltpu.CompilerParams(vmem_limit_bytes=32 * 1024 * 1024),
        cost_estimate=pl.CostEstimate(
            flops=points * 500, bytes_accessed=points * 40, transcendentals=0
        ),
    )(base, center, edge, eta_shift, cells, *extra)


def row_edges(fields):
    size = lax.axis_size("band")
    up = [(i, (i + 1) % size) for i in range(size - 1)]
    down = [(j, i) for i, j in up]
    rows = fields.shape[2]
    before = lax.ppermute(fields[:, :, rows - HALO :].astype(jnp.bfloat16), "band", up)
    after = lax.ppermute(fields[:, :, :HALO].astype(jnp.bfloat16), "band", down)
    return jnp.concatenate([after, before], axis=2)


def level_edges(array):
    size, count = (lax.axis_size("lev"), array.shape[1])
    last, first = (array[:, count - HALO :], array[:, :HALO])
    if size == 2:
        at_top = lax.axis_index("lev") == 0
        found = lax.ppermute(jnp.where(at_top, last, first), "lev", [(0, 1), (1, 0)])
        nothing = jnp.zeros_like(found)
        return jnp.where(at_top, nothing, found), jnp.where(at_top, found, nothing)
    up = [(i, i + 1) for i in range(size - 1)]
    down = [(j, i) for i, j in up]
    return lax.ppermute(last, "lev", up), lax.ppermute(first, "lev", down)


def with_edges(fields):
    rows = fields.shape[2]
    edge = row_edges(fields)
    both = jnp.concatenate([fields.astype(jnp.bfloat16), edge], axis=2)
    before, after = level_edges(both)
    center = jnp.concatenate(
        [
            before[:, :, :rows].astype(jnp.float32),
            fields,
            after[:, :, :rows].astype(jnp.float32),
        ],
        axis=1,
    )
    edge = jnp.concatenate([before[:, :, rows:], edge, after[:, :, rows:]], axis=1)
    return center, edge.astype(jnp.float32)


def up_to(value, step):
    return -(-value // step) * step


def legendre_kernel(pairing_ref, spectra_ref, table_ref, out_ref, columns, rows_here):
    _, level_fields, pairs, degrees = spectra_ref.shape
    bands = table_ref.shape[1]
    levels = level_fields // 4
    order = degrees - 1
    padded = columns.shape[1] // (2 * level_fields)
    blocks = columns.shape[0]
    full = degrees // LANES
    columns[blocks - 1] = jnp.zeros(columns.shape[1:], jnp.float32)
    rows_here[blocks - 1] = jnp.zeros(rows_here.shape[1:], jnp.float32)

    def spread(block, target, position):
        first = pl.multiple_of(position * padded, 8)
        for t in range(full):
            piece = block[:, t * LANES : (t + 1) * LANES].astype(jnp.float32)
            target[t, pl.ds(first, pairs), :] = piece
        rest = degrees - full * LANES
        if rest:
            piece = block[:, full * LANES :].astype(jnp.float32)
            target[full, pl.ds(first, pairs), :rest] = piece

    def spectra_step(level, carry):
        for part in range(2):
            for field in range(4):
                position = part * level_fields + field * levels + level
                spread(spectra_ref[part, 4 * level + field], columns, position)
        return carry

    def table_step(band, carry):
        for row in range(ROWS):
            spread(table_ref[row, band], rows_here, band * ROWS + row)
        return carry

    lax.fori_loop(0, levels, spectra_step, 0)
    lax.fori_loop(0, bands, table_step, 0)
    count = 2 * level_fields
    width = out_ref.shape[3]
    if width > 2 * count:
        out_ref[...] = jnp.zeros(out_ref.shape, out_ref.dtype)

    def pair_step(p, carry):
        edge = order - pairing_ref[p]
        left = []
        first_half = []
        second_half = []
        for t in range(blocks):
            left.append(rows_here[t, pl.ds(p, bands * ROWS, stride=padded), :].astype(jnp.bfloat16))
            block = columns[t, pl.ds(p, count, stride=padded), :]
            lane = lax.broadcasted_iota(jnp.int32, block.shape, 1) + t * LANES
            zero = jnp.zeros_like(block)
            first_half.append(jnp.where(lane < edge, block, zero).astype(jnp.bfloat16))
            second_half.append(jnp.where(lane < edge, zero, block).astype(jnp.bfloat16))
        halves = jnp.concatenate(
            [jnp.concatenate(first_half, axis=1), jnp.concatenate(second_half, axis=1)], axis=0
        )
        sums = lax.dot_general(
            jnp.concatenate(left, axis=1),
            halves,
            (((1,), (1,)), ((), ())),
            preferred_element_type=jnp.float32,
        )
        sums = sums.astype(jnp.bfloat16).reshape(bands, ROWS, 2 * count)
        out_ref[:, p, :, : 2 * count] = sums
        return carry

    lax.fori_loop(0, pairs, pair_step, 0)


def legendre_call(pairing, spectra, table):
    _, level_fields, pairs, degrees = spectra.shape
    bands = table.shape[1]
    padded = up_to(pairs, 8)
    blocks = up_to(degrees, LANES) // LANES
    width = up_to(4 * level_fields, LANES)
    in_vmem = pl.BlockSpec(memory_space=pltpu.VMEM)
    return pl.pallas_call(
        legendre_kernel,
        out_shape=jax.ShapeDtypeStruct((bands, pairs, ROWS, width), jnp.bfloat16),
        in_specs=[pl.BlockSpec(memory_space=pltpu.SMEM), in_vmem, in_vmem],
        out_specs=in_vmem,
        scratch_shapes=[
            pltpu.VMEM((blocks, 2 * level_fields * padded, LANES), jnp.float32),
            pltpu.VMEM((blocks, ROWS * bands * padded, LANES), jnp.float32),
        ],
        compiler_params=pltpu.CompilerParams(vmem_limit_bytes=48 * 1024 * 1024),
        cost_estimate=pl.CostEstimate(
            flops=2 * ROWS * bands * 4 * level_fields * pairs * degrees,
            bytes_accessed=8_000_000,
            transcendentals=0,
        ),
    )(pairing, spectra, table)


def fourier_table(pair_total, padded, lon_total):
    order_total = 2 * pair_total
    half = pair_total // 2
    low = 2 * np.arange(half)
    high = low + 1
    even = np.concatenate([low, order_total - 1 - high])
    odd = np.concatenate([order_total - 1 - low, high])
    lon = np.arange(lon_total // 2)
    table = np.zeros((2, 2, padded, lon_total // 2), np.float32)
    for parity, orders in enumerate((even, odd)):
        phase = (orders[:, None] * lon[None, :]) % lon_total * (2.0 * math.pi / lon_total)
        weight = np.where(orders == 0, 1.0, 2.0)[:, None]
        table[parity, 0, :pair_total] = weight * np.cos(phase)
        table[parity, 1, :pair_total] = -weight * np.sin(phase)
    return table.reshape(2, 2 * padded, lon_total // 2).astype(jnp.bfloat16)


def fourier_kernel(level_fields, sums_ref, place_ref, table_ref, wind_ref, tracer_ref, flat, lhs):
    pair_total, rows, width = sums_ref.shape
    padded = place_ref.shape[0]
    blocks = padded // LANES
    flat[...] = sums_ref[...].astype(jnp.float32).reshape(pair_total * rows, width)
    low = lax.broadcasted_iota(jnp.int32, (level_fields, padded), 1) < pair_total // 2
    for row in range(rows):
        here = flat[pl.ds(row, pair_total, stride=rows), :].astype(jnp.bfloat16)
        ordered = jnp.dot(place_ref[...], here, preferred_element_type=jnp.float32).T
        for part in range(2):
            start = part * level_fields
            straight = ordered[start : start + level_fields]
            start = start + 2 * level_fields
            crossed = ordered[start : start + level_fields]
            both = (jnp.where(low, straight, crossed), jnp.where(low, crossed, straight))
            for parity in range(2):
                for t in range(blocks):
                    lhs[parity, part * blocks + t, pl.ds(row, level_fields, stride=rows), :] = both[
                        parity
                    ][:, t * LANES : (t + 1) * LANES]
    half = table_ref.shape[2]
    group = level_fields * rows // 2
    for number, out_ref in enumerate((wind_ref, tracer_ref)):
        found = []
        for parity in range(2):
            left = jnp.concatenate(
                [
                    lhs[parity, t, number * group : (number + 1) * group, :].astype(jnp.bfloat16)
                    for t in range(2 * blocks)
                ],
                axis=1,
            )
            found.append(jnp.dot(left, table_ref[parity], preferred_element_type=jnp.float32))
        shape = out_ref.shape[:3] + (half,)
        for part, value in enumerate((found[0] + found[1], found[0] - found[1])):
            value = value.astype(jnp.bfloat16).astype(jnp.float32).reshape(shape)
            out_ref[:, :, :, part * half : (part + 1) * half] = value


def fourier_call(sums, place, lon_total, level_fields):
    pair_total, rows, width = sums.shape
    padded = place.shape[0]
    table = jnp.asarray(fourier_table(pair_total, padded, lon_total))
    shape = jax.ShapeDtypeStruct((2, level_fields // 4, rows, lon_total), jnp.float32)
    in_vmem = pl.BlockSpec(memory_space=pltpu.VMEM)
    return pl.pallas_call(
        functools.partial(fourier_kernel, level_fields),
        out_shape=(shape, shape),
        in_specs=[in_vmem, in_vmem, in_vmem],
        out_specs=(in_vmem, in_vmem),
        scratch_shapes=[
            pltpu.VMEM((pair_total * rows, width), jnp.float32),
            pltpu.VMEM((2, 2 * padded // LANES, level_fields * rows, LANES), jnp.float32),
        ],
        compiler_params=pltpu.CompilerParams(vmem_limit_bytes=48 * 1024 * 1024),
        cost_estimate=pl.CostEstimate(
            flops=4 * level_fields * rows * padded * lon_total,
            bytes_accessed=8_000_000,
            transcendentals=0,
        ),
    )(sums, place, table)


def pair_places(pairing, padded):
    count = pairing.shape[0]
    row = jnp.pad(pairing, (0, up_to(count, LANES) - count))
    tile = jnp.broadcast_to(row[None, None, :], (1, 8) + row.shape)
    orders = lax.all_gather(tile, "band", axis=0, tiled=True)[:, 0, :count].reshape(-1)
    half = orders.shape[0] // 2
    place = orders // 2 + jnp.where(orders % 2 == 0, 0, half)
    return place[None, :] == lax.broadcasted_iota(jnp.int32, (padded, orders.shape[0]), 0)


def per_device(spectra, legendre, pairing, eta_shift, cells):
    levels, rows, lon_total = eta_shift.shape
    pair_total = pairing.shape[0] * lax.axis_size("band")
    place = pair_places(pairing, up_to(pair_total, LANES)).astype(jnp.bfloat16)
    table = lax.all_gather(legendre, "lev", axis=0, tiled=True)
    sums = legendre_call(pairing, spectra, table)
    sums = lax.all_to_all(sums, "band", split_axis=0, concat_axis=0, tiled=True)
    sums = sums.reshape((pair_total,) + sums.shape[2:])
    winds, tracers = fourier_call(sums, place, lon_total, 4 * levels)
    base = jnp.stack([lax.axis_index("lev") * levels, lax.axis_index("band") * rows])
    base = base.astype(jnp.int32)
    displacement = interpolation_call(
        wind_levels, base, *with_edges(winds), eta_shift, cells, (), jnp.float32
    )
    advected = interpolation_call(
        tracer_levels,
        base,
        *with_edges(tracers),
        eta_shift,
        cells,
        (displacement,),
        jnp.bfloat16,
    )
    return advected, displacement


def solution(mesh):
    return jax.shard_map(
        per_device,
        mesh=mesh,
        in_specs=(
            P(None, "lev", "band", None),
            P("lev", None, "band", None),
            P("band"),
            P("lev", "band", None),
            P(None, "lev", "band", None),
        ),
        out_specs=(P(None, "lev", "band", None), P(None, "lev", "band", None)),
        check_vma=False,
    )
```

```python
import functools
import math

import jax
import jax.numpy as jnp
import numpy as np
from jax import lax
from jax.experimental import pallas as pl
from jax.experimental.pallas import tpu as pltpu
from jax.sharding import PartitionSpec as P

ITERS = 2


COURANT = 0.8
HALO = 2
LANES = 128
ROWS = 8
SLOTS = (-1, 0, 1, 2)


def slot_weights(place, here, low, high, sixth):
    z = jnp.minimum(jnp.maximum(place, low), high)
    square = z * z
    less = square - 1.0
    outer = less * z * sixth
    triple = 3.0 * outer
    half = 0.5 * z
    half_square = 0.5 * square
    return (
        half_square - half - jnp.where(here, outer, triple),
        triple - less,
        half_square + half - jnp.where(here, triple, outer),
        outer,
    )


def bounds(here):
    return (
        jnp.where(here, -0.5, -1.5),
        jnp.where(here, 1.5, 0.5),
        jnp.where(here, 1.0 / 6.0, -1.0 / 6.0),
    )


def weighted(weights, values):
    return (weights[0] * values[0] + weights[1] * values[1]) + (
        weights[2] * values[2] + weights[3] * values[3]
    )


def shifted_lanes(before, here, after, lane):
    return (
        jnp.where(lane < 2, pltpu.roll(before, 2, 1), pltpu.roll(here, 2, 1)),
        jnp.where(lane < 1, pltpu.roll(before, 1, 1), pltpu.roll(here, 1, 1)),
        here,
        jnp.where(lane < LANES - 1, pltpu.roll(here, LANES - 1, 1), pltpu.roll(after, LANES - 1, 1)),
        jnp.where(lane < LANES - 2, pltpu.roll(here, LANES - 2, 1), pltpu.roll(after, LANES - 2, 1)),
    )


def fill_units(slab, chunk, chunk_total, center_ref, edge_ref, scratch):
    _, field_count, rows, _ = center_ref.shape
    before = jnp.where(chunk == 0, chunk_total - 1, chunk - 1)
    after = jnp.where(chunk == chunk_total - 1, 0, chunk + 1)
    starts = [pl.multiple_of(c * LANES, LANES) for c in (before, chunk, after)]
    lane = lax.broadcasted_iota(jnp.int32, (rows, LANES), 1)
    tall = 3 * rows
    first = slab * (5 * tall)

    def edge_start():
        return shifted_lanes(*[edge_ref[slab, :, pl.ds(s, LANES)] for s in starts], lane)

    def edge_finish(values):
        for step, moved in enumerate(values):
            for field, offset in ((0, rows // 2), (0, 2 * rows), (1, 0), (1, rows + rows // 2)):
                scratch[field, pl.ds(first + (step * tall + offset), rows), :] = moved

    def center_unit(field):
        def start():
            blocks = [center_ref[slab, field, :, pl.ds(s, LANES)] for s in starts]
            return shifted_lanes(*blocks, lane)

        def finish(values):
            for step, moved in enumerate(values):
                scratch[field, pl.ds(first + (step * tall + rows), rows), :] = moved

        return start, finish

    return [(edge_start, edge_finish)] + [center_unit(field) for field in range(field_count)]


class Interleave:
    def __init__(self, units, ticks):
        self.units = list(units)
        self.every = max(1, ticks // max(1, len(self.units)))
        self.count = 0
        self.pending = None

    def advance(self):
        if self.pending is not None:
            self.pending[0](self.pending[1])
            self.pending = None
        if self.units:
            start, finish = self.units.pop(0)
            self.pending = (finish, start())

    def tick(self):
        if self.count % self.every == 0:
            self.advance()
        self.count += 1

    def flush(self):
        while self.units or self.pending is not None:
            self.advance()


def level_sums(scratch, field, base, rows, slot, points):
    tall = 3 * rows
    loaded = {}

    def load(a, b, c):
        if (a, b, c) not in loaded:
            offset = ((a + HALO) * 5 + c + HALO) * tall + rows + b
            loaded[a, b, c] = scratch[field, pl.ds(base + offset, rows), :]
        return loaded[a, b, c]

    def one(step, weights, level_here, row_here, lon_here):
        def pick_lon(a, b):
            if slot[1] == 2:
                return jnp.where(lon_here, load(a + step, b, 2), load(a + step, b, -2))
            return load(a + step, b, slot[1])

        def pick(a):
            if slot[0] == 2:
                return jnp.where(row_here, pick_lon(a, 2), pick_lon(a, -2))
            return pick_lon(a, slot[0])

        total = weights[0] * pick(-1) + weights[1] * pick(0)
        total = total + weights[2] * pick(1)
        return total + weights[3] * jnp.where(level_here, pick(2), pick(-2))

    return [one(step, *point) for step, point in enumerate(points)]


def across(sums, row_weights, lon_weights):
    return weighted(
        lon_weights, [weighted(row_weights, [sums[b, c] for b in SLOTS]) for c in SLOTS]
    )


def arrival(base_ref, eta_ref, cells_ref, k, chunk, lanes):
    shape = (cells_ref.shape[2], LANES)
    level_here = cells_ref[2, k, :, lanes] == base_ref[0] + k
    row_here = cells_ref[0, k, :, lanes] == base_ref[1] + lax.broadcasted_iota(jnp.int32, shape, 0)
    lon_here = cells_ref[1, k, :, lanes] == chunk * LANES + lax.broadcasted_iota(
        jnp.int32, shape, 1
    )
    weights = slot_weights(
        -eta_ref[k, :, lanes].astype(jnp.float32), level_here, *bounds(level_here)
    )
    return weights, level_here, row_here, lon_here


def wind_levels(base, lanes, k, points, scratch, filling, out_ref):
    rows = out_ref.shape[2]
    for step, point in enumerate(points):
        here = base + step * (15 * rows)
        sums = [{}, {}]
        for field in range(2):
            for c in SLOTS:
                for b in SLOTS:
                    filling.tick()
                    found = level_sums(scratch, field, here, rows, (b, c), [point])
                    sums[field][b, c] = found[0]
        middle = (HALO * 5 + HALO) * 3 * rows + rows
        east = scratch[0, pl.ds(here + middle, rows), :]
        north = scratch[1, pl.ds(here + middle, rows), :]
        _, _, row_here, lon_here = point
        row_bounds, lon_bounds = bounds(row_here), bounds(lon_here)
        shift_row = COURANT * north
        shift_lon = COURANT * east
        for sweep in range(ITERS):
            row_weights = slot_weights(-shift_row, row_here, *row_bounds)
            lon_weights = slot_weights(-shift_lon, lon_here, *lon_bounds)
            east_found = across(sums[0], row_weights, lon_weights)
            north_found = across(sums[1], row_weights, lon_weights)
            shift_row = 0.5 * COURANT * (north + north_found)
            shift_lon = 0.5 * COURANT * (east + east_found)
        out_ref[0, k + step, :, lanes] = shift_row
        out_ref[1, k + step, :, lanes] = shift_lon


def tracer_levels(shift_ref, base, lanes, k, points, scratch, filling, out_ref):
    rows = out_ref.shape[2]
    row_weights = []
    lon_weights = []
    for step, (_, _, row_here, lon_here) in enumerate(points):
        row_weights.append(
            slot_weights(-shift_ref[0, k + step, :, lanes], row_here, *bounds(row_here))
        )
        lon_weights.append(
            slot_weights(-shift_ref[1, k + step, :, lanes], lon_here, *bounds(lon_here))
        )
    for field in range(2):
        totals = [None] * len(points)
        for c, lon_slot in enumerate(SLOTS):
            columns = [None] * len(points)
            for b, row_slot in enumerate(SLOTS):
                filling.tick()
                found = level_sums(scratch, field, base, rows, (row_slot, lon_slot), points)
                for step, value in enumerate(found):
                    term = row_weights[step][b] * value
                    columns[step] = term if b == 0 else columns[step] + term
            for step, column in enumerate(columns):
                term = lon_weights[step][c] * column
                totals[step] = term if c == 0 else totals[step] + term
        for step, total in enumerate(totals):
            out_ref[field, k + step, :, lanes] = total.astype(out_ref.dtype)


def interpolation_kernel(
    levels_body, base_ref, center_ref, edge_ref, eta_ref, cells_ref, *others
):
    extra, (out_ref, even_scratch, odd_scratch) = others[:-3], others[-3:]
    levels, rows, lon_total = eta_ref.shape
    chunk_total = lon_total // LANES
    slabs = levels + 2 * HALO
    together = 2 if levels % 2 == 0 and slabs % (levels // 2) == 0 else 1
    steps = levels // together
    per_step = -(-slabs // steps)
    source = (center_ref, edge_ref)

    def first_fill(slab, carry):
        for start, finish in fill_units(slab, 0, chunk_total, *source, even_scratch):
            finish(start())
        return carry

    lax.fori_loop(0, slabs, first_fill, 0)

    def one_chunk(chunk, scratch, other):
        lanes = pl.ds(pl.multiple_of(chunk * LANES, LANES), LANES)
        following = jnp.where(chunk == chunk_total - 1, 0, chunk + 1)

        def level_step(step, carry):
            k = step * together
            units = []
            for n in range(per_step):
                slab = jnp.minimum(step * per_step + n, slabs - 1)
                units += fill_units(slab, following, chunk_total, *source, other)
            filling = Interleave(units, 32)
            points = [
                arrival(base_ref, eta_ref, cells_ref, k + n, chunk, lanes) for n in range(together)
            ]
            levels_body(*extra, k * (15 * rows), lanes, k, points, scratch, filling, out_ref)
            filling.flush()
            return carry

        lax.fori_loop(0, steps, level_step, 0)

    def chunk_pair(pair, carry):
        one_chunk(2 * pair, even_scratch, odd_scratch)
        one_chunk(2 * pair + 1, odd_scratch, even_scratch)
        return carry

    lax.fori_loop(0, chunk_total // 2, chunk_pair, 0)


def interpolation_call(levels_body, base, center, edge, eta_shift, cells, extra, out_dtype):
    levels, rows, lon_total = eta_shift.shape
    points = levels * rows * lon_total
    scratch = pltpu.VMEM((2, (levels + 2 * HALO) * 15 * rows, LANES), jnp.float32)
    in_vmem = pl.BlockSpec(memory_space=pltpu.VMEM)
    return pl.pallas_call(
        functools.partial(interpolation_kernel, levels_body),
        out_shape=jax.ShapeDtypeStruct((2, levels, rows, lon_total), out_dtype),
        in_specs=[pl.BlockSpec(memory_space=pltpu.SMEM)] + [in_vmem] * (4 + len(extra)),
        out_specs=in_vmem,
        scratch_shapes=[scratch, scratch],
        compiler_params=pltpu.CompilerParams(vmem_limit_bytes=32 * 1024 * 1024),
        cost_estimate=pl.CostEstimate(
            flops=points * 500, bytes_accessed=points * 40, transcendentals=0
        ),
    )(base, center, edge, eta_shift, cells, *extra)


def level_edges(array):
    size, count = (lax.axis_size("lev"), array.shape[0])
    last, first = (array[count - HALO :], array[:HALO])
    if size == 2:
        at_top = lax.axis_index("lev") == 0
        found = lax.ppermute(jnp.where(at_top, last, first), "lev", [(0, 1), (1, 0)])
        nothing = jnp.zeros_like(found)
        return jnp.where(at_top, nothing, found), jnp.where(at_top, found, nothing)
    up = [(i, i + 1) for i in range(size - 1)]
    down = [(j, i) for i, j in up]
    return lax.ppermute(last, "lev", up), lax.ppermute(first, "lev", down)


def with_levels(center, edge):
    levels, field_count, rows, lon_total = center.shape
    flat = center.reshape(levels, field_count * rows, lon_total)
    sides = level_edges(jnp.concatenate([flat, edge], axis=1).astype(jnp.bfloat16))
    before, after = [side.astype(jnp.float32) for side in sides]
    cut = field_count * rows
    flat = jnp.concatenate([before[:, :cut], flat, after[:, :cut]], axis=0)
    edge = jnp.concatenate([before[:, cut:], edge, after[:, cut:]], axis=0)
    return flat.reshape((-1,) + center.shape[1:]), edge


def up_to(value, step):
    return -(-value // step) * step


TALL = ROWS + 2 * HALO
CODE = 16


def legendre_kernel(numbers_ref, codes_ref, spectra_ref, *others):
    tables, (out_ref, sums, table_tail, column_tail) = others[:-4], others[-4:]
    _, pairs, level_fields, degrees = spectra_ref.shape
    bands, block, _ = out_ref.shape
    code_row = block - CODE
    full = degrees // LANES * LANES
    count = 2 * level_fields
    own = numbers_ref[0]
    sums[...] = jnp.zeros(sums.shape, jnp.float32)
    table_tail[...] = jnp.zeros(table_tail.shape, jnp.float32)
    column_tail[...] = jnp.zeros(column_tail.shape, jnp.float32)
    codes = codes_ref[...]
    for band in range(bands):
        first = (band + 1) * block + code_row
        sums[first : first + 1, :] = jnp.right_shift(codes, 4).astype(jnp.float32)
        sums[first + 1 : first + 2, :] = (codes & 15).astype(jnp.float32)

    def pair_step(p, carry):
        edge = degrees - 1 - numbers_ref[1 + p]
        left = []
        for number, table_ref in enumerate(tables):
            for row in range(table_ref.shape[0]):
                piece = table_ref[row, p]
                left.append(piece[:, :full])
                first = (number * table_ref.shape[0] + row) * bands
                table_tail[first : first + bands, : degrees - full] = piece[:, full:].astype(
                    jnp.float32
                )
        left = jnp.concatenate(left, axis=0)
        left = jnp.concatenate([left, table_tail[...].astype(jnp.bfloat16)], axis=1)
        halves = ([], [])
        for part in range(2):
            piece = spectra_ref[part, p]
            whole = piece[:, :full].astype(jnp.float32)
            lane = lax.broadcasted_iota(jnp.int32, whole.shape, 1)
            zero = jnp.zeros_like(whole)
            halves[0].append(jnp.where(lane < edge, whole, zero).astype(jnp.bfloat16))
            halves[1].append(jnp.where(lane < edge, zero, whole).astype(jnp.bfloat16))
            first = part * level_fields
            column_tail[first : first + level_fields, : degrees - full] = piece[:, full:].astype(
                jnp.float32
            )
        tail = column_tail[...].astype(jnp.bfloat16)
        right = jnp.concatenate(
            [
                jnp.concatenate([jnp.concatenate(halves[0], axis=0), jnp.zeros_like(tail)], axis=1),
                jnp.concatenate([jnp.concatenate(halves[1], axis=0), tail], axis=1),
            ],
            axis=0,
        )
        found = lax.dot_general(
            left, right, (((1,), (1,)), ((), ())), preferred_element_type=jnp.float32
        )
        found = [found[i * bands : (i + 1) * bands] for i in range(ROWS)]

        def put(band, row, value):
            start = band * block + p * TALL + row
            sums[pl.ds(start, bands, stride=block), : 2 * count] = value

        if len(tables) == 1:
            ordered = found
            for row in range(ROWS):
                put(1, HALO + row, found[row])
        else:
            part_rows = ROWS // 2
            at_top = own == 0
            for i in range(part_rows):
                put(1, HALO + own * part_rows + i, found[i])
                put(1, HALO + (1 - own) * part_rows + i, found[part_rows + i])
            low, high = found[:part_rows], found[part_rows:]
            ordered = [jnp.where(at_top, x, y) for x, y in zip(low, high)]
            ordered += [jnp.where(at_top, y, x) for x, y in zip(low, high)]
        for i in range(HALO):
            put(0, HALO + ROWS + i, ordered[i])
            put(2, i, ordered[ROWS - HALO + i])
        return carry

    lax.fori_loop(0, pairs, pair_step, 0)
    kept = sums[block : (bands + 1) * block, :]
    out_ref[...] = kept.astype(jnp.bfloat16).reshape(out_ref.shape)


def legendre_call(pairing, spectra, tables):
    _, pairs, level_fields, degrees = spectra.shape
    bands = tables[0].shape[2]
    block = up_to(pairs * TALL, 16) + CODE
    width = up_to(4 * level_fields, LANES)
    numbers = jnp.concatenate([lax.axis_index("lev").astype(jnp.int32)[None], pairing])
    codes = jnp.pad(pairing, (0, width - pairs))[None, :]
    in_vmem = pl.BlockSpec(memory_space=pltpu.VMEM)
    return pl.pallas_call(
        legendre_kernel,
        out_shape=jax.ShapeDtypeStruct((bands, block, width), jnp.bfloat16),
        in_specs=[pl.BlockSpec(memory_space=pltpu.SMEM)] + [in_vmem] * (2 + len(tables)),
        out_specs=in_vmem,
        scratch_shapes=[
            pltpu.VMEM(((bands + 2) * block, width), jnp.float32),
            pltpu.VMEM((ROWS * bands, LANES), jnp.float32),
            pltpu.VMEM((2 * level_fields, LANES), jnp.float32),
        ],
        compiler_params=pltpu.CompilerParams(vmem_limit_bytes=32 * 1024 * 1024),
        cost_estimate=pl.CostEstimate(
            flops=2 * ROWS * bands * 4 * level_fields * pairs * degrees,
            bytes_accessed=8_000_000,
            transcendentals=0,
        ),
    )(numbers, codes, spectra, *tables)


def fourier_table(pair_total, padded, lon_total):
    order_total = 2 * pair_total
    half = pair_total // 2
    low = 2 * np.arange(half)
    high = low + 1
    even = np.concatenate([low, order_total - 1 - high])
    odd = np.concatenate([order_total - 1 - low, high])
    lon = np.arange(lon_total // 2)
    table = np.zeros((2, 2, padded, lon_total // 2), np.float32)
    for parity, orders in enumerate((even, odd)):
        phase = (orders[:, None] * lon[None, :]) % lon_total * (2.0 * math.pi / lon_total)
        weight = np.where(orders == 0, 1.0, 2.0)[:, None]
        table[parity, 0, :pair_total] = weight * np.cos(phase)
        table[parity, 1, :pair_total] = -weight * np.sin(phase)
    return table.reshape(2, 2 * padded, lon_total // 2).astype(jnp.bfloat16)


def owner_tables(bands, pairs):
    slots = np.arange(bands * pairs)
    owner = slots[:, None] // pairs == np.arange(LANES)[None, :]
    lane = slots[:, None] % pairs == np.arange(LANES)[None, :]
    return owner.astype(jnp.bfloat16), lane.astype(np.float32)


def fourier_kernel(level_fields, pairs, sums_ref, owner_ref, lane_ref, table_ref, *others):
    wind_ref, tracer_ref, wind_edge_ref, tracer_edge_ref, flat, codes, gathered, lhs = others
    bands, block, width = sums_ref.shape
    pair_total = bands * pairs
    padded = gathered.shape[0]
    blocks = padded // LANES
    code_row = block - CODE
    flat[...] = sums_ref[...].astype(jnp.float32).reshape(bands * block, width)
    gathered[pair_total:, :] = jnp.zeros((padded - pair_total, width), jnp.float32)
    codes[...] = jnp.zeros(codes.shape, jnp.float32)
    numbers = []
    for part in range(2):
        found = flat[pl.ds(code_row + part, bands, stride=block), :LANES]
        codes[part, :bands, :] = found
        numbers.append(
            jnp.dot(
                owner_ref[...],
                codes[part].astype(jnp.bfloat16),
                preferred_element_type=jnp.float32,
            )
        )
    pair_id = jnp.sum(
        (16.0 * numbers[0] + numbers[1]) * lane_ref[...], axis=1, keepdims=True
    ).astype(jnp.int32)
    place = jnp.right_shift(pair_id, 1) + (pair_id & 1) * (pair_total // 2)
    columns = lax.broadcasted_iota(jnp.int32, (pair_total, padded), 1)
    place = jnp.where(columns == place, 1.0, 0.0)
    if padded > pair_total:
        place = jnp.concatenate(
            [place, jnp.zeros((padded - pair_total, padded), jnp.float32)], axis=0
        )
    place = place.astype(jnp.bfloat16)
    low = lax.broadcasted_iota(jnp.int32, (level_fields, padded), 1) < pair_total // 2
    middle = level_fields * ROWS
    for row in range(TALL):
        for band in range(bands):
            gathered[band * pairs : (band + 1) * pairs, :] = flat[
                pl.ds(band * block + row, pairs, stride=TALL), :
            ]
        ordered = jnp.dot(
            gathered[...].T.astype(jnp.bfloat16), place, preferred_element_type=jnp.float32
        )
        if HALO <= row < HALO + ROWS:
            first, stride = row - HALO, ROWS
        else:
            first, stride = middle + (row - HALO - ROWS) % TALL, 2 * HALO
        for part in range(2):
            start = part * level_fields
            straight = ordered[start : start + level_fields]
            start = start + 2 * level_fields
            crossed = ordered[start : start + level_fields]
            both = (jnp.where(low, straight, crossed), jnp.where(low, crossed, straight))
            for parity in range(2):
                for t in range(blocks):
                    lhs[
                        parity, part * blocks + t, pl.ds(first, level_fields, stride=stride), :
                    ] = both[parity][:, t * LANES : (t + 1) * LANES]
    half = table_ref.shape[2]
    levels = level_fields // 4

    def transform(first, count):
        found = []
        for parity in range(2):
            left = jnp.concatenate(
                [
                    lhs[parity, t, first : first + count, :].astype(jnp.bfloat16)
                    for t in range(2 * blocks)
                ],
                axis=1,
            )
            found.append(jnp.dot(left, table_ref[parity], preferred_element_type=jnp.float32))
        pieces = (found[0] + found[1], found[0] - found[1])
        return [piece.astype(jnp.bfloat16).astype(jnp.float32) for piece in pieces]

    group = 2 if levels % 2 == 0 else 1
    for level in range(0, levels, group):
        pieces = transform(level * 4 * ROWS, group * 4 * ROWS)
        for part, value in enumerate(pieces):
            value = value.reshape(group, 4, ROWS, half)
            lanes = slice(part * half, (part + 1) * half)
            wind_ref[level : level + group, :, :, lanes] = value[:, :2]
            tracer_ref[level : level + group, :, :, lanes] = value[:, 2:]
    for part, value in enumerate(transform(middle, level_fields * 2 * HALO)):
        value = value.reshape(levels, 8 * HALO, half)
        lanes = slice(part * half, (part + 1) * half)
        wind_edge_ref[:, :, lanes] = value[:, : 4 * HALO]
        tracer_edge_ref[:, :, lanes] = value[:, 4 * HALO :]


def fourier_call(sums, pairs, lon_total, level_fields):
    bands, block, width = sums.shape
    pair_total = bands * pairs
    padded = up_to(pair_total, LANES)
    table = jnp.asarray(fourier_table(pair_total, padded, lon_total))
    owner, lane = [jnp.asarray(x) for x in owner_tables(bands, pairs)]
    levels = level_fields // 4
    center = jax.ShapeDtypeStruct((levels, 2, ROWS, lon_total), jnp.float32)
    edge = jax.ShapeDtypeStruct((levels, 4 * HALO, lon_total), jnp.float32)
    in_vmem = pl.BlockSpec(memory_space=pltpu.VMEM)
    return pl.pallas_call(
        functools.partial(fourier_kernel, level_fields, pairs),
        out_shape=(center, center, edge, edge),
        in_specs=[in_vmem] * 4,
        out_specs=(in_vmem,) * 4,
        scratch_shapes=[
            pltpu.VMEM((bands * block, width), jnp.float32),
            pltpu.VMEM((2, LANES, LANES), jnp.float32),
            pltpu.VMEM((padded, width), jnp.float32),
            pltpu.VMEM((2, 2 * padded // LANES, level_fields * TALL, LANES), jnp.float32),
        ],
        compiler_params=pltpu.CompilerParams(vmem_limit_bytes=40 * 1024 * 1024),
        cost_estimate=pl.CostEstimate(
            flops=4 * level_fields * TALL * padded * lon_total,
            bytes_accessed=8_000_000,
            transcendentals=0,
        ),
    )(sums, owner, lane, table)


def per_device(spectra, legendre, pairing, eta_shift, cells):
    levels, rows, lon_total = eta_shift.shape
    spectra = jnp.transpose(spectra, (0, 2, 1, 3))
    table = jnp.transpose(legendre, (0, 2, 1, 3))
    if lax.axis_size("lev") == 2:
        tables = (table, lax.ppermute(table, "lev", [(0, 1), (1, 0)]))
    else:
        tables = (lax.all_gather(table, "lev", axis=0, tiled=True),)
    sums = legendre_call(pairing, spectra, tables)
    sums = lax.all_to_all(sums, "band", split_axis=0, concat_axis=0, tiled=True)
    winds, tracers, wind_edge, tracer_edge = fourier_call(
        sums, pairing.shape[0], lon_total, 4 * levels
    )
    base = jnp.stack([lax.axis_index("lev") * levels, lax.axis_index("band") * rows])
    base = base.astype(jnp.int32)
    displacement = interpolation_call(
        wind_levels, base, *with_levels(winds, wind_edge), eta_shift, cells, (), jnp.float32
    )
    advected = interpolation_call(
        tracer_levels,
        base,
        *with_levels(tracers, tracer_edge),
        eta_shift,
        cells,
        (displacement,),
        jnp.bfloat16,
    )
    return advected, displacement


def solution(mesh):
    return jax.shard_map(
        per_device,
        mesh=mesh,
        in_specs=(
            P(None, "lev", "band", None),
            P("lev", None, "band", None),
            P("band"),
            P("lev", "band", None),
            P(None, "lev", "band", None),
        ),
        out_specs=(P(None, "lev", "band", None), P(None, "lev", "band", None)),
        check_vma=False,
    )
```

```python
import functools
import math

import jax
import jax.numpy as jnp
import numpy as np
from jax import lax
from jax.experimental import pallas as pl
from jax.experimental.pallas import tpu as pltpu
from jax.sharding import PartitionSpec as P

ITERS = 2


COURANT = 0.8
HALO = 2
LANES = 128
ROWS = 8
SLOTS = (-1, 0, 1, 2)


def slot_weights(place, here, low, high, sixth):
    z = jnp.minimum(jnp.maximum(place, low), high)
    square = z * z
    less = square - 1.0
    outer = less * z * sixth
    triple = 3.0 * outer
    half = 0.5 * z
    half_square = 0.5 * square
    return (
        half_square - half - jnp.where(here, outer, triple),
        triple - less,
        half_square + half - jnp.where(here, triple, outer),
        outer,
    )


def bounds(here):
    return (
        jnp.where(here, -0.5, -1.5),
        jnp.where(here, 1.5, 0.5),
        jnp.where(here, 1.0 / 6.0, -1.0 / 6.0),
    )


def weighted(weights, values):
    return (weights[0] * values[0] + weights[1] * values[1]) + (
        weights[2] * values[2] + weights[3] * values[3]
    )


def shifted_lanes(before, here, after, lane):
    return (
        pltpu.roll(jnp.where(lane < LANES - 2, here, before), 2, 1),
        pltpu.roll(jnp.where(lane < LANES - 1, here, before), 1, 1),
        here,
        pltpu.roll(jnp.where(lane < 1, after, here), LANES - 1, 1),
        pltpu.roll(jnp.where(lane < 2, after, here), LANES - 2, 1),
    )


STACK = 5 * ROWS
FIELD_ROW = (ROWS, 3 * ROWS)


def fill_units(slab, chunk, chunk_total, center_ref, edge_ref, scratch):
    before = jnp.where(chunk == 0, chunk_total - 1, chunk - 1)
    after = jnp.where(chunk == chunk_total - 1, 0, chunk + 1)
    starts = [pl.multiple_of(c * LANES, LANES) for c in (before, chunk, after)]
    lane = lax.broadcasted_iota(jnp.int32, (ROWS, LANES), 1)
    first = pl.multiple_of(slab * (5 * STACK), ROWS)

    def edge_start():
        moved = shifted_lanes(*[edge_ref[slab, :, pl.ds(s, LANES)] for s in starts], lane)
        return [(value, pltpu.roll(value, ROWS // 2, 0)) for value in moved]

    def edge_finish(values):
        for step, (between, outside) in enumerate(values):
            for offset, value in ((0, outside), (2 * ROWS, between), (4 * ROWS, outside)):
                scratch[pl.ds(first + (step * STACK + offset), ROWS), :] = value

    def center_unit(field):
        def start():
            blocks = [center_ref[slab, field, :, pl.ds(s, LANES)] for s in starts]
            return shifted_lanes(*blocks, lane)

        def finish(values):
            for step, moved in enumerate(values):
                scratch[pl.ds(first + (step * STACK + FIELD_ROW[field]), ROWS), :] = moved

        return start, finish

    return [(edge_start, edge_finish)] + [center_unit(field) for field in range(2)]


class Interleave:
    def __init__(self, units, ticks):
        self.units = list(units)
        self.every = max(1, ticks // max(1, len(self.units)))
        self.count = 0
        self.pending = None

    def advance(self):
        if self.pending is not None:
            self.pending[0](self.pending[1])
            self.pending = None
        if self.units:
            start, finish = self.units.pop(0)
            self.pending = (finish, start())

    def tick(self):
        if self.count % self.every == 0:
            self.advance()
        self.count += 1

    def flush(self):
        while self.units or self.pending is not None:
            self.advance()


def level_sums(scratch, field, base, slot, points):
    loaded = {}

    def load(a, b, c):
        if (a, b, c) not in loaded:
            offset = ((a + HALO) * 5 + c + HALO) * STACK + FIELD_ROW[field] + b
            loaded[a, b, c] = scratch[pl.ds(base + offset, ROWS), :]
        return loaded[a, b, c]

    def one(step, weights, level_here, row_here, lon_here):
        def pick_lon(a, b):
            if slot[1] == 2:
                return jnp.where(lon_here, load(a + step, b, 2), load(a + step, b, -2))
            return load(a + step, b, slot[1])

        def pick(a):
            if slot[0] == 2:
                return jnp.where(row_here, pick_lon(a, 2), pick_lon(a, -2))
            return pick_lon(a, slot[0])

        total = weights[0] * pick(-1) + weights[1] * pick(0)
        total = total + weights[2] * pick(1)
        return total + weights[3] * jnp.where(level_here, pick(2), pick(-2))

    return [one(step, *point) for step, point in enumerate(points)]


def across(sums, row_weights, lon_weights):
    return weighted(
        lon_weights, [weighted(row_weights, [sums[b, c] for b in SLOTS]) for c in SLOTS]
    )


def arrival(base_ref, eta_ref, cells_ref, k, chunk, lanes):
    shape = (cells_ref.shape[2], LANES)
    level_here = cells_ref[2, k, :, lanes] == base_ref[0] + k
    row_here = cells_ref[0, k, :, lanes] == base_ref[1] + lax.broadcasted_iota(jnp.int32, shape, 0)
    lon_here = cells_ref[1, k, :, lanes] == chunk * LANES + lax.broadcasted_iota(
        jnp.int32, shape, 1
    )
    weights = slot_weights(
        -eta_ref[k, :, lanes].astype(jnp.float32), level_here, *bounds(level_here)
    )
    return weights, level_here, row_here, lon_here


def wind_levels(base, lanes, k, points, scratch, filling, out_ref):
    outputs = []
    for step, point in enumerate(points):
        here = base + step * (5 * STACK)
        sums = [{}, {}]
        for field in range(2):
            for c in SLOTS:
                for b in SLOTS:
                    filling.tick()
                    found = level_sums(scratch, field, here, (b, c), [point])
                    sums[field][b, c] = found[0]
        middle = (HALO * 5 + HALO) * STACK
        east = scratch[pl.ds(here + (middle + FIELD_ROW[0]), ROWS), :]
        north = scratch[pl.ds(here + (middle + FIELD_ROW[1]), ROWS), :]
        _, _, row_here, lon_here = point
        row_bounds, lon_bounds = bounds(row_here), bounds(lon_here)
        shift_row = COURANT * north
        shift_lon = COURANT * east
        for sweep in range(ITERS):
            row_weights = slot_weights(-shift_row, row_here, *row_bounds)
            lon_weights = slot_weights(-shift_lon, lon_here, *lon_bounds)
            east_found = across(sums[0], row_weights, lon_weights)
            north_found = across(sums[1], row_weights, lon_weights)
            shift_row = 0.5 * COURANT * (north + north_found)
            shift_lon = 0.5 * COURANT * (east + east_found)
        outputs.append((shift_row, shift_lon))
    filling.flush()
    for step, pair in enumerate(outputs):
        for part in range(2):
            out_ref[part, k + step, :, lanes] = pair[part]


def tracer_levels(shift_ref, base, lanes, k, points, scratch, filling, out_ref):
    outputs = []
    for first in range(0, len(points), 2):
        few = points[first : first + 2]
        row_weights = []
        lon_weights = []
        for step, (_, _, row_here, lon_here) in enumerate(few):
            place = k + first + step
            row_weights.append(
                slot_weights(-shift_ref[0, place, :, lanes], row_here, *bounds(row_here))
            )
            lon_weights.append(
                slot_weights(-shift_ref[1, place, :, lanes], lon_here, *bounds(lon_here))
            )
        for field in range(2):
            totals = [None] * len(few)
            for c, lon_slot in enumerate(SLOTS):
                columns = [None] * len(few)
                for b, row_slot in enumerate(SLOTS):
                    filling.tick()
                    here = base + first * (5 * STACK)
                    found = level_sums(scratch, field, here, (row_slot, lon_slot), few)
                    for step, value in enumerate(found):
                        term = row_weights[step][b] * value
                        columns[step] = term if b == 0 else columns[step] + term
                for step, column in enumerate(columns):
                    term = lon_weights[step][c] * column
                    totals[step] = term if c == 0 else totals[step] + term
            outputs += [(field, first + step, total) for step, total in enumerate(totals)]
    filling.flush()
    for field, step, total in outputs:
        out_ref[field, k + step, :, lanes] = total.astype(out_ref.dtype)


def interpolation_kernel(
    levels_body, slots_per_level, base_ref, center_ref, edge_ref, eta_ref, cells_ref, *others
):
    extra, (out_ref, even_scratch, odd_scratch) = others[:-3], others[-3:]
    levels, rows, lon_total = eta_ref.shape
    chunk_total = lon_total // LANES
    slabs = levels + 2 * HALO
    together = next(n for n in (4, 2, 1) if levels % n == 0)
    steps = levels // together
    per_step = -(-slabs // steps)
    source = (center_ref, edge_ref)

    def first_fill(slab, carry):
        for start, finish in fill_units(slab, 0, chunk_total, *source, even_scratch):
            finish(start())
        return carry

    lax.fori_loop(0, slabs, first_fill, 0)

    def one_chunk(chunk, scratch, other):
        lanes = pl.ds(pl.multiple_of(chunk * LANES, LANES), LANES)
        following = jnp.where(chunk == chunk_total - 1, 0, chunk + 1)

        def level_step(step, carry):
            k = step * together
            units = []
            for n in range(per_step):
                slab = jnp.minimum(step * per_step + n, slabs - 1)
                units += fill_units(slab, following, chunk_total, *source, other)
            filling = Interleave(units, slots_per_level * together)
            points = [
                arrival(base_ref, eta_ref, cells_ref, k + n, chunk, lanes) for n in range(together)
            ]
            base = pl.multiple_of(k * (5 * STACK), ROWS)
            levels_body(*extra, base, lanes, k, points, scratch, filling, out_ref)
            return carry

        lax.fori_loop(0, steps, level_step, 0)

    def chunk_pair(pair, carry):
        one_chunk(2 * pair, even_scratch, odd_scratch)
        one_chunk(2 * pair + 1, odd_scratch, even_scratch)
        return carry

    lax.fori_loop(0, chunk_total // 2, chunk_pair, 0)


def interpolation_call(levels_body, slots_per_level, base, center, edge, eta_shift, cells, extra, out_dtype):
    levels, rows, lon_total = eta_shift.shape
    points = levels * rows * lon_total
    scratch = pltpu.VMEM(((levels + 2 * HALO) * 5 * STACK, LANES), jnp.float32)
    in_vmem = pl.BlockSpec(memory_space=pltpu.VMEM)
    return pl.pallas_call(
        functools.partial(interpolation_kernel, levels_body, slots_per_level),
        out_shape=jax.ShapeDtypeStruct((2, levels, rows, lon_total), out_dtype),
        in_specs=[pl.BlockSpec(memory_space=pltpu.SMEM)] + [in_vmem] * (4 + len(extra)),
        out_specs=in_vmem,
        scratch_shapes=[scratch, scratch],
        compiler_params=pltpu.CompilerParams(vmem_limit_bytes=32 * 1024 * 1024),
        cost_estimate=pl.CostEstimate(
            flops=points * 500, bytes_accessed=points * 40, transcendentals=0
        ),
    )(base, center, edge, eta_shift, cells, *extra)


def level_edges(array):
    size, count = (lax.axis_size("lev"), array.shape[0])
    last, first = (array[count - HALO :], array[:HALO])
    if size == 2:
        at_top = lax.axis_index("lev") == 0
        found = lax.ppermute(jnp.where(at_top, last, first), "lev", [(0, 1), (1, 0)])
        nothing = jnp.zeros_like(found)
        return jnp.where(at_top, nothing, found), jnp.where(at_top, found, nothing)
    up = [(i, i + 1) for i in range(size - 1)]
    down = [(j, i) for i, j in up]
    return lax.ppermute(last, "lev", up), lax.ppermute(first, "lev", down)


def with_levels(center, edge):
    levels, field_count, rows, lon_total = center.shape
    flat = center.reshape(levels, field_count * rows, lon_total)
    sides = level_edges(jnp.concatenate([flat, edge], axis=1).astype(jnp.bfloat16))
    before, after = [side.astype(jnp.float32) for side in sides]
    cut = field_count * rows
    flat = jnp.concatenate([before[:, :cut], flat, after[:, :cut]], axis=0)
    edge = jnp.concatenate([before[:, cut:], edge, after[:, cut:]], axis=0)
    return flat.reshape((-1,) + center.shape[1:]), edge


def up_to(value, step):
    return -(-value // step) * step


TALL = ROWS + 2 * HALO
CODE = 16


def legendre_kernel(numbers_ref, codes_ref, spectra_ref, *others):
    tables, (out_ref, sums, table_tail, column_tail) = others[:-4], others[-4:]
    _, pairs, level_fields, degrees = spectra_ref.shape
    bands, block, _ = out_ref.shape
    code_row = block - CODE
    full = degrees // LANES * LANES
    count = 2 * level_fields
    own = numbers_ref[0]
    sums[...] = jnp.zeros(sums.shape, jnp.float32)
    table_tail[...] = jnp.zeros(table_tail.shape, jnp.float32)
    column_tail[...] = jnp.zeros(column_tail.shape, jnp.float32)
    codes = codes_ref[...]
    for band in range(bands):
        first = (band + 1) * block + code_row
        sums[first : first + 1, :] = jnp.right_shift(codes, 4).astype(jnp.float32)
        sums[first + 1 : first + 2, :] = (codes & 15).astype(jnp.float32)

    def pair_step(p, carry):
        edge = degrees - 1 - numbers_ref[1 + p]
        left = []
        for number, table_ref in enumerate(tables):
            for row in range(table_ref.shape[0]):
                piece = table_ref[row, p]
                left.append(piece[:, :full])
                first = (number * table_ref.shape[0] + row) * bands
                table_tail[first : first + bands, : degrees - full] = piece[:, full:].astype(
                    jnp.float32
                )
        left = jnp.concatenate(left, axis=0)
        left = jnp.concatenate([left, table_tail[...].astype(jnp.bfloat16)], axis=1)
        halves = ([], [])
        for part in range(2):
            piece = spectra_ref[part, p]
            whole = piece[:, :full].astype(jnp.float32)
            lane = lax.broadcasted_iota(jnp.int32, whole.shape, 1)
            zero = jnp.zeros_like(whole)
            halves[0].append(jnp.where(lane < edge, whole, zero).astype(jnp.bfloat16))
            halves[1].append(jnp.where(lane < edge, zero, whole).astype(jnp.bfloat16))
            first = part * level_fields
            column_tail[first : first + level_fields, : degrees - full] = piece[:, full:].astype(
                jnp.float32
            )
        tail = column_tail[...].astype(jnp.bfloat16)
        right = jnp.concatenate(
            [
                jnp.concatenate([jnp.concatenate(halves[0], axis=0), jnp.zeros_like(tail)], axis=1),
                jnp.concatenate([jnp.concatenate(halves[1], axis=0), tail], axis=1),
            ],
            axis=0,
        )
        found = lax.dot_general(
            left, right, (((1,), (1,)), ((), ())), preferred_element_type=jnp.float32
        )
        found = [found[i * bands : (i + 1) * bands] for i in range(ROWS)]

        def put(band, row, value):
            start = band * block + p * TALL + row
            sums[pl.ds(start, bands, stride=block), : 2 * count] = value

        if len(tables) == 1:
            ordered = found
            for row in range(ROWS):
                put(1, HALO + row, found[row])
        else:
            part_rows = ROWS // 2
            at_top = own == 0
            for i in range(part_rows):
                put(1, HALO + own * part_rows + i, found[i])
                put(1, HALO + (1 - own) * part_rows + i, found[part_rows + i])
            low, high = found[:part_rows], found[part_rows:]
            ordered = [jnp.where(at_top, x, y) for x, y in zip(low, high)]
            ordered += [jnp.where(at_top, y, x) for x, y in zip(low, high)]
        for i in range(HALO):
            put(0, HALO + ROWS + i, ordered[i])
            put(2, i, ordered[ROWS - HALO + i])
        return carry

    lax.fori_loop(0, pairs, pair_step, 0)
    kept = sums[block : (bands + 1) * block, :]
    out_ref[...] = kept.astype(jnp.bfloat16).reshape(out_ref.shape)


def legendre_call(pairing, spectra, tables):
    _, pairs, level_fields, degrees = spectra.shape
    bands = tables[0].shape[2]
    block = up_to(pairs * TALL, 16) + CODE
    width = up_to(4 * level_fields, LANES)
    numbers = jnp.concatenate([lax.axis_index("lev").astype(jnp.int32)[None], pairing])
    codes = jnp.pad(pairing, (0, width - pairs))[None, :]
    in_vmem = pl.BlockSpec(memory_space=pltpu.VMEM)
    return pl.pallas_call(
        legendre_kernel,
        out_shape=jax.ShapeDtypeStruct((bands, block, width), jnp.bfloat16),
        in_specs=[pl.BlockSpec(memory_space=pltpu.SMEM)] + [in_vmem] * (2 + len(tables)),
        out_specs=in_vmem,
        scratch_shapes=[
            pltpu.VMEM(((bands + 2) * block, width), jnp.float32),
            pltpu.VMEM((ROWS * bands, LANES), jnp.float32),
            pltpu.VMEM((2 * level_fields, LANES), jnp.float32),
        ],
        compiler_params=pltpu.CompilerParams(vmem_limit_bytes=32 * 1024 * 1024),
        cost_estimate=pl.CostEstimate(
            flops=2 * ROWS * bands * 4 * level_fields * pairs * degrees,
            bytes_accessed=8_000_000,
            transcendentals=0,
        ),
    )(numbers, codes, spectra, *tables)


def fourier_table(pair_total, padded, lon_total):
    order_total = 2 * pair_total
    half = pair_total // 2
    low = 2 * np.arange(half)
    high = low + 1
    even = np.concatenate([low, order_total - 1 - high])
    odd = np.concatenate([order_total - 1 - low, high])
    lon = np.arange(lon_total // 2)
    table = np.zeros((2, 2, padded, lon_total // 2), np.float32)
    for parity, orders in enumerate((even, odd)):
        phase = (orders[:, None] * lon[None, :]) % lon_total * (2.0 * math.pi / lon_total)
        weight = np.where(orders == 0, 1.0, 2.0)[:, None]
        table[parity, 0, :pair_total] = weight * np.cos(phase)
        table[parity, 1, :pair_total] = -weight * np.sin(phase)
    return table.reshape(2, 2 * padded, lon_total // 2).astype(jnp.bfloat16)


def owner_tables(bands, pairs):
    slots = np.arange(bands * pairs)
    owner = slots[:, None] // pairs == np.arange(LANES)[None, :]
    lane = slots[:, None] % pairs == np.arange(LANES)[None, :]
    return owner.astype(jnp.bfloat16), lane.astype(np.float32)


def fourier_kernel(level_fields, pairs, sums_ref, owner_ref, lane_ref, table_ref, *others):
    wind_ref, tracer_ref, wind_edge_ref, tracer_edge_ref, flat, codes, gathered, lhs = others
    bands, block, width = sums_ref.shape
    pair_total = bands * pairs
    padded = gathered.shape[0]
    blocks = padded // LANES
    code_row = block - CODE
    flat[...] = sums_ref[...].astype(jnp.float32).reshape(bands * block, width)
    gathered[pair_total:, :] = jnp.zeros((padded - pair_total, width), jnp.float32)
    codes[...] = jnp.zeros(codes.shape, jnp.float32)
    numbers = []
    for part in range(2):
        found = flat[pl.ds(code_row + part, bands, stride=block), :LANES]
        codes[part, :bands, :] = found
        numbers.append(
            jnp.dot(
                owner_ref[...],
                codes[part].astype(jnp.bfloat16),
                preferred_element_type=jnp.float32,
            )
        )
    pair_id = jnp.sum(
        (16.0 * numbers[0] + numbers[1]) * lane_ref[...], axis=1, keepdims=True
    ).astype(jnp.int32)
    place = jnp.right_shift(pair_id, 1) + (pair_id & 1) * (pair_total // 2)
    columns = lax.broadcasted_iota(jnp.int32, (pair_total, padded), 1)
    place = jnp.where(columns == place, 1.0, 0.0)
    if padded > pair_total:
        place = jnp.concatenate(
            [place, jnp.zeros((padded - pair_total, padded), jnp.float32)], axis=0
        )
    place = place.astype(jnp.bfloat16)
    low = lax.broadcasted_iota(jnp.int32, (level_fields, padded), 1) < pair_total // 2
    middle = level_fields * ROWS
    for row in range(TALL):
        for band in range(bands):
            gathered[band * pairs : (band + 1) * pairs, :] = flat[
                pl.ds(band * block + row, pairs, stride=TALL), :
            ]
        ordered = jnp.dot(
            gathered[...].T.astype(jnp.bfloat16), place, preferred_element_type=jnp.float32
        )
        if HALO <= row < HALO + ROWS:
            first, stride = row - HALO, ROWS
        else:
            first, stride = middle + (row - HALO - ROWS) % TALL, 2 * HALO
        for part in range(2):
            start = part * level_fields
            straight = ordered[start : start + level_fields]
            start = start + 2 * level_fields
            crossed = ordered[start : start + level_fields]
            both = (jnp.where(low, straight, crossed), jnp.where(low, crossed, straight))
            for parity in range(2):
                for t in range(blocks):
                    lhs[
                        parity, part * blocks + t, pl.ds(first, level_fields, stride=stride), :
                    ] = both[parity][:, t * LANES : (t + 1) * LANES]
    half = table_ref.shape[2]
    levels = level_fields // 4

    def transform(first, count):
        found = []
        for parity in range(2):
            left = jnp.concatenate(
                [
                    lhs[parity, t, first : first + count, :].astype(jnp.bfloat16)
                    for t in range(2 * blocks)
                ],
                axis=1,
            )
            found.append(jnp.dot(left, table_ref[parity], preferred_element_type=jnp.float32))
        pieces = (found[0] + found[1], found[0] - found[1])
        return [piece.astype(jnp.bfloat16).astype(jnp.float32) for piece in pieces]

    group = 2 if levels % 2 == 0 else 1
    for level in range(0, levels, group):
        pieces = transform(level * 4 * ROWS, group * 4 * ROWS)
        for part, value in enumerate(pieces):
            value = value.reshape(group, 4, ROWS, half)
            lanes = slice(part * half, (part + 1) * half)
            wind_ref[level : level + group, :, :, lanes] = value[:, :2]
            tracer_ref[level : level + group, :, :, lanes] = value[:, 2:]
    for part, value in enumerate(transform(middle, level_fields * 2 * HALO)):
        value = value.reshape(levels, 8 * HALO, half)
        lanes = slice(part * half, (part + 1) * half)
        wind_edge_ref[:, :, lanes] = value[:, : 4 * HALO]
        tracer_edge_ref[:, :, lanes] = value[:, 4 * HALO :]


def fourier_call(sums, pairs, lon_total, level_fields):
    bands, block, width = sums.shape
    pair_total = bands * pairs
    padded = up_to(pair_total, LANES)
    table = jnp.asarray(fourier_table(pair_total, padded, lon_total))
    owner, lane = [jnp.asarray(x) for x in owner_tables(bands, pairs)]
    levels = level_fields // 4
    center = jax.ShapeDtypeStruct((levels, 2, ROWS, lon_total), jnp.float32)
    edge = jax.ShapeDtypeStruct((levels, 4 * HALO, lon_total), jnp.float32)
    in_vmem = pl.BlockSpec(memory_space=pltpu.VMEM)
    return pl.pallas_call(
        functools.partial(fourier_kernel, level_fields, pairs),
        out_shape=(center, center, edge, edge),
        in_specs=[in_vmem] * 4,
        out_specs=(in_vmem,) * 4,
        scratch_shapes=[
            pltpu.VMEM((bands * block, width), jnp.float32),
            pltpu.VMEM((2, LANES, LANES), jnp.float32),
            pltpu.VMEM((padded, width), jnp.float32),
            pltpu.VMEM((2, 2 * padded // LANES, level_fields * TALL, LANES), jnp.float32),
        ],
        compiler_params=pltpu.CompilerParams(vmem_limit_bytes=40 * 1024 * 1024),
        cost_estimate=pl.CostEstimate(
            flops=4 * level_fields * TALL * padded * lon_total,
            bytes_accessed=8_000_000,
            transcendentals=0,
        ),
    )(sums, owner, lane, table)


def per_device(spectra, legendre, pairing, eta_shift, cells):
    levels, rows, lon_total = eta_shift.shape
    spectra = jnp.transpose(spectra, (0, 2, 1, 3))
    table = jnp.transpose(legendre, (0, 2, 1, 3))
    if lax.axis_size("lev") == 2:
        tables = (table, lax.ppermute(table, "lev", [(0, 1), (1, 0)]))
    else:
        tables = (lax.all_gather(table, "lev", axis=0, tiled=True),)
    sums = legendre_call(pairing, spectra, tables)
    sums = lax.all_to_all(sums, "band", split_axis=0, concat_axis=0, tiled=True)
    winds, tracers, wind_edge, tracer_edge = fourier_call(
        sums, pairing.shape[0], lon_total, 4 * levels
    )
    base = jnp.stack([lax.axis_index("lev") * levels, lax.axis_index("band") * rows])
    base = base.astype(jnp.int32)
    displacement = interpolation_call(
        wind_levels, 32, base, *with_levels(winds, wind_edge), eta_shift, cells, (), jnp.float32
    )
    advected = interpolation_call(
        tracer_levels,
        16,
        base,
        *with_levels(tracers, tracer_edge),
        eta_shift,
        cells,
        (displacement,),
        jnp.bfloat16,
    )
    return advected, displacement


def solution(mesh):
    return jax.shard_map(
        per_device,
        mesh=mesh,
        in_specs=(
            P(None, "lev", "band", None),
            P("lev", None, "band", None),
            P("band"),
            P("lev", "band", None),
            P(None, "lev", "band", None),
        ),
        out_specs=(P(None, "lev", "band", None), P(None, "lev", "band", None)),
        check_vma=False,
    )
```

```python
import functools
import math

import jax
import jax.numpy as jnp
import numpy as np
from jax import lax
from jax.experimental import pallas as pl
from jax.experimental.pallas import tpu as pltpu
from jax.sharding import PartitionSpec as P

ITERS = 2


COURANT = 0.8
HALO = 2
LANES = 128
ROWS = 8
SLOTS = (-1, 0, 1, 2)


def slot_weights(place, here, low, high, sixth):
    z = jnp.minimum(jnp.maximum(place, low), high)
    square = z * z
    less = square - 1.0
    outer = less * z * sixth
    triple = 3.0 * outer
    half = 0.5 * z
    half_square = 0.5 * square
    return (
        half_square - half - jnp.where(here, outer, triple),
        triple - less,
        half_square + half - jnp.where(here, triple, outer),
        outer,
    )


def bounds(here):
    return (
        jnp.where(here, -0.5, -1.5),
        jnp.where(here, 1.5, 0.5),
        jnp.where(here, 1.0 / 6.0, -1.0 / 6.0),
    )


def weighted(weights, values):
    return (weights[0] * values[0] + weights[1] * values[1]) + (
        weights[2] * values[2] + weights[3] * values[3]
    )


def shifted_lanes(before, here, after, lane):
    return (
        pltpu.roll(jnp.where(lane < LANES - 2, here, before), 2, 1),
        pltpu.roll(jnp.where(lane < LANES - 1, here, before), 1, 1),
        here,
        pltpu.roll(jnp.where(lane < 1, after, here), LANES - 1, 1),
        pltpu.roll(jnp.where(lane < 2, after, here), LANES - 2, 1),
    )


STACK = 5 * ROWS
FIELD_ROW = (ROWS, 3 * ROWS)


def fill_units(slab, chunk, chunk_total, field_ref, scratch):
    before = jnp.where(chunk == 0, chunk_total - 1, chunk - 1)
    after = jnp.where(chunk == chunk_total - 1, 0, chunk + 1)
    starts = [pl.multiple_of(c * LANES, LANES) for c in (before, chunk, after)]
    lane = lax.broadcasted_iota(jnp.int32, (ROWS, LANES), 1)
    first = pl.multiple_of(slab * (5 * STACK), ROWS)

    def edge_start():
        moved = shifted_lanes(
            *[field_ref[slab, 2 * ROWS : 3 * ROWS, pl.ds(s, LANES)] for s in starts], lane
        )
        return [(value, pltpu.roll(value, ROWS // 2, 0)) for value in moved]

    def edge_finish(values):
        for step, (between, outside) in enumerate(values):
            for offset, value in ((0, outside), (2 * ROWS, between), (4 * ROWS, outside)):
                scratch[pl.ds(first + (step * STACK + offset), ROWS), :] = value

    def center_unit(field):
        def start():
            rows = slice(field * ROWS, (field + 1) * ROWS)
            blocks = [field_ref[slab, rows, pl.ds(s, LANES)] for s in starts]
            return shifted_lanes(*blocks, lane)

        def finish(values):
            for step, moved in enumerate(values):
                scratch[pl.ds(first + (step * STACK + FIELD_ROW[field]), ROWS), :] = moved

        return start, finish

    return [(edge_start, edge_finish)] + [center_unit(field) for field in range(2)]


class Interleave:
    def __init__(self, units, ticks):
        self.units = list(units)
        self.every = max(1, ticks // max(1, len(self.units)))
        self.count = 0
        self.pending = None

    def advance(self):
        if self.pending is not None:
            self.pending[0](self.pending[1])
            self.pending = None
        if self.units:
            start, finish = self.units.pop(0)
            self.pending = (finish, start())

    def tick(self):
        if self.count % self.every == 0:
            self.advance()
        self.count += 1

    def flush(self):
        while self.units or self.pending is not None:
            self.advance()


def level_sums(scratch, field, base, slot, points):
    loaded = {}

    def load(a, b, c):
        if (a, b, c) not in loaded:
            offset = ((a + HALO) * 5 + c + HALO) * STACK + FIELD_ROW[field] + b
            loaded[a, b, c] = scratch[pl.ds(base + offset, ROWS), :]
        return loaded[a, b, c]

    def one(step, weights, level_here, row_here, lon_here):
        def pick_lon(a, b):
            if slot[1] == 2:
                return jnp.where(lon_here, load(a + step, b, 2), load(a + step, b, -2))
            return load(a + step, b, slot[1])

        def pick(a):
            if slot[0] == 2:
                return jnp.where(row_here, pick_lon(a, 2), pick_lon(a, -2))
            return pick_lon(a, slot[0])

        total = weights[0] * pick(-1) + weights[1] * pick(0)
        total = total + weights[2] * pick(1)
        return total + weights[3] * jnp.where(level_here, pick(2), pick(-2))

    return [one(step, *point) for step, point in enumerate(points)]


def across(sums, row_weights, lon_weights):
    return weighted(
        lon_weights, [weighted(row_weights, [sums[b, c] for b in SLOTS]) for c in SLOTS]
    )


def arrival(base_ref, eta_ref, cells_ref, k, chunk, lanes):
    shape = (cells_ref.shape[2], LANES)
    level_here = cells_ref[2, k, :, lanes] == base_ref[0] + k
    row_here = cells_ref[0, k, :, lanes] == base_ref[1] + lax.broadcasted_iota(jnp.int32, shape, 0)
    lon_here = cells_ref[1, k, :, lanes] == chunk * LANES + lax.broadcasted_iota(
        jnp.int32, shape, 1
    )
    weights = slot_weights(
        -eta_ref[k, :, lanes].astype(jnp.float32), level_here, *bounds(level_here)
    )
    return weights, level_here, row_here, lon_here


def wind_levels(base, lanes, k, points, scratch, filling, out_ref):
    for step, point in enumerate(points):
        here = base + step * (5 * STACK)
        sums = [{}, {}]
        for field in range(2):
            for c in SLOTS:
                for b in SLOTS:
                    filling.tick()
                    found = level_sums(scratch, field, here, (b, c), [point])
                    sums[field][b, c] = found[0]
        middle = (HALO * 5 + HALO) * STACK
        east = scratch[pl.ds(here + (middle + FIELD_ROW[0]), ROWS), :]
        north = scratch[pl.ds(here + (middle + FIELD_ROW[1]), ROWS), :]
        _, _, row_here, lon_here = point
        row_bounds, lon_bounds = bounds(row_here), bounds(lon_here)
        shift_row = COURANT * north
        shift_lon = COURANT * east
        for sweep in range(ITERS):
            row_weights = slot_weights(-shift_row, row_here, *row_bounds)
            lon_weights = slot_weights(-shift_lon, lon_here, *lon_bounds)
            east_found = across(sums[0], row_weights, lon_weights)
            north_found = across(sums[1], row_weights, lon_weights)
            shift_row = 0.5 * COURANT * (north + north_found)
            shift_lon = 0.5 * COURANT * (east + east_found)
        if step == len(points) - 1:
            filling.flush()
        out_ref[0, k + step, :, lanes] = shift_row
        out_ref[1, k + step, :, lanes] = shift_lon


def tracer_levels(shift_ref, base, lanes, k, points, scratch, filling, out_ref):
    outputs = []
    for step, point in enumerate(points):
        here = base + step * (5 * STACK)
        _, _, row_here, lon_here = point
        row_weights = slot_weights(
            -shift_ref[0, k + step, :, lanes], row_here, *bounds(row_here)
        )
        lon_weights = slot_weights(
            -shift_ref[1, k + step, :, lanes], lon_here, *bounds(lon_here)
        )
        for field in range(2):
            total = None
            for c, lon_slot in enumerate(SLOTS):
                column = None
                for b, row_slot in enumerate(SLOTS):
                    filling.tick()
                    found = level_sums(scratch, field, here, (row_slot, lon_slot), [point])[0]
                    term = row_weights[b] * found
                    column = term if b == 0 else column + term
                term = lon_weights[c] * column
                total = term if c == 0 else total + term
            outputs.append((field, step, total))
    filling.flush()
    for field, step, total in outputs:
        out_ref[field, k + step, :, lanes] = total.astype(out_ref.dtype)


def interpolation_kernel(levels_body, together, near_count, base_ref, field_ref, *others):
    nears, others = others[:near_count], others[near_count:]
    point_count = (len(others) - 6) // 2
    point_sources, others = others[:point_count], others[point_count:]
    out_ref, done_ref, full, even_scratch, odd_scratch = others[:5]
    points_here, arrivals = others[5:-1], others[-1]
    done_ref[...] = jnp.zeros(done_ref.shape, done_ref.dtype)
    copies = [
        pltpu.make_async_copy(source, target, arrivals.at[n])
        for n, (source, target) in enumerate(zip(point_sources, points_here))
    ]
    for copy in copies:
        copy.start()
    eta_ref, cells_ref = points_here[:2]
    levels, rows, lon_total = eta_ref.shape
    chunk_total = lon_total // LANES
    slabs = levels + 2 * HALO
    steps = levels // together
    per_step = -(-slabs // steps)
    full[HALO : HALO + levels] = field_ref[...]
    if near_count == 1:
        found = jnp.where(base_ref[0] == 0, levels + HALO, 0)
        full[pl.ds(found, HALO)] = nears[0][...].astype(jnp.float32)
        empty = levels + HALO - found
        full[pl.ds(empty, HALO)] = jnp.zeros((HALO,) + full.shape[1:], jnp.float32)
    else:
        full[:HALO] = nears[0][...].astype(jnp.float32)
        full[HALO + levels :] = nears[1][...].astype(jnp.float32)

    def first_fill(slab, carry):
        for start, finish in fill_units(slab, 0, chunk_total, full, even_scratch):
            finish(start())
        return carry

    lax.fori_loop(0, slabs, first_fill, 0)
    for copy in copies:
        copy.wait()

    def one_chunk(chunk, scratch, other):
        lanes = pl.ds(pl.multiple_of(chunk * LANES, LANES), LANES)
        following = jnp.where(chunk == chunk_total - 1, 0, chunk + 1)

        def level_step(step, carry):
            k = step * together
            units = []
            for n in range(per_step):
                slab = jnp.minimum(step * per_step + n, slabs - 1)
                units += fill_units(slab, following, chunk_total, full, other)
            filling = Interleave(units, 32 * together)
            points = [
                arrival(base_ref, eta_ref, cells_ref, k + n, chunk, lanes) for n in range(together)
            ]
            base = pl.multiple_of(k * (5 * STACK), ROWS)
            levels_body(
                *points_here[2:], base, lanes, k, points, scratch, filling, out_ref
            )
            return carry

        lax.fori_loop(0, steps, level_step, 0)

    def chunk_pair(pair, carry):
        one_chunk(2 * pair, even_scratch, odd_scratch)
        one_chunk(2 * pair + 1, odd_scratch, even_scratch)
        return carry

    lax.fori_loop(0, chunk_total // 2, chunk_pair, 0)


def interpolation_call(levels_body, base, fields, nears, points, out_dtype):
    levels, rows, lon_total = points[0].shape
    count = levels * rows * lon_total
    together = 2 if levels % 2 == 0 else 1
    scratch = pltpu.VMEM(((levels + 2 * HALO) * 5 * STACK, LANES), jnp.float32)
    in_vmem = pl.BlockSpec(memory_space=pltpu.VMEM)
    return pl.pallas_call(
        functools.partial(interpolation_kernel, levels_body, together, len(nears)),
        out_shape=(
            jax.ShapeDtypeStruct((2, levels, rows, lon_total), out_dtype),
            jax.ShapeDtypeStruct((ROWS, LANES), jnp.float32),
        ),
        in_specs=[pl.BlockSpec(memory_space=pltpu.SMEM)]
        + [in_vmem] * (1 + len(nears))
        + [pl.BlockSpec(memory_space=pl.ANY)] * len(points),
        out_specs=(in_vmem, in_vmem),
        scratch_shapes=[
            pltpu.VMEM((levels + 2 * HALO,) + fields.shape[1:], jnp.float32),
            scratch,
            scratch,
        ]
        + [pltpu.VMEM(x.shape, x.dtype) for x in points]
        + [pltpu.SemaphoreType.DMA((len(points),))],
        compiler_params=pltpu.CompilerParams(vmem_limit_bytes=32 * 1024 * 1024),
        cost_estimate=pl.CostEstimate(
            flops=count * 500, bytes_accessed=count * 40, transcendentals=0
        ),
    )(base, fields, *nears, *points)


def swap_levels(send):
    if lax.axis_size("lev") == 2:
        return (lax.ppermute(send[0], "lev", [(0, 1), (1, 0)]),)
    up = [(i, i + 1) for i in range(lax.axis_size("lev") - 1)]
    down = [(j, i) for i, j in up]
    return lax.ppermute(send[1], "lev", up), lax.ppermute(send[0], "lev", down)


def up_to(value, step):
    return -(-value // step) * step


TALL = ROWS + 2 * HALO
PAIRED = TALL // 2
HALF = LANES // 2


def legendre_kernel(numbers_ref, codes_ref, order_ref, spectra_ref, *others):
    tables, others = others[:-6], others[-6:]
    wind_ref, tracer_ref, wind_sums, tracer_sums, table_tail, column_tail = others
    _, group, level_fields, degrees = spectra_ref.shape
    bands, block, _ = wind_ref.shape
    full = degrees // LANES * LANES
    at_top = numbers_ref[0] == 0
    step = pl.program_id(0)

    @pl.when(step == 0)
    def _():
        wind_sums[...] = jnp.zeros(wind_sums.shape, jnp.float32)
        tracer_sums[...] = jnp.zeros(tracer_sums.shape, jnp.float32)
        table_tail[...] = jnp.zeros(table_tail.shape, jnp.float32)
        column_tail[...] = jnp.zeros(column_tail.shape, jnp.float32)
        codes = codes_ref[...]
        code_row = up_to(pl.num_programs(0) * group * PAIRED, ROWS)
        for band in range(bands):
            first = band * block + code_row
            wind_sums[pl.ds(first, 1), :] = jnp.right_shift(codes, 4).astype(jnp.float32)
            wind_sums[pl.ds(first + 1, 1), :] = (codes & 15).astype(jnp.float32)

    band_row = lax.broadcasted_iota(jnp.int32, (bands, LANES), 0)
    first_half = lax.broadcasted_iota(jnp.int32, (bands, LANES), 1) < HALF
    nothing = jnp.zeros((bands, LANES), jnp.float32)
    for p in range(group):
        slot = step * group + p
        edge = degrees - 1 - numbers_ref[1 + slot]
        left = []
        for number, table_ref in enumerate(tables):
            for row in range(table_ref.shape[0]):
                piece = table_ref[row, p]
                left.append(piece[:, :full])
                first = (number * table_ref.shape[0] + row) * bands
                table_tail[p, first : first + bands, : degrees - full] = piece[:, full:].astype(
                    jnp.float32
                )
        left = jnp.concatenate(left, axis=0)
        left = jnp.concatenate([left, table_tail[p].astype(jnp.bfloat16)], axis=1)
        halves = ([], [])
        for part in range(2):
            piece = spectra_ref[part, p]
            whole = piece[:, :full].astype(jnp.float32)
            lane = lax.broadcasted_iota(jnp.int32, whole.shape, 1)
            zero = jnp.zeros_like(whole)
            halves[0].append(jnp.where(lane < edge, whole, zero).astype(jnp.bfloat16))
            halves[1].append(jnp.where(lane < edge, zero, whole).astype(jnp.bfloat16))
            first = part * level_fields
            column_tail[p, first : first + level_fields, : degrees - full] = piece[
                :, full:
            ].astype(jnp.float32)
        tail = column_tail[p].astype(jnp.bfloat16)
        right = jnp.concatenate(
            [
                jnp.concatenate([jnp.concatenate(halves[0], axis=0), jnp.zeros_like(tail)], axis=1),
                jnp.concatenate([jnp.concatenate(halves[1], axis=0), tail], axis=1),
            ],
            axis=0,
        )
        found = lax.dot_general(
            left, right, (((1,), (1,)), ((), ())), preferred_element_type=jnp.float32
        )
        found = jnp.dot(
            found.astype(jnp.bfloat16), order_ref[...], preferred_element_type=jnp.float32
        )
        found = [found[i * bands : (i + 1) * bands] for i in range(ROWS)]
        if len(tables) == 2:
            low, high = found[: ROWS // 2], found[ROWS // 2 :]
            found = [jnp.where(at_top, x, y) for x, y in zip(low, high)]
            found += [jnp.where(at_top, y, x) for x, y in zip(low, high)]
        above = [
            jnp.where(band_row == 0, nothing, pltpu.roll(x, 1, 0)) for x in found[ROWS - HALO :]
        ]
        below = [
            jnp.where(band_row == bands - 1, nothing, pltpu.roll(x, bands - 1, 0))
            for x in found[:HALO]
        ]
        rows = above + found + below
        for i in range(PAIRED):
            low, high = rows[i], rows[PAIRED + i]
            place = pl.ds(slot * PAIRED + i, bands, stride=block)
            wind_sums[place, :] = jnp.where(first_half, low, pltpu.roll(high, HALF, 1))
            tracer_sums[place, :] = jnp.where(first_half, pltpu.roll(low, HALF, 1), high)

    @pl.when(step == pl.num_programs(0) - 1)
    def _():
        wind_ref[...] = wind_sums[...].astype(jnp.bfloat16).reshape(wind_ref.shape)
        tracer_ref[...] = tracer_sums[...].astype(jnp.bfloat16).reshape(tracer_ref.shape)


def column_order(level_fields):
    levels = level_fields // 4
    order = np.zeros((4 * level_fields, LANES), np.float32)
    for column in range(4 * level_fields):
        part, rest = divmod(column, level_fields)
        level, field = divmod(rest, 4)
        target = (field // 2) * HALF + part * 2 * levels + 2 * level + field % 2
        order[column, target] = 1.0
    return order.astype(jnp.bfloat16)


def block_rows(pairs):
    return up_to(up_to(pairs * PAIRED, ROWS) + 2, 16)


def legendre_call(pairing, spectra, tables):
    _, pairs, level_fields, degrees = spectra.shape
    bands = tables[0].shape[2]
    block = block_rows(pairs)
    group = next(n for n in (4, 5, 2, 1) if pairs % n == 0)
    numbers = jnp.concatenate([lax.axis_index("lev").astype(jnp.int32)[None], pairing])
    codes = jnp.pad(pairing, (0, LANES - pairs))[None, :]
    shape = jax.ShapeDtypeStruct((bands, block, LANES), jnp.bfloat16)
    whole = pl.BlockSpec((bands, block, LANES), lambda i: (0, 0, 0))
    by_pair = lambda array: pl.BlockSpec(
        (array.shape[0], group) + array.shape[2:], lambda i: (0, i, 0, 0)
    )
    return pl.pallas_call(
        legendre_kernel,
        grid=(pairs // group,),
        out_shape=(shape, shape),
        in_specs=[
            pl.BlockSpec(memory_space=pltpu.SMEM),
            pl.BlockSpec((1, LANES), lambda i: (0, 0)),
            pl.BlockSpec((4 * level_fields, LANES), lambda i: (0, 0)),
            by_pair(spectra),
        ]
        + [by_pair(table) for table in tables],
        out_specs=(whole, whole),
        scratch_shapes=[
            pltpu.VMEM((bands * block, LANES), jnp.float32),
            pltpu.VMEM((bands * block, LANES), jnp.float32),
            pltpu.VMEM((group, ROWS * bands, LANES), jnp.float32),
            pltpu.VMEM((group, 2 * level_fields, LANES), jnp.float32),
        ],
        compiler_params=pltpu.CompilerParams(vmem_limit_bytes=32 * 1024 * 1024),
        cost_estimate=pl.CostEstimate(
            flops=2 * ROWS * bands * 4 * level_fields * pairs * degrees,
            bytes_accessed=8_000_000,
            transcendentals=0,
        ),
    )(numbers, codes, jnp.asarray(column_order(level_fields)), spectra, *tables)


def fourier_table(pair_total, padded, lon_total):
    order_total = 2 * pair_total
    half = pair_total // 2
    low = 2 * np.arange(half)
    high = low + 1
    even = np.concatenate([low, order_total - 1 - high])
    odd = np.concatenate([order_total - 1 - low, high])
    lon = np.arange(lon_total // 2)
    table = np.zeros((2, 2, padded, lon_total // 2), np.float32)
    for parity, orders in enumerate((even, odd)):
        phase = (orders[:, None] * lon[None, :]) % lon_total * (2.0 * math.pi / lon_total)
        weight = np.where(orders == 0, 1.0, 2.0)[:, None]
        table[parity, 0, :pair_total] = weight * np.cos(phase)
        table[parity, 1, :pair_total] = -weight * np.sin(phase)
    return table.reshape(2, 2 * padded, lon_total // 2).astype(jnp.bfloat16)


def owner_tables(bands, pairs):
    slots = np.arange(bands * pairs)
    owner = slots[:, None] // pairs == np.arange(LANES)[None, :]
    lane = slots[:, None] % pairs == np.arange(LANES)[None, :]
    return owner.astype(jnp.bfloat16), lane.astype(np.float32)


def pair_places(flat, owner_ref, lane_ref, codes, bands, block, code_row, padded):
    pair_total = owner_ref.shape[0]
    codes[...] = jnp.zeros(codes.shape, jnp.float32)
    numbers = []
    for part in range(2):
        codes[part, :bands, :] = flat[pl.ds(code_row + part, bands, stride=block), :]
        numbers.append(
            jnp.dot(
                owner_ref[...],
                codes[part].astype(jnp.bfloat16),
                preferred_element_type=jnp.float32,
            )
        )
    pair_id = jnp.sum(
        (16.0 * numbers[0] + numbers[1]) * lane_ref[...], axis=1, keepdims=True
    ).astype(jnp.int32)
    place = jnp.right_shift(pair_id, 1) + (pair_id & 1) * (pair_total // 2)
    columns = lax.broadcasted_iota(jnp.int32, (pair_total, padded), 1)
    place = jnp.where(columns == place, 1.0, 0.0)
    if padded > pair_total:
        place = jnp.concatenate(
            [place, jnp.zeros((padded - pair_total, padded), jnp.float32)], axis=0
        )
    return place.astype(jnp.bfloat16)


def fourier_kernel(pairs, levels, leads, base_ref, sums_ref, table_ref, *others):
    if leads:
        owner_ref, lane_ref, field_ref, send_ref, place_ref = others[:5]
    else:
        place_ref, _, field_ref, send_ref = others[:4]
    codes, flat, gathered, lhs, table, arrival_sem = others[-6:]
    copy = pltpu.make_async_copy(table_ref, table, arrival_sem)
    copy.start()
    bands, block, width = sums_ref.shape
    pair_total = bands * pairs
    padded = gathered.shape[0]
    blocks = padded // LANES
    fields = 2 * levels
    flat[...] = sums_ref[...].astype(jnp.float32).reshape(bands * block, width)
    gathered[pair_total:, :] = jnp.zeros((padded - pair_total, width), jnp.float32)
    if leads:
        code_row = up_to(pairs * PAIRED, ROWS)
        place_ref[...] = pair_places(
            flat, owner_ref, lane_ref, codes, bands, block, code_row, padded
        )
    place = place_ref[...]
    low = lax.broadcasted_iota(jnp.int32, (fields, padded), 1) < pair_total // 2
    middle = fields * ROWS
    for i in range(PAIRED):
        for band in range(bands):
            gathered[band * pairs : (band + 1) * pairs, :] = flat[
                pl.ds(band * block + i, pairs, stride=PAIRED), :
            ]
        ordered = jnp.dot(
            gathered[...].T.astype(jnp.bfloat16), place, preferred_element_type=jnp.float32
        )
        for side in range(2):
            row = side * PAIRED + i
            if HALO <= row < HALO + ROWS:
                first, stride = row - HALO, ROWS
            else:
                first, stride = middle + (row - HALO - ROWS) % TALL, 2 * HALO
            for part in range(2):
                start = side * HALF + part * fields
                straight = ordered[start : start + fields]
                start = start + 2 * fields
                crossed = ordered[start : start + fields]
                both = (jnp.where(low, straight, crossed), jnp.where(low, crossed, straight))
                for parity in range(2):
                    for t in range(blocks):
                        lhs[parity, part * blocks + t, pl.ds(first, fields, stride=stride), :] = (
                            both[parity][:, t * LANES : (t + 1) * LANES]
                        )
    copy.wait()
    half = table.shape[2]

    def transform(first, count):
        found = []
        for parity in range(2):
            left = jnp.concatenate(
                [
                    lhs[parity, t, first : first + count, :].astype(jnp.bfloat16)
                    for t in range(2 * blocks)
                ],
                axis=1,
            )
            found.append(jnp.dot(left, table[parity], preferred_element_type=jnp.float32))
        pieces = (found[0] + found[1], found[0] - found[1])
        return [piece.astype(jnp.bfloat16).astype(jnp.float32) for piece in pieces]

    group = next(n for n in (4, 2, 1) if levels % n == 0)
    for level in range(0, levels, group):
        pieces = transform(level * 2 * ROWS, group * 2 * ROWS)
        for part, value in enumerate(pieces):
            value = value.reshape(group, 2 * ROWS, half)
            field_ref[level : level + group, : 2 * ROWS, part * half : (part + 1) * half] = value
    for part, value in enumerate(transform(middle, fields * 2 * HALO)):
        value = value.reshape(levels, 4 * HALO, half)
        field_ref[:, 2 * ROWS :, part * half : (part + 1) * half] = value
    if send_ref.shape[0] == 1:
        start = jnp.where(base_ref[0] == 0, levels - HALO, 0)
        send_ref[0] = field_ref[pl.ds(start, HALO)].astype(jnp.bfloat16)
    else:
        send_ref[0] = field_ref[:HALO].astype(jnp.bfloat16)
        send_ref[1] = field_ref[levels - HALO :].astype(jnp.bfloat16)


def fourier_call(base, sums, table, pairs, levels, lon_total, place=None, after=None):
    bands, block, width = sums.shape
    pair_total = bands * pairs
    padded = up_to(pair_total, LANES)
    leads = place is None
    sends = 1 if lax.axis_size("lev") == 2 else 2
    field_shape = (levels, 3 * ROWS, lon_total)
    out_shape = [
        jax.ShapeDtypeStruct(field_shape, jnp.float32),
        jax.ShapeDtypeStruct((sends, HALO) + field_shape[1:], jnp.bfloat16),
    ]
    extra = [place, after]
    if leads:
        out_shape.append(jax.ShapeDtypeStruct((padded, padded), jnp.bfloat16))
        extra = [jnp.asarray(x) for x in owner_tables(bands, pairs)]
    in_vmem = pl.BlockSpec(memory_space=pltpu.VMEM)
    return pl.pallas_call(
        functools.partial(fourier_kernel, pairs, levels, leads),
        out_shape=tuple(out_shape),
        in_specs=[
            pl.BlockSpec(memory_space=pltpu.SMEM),
            in_vmem,
            pl.BlockSpec(memory_space=pl.ANY),
        ]
        + [in_vmem] * 2,
        out_specs=(in_vmem,) * len(out_shape),
        scratch_shapes=[
            pltpu.VMEM((2, LANES, LANES), jnp.float32),
            pltpu.VMEM((bands * block, width), jnp.float32),
            pltpu.VMEM((padded, width), jnp.float32),
            pltpu.VMEM((2, 2 * padded // LANES, 2 * levels * TALL, LANES), jnp.float32),
            pltpu.VMEM(table.shape, table.dtype),
            pltpu.SemaphoreType.DMA,
        ],
        compiler_params=pltpu.CompilerParams(vmem_limit_bytes=32 * 1024 * 1024),
        cost_estimate=pl.CostEstimate(
            flops=2 * levels * 4 * TALL * padded * lon_total,
            bytes_accessed=8_000_000,
            transcendentals=0,
        ),
    )(base, sums, table, *extra)


def exchange(sums):
    return lax.all_to_all(sums, "band", split_axis=0, concat_axis=0, tiled=True)


def per_device(spectra, legendre, pairing, eta_shift, cells):
    levels, rows, lon_total = eta_shift.shape
    pairs = pairing.shape[0]
    spectra = jnp.transpose(spectra, (0, 2, 1, 3))
    table = jnp.transpose(legendre, (0, 2, 1, 3))
    if lax.axis_size("lev") == 2:
        tables = (table, lax.ppermute(table, "lev", [(0, 1), (1, 0)]))
    else:
        tables = (lax.all_gather(table, "lev", axis=0, tiled=True),)
    base = jnp.stack([lax.axis_index("lev") * levels, lax.axis_index("band") * rows])
    base = base.astype(jnp.int32)
    wind_sums, tracer_sums = legendre_call(pairing, spectra, tables)
    wind_sums = exchange(wind_sums)
    wind_sums, tracer_sums = lax.optimization_barrier((wind_sums, tracer_sums))
    tracer_sums = exchange(tracer_sums)
    pair_total = pairs * lax.axis_size("band")
    twiddles = jnp.asarray(fourier_table(pair_total, up_to(pair_total, LANES), lon_total))
    size = (pairs, levels, lon_total)
    winds, send, place = fourier_call(base, wind_sums, twiddles, *size)
    displacement, done = interpolation_call(
        wind_levels, base, winds, swap_levels(send), (eta_shift, cells), jnp.float32
    )
    tracers, send = fourier_call(base, tracer_sums, twiddles, *size, place, done)
    advected, _ = interpolation_call(
        tracer_levels,
        base,
        tracers,
        swap_levels(send),
        (eta_shift, cells, displacement),
        jnp.bfloat16,
    )
    return advected, displacement


def solution(mesh):
    return jax.shard_map(
        per_device,
        mesh=mesh,
        in_specs=(
            P(None, "lev", "band", None),
            P("lev", None, "band", None),
            P("band"),
            P("lev", "band", None),
            P(None, "lev", "band", None),
        ),
        out_specs=(P(None, "lev", "band", None), P(None, "lev", "band", None)),
        check_vma=False,
    )
```

```python
import functools
import math

import jax
import jax.numpy as jnp
import numpy as np
from jax import lax
from jax.experimental import pallas as pl
from jax.experimental.pallas import tpu as pltpu
from jax.sharding import PartitionSpec as P

ITERS = 2


COURANT = 0.8
HALO = 2
LANES = 128
ROWS = 8
SLOTS = (-1, 0, 1, 2)


def slot_weights(place, here, low, high, sixth):
    z = jnp.minimum(jnp.maximum(place, low), high)
    square = z * z
    less = square - 1.0
    outer = less * z * sixth
    triple = 3.0 * outer
    half = 0.5 * z
    half_square = 0.5 * square
    return (
        half_square - half - jnp.where(here, outer, triple),
        triple - less,
        half_square + half - jnp.where(here, triple, outer),
        outer,
    )


def bounds(here):
    return (
        jnp.where(here, -0.5, -1.5),
        jnp.where(here, 1.5, 0.5),
        jnp.where(here, 1.0 / 6.0, -1.0 / 6.0),
    )


def weighted(weights, values):
    return (weights[0] * values[0] + weights[1] * values[1]) + (
        weights[2] * values[2] + weights[3] * values[3]
    )


def shifted_lanes(before, here, after, lane):
    return (
        pltpu.roll(jnp.where(lane < LANES - 2, here, before), 2, 1),
        pltpu.roll(jnp.where(lane < LANES - 1, here, before), 1, 1),
        here,
        pltpu.roll(jnp.where(lane < 1, after, here), LANES - 1, 1),
        pltpu.roll(jnp.where(lane < 2, after, here), LANES - 2, 1),
    )


STACK = 5 * ROWS
FIELD_ROW = (ROWS, 3 * ROWS)


def fill_units(slab, chunk, chunk_total, field_ref, scratch):
    before = jnp.where(chunk == 0, chunk_total - 1, chunk - 1)
    after = jnp.where(chunk == chunk_total - 1, 0, chunk + 1)
    starts = [pl.multiple_of(c * LANES, LANES) for c in (before, chunk, after)]
    lane = lax.broadcasted_iota(jnp.int32, (ROWS, LANES), 1)
    first = pl.multiple_of(slab * (5 * STACK), ROWS)

    def edge_start():
        moved = shifted_lanes(
            *[field_ref[slab, 2 * ROWS : 3 * ROWS, pl.ds(s, LANES)] for s in starts], lane
        )
        return [(value, pltpu.roll(value, ROWS // 2, 0)) for value in moved]

    def edge_finish(values):
        for step, (between, outside) in enumerate(values):
            for offset, value in ((0, outside), (2 * ROWS, between), (4 * ROWS, outside)):
                scratch[pl.ds(first + (step * STACK + offset), ROWS), :] = value

    def center_unit(field):
        def start():
            rows = slice(field * ROWS, (field + 1) * ROWS)
            blocks = [field_ref[slab, rows, pl.ds(s, LANES)] for s in starts]
            return shifted_lanes(*blocks, lane)

        def finish(values):
            for step, moved in enumerate(values):
                scratch[pl.ds(first + (step * STACK + FIELD_ROW[field]), ROWS), :] = moved

        return start, finish

    return [(edge_start, edge_finish)] + [center_unit(field) for field in range(2)]


class Interleave:
    def __init__(self, units, ticks):
        self.units = list(units)
        self.every = max(1, ticks // max(1, len(self.units)))
        self.count = 0
        self.pending = None

    def advance(self):
        if self.pending is not None:
            self.pending[0](self.pending[1])
            self.pending = None
        if self.units:
            start, finish = self.units.pop(0)
            self.pending = (finish, start())

    def tick(self):
        if self.count % self.every == 0:
            self.advance()
        self.count += 1

    def flush(self):
        while self.units or self.pending is not None:
            self.advance()


def level_sums(scratch, field, base, slot, points):
    loaded = {}

    def load(a, b, c):
        offset = ((a + HALO) * 5 + c + HALO) * STACK + FIELD_ROW[field] + b
        if slot == (2, 2):
            return scratch[pl.ds(base + offset, ROWS), :]
        if (a, b, c) not in loaded:
            loaded[a, b, c] = scratch[pl.ds(base + offset, ROWS), :]
        return loaded[a, b, c]

    def one(step, weights, level_here, row_here, lon_here):
        def pick_lon(a, b):
            if slot[1] == 2:
                return jnp.where(lon_here, load(a + step, b, 2), load(a + step, b, -2))
            return load(a + step, b, slot[1])

        def pick(a):
            if slot[0] == 2:
                return jnp.where(row_here, pick_lon(a, 2), pick_lon(a, -2))
            return pick_lon(a, slot[0])

        total = weights[0] * pick(-1) + weights[1] * pick(0)
        total = total + weights[2] * pick(1)
        return total + weights[3] * jnp.where(level_here, pick(2), pick(-2))

    return [one(step, *point) for step, point in enumerate(points)]


def across(scratch, field, base, points, row_weights, lon_weights, filling, keep=None):
    columns = [[None] * 4 for _ in points]
    for b, row_slot in enumerate(SLOTS):
        for c, lon_slot in enumerate(SLOTS):
            filling.tick()
            found = level_sums(scratch, field, base, (row_slot, lon_slot), points)
            for step, value in enumerate(found):
                if keep is not None:
                    keep[field, step, 4 * b + c] = value
                term = row_weights[step][b] * value
                columns[step][c] = term if b == 0 else columns[step][c] + term
    return [weighted(weights, column) for weights, column in zip(lon_weights, columns)]


def across_kept(keep, field, step, row_weights, lon_weights):
    return weighted(
        lon_weights,
        [
            weighted(row_weights, [keep[field, step, 4 * b + c] for b in range(4)])
            for c in range(4)
        ],
    )


def prepare_kernel(base_ref, after_ref, eta_ref, cells_ref, table_ref, points_ref, out_ref, sem):
    copy = pltpu.make_async_copy(table_ref, out_ref, sem)
    copy.start()
    levels, rows, lon_total = eta_ref.shape
    shape = (rows, LANES)
    row_here = base_ref[1] + lax.broadcasted_iota(jnp.int32, shape, 0)
    lane = lax.broadcasted_iota(jnp.int32, shape, 1)

    def chunk_step(chunk, carry):
        lanes = pl.ds(pl.multiple_of(chunk * LANES, LANES), LANES)
        for k in range(levels):
            level_here = cells_ref[2, k, :, lanes] == base_ref[0] + k
            weights = slot_weights(
                -eta_ref[k, :, lanes].astype(jnp.float32), level_here, *bounds(level_here)
            )
            here = (
                level_here,
                cells_ref[0, k, :, lanes] == row_here,
                cells_ref[1, k, :, lanes] == chunk * LANES + lane,
            )
            for n, value in enumerate(weights + tuple(bounds(x)[0] for x in here)):
                points_ref[n, k, :, lanes] = value
        return carry

    lax.fori_loop(0, lon_total // LANES, chunk_step, 0)
    copy.wait()


def prepare_call(base, after, eta_shift, cells, table):
    in_vmem = pl.BlockSpec(memory_space=pltpu.VMEM)
    return pl.pallas_call(
        prepare_kernel,
        out_shape=(
            jax.ShapeDtypeStruct((7,) + eta_shift.shape, jnp.float32),
            jax.ShapeDtypeStruct(table.shape, table.dtype),
        ),
        in_specs=[pl.BlockSpec(memory_space=pltpu.SMEM)]
        + [in_vmem] * 3
        + [pl.BlockSpec(memory_space=pl.ANY)],
        out_specs=(in_vmem, in_vmem),
        scratch_shapes=[pltpu.SemaphoreType.DMA],
        compiler_params=pltpu.CompilerParams(vmem_limit_bytes=32 * 1024 * 1024),
        cost_estimate=pl.CostEstimate(
            flops=40 * eta_shift.size, bytes_accessed=20_000_000, transcendentals=0
        ),
    )(base, after, eta_shift, cells, table)


def arrival(points_ref, k, lanes):
    here = [points_ref[n, k, :, lanes] > -1.0 for n in range(4, 7)]
    return tuple(points_ref[n, k, :, lanes] for n in range(4)), *here


def both_weights(shift_row, shift_lon, point):
    _, _, row_here, lon_here = point
    return (
        slot_weights(-shift_row, row_here, *bounds(row_here)),
        slot_weights(-shift_lon, lon_here, *bounds(lon_here)),
    )


def wind_levels(base, lanes, k, points, scratch, keep, filling, *out_refs):
    def arrival_wind(field, step):
        middle = (HALO * 5 + HALO) * STACK + step * (5 * STACK) + FIELD_ROW[field]
        return scratch[pl.ds(base + middle, ROWS), :]

    count = range(len(points))
    weights = [
        both_weights(
            COURANT * arrival_wind(1, step), COURANT * arrival_wind(0, step), points[step]
        )
        for step in count
    ]
    row_weights, lon_weights = zip(*weights)
    found = [
        across(scratch, field, base, points, row_weights, lon_weights, filling, keep)
        for field in range(2)
    ]
    filling.flush()
    for step in count:
        east, north = arrival_wind(0, step), arrival_wind(1, step)
        east_found, north_found = found[0][step], found[1][step]
        for sweep in range(ITERS):
            shift_row = 0.5 * COURANT * (north + north_found)
            shift_lon = 0.5 * COURANT * (east + east_found)
            if sweep < ITERS - 1:
                weights = both_weights(shift_row, shift_lon, points[step])
                east_found = across_kept(keep, 0, step, *weights)
                north_found = across_kept(keep, 1, step, *weights)
        for out_ref in out_refs:
            out_ref[0, k + step, :, lanes] = shift_row
            out_ref[1, k + step, :, lanes] = shift_lon


def tracer_levels(shift_ref, base, lanes, k, points, scratch, keep, filling, out_ref):
    weights = [
        both_weights(
            shift_ref[0, k + step, :, lanes], shift_ref[1, k + step, :, lanes], points[step]
        )
        for step in range(len(points))
    ]
    row_weights, lon_weights = zip(*weights)
    found = [
        across(scratch, field, base, points, row_weights, lon_weights, filling)
        for field in range(2)
    ]
    filling.flush()
    for field in range(2):
        for step, total in enumerate(found[field]):
            out_ref[field, k + step, :, lanes] = total.astype(out_ref.dtype)


def interpolation_kernel(
    levels_body, together, near_count, out_count, base_ref, field_ref, points_ref, *others
):
    nears, others = others[:near_count], others[near_count:]
    full, even_scratch, odd_scratch, keep = others[-4:]
    extra, out_refs, done_ref = others[: -5 - out_count], others[-5 - out_count : -5], others[-5]
    done_ref[...] = jnp.zeros(done_ref.shape, done_ref.dtype)
    _, levels, rows, lon_total = points_ref.shape
    chunk_total = lon_total // LANES
    slabs = levels + 2 * HALO
    steps = levels // together
    per_step = -(-slabs // steps)
    full[HALO : HALO + levels] = field_ref[...]
    if near_count == 1:
        found = jnp.where(base_ref[0] == 0, levels + HALO, 0)
        full[pl.ds(found, HALO)] = nears[0][...].astype(jnp.float32)
        empty = levels + HALO - found
        full[pl.ds(empty, HALO)] = jnp.zeros((HALO,) + full.shape[1:], jnp.float32)
    else:
        full[:HALO] = nears[0][...].astype(jnp.float32)
        full[HALO + levels :] = nears[1][...].astype(jnp.float32)

    def first_fill(slab, carry):
        for start, finish in fill_units(slab, 0, chunk_total, full, even_scratch):
            finish(start())
        return carry

    lax.fori_loop(0, slabs, first_fill, 0)

    def one_chunk(chunk, scratch, other):
        lanes = pl.ds(pl.multiple_of(chunk * LANES, LANES), LANES)
        following = jnp.where(chunk == chunk_total - 1, 0, chunk + 1)

        def level_step(step, carry):
            k = step * together
            units = []
            for n in range(per_step):
                slab = jnp.minimum(step * per_step + n, slabs - 1)
                units += fill_units(slab, following, chunk_total, full, other)
            filling = Interleave(units, 32)
            points = [arrival(points_ref, k + n, lanes) for n in range(together)]
            base = pl.multiple_of(k * (5 * STACK), ROWS)
            levels_body(
                *extra, base, lanes, k, points, scratch, keep, filling, *out_refs
            )
            return carry

        lax.fori_loop(0, steps, level_step, 0)

    def chunk_pair(pair, carry):
        one_chunk(2 * pair, even_scratch, odd_scratch)
        one_chunk(2 * pair + 1, odd_scratch, even_scratch)
        return carry

    lax.fori_loop(0, chunk_total // 2, chunk_pair, 0)


def interpolation_call(levels_body, base, fields, points, nears, extra, out_dtype, out_count):
    _, levels, rows, lon_total = points.shape
    count = levels * rows * lon_total
    together = next(n for n in (4, 2, 1) if levels % n == 0)
    scratch = pltpu.VMEM(((levels + 2 * HALO) * 5 * STACK, LANES), jnp.float32)
    in_vmem = pl.BlockSpec(memory_space=pltpu.VMEM)
    out = jax.ShapeDtypeStruct((2, levels, rows, lon_total), out_dtype)
    done = jax.ShapeDtypeStruct((ROWS, LANES), jnp.float32)
    return pl.pallas_call(
        functools.partial(interpolation_kernel, levels_body, together, len(nears), out_count),
        out_shape=(out,) * out_count + (done,),
        in_specs=[pl.BlockSpec(memory_space=pltpu.SMEM)]
        + [in_vmem] * (2 + len(nears) + len(extra)),
        out_specs=(in_vmem,) * (out_count + 1),
        scratch_shapes=[
            pltpu.VMEM((levels + 2 * HALO,) + fields.shape[1:], jnp.float32),
            scratch,
            scratch,
            pltpu.VMEM((2, together, 16, ROWS, LANES), jnp.float32),
        ],
        compiler_params=pltpu.CompilerParams(vmem_limit_bytes=32 * 1024 * 1024),
        cost_estimate=pl.CostEstimate(
            flops=count * 500, bytes_accessed=count * 40, transcendentals=0
        ),
    )(base, fields, points, *nears, *extra)


def swap_levels(send):
    if lax.axis_size("lev") == 2:
        return (lax.ppermute(send[0], "lev", [(0, 1), (1, 0)]),)
    up = [(i, i + 1) for i in range(lax.axis_size("lev") - 1)]
    down = [(j, i) for i, j in up]
    return lax.ppermute(send[1], "lev", up), lax.ppermute(send[0], "lev", down)


def up_to(value, step):
    return -(-value // step) * step


TALL = ROWS + 2 * HALO
PAIRED = TALL // 2
HALF = LANES // 2


def legendre_kernel(numbers_ref, codes_ref, order_ref, spectra_ref, *others):
    tables, others = others[:-7], others[-7:]
    wind_ref, tracer_ref, done_ref, wind_sums, tracer_sums, table_tail, column_tail = others
    _, pairs, level_fields, degrees = spectra_ref.shape
    group = table_tail.shape[0]
    bands, block, _ = wind_ref.shape
    full = degrees // LANES * LANES
    at_top = numbers_ref[0] == 0
    step = pl.program_id(0)

    @pl.when(step == 0)
    def _():
        wind_sums[...] = jnp.zeros(wind_sums.shape, jnp.float32)
        tracer_sums[...] = jnp.zeros(tracer_sums.shape, jnp.float32)
        done_ref[...] = jnp.zeros(done_ref.shape, jnp.float32)
        table_tail[...] = jnp.zeros(table_tail.shape, jnp.float32)
        column_tail[...] = jnp.zeros(column_tail.shape, jnp.float32)
        codes = codes_ref[...]
        code_row = up_to(pl.num_programs(0) * group * PAIRED, ROWS)
        for band in range(bands):
            first = band * block + code_row
            wind_sums[pl.ds(first, 1), :] = jnp.right_shift(codes, 4).astype(jnp.float32)
            wind_sums[pl.ds(first + 1, 1), :] = (codes & 15).astype(jnp.float32)

    band_row = lax.broadcasted_iota(jnp.int32, (bands, LANES), 0)
    first_half = lax.broadcasted_iota(jnp.int32, (bands, LANES), 1) < HALF
    nothing = jnp.zeros((bands, LANES), jnp.float32)
    for p in range(group):
        slot = step * group + p
        edge = degrees - 1 - numbers_ref[1 + slot]
        left = []
        for number, table_ref in enumerate(tables):
            for row in range(table_ref.shape[0]):
                piece = table_ref[row, slot]
                left.append(piece[:, :full])
                first = (number * table_ref.shape[0] + row) * bands
                table_tail[p, first : first + bands, : degrees - full] = piece[:, full:].astype(
                    jnp.float32
                )
        left = jnp.concatenate(left, axis=0)
        left = jnp.concatenate([left, table_tail[p].astype(jnp.bfloat16)], axis=1)
        halves = ([], [])
        for part in range(2):
            piece = spectra_ref[part, slot]
            whole = piece[:, :full].astype(jnp.float32)
            lane = lax.broadcasted_iota(jnp.int32, whole.shape, 1)
            zero = jnp.zeros_like(whole)
            halves[0].append(jnp.where(lane < edge, whole, zero).astype(jnp.bfloat16))
            halves[1].append(jnp.where(lane < edge, zero, whole).astype(jnp.bfloat16))
            first = part * level_fields
            column_tail[p, first : first + level_fields, : degrees - full] = piece[
                :, full:
            ].astype(jnp.float32)
        tail = column_tail[p].astype(jnp.bfloat16)
        right = jnp.concatenate(
            [
                jnp.concatenate([jnp.concatenate(halves[0], axis=0), jnp.zeros_like(tail)], axis=1),
                jnp.concatenate([jnp.concatenate(halves[1], axis=0), tail], axis=1),
            ],
            axis=0,
        )
        found = lax.dot_general(
            left, right, (((1,), (1,)), ((), ())), preferred_element_type=jnp.float32
        )
        found = jnp.dot(
            found.astype(jnp.bfloat16), order_ref[...], preferred_element_type=jnp.float32
        )
        found = [found[i * bands : (i + 1) * bands] for i in range(ROWS)]
        if len(tables) == 2:
            low, high = found[: ROWS // 2], found[ROWS // 2 :]
            found = [jnp.where(at_top, x, y) for x, y in zip(low, high)]
            found += [jnp.where(at_top, y, x) for x, y in zip(low, high)]
        above = [
            jnp.where(band_row == 0, nothing, pltpu.roll(x, 1, 0)) for x in found[ROWS - HALO :]
        ]
        below = [
            jnp.where(band_row == bands - 1, nothing, pltpu.roll(x, bands - 1, 0))
            for x in found[:HALO]
        ]
        rows = above + found + below
        for i in range(PAIRED):
            low, high = rows[i], rows[PAIRED + i]
            place = pl.ds(slot * PAIRED + i, bands, stride=block)
            wind_sums[place, :] = jnp.where(first_half, low, pltpu.roll(high, HALF, 1))
            tracer_sums[place, :] = jnp.where(first_half, pltpu.roll(low, HALF, 1), high)

    @pl.when(step == pl.num_programs(0) - 1)
    def _():
        wind_ref[...] = wind_sums[...].astype(jnp.bfloat16).reshape(wind_ref.shape)
        tracer_ref[...] = tracer_sums[...].astype(jnp.bfloat16).reshape(tracer_ref.shape)


def column_order(level_fields):
    levels = level_fields // 4
    order = np.zeros((4 * level_fields, LANES), np.float32)
    for column in range(4 * level_fields):
        part, rest = divmod(column, level_fields)
        level, field = divmod(rest, 4)
        target = (field // 2) * HALF + part * 2 * levels + 2 * level + field % 2
        order[column, target] = 1.0
    return order.astype(jnp.bfloat16)


def block_rows(pairs):
    return up_to(up_to(pairs * PAIRED, ROWS) + 2, 16)


def legendre_call(pairing, spectra, tables):
    _, pairs, level_fields, degrees = spectra.shape
    bands = tables[0].shape[2]
    block = block_rows(pairs)
    group = next(n for n in (4, 5, 2, 1) if pairs % n == 0)
    numbers = jnp.concatenate([lax.axis_index("lev").astype(jnp.int32)[None], pairing])
    codes = jnp.pad(pairing, (0, LANES - pairs))[None, :]
    shape = jax.ShapeDtypeStruct((bands, block, LANES), jnp.bfloat16)
    whole = pl.BlockSpec((bands, block, LANES), lambda i: (0, 0, 0))
    in_vmem = pl.BlockSpec(memory_space=pltpu.VMEM)
    return pl.pallas_call(
        legendre_kernel,
        grid=(pairs // group,),
        out_shape=(shape, shape, jax.ShapeDtypeStruct((ROWS, LANES), jnp.float32)),
        in_specs=[
            pl.BlockSpec(memory_space=pltpu.SMEM),
            pl.BlockSpec((1, LANES), lambda i: (0, 0)),
            pl.BlockSpec((4 * level_fields, LANES), lambda i: (0, 0)),
            in_vmem,
        ]
        + [in_vmem] * len(tables),
        out_specs=(whole, whole, in_vmem),
        scratch_shapes=[
            pltpu.VMEM((bands * block, LANES), jnp.float32),
            pltpu.VMEM((bands * block, LANES), jnp.float32),
            pltpu.VMEM((group, ROWS * bands, LANES), jnp.float32),
            pltpu.VMEM((group, 2 * level_fields, LANES), jnp.float32),
        ],
        compiler_params=pltpu.CompilerParams(vmem_limit_bytes=32 * 1024 * 1024),
        cost_estimate=pl.CostEstimate(
            flops=2 * ROWS * bands * 4 * level_fields * pairs * degrees,
            bytes_accessed=8_000_000,
            transcendentals=0,
        ),
    )(numbers, codes, jnp.asarray(column_order(level_fields)), spectra, *tables)


def fourier_table(pair_total, padded, lon_total):
    order_total = 2 * pair_total
    half = pair_total // 2
    low = 2 * np.arange(half)
    high = low + 1
    even = np.concatenate([low, order_total - 1 - high])
    odd = np.concatenate([order_total - 1 - low, high])
    lon = np.arange(lon_total // 2)
    table = np.zeros((2, 2, padded, lon_total // 2), np.float32)
    for parity, orders in enumerate((even, odd)):
        phase = (orders[:, None] * lon[None, :]) % lon_total * (2.0 * math.pi / lon_total)
        weight = np.where(orders == 0, 1.0, 2.0)[:, None]
        table[parity, 0, :pair_total] = weight * np.cos(phase)
        table[parity, 1, :pair_total] = -weight * np.sin(phase)
    return table.reshape(2, 2 * padded, lon_total // 2).astype(jnp.bfloat16)


def owner_tables(bands, pairs):
    slots = np.arange(bands * pairs)
    owner = slots[:, None] // pairs == np.arange(LANES)[None, :]
    lane = slots[:, None] % pairs == np.arange(LANES)[None, :]
    return owner.astype(jnp.bfloat16), lane.astype(np.float32)


def pair_places(flat, owner_ref, lane_ref, codes, bands, block, code_row, padded):
    pair_total = owner_ref.shape[0]
    codes[...] = jnp.zeros(codes.shape, jnp.float32)
    numbers = []
    for part in range(2):
        codes[part, :bands, :] = flat[pl.ds(code_row + part, bands, stride=block), :]
        numbers.append(
            jnp.dot(
                owner_ref[...],
                codes[part].astype(jnp.bfloat16),
                preferred_element_type=jnp.float32,
            )
        )
    pair_id = jnp.sum(
        (16.0 * numbers[0] + numbers[1]) * lane_ref[...], axis=1, keepdims=True
    ).astype(jnp.int32)
    place = jnp.right_shift(pair_id, 1) + (pair_id & 1) * (pair_total // 2)
    columns = lax.broadcasted_iota(jnp.int32, (pair_total, padded), 1)
    place = jnp.where(columns == place, 1.0, 0.0)
    if padded > pair_total:
        place = jnp.concatenate(
            [place, jnp.zeros((padded - pair_total, padded), jnp.float32)], axis=0
        )
    return place.astype(jnp.bfloat16)


def fourier_kernel(pairs, levels, leads, base_ref, sums_ref, table_ref, *others):
    if leads:
        owner_ref, lane_ref, field_ref, send_ref, place_ref = others[:5]
    else:
        place_ref, _, field_ref, send_ref = others[:4]
    codes, flat, gathered, lhs = others[-4:]
    bands, block, width = sums_ref.shape
    pair_total = bands * pairs
    padded = gathered.shape[0]
    blocks = padded // LANES
    fields = 2 * levels
    flat[...] = sums_ref[...].astype(jnp.float32).reshape(bands * block, width)
    gathered[pair_total:, :] = jnp.zeros((padded - pair_total, width), jnp.float32)
    if leads:
        code_row = up_to(pairs * PAIRED, ROWS)
        place_ref[...] = pair_places(
            flat, owner_ref, lane_ref, codes, bands, block, code_row, padded
        )
    place = place_ref[...]
    low = lax.broadcasted_iota(jnp.int32, (fields, padded), 1) < pair_total // 2
    middle = fields * ROWS
    for i in range(PAIRED):
        for band in range(bands):
            gathered[band * pairs : (band + 1) * pairs, :] = flat[
                pl.ds(band * block + i, pairs, stride=PAIRED), :
            ]
        ordered = jnp.dot(
            gathered[...].T.astype(jnp.bfloat16), place, preferred_element_type=jnp.float32
        )
        for side in range(2):
            row = side * PAIRED + i
            if HALO <= row < HALO + ROWS:
                first, stride = row - HALO, ROWS
            else:
                first, stride = middle + (row - HALO - ROWS) % TALL, 2 * HALO
            for part in range(2):
                start = side * HALF + part * fields
                straight = ordered[start : start + fields]
                start = start + 2 * fields
                crossed = ordered[start : start + fields]
                both = (jnp.where(low, straight, crossed), jnp.where(low, crossed, straight))
                for parity in range(2):
                    for t in range(blocks):
                        lhs[parity, part * blocks + t, pl.ds(first, fields, stride=stride), :] = (
                            both[parity][:, t * LANES : (t + 1) * LANES]
                        )
    half = table_ref.shape[2]

    def transform(first, count):
        found = []
        for parity in range(2):
            left = jnp.concatenate(
                [
                    lhs[parity, t, first : first + count, :].astype(jnp.bfloat16)
                    for t in range(2 * blocks)
                ],
                axis=1,
            )
            found.append(jnp.dot(left, table_ref[parity], preferred_element_type=jnp.float32))
        pieces = (found[0] + found[1], found[0] - found[1])
        return [piece.astype(jnp.bfloat16).astype(jnp.float32) for piece in pieces]

    group = next(n for n in (4, 2, 1) if levels % n == 0)
    for level in range(0, levels, group):
        pieces = transform(level * 2 * ROWS, group * 2 * ROWS)
        for part, value in enumerate(pieces):
            value = value.reshape(group, 2 * ROWS, half)
            field_ref[level : level + group, : 2 * ROWS, part * half : (part + 1) * half] = value
    for part, value in enumerate(transform(middle, fields * 2 * HALO)):
        value = value.reshape(levels, 4 * HALO, half)
        field_ref[:, 2 * ROWS :, part * half : (part + 1) * half] = value
    if send_ref.shape[0] == 1:
        start = jnp.where(base_ref[0] == 0, levels - HALO, 0)
        send_ref[0] = field_ref[pl.ds(start, HALO)].astype(jnp.bfloat16)
    else:
        send_ref[0] = field_ref[:HALO].astype(jnp.bfloat16)
        send_ref[1] = field_ref[levels - HALO :].astype(jnp.bfloat16)


def fourier_call(base, sums, table, pairs, levels, lon_total, place=None, after=None):
    bands, block, width = sums.shape
    pair_total = bands * pairs
    padded = up_to(pair_total, LANES)
    leads = place is None
    sends = 1 if lax.axis_size("lev") == 2 else 2
    field_shape = (levels, 3 * ROWS, lon_total)
    out_shape = [
        jax.ShapeDtypeStruct(field_shape, jnp.float32),
        jax.ShapeDtypeStruct((sends, HALO) + field_shape[1:], jnp.bfloat16),
    ]
    extra = [place, after]
    if leads:
        out_shape.append(jax.ShapeDtypeStruct((padded, padded), jnp.bfloat16))
        extra = [jnp.asarray(x) for x in owner_tables(bands, pairs)]
    in_vmem = pl.BlockSpec(memory_space=pltpu.VMEM)
    return pl.pallas_call(
        functools.partial(fourier_kernel, pairs, levels, leads),
        out_shape=tuple(out_shape),
        in_specs=[
            pl.BlockSpec(memory_space=pltpu.SMEM),
            in_vmem,
            in_vmem,
        ]
        + [in_vmem] * 2,
        out_specs=(in_vmem,) * len(out_shape),
        scratch_shapes=[
            pltpu.VMEM((2, LANES, LANES), jnp.float32),
            pltpu.VMEM((bands * block, width), jnp.float32),
            pltpu.VMEM((padded, width), jnp.float32),
            pltpu.VMEM((2, 2 * padded // LANES, 2 * levels * TALL, LANES), jnp.float32),
        ],
        compiler_params=pltpu.CompilerParams(vmem_limit_bytes=32 * 1024 * 1024),
        cost_estimate=pl.CostEstimate(
            flops=2 * levels * 4 * TALL * padded * lon_total,
            bytes_accessed=8_000_000,
            transcendentals=0,
        ),
    )(base, sums, table, *extra)


def exchange(sums):
    return lax.all_to_all(sums, "band", split_axis=0, concat_axis=0, tiled=True)


def per_device(spectra, legendre, pairing, eta_shift, cells):
    levels, rows, lon_total = eta_shift.shape
    pairs = pairing.shape[0]
    spectra = jnp.transpose(spectra, (0, 2, 1, 3))
    table = jnp.transpose(legendre, (0, 2, 1, 3))
    if lax.axis_size("lev") == 2:
        tables = (table, lax.ppermute(table, "lev", [(0, 1), (1, 0)]))
    else:
        tables = (lax.all_gather(table, "lev", axis=0, tiled=True),)
    base = jnp.stack([lax.axis_index("lev") * levels, lax.axis_index("band") * rows])
    base = base.astype(jnp.int32)
    wind_sums, tracer_sums, done = legendre_call(pairing, spectra, tables)
    wind_sums = exchange(wind_sums)
    tracer_sums = exchange(tracer_sums)
    pair_total = pairs * lax.axis_size("band")
    twiddles = jnp.asarray(fourier_table(pair_total, up_to(pair_total, LANES), lon_total))
    points, twiddles = prepare_call(base, done, eta_shift, cells, twiddles)
    size = (pairs, levels, lon_total)
    winds, send, place = fourier_call(base, wind_sums, twiddles, *size)
    displacement, moved, done = interpolation_call(
        wind_levels, base, winds, points, swap_levels(send), (), jnp.float32, 2
    )
    tracers, send = fourier_call(base, tracer_sums, twiddles, *size, place, done)
    advected, _ = interpolation_call(
        tracer_levels, base, tracers, points, swap_levels(send), (moved,), jnp.bfloat16, 1
    )
    return advected, displacement


def solution(mesh):
    return jax.shard_map(
        per_device,
        mesh=mesh,
        in_specs=(
            P(None, "lev", "band", None),
            P("lev", None, "band", None),
            P("band"),
            P("lev", "band", None),
            P(None, "lev", "band", None),
        ),
        out_specs=(P(None, "lev", "band", None), P(None, "lev", "band", None)),
        check_vma=False,
    )
```

```python
import functools
import math

import jax
import jax.numpy as jnp
import numpy as np
from jax import lax
from jax.experimental import pallas as pl
from jax.experimental.pallas import tpu as pltpu
from jax.sharding import PartitionSpec as P

ITERS = 2


COURANT = 0.8
HALO = 2
LANES = 128
ROWS = 8
SLOTS = (-1, 0, 1, 2)


def slot_weights(place, here, low, high, sixth):
    z = jnp.minimum(jnp.maximum(place, low), high)
    square = z * z
    less = square - 1.0
    outer = less * z * sixth
    triple = 3.0 * outer
    half = 0.5 * z
    half_square = 0.5 * square
    return (
        half_square - half - jnp.where(here, outer, triple),
        triple - less,
        half_square + half - jnp.where(here, triple, outer),
        outer,
    )


def bounds(here):
    return (
        jnp.where(here, -0.5, -1.5),
        jnp.where(here, 1.5, 0.5),
        jnp.where(here, 1.0 / 6.0, -1.0 / 6.0),
    )


def weighted(weights, values):
    return (weights[0] * values[0] + weights[1] * values[1]) + (
        weights[2] * values[2] + weights[3] * values[3]
    )


def shifted_lanes(before, here, after, lane):
    return (
        pltpu.roll(jnp.where(lane < LANES - 2, here, before), 2, 1),
        pltpu.roll(jnp.where(lane < LANES - 1, here, before), 1, 1),
        here,
        pltpu.roll(jnp.where(lane < 1, after, here), LANES - 1, 1),
        pltpu.roll(jnp.where(lane < 2, after, here), LANES - 2, 1),
    )


STACK = 5 * ROWS
FIELD_ROW = (ROWS, 3 * ROWS)


def fill_units(slab, chunk, chunk_total, field_ref, scratch):
    before = jnp.where(chunk == 0, chunk_total - 1, chunk - 1)
    after = jnp.where(chunk == chunk_total - 1, 0, chunk + 1)
    starts = [pl.multiple_of(c * LANES, LANES) for c in (before, chunk, after)]
    lane = lax.broadcasted_iota(jnp.int32, (ROWS, LANES), 1)
    first = pl.multiple_of(slab * (5 * STACK), ROWS)

    def edge_start():
        moved = shifted_lanes(
            *[field_ref[slab, 2 * ROWS : 3 * ROWS, pl.ds(s, LANES)] for s in starts], lane
        )
        return [(value, pltpu.roll(value, ROWS // 2, 0)) for value in moved]

    def edge_finish(values):
        for step, (between, outside) in enumerate(values):
            for offset, value in ((0, outside), (2 * ROWS, between), (4 * ROWS, outside)):
                scratch[pl.ds(first + (step * STACK + offset), ROWS), :] = value

    def center_unit(field):
        def start():
            rows = slice(field * ROWS, (field + 1) * ROWS)
            blocks = [field_ref[slab, rows, pl.ds(s, LANES)] for s in starts]
            return shifted_lanes(*blocks, lane)

        def finish(values):
            for step, moved in enumerate(values):
                scratch[pl.ds(first + (step * STACK + FIELD_ROW[field]), ROWS), :] = moved

        return start, finish

    return [(edge_start, edge_finish)] + [center_unit(field) for field in range(2)]


class Interleave:
    def __init__(self, units, ticks):
        self.units = list(units)
        self.every = max(1, ticks // max(1, len(self.units)))
        self.count = 0
        self.pending = None

    def advance(self):
        if self.pending is not None:
            self.pending[0](self.pending[1])
            self.pending = None
        if self.units:
            start, finish = self.units.pop(0)
            self.pending = (finish, start())

    def tick(self):
        if self.count % self.every == 0:
            self.advance()
        self.count += 1

    def flush(self):
        while self.units or self.pending is not None:
            self.advance()


def level_sums(scratch, field, base, slot, points):
    loaded = {}

    def load(a, b, c):
        offset = ((a + HALO) * 5 + c + HALO) * STACK + FIELD_ROW[field] + b
        if slot == (2, 2):
            return scratch[pl.ds(base + offset, ROWS), :]
        if (a, b, c) not in loaded:
            loaded[a, b, c] = scratch[pl.ds(base + offset, ROWS), :]
        return loaded[a, b, c]

    def one(step, weights, level_here, row_here, lon_here):
        def pick_lon(a, b):
            if slot[1] == 2:
                return jnp.where(lon_here, load(a + step, b, 2), load(a + step, b, -2))
            return load(a + step, b, slot[1])

        def pick(a):
            if slot[0] == 2:
                return jnp.where(row_here, pick_lon(a, 2), pick_lon(a, -2))
            return pick_lon(a, slot[0])

        total = weights[0] * pick(-1) + weights[1] * pick(0)
        total = total + weights[2] * pick(1)
        return total + weights[3] * jnp.where(level_here, pick(2), pick(-2))

    return [one(step, *point) for step, point in enumerate(points)]


def across(scratch, field, base, points, row_weights, lon_weights, filling, keep=None):
    columns = [[None] * 4 for _ in points]
    for b, row_slot in enumerate(SLOTS):
        for c, lon_slot in enumerate(SLOTS):
            filling.tick()
            found = level_sums(scratch, field, base, (row_slot, lon_slot), points)
            for step, value in enumerate(found):
                if keep is not None:
                    keep[field, step, 4 * b + c] = value
                term = row_weights[step][b] * value
                columns[step][c] = term if b == 0 else columns[step][c] + term
    return [weighted(weights, column) for weights, column in zip(lon_weights, columns)]


def across_kept(keep, field, step, row_weights, lon_weights):
    return weighted(
        lon_weights,
        [
            weighted(row_weights, [keep[field, step, 4 * b + c] for b in range(4)])
            for c in range(4)
        ],
    )


def prepare_kernel(
    base_ref, eta_ref, cells_ref, table_ref, sums_ref, points_ref, table_out, sums_out, sems
):
    copies = [
        pltpu.make_async_copy(table_ref, table_out, sems.at[0]),
        pltpu.make_async_copy(sums_ref, sums_out, sems.at[1]),
    ]
    for copy in copies:
        copy.start()
    levels, rows, lon_total = eta_ref.shape
    shape = (rows, LANES)
    row_here = base_ref[1] + lax.broadcasted_iota(jnp.int32, shape, 0)
    lane = lax.broadcasted_iota(jnp.int32, shape, 1)

    def chunk_step(chunk, carry):
        lanes = pl.ds(pl.multiple_of(chunk * LANES, LANES), LANES)
        for k in range(levels):
            level_here = cells_ref[2, k, :, lanes] == base_ref[0] + k
            weights = slot_weights(
                -eta_ref[k, :, lanes].astype(jnp.float32), level_here, *bounds(level_here)
            )
            here = (
                level_here,
                cells_ref[0, k, :, lanes] == row_here,
                cells_ref[1, k, :, lanes] == chunk * LANES + lane,
            )
            for n, value in enumerate(weights + tuple(bounds(x)[0] for x in here)):
                points_ref[n, k, :, lanes] = value
        return carry

    lax.fori_loop(0, lon_total // LANES, chunk_step, 0)
    for copy in copies:
        copy.wait()


def prepare_call(base, eta_shift, cells, table, sums):
    in_vmem = pl.BlockSpec(memory_space=pltpu.VMEM)
    return pl.pallas_call(
        prepare_kernel,
        out_shape=(
            jax.ShapeDtypeStruct((7,) + eta_shift.shape, jnp.float32),
            jax.ShapeDtypeStruct(table.shape, table.dtype),
            jax.ShapeDtypeStruct(sums.shape, sums.dtype),
        ),
        in_specs=[pl.BlockSpec(memory_space=pltpu.SMEM)]
        + [in_vmem] * 2
        + [pl.BlockSpec(memory_space=pl.ANY)] * 2,
        out_specs=(in_vmem, in_vmem, pl.BlockSpec(memory_space=pl.ANY)),
        scratch_shapes=[pltpu.SemaphoreType.DMA((2,))],
        compiler_params=pltpu.CompilerParams(vmem_limit_bytes=16 * 1024 * 1024),
        cost_estimate=pl.CostEstimate(
            flops=40 * eta_shift.size, bytes_accessed=20_000_000, transcendentals=0
        ),
    )(base, eta_shift, cells, table, sums)


def arrival(points_ref, k, lanes):
    here = [points_ref[n, k, :, lanes] > -1.0 for n in range(4, 7)]
    return tuple(points_ref[n, k, :, lanes] for n in range(4)), *here


def both_weights(shift_row, shift_lon, point):
    _, _, row_here, lon_here = point
    return (
        slot_weights(-shift_row, row_here, *bounds(row_here)),
        slot_weights(-shift_lon, lon_here, *bounds(lon_here)),
    )


def wind_levels(base, lanes, k, points, scratch, keep, filling, *out_refs):
    def arrival_wind(field, step):
        middle = (HALO * 5 + HALO) * STACK + step * (5 * STACK) + FIELD_ROW[field]
        return scratch[pl.ds(base + middle, ROWS), :]

    count = range(len(points))
    weights = [
        both_weights(
            COURANT * arrival_wind(1, step), COURANT * arrival_wind(0, step), points[step]
        )
        for step in count
    ]
    row_weights, lon_weights = zip(*weights)
    found = [
        across(scratch, field, base, points, row_weights, lon_weights, filling, keep)
        for field in range(2)
    ]
    filling.flush()
    for step in count:
        east, north = arrival_wind(0, step), arrival_wind(1, step)
        east_found, north_found = found[0][step], found[1][step]
        for sweep in range(ITERS):
            shift_row = 0.5 * COURANT * (north + north_found)
            shift_lon = 0.5 * COURANT * (east + east_found)
            if sweep < ITERS - 1:
                weights = both_weights(shift_row, shift_lon, points[step])
                east_found = across_kept(keep, 0, step, *weights)
                north_found = across_kept(keep, 1, step, *weights)
        for out_ref in out_refs:
            out_ref[0, k + step, :, lanes] = shift_row
            out_ref[1, k + step, :, lanes] = shift_lon


def tracer_levels(shift_ref, base, lanes, k, points, scratch, keep, filling, out_ref):
    weights = [
        both_weights(
            shift_ref[0, k + step, :, lanes], shift_ref[1, k + step, :, lanes], points[step]
        )
        for step in range(len(points))
    ]
    row_weights, lon_weights = zip(*weights)
    found = [
        across(scratch, field, base, points, row_weights, lon_weights, filling)
        for field in range(2)
    ]
    filling.flush()
    for field in range(2):
        for step, total in enumerate(found[field]):
            out_ref[field, k + step, :, lanes] = total.astype(out_ref.dtype)


def interpolation_kernel(
    levels_body, together, near_count, out_count, base_ref, field_ref, points_ref, *others
):
    nears, others = others[:near_count], others[near_count:]
    full, even_scratch, odd_scratch, keep = others[-4:]
    extra, out_refs, done_ref = others[: -5 - out_count], others[-5 - out_count : -5], others[-5]
    done_ref[...] = jnp.zeros(done_ref.shape, done_ref.dtype)
    _, levels, rows, lon_total = points_ref.shape
    chunk_total = lon_total // LANES
    slabs = levels + 2 * HALO
    steps = levels // together
    per_step = -(-slabs // steps)
    full[HALO : HALO + levels] = field_ref[...]
    if near_count == 1:
        found = jnp.where(base_ref[0] == 0, levels + HALO, 0)
        full[pl.ds(found, HALO)] = nears[0][...].astype(jnp.float32)
        empty = levels + HALO - found
        full[pl.ds(empty, HALO)] = jnp.zeros((HALO,) + full.shape[1:], jnp.float32)
    else:
        full[:HALO] = nears[0][...].astype(jnp.float32)
        full[HALO + levels :] = nears[1][...].astype(jnp.float32)

    def first_fill(slab, carry):
        for start, finish in fill_units(slab, 0, chunk_total, full, even_scratch):
            finish(start())
        return carry

    lax.fori_loop(0, slabs, first_fill, 0)

    def one_chunk(chunk, scratch, other):
        lanes = pl.ds(pl.multiple_of(chunk * LANES, LANES), LANES)
        following = jnp.where(chunk == chunk_total - 1, 0, chunk + 1)

        def level_step(step, carry):
            k = step * together
            units = []
            for n in range(per_step):
                slab = jnp.minimum(step * per_step + n, slabs - 1)
                units += fill_units(slab, following, chunk_total, full, other)
            filling = Interleave(units, 32)
            points = [arrival(points_ref, k + n, lanes) for n in range(together)]
            base = pl.multiple_of(k * (5 * STACK), ROWS)
            levels_body(
                *extra, base, lanes, k, points, scratch, keep, filling, *out_refs
            )
            return carry

        lax.fori_loop(0, steps, level_step, 0)

    def chunk_pair(pair, carry):
        one_chunk(2 * pair, even_scratch, odd_scratch)
        one_chunk(2 * pair + 1, odd_scratch, even_scratch)
        return carry

    lax.fori_loop(0, chunk_total // 2, chunk_pair, 0)


def interpolation_call(levels_body, base, fields, points, nears, extra, out_dtype, out_count):
    _, levels, rows, lon_total = points.shape
    count = levels * rows * lon_total
    together = next(n for n in (4, 2, 1) if levels % n == 0)
    scratch = pltpu.VMEM(((levels + 2 * HALO) * 5 * STACK, LANES), jnp.float32)
    in_vmem = pl.BlockSpec(memory_space=pltpu.VMEM)
    out = jax.ShapeDtypeStruct((2, levels, rows, lon_total), out_dtype)
    done = jax.ShapeDtypeStruct((ROWS, LANES), jnp.float32)
    return pl.pallas_call(
        functools.partial(interpolation_kernel, levels_body, together, len(nears), out_count),
        out_shape=(out,) * out_count + (done,),
        in_specs=[pl.BlockSpec(memory_space=pltpu.SMEM)]
        + [in_vmem] * (2 + len(nears) + len(extra)),
        out_specs=(in_vmem,) * (out_count + 1),
        scratch_shapes=[
            pltpu.VMEM((levels + 2 * HALO,) + fields.shape[1:], jnp.float32),
            scratch,
            scratch,
            pltpu.VMEM((2, together, 16, ROWS, LANES), jnp.float32),
        ],
        compiler_params=pltpu.CompilerParams(vmem_limit_bytes=16 * 1024 * 1024),
        cost_estimate=pl.CostEstimate(
            flops=count * 500, bytes_accessed=count * 40, transcendentals=0
        ),
    )(base, fields, points, *nears, *extra)


def swap_levels(send):
    if lax.axis_size("lev") == 2:
        return (lax.ppermute(send[0], "lev", [(0, 1), (1, 0)]),)
    up = [(i, i + 1) for i in range(lax.axis_size("lev") - 1)]
    down = [(j, i) for i, j in up]
    return lax.ppermute(send[1], "lev", up), lax.ppermute(send[0], "lev", down)


def up_to(value, step):
    return -(-value // step) * step


TALL = ROWS + 2 * HALO
PAIRED = TALL // 2
HALF = LANES // 2


def touch_kernel(numbers_ref, spectra_ref, table_ref, out_ref):
    out_ref[...] = numbers_ref[...]


def legendre_kernel(numbers_ref, codes_ref, spectra_ref, *others):
    tables, others = others[:-8], others[-8:]
    wind_ref, tracer_ref, done_ref, wind_sums, tracer_sums = others[:5]
    table_tail, column_tail, order_ref = others[5:]
    _, pairs, level_fields, degrees = spectra_ref.shape
    group = table_tail.shape[0]
    bands, block, _ = wind_ref.shape
    full = degrees // LANES * LANES
    at_top = numbers_ref[0] == 0
    step = pl.program_id(0)

    @pl.when(step == 0)
    def _():
        wind_sums[...] = jnp.zeros(wind_sums.shape, jnp.float32)
        tracer_sums[...] = jnp.zeros(tracer_sums.shape, jnp.float32)
        done_ref[...] = jnp.zeros(done_ref.shape, jnp.float32)
        table_tail[...] = jnp.zeros(table_tail.shape, jnp.float32)
        column_tail[...] = jnp.zeros(column_tail.shape, jnp.float32)
        order_ref[...] = column_order(level_fields)
        codes = codes_ref[...]
        code_row = up_to(pl.num_programs(0) * group * PAIRED, ROWS)
        for band in range(bands):
            first = band * block + code_row
            wind_sums[pl.ds(first, 1), :] = jnp.right_shift(codes, 4).astype(jnp.float32)
            wind_sums[pl.ds(first + 1, 1), :] = (codes & 15).astype(jnp.float32)

    band_row = lax.broadcasted_iota(jnp.int32, (bands, LANES), 0)
    first_half = lax.broadcasted_iota(jnp.int32, (bands, LANES), 1) < HALF
    nothing = jnp.zeros((bands, LANES), jnp.float32)
    for p in range(group):
        slot = step * group + p
        edge = degrees - 1 - numbers_ref[1 + slot]
        left = []
        for number, table_ref in enumerate(tables):
            for row in range(table_ref.shape[0]):
                piece = table_ref[row, slot]
                left.append(piece[:, :full])
                first = (number * table_ref.shape[0] + row) * bands
                table_tail[p, first : first + bands, : degrees - full] = piece[:, full:].astype(
                    jnp.float32
                )
        left = jnp.concatenate(left, axis=0)
        left = jnp.concatenate([left, table_tail[p].astype(jnp.bfloat16)], axis=1)
        halves = ([], [])
        for part in range(2):
            piece = spectra_ref[part, slot]
            whole = piece[:, :full].astype(jnp.float32)
            lane = lax.broadcasted_iota(jnp.int32, whole.shape, 1)
            zero = jnp.zeros_like(whole)
            halves[0].append(jnp.where(lane < edge, whole, zero).astype(jnp.bfloat16))
            halves[1].append(jnp.where(lane < edge, zero, whole).astype(jnp.bfloat16))
            first = part * level_fields
            column_tail[p, first : first + level_fields, : degrees - full] = piece[
                :, full:
            ].astype(jnp.float32)
        tail = column_tail[p].astype(jnp.bfloat16)
        right = jnp.concatenate(
            [
                jnp.concatenate([jnp.concatenate(halves[0], axis=0), jnp.zeros_like(tail)], axis=1),
                jnp.concatenate([jnp.concatenate(halves[1], axis=0), tail], axis=1),
            ],
            axis=0,
        )
        found = lax.dot_general(
            left, right, (((1,), (1,)), ((), ())), preferred_element_type=jnp.float32
        )
        found = jnp.dot(
            found.astype(jnp.bfloat16), order_ref[...], preferred_element_type=jnp.float32
        )
        found = [found[i * bands : (i + 1) * bands] for i in range(ROWS)]
        if len(tables) == 2:
            low, high = found[: ROWS // 2], found[ROWS // 2 :]
            found = [jnp.where(at_top, x, y) for x, y in zip(low, high)]
            found += [jnp.where(at_top, y, x) for x, y in zip(low, high)]
        above = [
            jnp.where(band_row == 0, nothing, pltpu.roll(x, 1, 0)) for x in found[ROWS - HALO :]
        ]
        below = [
            jnp.where(band_row == bands - 1, nothing, pltpu.roll(x, bands - 1, 0))
            for x in found[:HALO]
        ]
        rows = above + found + below
        for i in range(PAIRED):
            low, high = rows[i], rows[PAIRED + i]
            place = pl.ds(slot * PAIRED + i, bands, stride=block)
            wind_sums[place, :] = jnp.where(first_half, low, pltpu.roll(high, HALF, 1))
            tracer_sums[place, :] = jnp.where(first_half, pltpu.roll(low, HALF, 1), high)

    @pl.when(step == pl.num_programs(0) - 1)
    def _():
        wind_ref[...] = wind_sums[...].astype(jnp.bfloat16).reshape(wind_ref.shape)
        tracer_ref[...] = tracer_sums[...].astype(jnp.bfloat16).reshape(tracer_ref.shape)


def column_order(level_fields):
    shift = level_fields.bit_length() - 1
    shape = (4 * level_fields, LANES)
    column = lax.broadcasted_iota(jnp.int32, shape, 0)
    part = jnp.right_shift(column, shift)
    rest = column & (level_fields - 1)
    target = jnp.right_shift(rest & 3, 1) * HALF + part * (level_fields // 2)
    target = target + 2 * jnp.right_shift(rest, 2) + (rest & 1)
    here = lax.broadcasted_iota(jnp.int32, shape, 1) == target
    return jnp.where(here, 1.0, 0.0).astype(jnp.bfloat16)


def block_rows(pairs):
    return up_to(up_to(pairs * PAIRED, ROWS) + 2, 16)


def legendre_call(pairing, spectra, tables):
    _, pairs, level_fields, degrees = spectra.shape
    bands = tables[0].shape[2]
    block = block_rows(pairs)
    group = next(n for n in (4, 5, 2, 1) if pairs % n == 0)
    numbers = jnp.concatenate([lax.axis_index("lev").astype(jnp.int32)[None], pairing])
    codes = pl.pallas_call(
        touch_kernel,
        out_shape=jax.ShapeDtypeStruct((1, LANES), jnp.int32),
        in_specs=[pl.BlockSpec(memory_space=pltpu.VMEM)] * 3,
        out_specs=pl.BlockSpec(memory_space=pltpu.VMEM),
        cost_estimate=pl.CostEstimate(flops=0, bytes_accessed=4_000_000, transcendentals=0),
    )(jnp.pad(pairing, (0, LANES - pairs))[None, :], spectra, tables[0])
    shape = jax.ShapeDtypeStruct((bands, block, LANES), jnp.bfloat16)
    whole = pl.BlockSpec((bands, block, LANES), lambda i: (0, 0, 0))
    in_vmem = pl.BlockSpec(memory_space=pltpu.VMEM)
    return pl.pallas_call(
        legendre_kernel,
        grid=(pairs // group,),
        out_shape=(shape, shape, jax.ShapeDtypeStruct((ROWS, LANES), jnp.float32)),
        in_specs=[
            pl.BlockSpec(memory_space=pltpu.SMEM),
            pl.BlockSpec((1, LANES), lambda i: (0, 0)),
            in_vmem,
        ]
        + [in_vmem] * len(tables),
        out_specs=(whole, whole, in_vmem),
        scratch_shapes=[
            pltpu.VMEM((bands * block, LANES), jnp.float32),
            pltpu.VMEM((bands * block, LANES), jnp.float32),
            pltpu.VMEM((group, ROWS * bands, LANES), jnp.float32),
            pltpu.VMEM((group, 2 * level_fields, LANES), jnp.float32),
            pltpu.VMEM((4 * level_fields, LANES), jnp.bfloat16),
        ],
        compiler_params=pltpu.CompilerParams(vmem_limit_bytes=16 * 1024 * 1024),
        cost_estimate=pl.CostEstimate(
            flops=2 * ROWS * bands * 4 * level_fields * pairs * degrees,
            bytes_accessed=8_000_000,
            transcendentals=0,
        ),
    )(numbers, codes, spectra, *tables)


def fourier_table(pair_total, padded, lon_total):
    order_total = 2 * pair_total
    half = pair_total // 2
    low = 2 * np.arange(half)
    high = low + 1
    even = np.concatenate([low, order_total - 1 - high])
    odd = np.concatenate([order_total - 1 - low, high])
    lon = np.arange(lon_total // 2)
    table = np.zeros((2, 2, padded, lon_total // 2), np.float32)
    for parity, orders in enumerate((even, odd)):
        phase = (orders[:, None] * lon[None, :]) % lon_total * (2.0 * math.pi / lon_total)
        weight = np.where(orders == 0, 1.0, 2.0)[:, None]
        table[parity, 0, :pair_total] = weight * np.cos(phase)
        table[parity, 1, :pair_total] = -weight * np.sin(phase)
    return table.reshape(2, 2 * padded, lon_total // 2).astype(jnp.bfloat16)


def owner_tables(bands, pairs):
    slots = np.arange(bands * pairs)
    owner = slots[:, None] // pairs == np.arange(LANES)[None, :]
    lane = slots[:, None] % pairs == np.arange(LANES)[None, :]
    return owner.astype(jnp.bfloat16), lane.astype(np.float32)


def pair_places(flat, owner_ref, lane_ref, codes, bands, block, code_row, padded):
    pair_total = owner_ref.shape[0]
    codes[...] = jnp.zeros(codes.shape, jnp.float32)
    numbers = []
    for part in range(2):
        codes[part, :bands, :] = flat[pl.ds(code_row + part, bands, stride=block), :]
        numbers.append(
            jnp.dot(
                owner_ref[...],
                codes[part].astype(jnp.bfloat16),
                preferred_element_type=jnp.float32,
            )
        )
    pair_id = jnp.sum(
        (16.0 * numbers[0] + numbers[1]) * lane_ref[...], axis=1, keepdims=True
    ).astype(jnp.int32)
    place = jnp.right_shift(pair_id, 1) + (pair_id & 1) * (pair_total // 2)
    columns = lax.broadcasted_iota(jnp.int32, (pair_total, padded), 1)
    place = jnp.where(columns == place, 1.0, 0.0)
    if padded > pair_total:
        place = jnp.concatenate(
            [place, jnp.zeros((padded - pair_total, padded), jnp.float32)], axis=0
        )
    return place.astype(jnp.bfloat16)


def fourier_kernel(pairs, levels, leads, base_ref, sums_ref, table_ref, *others):
    if leads:
        owner_ref, lane_ref, field_ref, send_ref, place_ref = others[:5]
    else:
        place_ref, _, field_ref, send_ref = others[:4]
    codes, flat, gathered, lhs = others[-4:]
    bands, block, width = sums_ref.shape
    pair_total = bands * pairs
    padded = gathered.shape[0]
    blocks = padded // LANES
    fields = 2 * levels
    flat[...] = sums_ref[...].astype(jnp.float32).reshape(bands * block, width)
    gathered[pair_total:, :] = jnp.zeros((padded - pair_total, width), jnp.float32)
    if leads:
        code_row = up_to(pairs * PAIRED, ROWS)
        place_ref[...] = pair_places(
            flat, owner_ref, lane_ref, codes, bands, block, code_row, padded
        )
    place = place_ref[...]
    low = lax.broadcasted_iota(jnp.int32, (fields, padded), 1) < pair_total // 2
    middle = fields * ROWS
    for i in range(PAIRED):
        for band in range(bands):
            gathered[band * pairs : (band + 1) * pairs, :] = flat[
                pl.ds(band * block + i, pairs, stride=PAIRED), :
            ]
        ordered = jnp.dot(
            gathered[...].T.astype(jnp.bfloat16), place, preferred_element_type=jnp.float32
        )
        for side in range(2):
            row = side * PAIRED + i
            if HALO <= row < HALO + ROWS:
                first, stride = row - HALO, ROWS
            else:
                first, stride = middle + (row - HALO - ROWS) % TALL, 2 * HALO
            for part in range(2):
                start = side * HALF + part * fields
                straight = ordered[start : start + fields]
                start = start + 2 * fields
                crossed = ordered[start : start + fields]
                both = (jnp.where(low, straight, crossed), jnp.where(low, crossed, straight))
                for parity in range(2):
                    for t in range(blocks):
                        lhs[parity, part * blocks + t, pl.ds(first, fields, stride=stride), :] = (
                            both[parity][:, t * LANES : (t + 1) * LANES]
                        )
    half = table_ref.shape[2]

    def transform(first, count):
        found = []
        for parity in range(2):
            left = jnp.concatenate(
                [
                    lhs[parity, t, first : first + count, :].astype(jnp.bfloat16)
                    for t in range(2 * blocks)
                ],
                axis=1,
            )
            found.append(jnp.dot(left, table_ref[parity], preferred_element_type=jnp.float32))
        pieces = (found[0] + found[1], found[0] - found[1])
        return [piece.astype(jnp.bfloat16).astype(jnp.float32) for piece in pieces]

    group = next(n for n in (4, 2, 1) if levels % n == 0)
    for level in range(0, levels, group):
        pieces = transform(level * 2 * ROWS, group * 2 * ROWS)
        for part, value in enumerate(pieces):
            value = value.reshape(group, 2 * ROWS, half)
            field_ref[level : level + group, : 2 * ROWS, part * half : (part + 1) * half] = value
    for part, value in enumerate(transform(middle, fields * 2 * HALO)):
        value = value.reshape(levels, 4 * HALO, half)
        field_ref[:, 2 * ROWS :, part * half : (part + 1) * half] = value
    if send_ref.shape[0] == 1:
        start = jnp.where(base_ref[0] == 0, levels - HALO, 0)
        send_ref[0] = field_ref[pl.ds(start, HALO)].astype(jnp.bfloat16)
    else:
        send_ref[0] = field_ref[:HALO].astype(jnp.bfloat16)
        send_ref[1] = field_ref[levels - HALO :].astype(jnp.bfloat16)


def fourier_call(base, sums, table, pairs, levels, lon_total, place=None, after=None):
    bands, block, width = sums.shape
    pair_total = bands * pairs
    padded = up_to(pair_total, LANES)
    leads = place is None
    sends = 1 if lax.axis_size("lev") == 2 else 2
    field_shape = (levels, 3 * ROWS, lon_total)
    out_shape = [
        jax.ShapeDtypeStruct(field_shape, jnp.float32),
        jax.ShapeDtypeStruct((sends, HALO) + field_shape[1:], jnp.bfloat16),
    ]
    extra = [place, after]
    if leads:
        out_shape.append(jax.ShapeDtypeStruct((padded, padded), jnp.bfloat16))
        extra = [jnp.asarray(x) for x in owner_tables(bands, pairs)]
    in_vmem = pl.BlockSpec(memory_space=pltpu.VMEM)
    return pl.pallas_call(
        functools.partial(fourier_kernel, pairs, levels, leads),
        out_shape=tuple(out_shape),
        in_specs=[
            pl.BlockSpec(memory_space=pltpu.SMEM),
            in_vmem,
            in_vmem,
        ]
        + [in_vmem] * 2,
        out_specs=(in_vmem,) * len(out_shape),
        scratch_shapes=[
            pltpu.VMEM((2, LANES, LANES), jnp.float32),
            pltpu.VMEM((bands * block, width), jnp.float32),
            pltpu.VMEM((padded, width), jnp.float32),
            pltpu.VMEM((2, 2 * padded // LANES, 2 * levels * TALL, LANES), jnp.float32),
        ],
        compiler_params=pltpu.CompilerParams(vmem_limit_bytes=16 * 1024 * 1024),
        cost_estimate=pl.CostEstimate(
            flops=2 * levels * 4 * TALL * padded * lon_total,
            bytes_accessed=8_000_000,
            transcendentals=0,
        ),
    )(base, sums, table, *extra)


def exchange(sums):
    return lax.all_to_all(sums, "band", split_axis=0, concat_axis=0, tiled=True)


def per_device(spectra, legendre, pairing, eta_shift, cells):
    levels, rows, lon_total = eta_shift.shape
    pairs = pairing.shape[0]
    spectra = jnp.transpose(spectra, (0, 2, 1, 3))
    table = jnp.transpose(legendre, (0, 2, 1, 3))
    if lax.axis_size("lev") == 2:
        tables = (table, lax.ppermute(table, "lev", [(0, 1), (1, 0)]))
    else:
        tables = (lax.all_gather(table, "lev", axis=0, tiled=True),)
    base = jnp.stack([lax.axis_index("lev") * levels, lax.axis_index("band") * rows])
    base = base.astype(jnp.int32)
    wind_sums, tracer_sums, _ = legendre_call(pairing, spectra, tables)
    wind_sums = exchange(wind_sums)
    pair_total = pairs * lax.axis_size("band")
    twiddles = jnp.asarray(fourier_table(pair_total, up_to(pair_total, LANES), lon_total))
    points, twiddles, tracer_sums = prepare_call(base, eta_shift, cells, twiddles, tracer_sums)
    tracer_sums = exchange(tracer_sums)
    size = (pairs, levels, lon_total)
    winds, send, place = fourier_call(base, wind_sums, twiddles, *size)
    displacement, moved, done = interpolation_call(
        wind_levels, base, winds, points, swap_levels(send), (), jnp.float32, 2
    )
    tracers, send = fourier_call(base, tracer_sums, twiddles, *size, place, done)
    advected, _ = interpolation_call(
        tracer_levels, base, tracers, points, swap_levels(send), (moved,), jnp.bfloat16, 1
    )
    return advected, displacement


def solution(mesh):
    return jax.shard_map(
        per_device,
        mesh=mesh,
        in_specs=(
            P(None, "lev", "band", None),
            P("lev", None, "band", None),
            P("band"),
            P("lev", "band", None),
            P(None, "lev", "band", None),
        ),
        out_specs=(P(None, "lev", "band", None), P(None, "lev", "band", None)),
        check_vma=False,
    )
```

```python
import functools
import math

import jax
import jax.numpy as jnp
import numpy as np
from jax import lax
from jax.experimental import pallas as pl
from jax.experimental.pallas import tpu as pltpu
from jax.sharding import PartitionSpec as P

ITERS = 2


COURANT = 0.8
HALO = 2
LANES = 128
ROWS = 8
SLOTS = (-1, 0, 1, 2)


def slot_weights(place, here, low, high, sixth):
    z = jnp.minimum(jnp.maximum(place, low), high)
    square = z * z
    less = square - 1.0
    outer = less * z * sixth
    triple = 3.0 * outer
    half = 0.5 * z
    half_square = 0.5 * square
    return (
        half_square - half - jnp.where(here, outer, triple),
        triple - less,
        half_square + half - jnp.where(here, triple, outer),
        outer,
    )


def bounds(here):
    return (
        jnp.where(here, -0.5, -1.5),
        jnp.where(here, 1.5, 0.5),
        jnp.where(here, 1.0 / 6.0, -1.0 / 6.0),
    )


def weighted(weights, values):
    return (weights[0] * values[0] + weights[1] * values[1]) + (
        weights[2] * values[2] + weights[3] * values[3]
    )


def shifted_lanes(before, here, after, lane):
    return (
        pltpu.roll(jnp.where(lane < LANES - 2, here, before), 2, 1),
        pltpu.roll(jnp.where(lane < LANES - 1, here, before), 1, 1),
        here,
        pltpu.roll(jnp.where(lane < 1, after, here), LANES - 1, 1),
        pltpu.roll(jnp.where(lane < 2, after, here), LANES - 2, 1),
    )


STACK = 5 * ROWS
FIELD_ROW = (ROWS, 3 * ROWS)


def fill_units(slab, chunk, chunk_total, field_ref, scratch):
    before = jnp.where(chunk == 0, chunk_total - 1, chunk - 1)
    after = jnp.where(chunk == chunk_total - 1, 0, chunk + 1)
    starts = [pl.multiple_of(c * LANES, LANES) for c in (before, chunk, after)]
    lane = lax.broadcasted_iota(jnp.int32, (ROWS, LANES), 1)
    first = pl.multiple_of(slab * (5 * STACK), ROWS)

    def edge_start():
        moved = shifted_lanes(
            *[field_ref[slab, 2 * ROWS : 3 * ROWS, pl.ds(s, LANES)] for s in starts], lane
        )
        return [(value, pltpu.roll(value, ROWS // 2, 0)) for value in moved]

    def edge_finish(values):
        for step, (between, outside) in enumerate(values):
            for offset, value in ((0, outside), (2 * ROWS, between), (4 * ROWS, outside)):
                scratch[pl.ds(first + (step * STACK + offset), ROWS), :] = value

    def center_unit(field):
        def start():
            rows = slice(field * ROWS, (field + 1) * ROWS)
            blocks = [field_ref[slab, rows, pl.ds(s, LANES)] for s in starts]
            return shifted_lanes(*blocks, lane)

        def finish(values):
            for step, moved in enumerate(values):
                scratch[pl.ds(first + (step * STACK + FIELD_ROW[field]), ROWS), :] = moved

        return start, finish

    return [(edge_start, edge_finish)] + [center_unit(field) for field in range(2)]


class Interleave:
    def __init__(self, units, ticks):
        self.units = list(units)
        self.every = max(1, ticks // max(1, len(self.units)))
        self.count = 0
        self.pending = None

    def advance(self):
        if self.pending is not None:
            self.pending[0](self.pending[1])
            self.pending = None
        if self.units:
            start, finish = self.units.pop(0)
            self.pending = (finish, start())

    def tick(self):
        if self.count % self.every == 0:
            self.advance()
        self.count += 1

    def flush(self):
        while self.units or self.pending is not None:
            self.advance()


def level_sums(scratch, field, base, slot, points):
    loaded = {}

    def load(a, b, c):
        offset = ((a + HALO) * 5 + c + HALO) * STACK + FIELD_ROW[field] + b
        if slot == (2, 2):
            return scratch[pl.ds(base + offset, ROWS), :]
        if (a, b, c) not in loaded:
            loaded[a, b, c] = scratch[pl.ds(base + offset, ROWS), :]
        return loaded[a, b, c]

    def one(step, weights, level_here, row_here, lon_here):
        def pick_lon(a, b):
            if slot[1] == 2:
                return jnp.where(lon_here, load(a + step, b, 2), load(a + step, b, -2))
            return load(a + step, b, slot[1])

        def pick(a):
            if slot[0] == 2:
                return jnp.where(row_here, pick_lon(a, 2), pick_lon(a, -2))
            return pick_lon(a, slot[0])

        total = weights[0] * pick(-1) + weights[1] * pick(0)
        total = total + weights[2] * pick(1)
        return total + weights[3] * jnp.where(level_here, pick(2), pick(-2))

    return [one(step, *point) for step, point in enumerate(points)]


def across(scratch, field, base, points, row_weights, lon_weights, filling, keep=None):
    columns = [[None] * 4 for _ in points]
    for b, row_slot in enumerate(SLOTS):
        for c, lon_slot in enumerate(SLOTS):
            filling.tick()
            found = level_sums(scratch, field, base, (row_slot, lon_slot), points)
            for step, value in enumerate(found):
                if keep is not None:
                    keep[field, step, 4 * b + c] = value
                term = row_weights[step][b] * value
                columns[step][c] = term if b == 0 else columns[step][c] + term
    return [weighted(weights, column) for weights, column in zip(lon_weights, columns)]


def across_kept(keep, field, step, row_weights, lon_weights):
    return weighted(
        lon_weights,
        [
            weighted(row_weights, [keep[field, step, 4 * b + c] for b in range(4)])
            for c in range(4)
        ],
    )


def prepare_kernel(base_ref, after_ref, eta_ref, cells_ref, points_ref, done_ref):
    done_ref[...] = after_ref[...]
    levels, rows, lon_total = eta_ref.shape
    shape = (rows, LANES)
    row_here = base_ref[1] + lax.broadcasted_iota(jnp.int32, shape, 0)
    lane = lax.broadcasted_iota(jnp.int32, shape, 1)

    def chunk_step(chunk, carry):
        lanes = pl.ds(pl.multiple_of(chunk * LANES, LANES), LANES)
        for k in range(levels):
            level_here = cells_ref[2, k, :, lanes] == base_ref[0] + k
            weights = slot_weights(
                -eta_ref[k, :, lanes].astype(jnp.float32), level_here, *bounds(level_here)
            )
            here = (
                level_here,
                cells_ref[0, k, :, lanes] == row_here,
                cells_ref[1, k, :, lanes] == chunk * LANES + lane,
            )
            for n, value in enumerate(weights + tuple(bounds(x)[0] for x in here)):
                points_ref[n, k, :, lanes] = value
        return carry

    lax.fori_loop(0, lon_total // LANES, chunk_step, 0)


def prepare_call(base, after, eta_shift, cells):
    in_vmem = pl.BlockSpec(memory_space=pltpu.VMEM)
    return pl.pallas_call(
        prepare_kernel,
        out_shape=(
            jax.ShapeDtypeStruct((7,) + eta_shift.shape, jnp.float32),
            jax.ShapeDtypeStruct(after.shape, after.dtype),
        ),
        in_specs=[pl.BlockSpec(memory_space=pltpu.SMEM)] + [in_vmem] * 3,
        out_specs=(in_vmem, in_vmem),
        compiler_params=pltpu.CompilerParams(vmem_limit_bytes=16 * 1024 * 1024),
        cost_estimate=pl.CostEstimate(
            flops=40 * eta_shift.size, bytes_accessed=20_000_000, transcendentals=0
        ),
    )(base, after, eta_shift, cells)


def arrival(points_ref, k, lanes):
    here = [points_ref[n, k, :, lanes] > -1.0 for n in range(4, 7)]
    return tuple(points_ref[n, k, :, lanes] for n in range(4)), *here


def both_weights(shift_row, shift_lon, point):
    _, _, row_here, lon_here = point
    return (
        slot_weights(-shift_row, row_here, *bounds(row_here)),
        slot_weights(-shift_lon, lon_here, *bounds(lon_here)),
    )


def wind_levels(base, lanes, k, points, scratch, keep, filling, *out_refs):
    def arrival_wind(field, step):
        middle = (HALO * 5 + HALO) * STACK + step * (5 * STACK) + FIELD_ROW[field]
        return scratch[pl.ds(base + middle, ROWS), :]

    count = range(len(points))
    weights = [
        both_weights(
            COURANT * arrival_wind(1, step), COURANT * arrival_wind(0, step), points[step]
        )
        for step in count
    ]
    row_weights, lon_weights = zip(*weights)
    found = [
        across(scratch, field, base, points, row_weights, lon_weights, filling, keep)
        for field in range(2)
    ]
    filling.flush()
    for step in count:
        east, north = arrival_wind(0, step), arrival_wind(1, step)
        east_found, north_found = found[0][step], found[1][step]
        for sweep in range(ITERS):
            shift_row = 0.5 * COURANT * (north + north_found)
            shift_lon = 0.5 * COURANT * (east + east_found)
            if sweep < ITERS - 1:
                weights = both_weights(shift_row, shift_lon, points[step])
                east_found = across_kept(keep, 0, step, *weights)
                north_found = across_kept(keep, 1, step, *weights)
        for out_ref in out_refs:
            out_ref[0, k + step, :, lanes] = shift_row
            out_ref[1, k + step, :, lanes] = shift_lon


def tracer_levels(shift_ref, base, lanes, k, points, scratch, keep, filling, out_ref):
    weights = [
        both_weights(
            shift_ref[0, k + step, :, lanes], shift_ref[1, k + step, :, lanes], points[step]
        )
        for step in range(len(points))
    ]
    row_weights, lon_weights = zip(*weights)
    found = [
        across(scratch, field, base, points, row_weights, lon_weights, filling)
        for field in range(2)
    ]
    filling.flush()
    for field in range(2):
        for step, total in enumerate(found[field]):
            out_ref[field, k + step, :, lanes] = total.astype(out_ref.dtype)


def interpolation_kernel(
    levels_body, together, near_count, out_count, base_ref, field_ref, points_ref, *others
):
    nears, others = others[:near_count], others[near_count:]
    full, even_scratch, odd_scratch, keep = others[-4:]
    extra, out_refs, done_ref = others[: -5 - out_count], others[-5 - out_count : -5], others[-5]
    done_ref[...] = jnp.zeros(done_ref.shape, done_ref.dtype)
    _, levels, rows, lon_total = points_ref.shape
    chunk_total = lon_total // LANES
    slabs = levels + 2 * HALO
    steps = levels // together
    per_step = -(-slabs // steps)
    full[HALO : HALO + levels] = field_ref[...]
    if near_count == 1:
        found = jnp.where(base_ref[0] == 0, levels + HALO, 0)
        full[pl.ds(found, HALO)] = nears[0][...].astype(jnp.float32)
        empty = levels + HALO - found
        full[pl.ds(empty, HALO)] = jnp.zeros((HALO,) + full.shape[1:], jnp.float32)
    else:
        full[:HALO] = nears[0][...].astype(jnp.float32)
        full[HALO + levels :] = nears[1][...].astype(jnp.float32)

    def first_fill(slab, carry):
        for start, finish in fill_units(slab, 0, chunk_total, full, even_scratch):
            finish(start())
        return carry

    lax.fori_loop(0, slabs, first_fill, 0)

    def one_chunk(chunk, scratch, other):
        lanes = pl.ds(pl.multiple_of(chunk * LANES, LANES), LANES)
        following = jnp.where(chunk == chunk_total - 1, 0, chunk + 1)

        def level_step(step, carry):
            k = step * together
            units = []
            for n in range(per_step):
                slab = jnp.minimum(step * per_step + n, slabs - 1)
                units += fill_units(slab, following, chunk_total, full, other)
            filling = Interleave(units, 32)
            points = [arrival(points_ref, k + n, lanes) for n in range(together)]
            base = pl.multiple_of(k * (5 * STACK), ROWS)
            levels_body(
                *extra, base, lanes, k, points, scratch, keep, filling, *out_refs
            )
            return carry

        lax.fori_loop(0, steps, level_step, 0)

    def chunk_pair(pair, carry):
        one_chunk(2 * pair, even_scratch, odd_scratch)
        one_chunk(2 * pair + 1, odd_scratch, even_scratch)
        return carry

    lax.fori_loop(0, chunk_total // 2, chunk_pair, 0)


def interpolation_call(levels_body, base, fields, points, nears, extra, out_dtype, out_count):
    _, levels, rows, lon_total = points.shape
    count = levels * rows * lon_total
    together = next(n for n in (4, 2, 1) if levels % n == 0)
    scratch = pltpu.VMEM(((levels + 2 * HALO) * 5 * STACK, LANES), jnp.float32)
    in_vmem = pl.BlockSpec(memory_space=pltpu.VMEM)
    out = jax.ShapeDtypeStruct((2, levels, rows, lon_total), out_dtype)
    done = jax.ShapeDtypeStruct((ROWS, LANES), jnp.float32)
    return pl.pallas_call(
        functools.partial(interpolation_kernel, levels_body, together, len(nears), out_count),
        out_shape=(out,) * out_count + (done,),
        in_specs=[pl.BlockSpec(memory_space=pltpu.SMEM)]
        + [in_vmem] * (2 + len(nears) + len(extra)),
        out_specs=(in_vmem,) * (out_count + 1),
        scratch_shapes=[
            pltpu.VMEM((levels + 2 * HALO,) + fields.shape[1:], jnp.float32),
            scratch,
            scratch,
            pltpu.VMEM((2, together, 16, ROWS, LANES), jnp.float32),
        ],
        compiler_params=pltpu.CompilerParams(vmem_limit_bytes=16 * 1024 * 1024),
        cost_estimate=pl.CostEstimate(
            flops=count * 500, bytes_accessed=count * 40, transcendentals=0
        ),
    )(base, fields, points, *nears, *extra)


def swap_levels(send):
    if lax.axis_size("lev") == 2:
        return (lax.ppermute(send[0], "lev", [(0, 1), (1, 0)]),)
    up = [(i, i + 1) for i in range(lax.axis_size("lev") - 1)]
    down = [(j, i) for i, j in up]
    return lax.ppermute(send[1], "lev", up), lax.ppermute(send[0], "lev", down)


def up_to(value, step):
    return -(-value // step) * step


TALL = ROWS + 2 * HALO
PAIRED = TALL // 2
HALF = LANES // 2


def touch_kernel(numbers_ref, spectra_ref, table_ref, out_ref):
    out_ref[...] = numbers_ref[...]


def legendre_kernel(numbers_ref, codes_ref, spectra_ref, *others):
    tables, others = others[:-6], others[-6:]
    out_ref, done_ref, sums = others[:3]
    table_tail, column_tail, order_ref = others[3:]
    _, pairs, level_fields, degrees = spectra_ref.shape
    group = table_tail.shape[0]
    bands, block, _ = out_ref.shape
    full = degrees // LANES * LANES
    at_top = numbers_ref[0] == 0
    step = pl.program_id(0)

    @pl.when(step == 0)
    def _():
        sums[...] = jnp.zeros(sums.shape, jnp.float32)
        done_ref[...] = jnp.zeros(done_ref.shape, jnp.float32)
        table_tail[...] = jnp.zeros(table_tail.shape, jnp.float32)
        column_tail[...] = jnp.zeros(column_tail.shape, jnp.float32)
        order_ref[...] = column_order(level_fields)
        codes = codes_ref[...]
        code_row = up_to(pl.num_programs(0) * group * PAIRED, ROWS)
        for band in range(bands):
            first = band * block + code_row
            sums[pl.ds(first, 1), :] = jnp.right_shift(codes, 4).astype(jnp.float32)
            sums[pl.ds(first + 1, 1), :] = (codes & 15).astype(jnp.float32)

    band_row = lax.broadcasted_iota(jnp.int32, (bands, LANES), 0)
    first_half = lax.broadcasted_iota(jnp.int32, (bands, LANES), 1) < HALF
    nothing = jnp.zeros((bands, LANES), jnp.float32)
    for p in range(group):
        slot = step * group + p
        edge = degrees - 1 - numbers_ref[1 + slot]
        left = []
        for number, table_ref in enumerate(tables):
            for row in range(table_ref.shape[0]):
                piece = table_ref[row, slot]
                left.append(piece[:, :full])
                first = (number * table_ref.shape[0] + row) * bands
                table_tail[p, first : first + bands, : degrees - full] = piece[:, full:].astype(
                    jnp.float32
                )
        left = jnp.concatenate(left, axis=0)
        left = jnp.concatenate([left, table_tail[p].astype(jnp.bfloat16)], axis=1)
        halves = ([], [])
        for part in range(2):
            piece = spectra_ref[part, slot]
            whole = piece[:, :full].astype(jnp.float32)
            lane = lax.broadcasted_iota(jnp.int32, whole.shape, 1)
            zero = jnp.zeros_like(whole)
            halves[0].append(jnp.where(lane < edge, whole, zero).astype(jnp.bfloat16))
            halves[1].append(jnp.where(lane < edge, zero, whole).astype(jnp.bfloat16))
            first = part * level_fields
            column_tail[p, first : first + level_fields, : degrees - full] = piece[
                :, full:
            ].astype(jnp.float32)
        tail = column_tail[p].astype(jnp.bfloat16)
        right = jnp.concatenate(
            [
                jnp.concatenate([jnp.concatenate(halves[0], axis=0), jnp.zeros_like(tail)], axis=1),
                jnp.concatenate([jnp.concatenate(halves[1], axis=0), tail], axis=1),
            ],
            axis=0,
        )
        found = lax.dot_general(
            left, right, (((1,), (1,)), ((), ())), preferred_element_type=jnp.float32
        )
        found = jnp.dot(
            found.astype(jnp.bfloat16), order_ref[...], preferred_element_type=jnp.float32
        )
        found = [found[i * bands : (i + 1) * bands] for i in range(ROWS)]
        if len(tables) == 2:
            low, high = found[: ROWS // 2], found[ROWS // 2 :]
            found = [jnp.where(at_top, x, y) for x, y in zip(low, high)]
            found += [jnp.where(at_top, y, x) for x, y in zip(low, high)]
        above = [
            jnp.where(band_row == 0, nothing, pltpu.roll(x, 1, 0)) for x in found[ROWS - HALO :]
        ]
        below = [
            jnp.where(band_row == bands - 1, nothing, pltpu.roll(x, bands - 1, 0))
            for x in found[:HALO]
        ]
        rows = above + found + below
        for i in range(PAIRED):
            low, high = rows[i], rows[PAIRED + i]
            place = slot * PAIRED + i
            pairs_of = (
                jnp.where(first_half, low, pltpu.roll(high, HALF, 1)),
                jnp.where(first_half, pltpu.roll(low, HALF, 1), high),
            )
            for number, value in enumerate(pairs_of):
                sums[pl.ds(number * (block // 2) + place, bands, stride=block), :] = value

    @pl.when(step == pl.num_programs(0) - 1)
    def _():
        out_ref[...] = sums[...].astype(jnp.bfloat16).reshape(out_ref.shape)


def column_order(level_fields):
    shift = level_fields.bit_length() - 1
    shape = (4 * level_fields, LANES)
    column = lax.broadcasted_iota(jnp.int32, shape, 0)
    part = jnp.right_shift(column, shift)
    rest = column & (level_fields - 1)
    target = jnp.right_shift(rest & 3, 1) * HALF + part * (level_fields // 2)
    target = target + 2 * jnp.right_shift(rest, 2) + (rest & 1)
    here = lax.broadcasted_iota(jnp.int32, shape, 1) == target
    return jnp.where(here, 1.0, 0.0).astype(jnp.bfloat16)


def block_rows(pairs):
    return up_to(up_to(pairs * PAIRED, ROWS) + 2, 16)


def legendre_call(pairing, spectra, tables):
    _, pairs, level_fields, degrees = spectra.shape
    bands = tables[0].shape[2]
    block = 2 * block_rows(pairs)
    group = next(n for n in (4, 5, 2, 1) if pairs % n == 0)
    numbers = jnp.concatenate([lax.axis_index("lev").astype(jnp.int32)[None], pairing])
    codes = pl.pallas_call(
        touch_kernel,
        out_shape=jax.ShapeDtypeStruct((1, LANES), jnp.int32),
        in_specs=[pl.BlockSpec(memory_space=pltpu.VMEM)] * 3,
        out_specs=pl.BlockSpec(memory_space=pltpu.VMEM),
        compiler_params=pltpu.CompilerParams(vmem_limit_bytes=4 * 1024 * 1024),
        cost_estimate=pl.CostEstimate(flops=0, bytes_accessed=4_000_000, transcendentals=0),
    )(jnp.pad(pairing, (0, LANES - pairs))[None, :], spectra, tables[0])
    shape = jax.ShapeDtypeStruct((bands, block, LANES), jnp.bfloat16)
    whole = pl.BlockSpec((bands, block, LANES), lambda i: (0, 0, 0))
    in_vmem = pl.BlockSpec(memory_space=pltpu.VMEM)
    return pl.pallas_call(
        legendre_kernel,
        grid=(pairs // group,),
        out_shape=(shape, jax.ShapeDtypeStruct((ROWS, LANES), jnp.float32)),
        in_specs=[
            pl.BlockSpec(memory_space=pltpu.SMEM),
            pl.BlockSpec((1, LANES), lambda i: (0, 0)),
            in_vmem,
        ]
        + [in_vmem] * len(tables),
        out_specs=(whole, in_vmem),
        scratch_shapes=[
            pltpu.VMEM((bands * block, LANES), jnp.float32),
            pltpu.VMEM((group, ROWS * bands, LANES), jnp.float32),
            pltpu.VMEM((group, 2 * level_fields, LANES), jnp.float32),
            pltpu.VMEM((4 * level_fields, LANES), jnp.bfloat16),
        ],
        compiler_params=pltpu.CompilerParams(vmem_limit_bytes=16 * 1024 * 1024),
        cost_estimate=pl.CostEstimate(
            flops=2 * ROWS * bands * 4 * level_fields * pairs * degrees,
            bytes_accessed=8_000_000,
            transcendentals=0,
        ),
    )(numbers, codes, spectra, *tables)


def fourier_table(pair_total, padded, lon_total):
    order_total = 2 * pair_total
    half = pair_total // 2
    low = 2 * np.arange(half)
    high = low + 1
    even = np.concatenate([low, order_total - 1 - high])
    odd = np.concatenate([order_total - 1 - low, high])
    lon = np.arange(lon_total // 2)
    table = np.zeros((2, 2, padded, lon_total // 2), np.float32)
    for parity, orders in enumerate((even, odd)):
        phase = (orders[:, None] * lon[None, :]) % lon_total * (2.0 * math.pi / lon_total)
        weight = np.where(orders == 0, 1.0, 2.0)[:, None]
        table[parity, 0, :pair_total] = weight * np.cos(phase)
        table[parity, 1, :pair_total] = -weight * np.sin(phase)
    return table.reshape(2, 2 * padded, lon_total // 2).astype(jnp.bfloat16)


def owner_tables(bands, pairs):
    slots = np.arange(bands * pairs)
    owner = slots[:, None] // pairs == np.arange(LANES)[None, :]
    lane = slots[:, None] % pairs == np.arange(LANES)[None, :]
    return owner.astype(jnp.bfloat16), lane.astype(np.float32)


def pair_places(flat, owner_ref, lane_ref, codes, bands, block, code_row, padded):
    pair_total = owner_ref.shape[0]
    codes[...] = jnp.zeros(codes.shape, jnp.float32)
    numbers = []
    for part in range(2):
        codes[part, :bands, :] = flat[pl.ds(code_row + part, bands, stride=block), :]
        numbers.append(
            jnp.dot(
                owner_ref[...],
                codes[part].astype(jnp.bfloat16),
                preferred_element_type=jnp.float32,
            )
        )
    pair_id = jnp.sum(
        (16.0 * numbers[0] + numbers[1]) * lane_ref[...], axis=1, keepdims=True
    ).astype(jnp.int32)
    place = jnp.right_shift(pair_id, 1) + (pair_id & 1) * (pair_total // 2)
    columns = lax.broadcasted_iota(jnp.int32, (pair_total, padded), 1)
    place = jnp.where(columns == place, 1.0, 0.0)
    if padded > pair_total:
        place = jnp.concatenate(
            [place, jnp.zeros((padded - pair_total, padded), jnp.float32)], axis=0
        )
    return place.astype(jnp.bfloat16)


def order_kernel(pairs, levels, after_ref, sums_ref, owner_ref, lane_ref, *others):
    out_refs, (codes, flat, gathered, lhs) = others[:2], others[2:]
    bands, block, width = sums_ref.shape
    pair_total = bands * pairs
    padded = gathered.shape[0]
    blocks = padded // LANES
    fields = 2 * levels
    flat[...] = sums_ref[...].astype(jnp.float32).reshape(bands * block, width)
    gathered[pair_total:, :] = jnp.zeros((padded - pair_total, width), jnp.float32)
    code_row = up_to(pairs * PAIRED, ROWS)
    place = pair_places(flat, owner_ref, lane_ref, codes, bands, block, code_row, padded)
    low = lax.broadcasted_iota(jnp.int32, (fields, padded), 1) < pair_total // 2
    middle = fields * ROWS
    for number, out_ref in enumerate(out_refs):
        for i in range(PAIRED):
            for band in range(bands):
                first = band * block + number * (block // 2) + i
                gathered[band * pairs : (band + 1) * pairs, :] = flat[
                    pl.ds(first, pairs, stride=PAIRED), :
                ]
            ordered = jnp.dot(
                gathered[...].T.astype(jnp.bfloat16), place, preferred_element_type=jnp.float32
            )
            for side in range(2):
                row = side * PAIRED + i
                if HALO <= row < HALO + ROWS:
                    first, stride = row - HALO, ROWS
                else:
                    first, stride = middle + (row - HALO - ROWS) % TALL, 2 * HALO
                for part in range(2):
                    start = side * HALF + part * fields
                    straight = ordered[start : start + fields]
                    start = start + 2 * fields
                    crossed = ordered[start : start + fields]
                    both = (jnp.where(low, straight, crossed), jnp.where(low, crossed, straight))
                    for parity in range(2):
                        for t in range(blocks):
                            lhs[
                                parity, part * blocks + t, pl.ds(first, fields, stride=stride), :
                            ] = both[parity][:, t * LANES : (t + 1) * LANES]
        for parity in range(2):
            for t in range(2 * blocks):
                out_ref[parity, :, t * LANES : (t + 1) * LANES] = lhs[parity, t].astype(
                    jnp.bfloat16
                )


def order_call(after, sums, pairs, levels):
    bands, block, width = sums.shape
    padded = up_to(bands * pairs, LANES)
    extra = [jnp.asarray(x) for x in owner_tables(bands, pairs)]
    shape = jax.ShapeDtypeStruct((2, 2 * levels * TALL, 2 * padded), jnp.bfloat16)
    in_vmem = pl.BlockSpec(memory_space=pltpu.VMEM)
    return pl.pallas_call(
        functools.partial(order_kernel, pairs, levels),
        out_shape=(shape, shape),
        in_specs=[in_vmem] * 4,
        out_specs=(in_vmem, in_vmem),
        scratch_shapes=[
            pltpu.VMEM((2, LANES, LANES), jnp.float32),
            pltpu.VMEM((bands * block, width), jnp.float32),
            pltpu.VMEM((padded, width), jnp.float32),
            pltpu.VMEM((2, 2 * padded // LANES, 2 * levels * TALL, LANES), jnp.float32),
        ],
        compiler_params=pltpu.CompilerParams(vmem_limit_bytes=16 * 1024 * 1024),
        cost_estimate=pl.CostEstimate(
            flops=4_000_000_000, bytes_accessed=8_000_000, transcendentals=0
        ),
    )(after, sums, *extra)


def transform_kernel(levels, base_ref, lhs_ref, table_ref, field_ref, send_ref):
    half = table_ref.shape[2]
    middle = 2 * levels * ROWS

    def transform(first, count):
        found = [
            jnp.dot(
                lhs_ref[parity, first : first + count, :],
                table_ref[parity],
                preferred_element_type=jnp.float32,
            )
            for parity in range(2)
        ]
        pieces = (found[0] + found[1], found[0] - found[1])
        return [piece.astype(jnp.bfloat16).astype(jnp.float32) for piece in pieces]

    group = next(n for n in (4, 2, 1) if levels % n == 0)
    for level in range(0, levels, group):
        pieces = transform(level * 2 * ROWS, group * 2 * ROWS)
        for part, value in enumerate(pieces):
            value = value.reshape(group, 2 * ROWS, half)
            field_ref[level : level + group, : 2 * ROWS, part * half : (part + 1) * half] = value
    for part, value in enumerate(transform(middle, 2 * levels * 2 * HALO)):
        value = value.reshape(levels, 4 * HALO, half)
        field_ref[:, 2 * ROWS :, part * half : (part + 1) * half] = value
    if send_ref.shape[0] == 1:
        start = jnp.where(base_ref[0] == 0, levels - HALO, 0)
        send_ref[0] = field_ref[pl.ds(start, HALO)].astype(jnp.bfloat16)
    else:
        send_ref[0] = field_ref[:HALO].astype(jnp.bfloat16)
        send_ref[1] = field_ref[levels - HALO :].astype(jnp.bfloat16)


def transform_call(base, lhs, table, levels, lon_total):
    sends = 1 if lax.axis_size("lev") == 2 else 2
    field_shape = (levels, 3 * ROWS, lon_total)
    in_vmem = pl.BlockSpec(memory_space=pltpu.VMEM)
    return pl.pallas_call(
        functools.partial(transform_kernel, levels),
        out_shape=(
            jax.ShapeDtypeStruct(field_shape, jnp.float32),
            jax.ShapeDtypeStruct((sends, HALO) + field_shape[1:], jnp.bfloat16),
        ),
        in_specs=[pl.BlockSpec(memory_space=pltpu.SMEM), in_vmem, in_vmem],
        out_specs=(in_vmem, in_vmem),
        compiler_params=pltpu.CompilerParams(vmem_limit_bytes=16 * 1024 * 1024),
        cost_estimate=pl.CostEstimate(
            flops=3_000_000_000, bytes_accessed=8_000_000, transcendentals=0
        ),
    )(base, lhs, table)


def exchange(sums):
    return lax.all_to_all(sums, "band", split_axis=0, concat_axis=0, tiled=True)


def per_device(spectra, legendre, pairing, eta_shift, cells):
    levels, rows, lon_total = eta_shift.shape
    pairs = pairing.shape[0]
    spectra = jnp.transpose(spectra, (0, 2, 1, 3))
    table = jnp.transpose(legendre, (0, 2, 1, 3))
    if lax.axis_size("lev") == 2:
        tables = (table, lax.ppermute(table, "lev", [(0, 1), (1, 0)]))
    else:
        tables = (lax.all_gather(table, "lev", axis=0, tiled=True),)
    base = jnp.stack([lax.axis_index("lev") * levels, lax.axis_index("band") * rows])
    base = base.astype(jnp.int32)
    sums, done = legendre_call(pairing, spectra, tables)
    sums = exchange(sums)
    points, done = prepare_call(base, done, eta_shift, cells)
    pair_total = pairs * lax.axis_size("band")
    twiddles = jnp.asarray(fourier_table(pair_total, up_to(pair_total, LANES), lon_total))
    ordered = order_call(done, sums, pairs, levels)
    winds, wind_send = transform_call(base, ordered[0], twiddles, levels, lon_total)
    tracers, tracer_send = transform_call(base, ordered[1], twiddles, levels, lon_total)
    displacement, moved, _ = interpolation_call(
        wind_levels, base, winds, points, swap_levels(wind_send), (), jnp.float32, 2
    )
    advected, _ = interpolation_call(
        tracer_levels, base, tracers, points, swap_levels(tracer_send), (moved,), jnp.bfloat16, 1
    )
    return advected, displacement


def solution(mesh):
    return jax.shard_map(
        per_device,
        mesh=mesh,
        in_specs=(
            P(None, "lev", "band", None),
            P("lev", None, "band", None),
            P("band"),
            P("lev", "band", None),
            P(None, "lev", "band", None),
        ),
        out_specs=(P(None, "lev", "band", None), P(None, "lev", "band", None)),
        check_vma=False,
    )
```

```python
import functools
import math

import jax
import jax.numpy as jnp
import numpy as np
from jax import lax
from jax.experimental import pallas as pl
from jax.experimental.pallas import tpu as pltpu
from jax.sharding import PartitionSpec as P

ITERS = 2


COURANT = 0.8
HALO = 2
LANES = 128
ROWS = 8
SLOTS = (-1, 0, 1, 2)


def slot_weights(place, here, low, high, sixth):
    z = jnp.minimum(jnp.maximum(place, low), high)
    square = z * z
    less = square - 1.0
    outer = less * z * sixth
    triple = 3.0 * outer
    half = 0.5 * z
    half_square = 0.5 * square
    return (
        half_square - half - jnp.where(here, outer, triple),
        triple - less,
        half_square + half - jnp.where(here, triple, outer),
        outer,
    )


def bounds(here):
    return (
        jnp.where(here, -0.5, -1.5),
        jnp.where(here, 1.5, 0.5),
        jnp.where(here, 1.0 / 6.0, -1.0 / 6.0),
    )


def weighted(weights, values):
    return (weights[0] * values[0] + weights[1] * values[1]) + (
        weights[2] * values[2] + weights[3] * values[3]
    )


def shifted_lanes(before, here, after, lane):
    return (
        pltpu.roll(jnp.where(lane < LANES - 2, here, before), 2, 1),
        pltpu.roll(jnp.where(lane < LANES - 1, here, before), 1, 1),
        here,
        pltpu.roll(jnp.where(lane < 1, after, here), LANES - 1, 1),
        pltpu.roll(jnp.where(lane < 2, after, here), LANES - 2, 1),
    )


STACK = 5 * ROWS
FIELD_ROW = (ROWS, 3 * ROWS)


def fill_units(slab, chunk, chunk_total, field_ref, scratch):
    before = jnp.where(chunk == 0, chunk_total - 1, chunk - 1)
    after = jnp.where(chunk == chunk_total - 1, 0, chunk + 1)
    starts = [pl.multiple_of(c * LANES, LANES) for c in (before, chunk, after)]
    lane = lax.broadcasted_iota(jnp.int32, (ROWS, LANES), 1)
    first = pl.multiple_of(slab * (5 * STACK), ROWS)

    def edge_start():
        moved = shifted_lanes(
            *[field_ref[slab, 2 * ROWS : 3 * ROWS, pl.ds(s, LANES)] for s in starts], lane
        )
        return [(value, pltpu.roll(value, ROWS // 2, 0)) for value in moved]

    def edge_finish(values):
        for step, (between, outside) in enumerate(values):
            for offset, value in ((0, outside), (2 * ROWS, between), (4 * ROWS, outside)):
                scratch[pl.ds(first + (step * STACK + offset), ROWS), :] = value

    def center_unit(field):
        def start():
            rows = slice(field * ROWS, (field + 1) * ROWS)
            blocks = [field_ref[slab, rows, pl.ds(s, LANES)] for s in starts]
            return shifted_lanes(*blocks, lane)

        def finish(values):
            for step, moved in enumerate(values):
                scratch[pl.ds(first + (step * STACK + FIELD_ROW[field]), ROWS), :] = moved

        return start, finish

    return [(edge_start, edge_finish)] + [center_unit(field) for field in range(2)]


class Interleave:
    def __init__(self, units, ticks):
        self.units = list(units)
        self.every = max(1, ticks // max(1, len(self.units)))
        self.count = 0
        self.pending = None

    def advance(self):
        if self.pending is not None:
            self.pending[0](self.pending[1])
            self.pending = None
        if self.units:
            start, finish = self.units.pop(0)
            self.pending = (finish, start())

    def tick(self):
        if self.count % self.every == 0:
            self.advance()
        self.count += 1

    def flush(self):
        while self.units or self.pending is not None:
            self.advance()


def level_sums(scratch, field, base, slot, points):
    loaded = {}

    def load(a, b, c):
        offset = ((a + HALO) * 5 + c + HALO) * STACK + FIELD_ROW[field] + b
        if slot == (2, 2):
            return scratch[pl.ds(base + offset, ROWS), :]
        if (a, b, c) not in loaded:
            loaded[a, b, c] = scratch[pl.ds(base + offset, ROWS), :]
        return loaded[a, b, c]

    def one(step, weights, level_here, row_here, lon_here):
        def pick_lon(a, b):
            if slot[1] == 2:
                return jnp.where(lon_here, load(a + step, b, 2), load(a + step, b, -2))
            return load(a + step, b, slot[1])

        def pick(a):
            if slot[0] == 2:
                return jnp.where(row_here, pick_lon(a, 2), pick_lon(a, -2))
            return pick_lon(a, slot[0])

        total = weights[0] * pick(-1) + weights[1] * pick(0)
        total = total + weights[2] * pick(1)
        return total + weights[3] * jnp.where(level_here, pick(2), pick(-2))

    return [one(step, *point) for step, point in enumerate(points)]


def across(scratch, field, base, points, row_weights, lon_weights, filling, keep=None):
    columns = [[None] * 4 for _ in points]
    for b, row_slot in enumerate(SLOTS):
        for c, lon_slot in enumerate(SLOTS):
            filling.tick()
            found = level_sums(scratch, field, base, (row_slot, lon_slot), points)
            for step, value in enumerate(found):
                if keep is not None:
                    keep[field, step, 4 * b + c] = value
                term = row_weights[step][b] * value
                columns[step][c] = term if b == 0 else columns[step][c] + term
    return [weighted(weights, column) for weights, column in zip(lon_weights, columns)]


def across_kept(keep, field, step, row_weights, lon_weights):
    return weighted(
        lon_weights,
        [
            weighted(row_weights, [keep[field, step, 4 * b + c] for b in range(4)])
            for c in range(4)
        ],
    )


def prepare_kernel(base_ref, after_ref, eta_ref, cells_ref, points_ref, done_ref):
    done_ref[...] = after_ref[...]
    levels, rows, lon_total = eta_ref.shape
    shape = (rows, LANES)
    row_here = base_ref[1] + lax.broadcasted_iota(jnp.int32, shape, 0)
    lane = lax.broadcasted_iota(jnp.int32, shape, 1)

    def chunk_step(chunk, carry):
        lanes = pl.ds(pl.multiple_of(chunk * LANES, LANES), LANES)
        for k in range(levels):
            level_here = cells_ref[2, k, :, lanes] == base_ref[0] + k
            weights = slot_weights(
                -eta_ref[k, :, lanes].astype(jnp.float32), level_here, *bounds(level_here)
            )
            here = (
                level_here,
                cells_ref[0, k, :, lanes] == row_here,
                cells_ref[1, k, :, lanes] == chunk * LANES + lane,
            )
            for n, value in enumerate(weights + tuple(bounds(x)[0] for x in here)):
                points_ref[n, k, :, lanes] = value
        return carry

    lax.fori_loop(0, lon_total // LANES, chunk_step, 0)


def prepare_call(base, after, eta_shift, cells):
    in_vmem = pl.BlockSpec(memory_space=pltpu.VMEM)
    return pl.pallas_call(
        prepare_kernel,
        out_shape=(
            jax.ShapeDtypeStruct((7,) + eta_shift.shape, jnp.float32),
            jax.ShapeDtypeStruct(after.shape, after.dtype),
        ),
        in_specs=[pl.BlockSpec(memory_space=pltpu.SMEM)] + [in_vmem] * 3,
        out_specs=(in_vmem, in_vmem),
        compiler_params=pltpu.CompilerParams(vmem_limit_bytes=16 * 1024 * 1024),
        cost_estimate=pl.CostEstimate(
            flops=40 * eta_shift.size, bytes_accessed=20_000_000, transcendentals=0
        ),
    )(base, after, eta_shift, cells)


def arrival(points_ref, k, lanes):
    here = [points_ref[n, k, :, lanes] > -1.0 for n in range(4, 7)]
    return tuple(points_ref[n, k, :, lanes] for n in range(4)), *here


def both_weights(shift_row, shift_lon, point):
    _, _, row_here, lon_here = point
    return (
        slot_weights(-shift_row, row_here, *bounds(row_here)),
        slot_weights(-shift_lon, lon_here, *bounds(lon_here)),
    )


def wind_levels(base, lanes, k, points, scratch, keep, filling, *out_refs):
    def arrival_wind(field, step):
        middle = (HALO * 5 + HALO) * STACK + step * (5 * STACK) + FIELD_ROW[field]
        return scratch[pl.ds(base + middle, ROWS), :]

    count = range(len(points))
    weights = [
        both_weights(
            COURANT * arrival_wind(1, step), COURANT * arrival_wind(0, step), points[step]
        )
        for step in count
    ]
    row_weights, lon_weights = zip(*weights)
    found = [
        across(scratch, field, base, points, row_weights, lon_weights, filling, keep)
        for field in range(2)
    ]
    filling.flush()
    for step in count:
        east, north = arrival_wind(0, step), arrival_wind(1, step)
        east_found, north_found = found[0][step], found[1][step]
        for sweep in range(ITERS):
            shift_row = 0.5 * COURANT * (north + north_found)
            shift_lon = 0.5 * COURANT * (east + east_found)
            if sweep < ITERS - 1:
                weights = both_weights(shift_row, shift_lon, points[step])
                east_found = across_kept(keep, 0, step, *weights)
                north_found = across_kept(keep, 1, step, *weights)
        for out_ref in out_refs:
            out_ref[0, k + step, :, lanes] = shift_row
            out_ref[1, k + step, :, lanes] = shift_lon


def tracer_levels(shift_ref, base, lanes, k, points, scratch, keep, filling, out_ref):
    weights = [
        both_weights(
            shift_ref[0, k + step, :, lanes], shift_ref[1, k + step, :, lanes], points[step]
        )
        for step in range(len(points))
    ]
    row_weights, lon_weights = zip(*weights)
    found = [
        across(scratch, field, base, points, row_weights, lon_weights, filling)
        for field in range(2)
    ]
    filling.flush()
    for field in range(2):
        for step, total in enumerate(found[field]):
            out_ref[field, k + step, :, lanes] = total.astype(out_ref.dtype)


def interpolation_kernel(
    levels_body, together, number, near_count, out_count, base_ref, field_ref, points_ref, *others
):
    nears, others = others[:near_count], others[near_count:]
    full, even_scratch, odd_scratch, keep = others[-4:]
    extra, out_refs, done_ref = others[: -5 - out_count], others[-5 - out_count : -5], others[-5]
    done_ref[...] = jnp.zeros(done_ref.shape, done_ref.dtype)
    _, levels, rows, lon_total = points_ref.shape
    chunk_total = lon_total // LANES
    slabs = levels + 2 * HALO
    steps = levels // together
    per_step = -(-slabs // steps)
    full[HALO : HALO + levels] = field_ref[...]
    if near_count == 1:
        found = jnp.where(base_ref[0] == 0, levels + HALO, 0)
        full[pl.ds(found, HALO)] = nears[0][number].astype(jnp.float32)
        empty = levels + HALO - found
        full[pl.ds(empty, HALO)] = jnp.zeros((HALO,) + full.shape[1:], jnp.float32)
    else:
        full[:HALO] = nears[0][number].astype(jnp.float32)
        full[HALO + levels :] = nears[1][number].astype(jnp.float32)

    def first_fill(slab, carry):
        for start, finish in fill_units(slab, 0, chunk_total, full, even_scratch):
            finish(start())
        return carry

    lax.fori_loop(0, slabs, first_fill, 0)

    def one_chunk(chunk, scratch, other):
        lanes = pl.ds(pl.multiple_of(chunk * LANES, LANES), LANES)
        following = jnp.where(chunk == chunk_total - 1, 0, chunk + 1)

        def level_step(step, carry):
            k = step * together
            units = []
            for n in range(per_step):
                slab = jnp.minimum(step * per_step + n, slabs - 1)
                units += fill_units(slab, following, chunk_total, full, other)
            filling = Interleave(units, 32)
            points = [arrival(points_ref, k + n, lanes) for n in range(together)]
            base = pl.multiple_of(k * (5 * STACK), ROWS)
            levels_body(
                *extra, base, lanes, k, points, scratch, keep, filling, *out_refs
            )
            return carry

        lax.fori_loop(0, steps, level_step, 0)

    def chunk_pair(pair, carry):
        one_chunk(2 * pair, even_scratch, odd_scratch)
        one_chunk(2 * pair + 1, odd_scratch, even_scratch)
        return carry

    lax.fori_loop(0, chunk_total // 2, chunk_pair, 0)


def interpolation_call(
    levels_body, base, number, fields, points, nears, extra, out_dtype, out_count
):
    _, levels, rows, lon_total = points.shape
    count = levels * rows * lon_total
    together = 2 if levels % 2 == 0 else 1
    scratch = pltpu.VMEM(((levels + 2 * HALO) * 5 * STACK, LANES), jnp.float32)
    in_vmem = pl.BlockSpec(memory_space=pltpu.VMEM)
    out = jax.ShapeDtypeStruct((2, levels, rows, lon_total), out_dtype)
    done = jax.ShapeDtypeStruct((ROWS, LANES), jnp.float32)
    return pl.pallas_call(
        functools.partial(
            interpolation_kernel, levels_body, together, number, len(nears), out_count
        ),
        out_shape=(out,) * out_count + (done,),
        in_specs=[pl.BlockSpec(memory_space=pltpu.SMEM)]
        + [in_vmem] * (2 + len(nears) + len(extra)),
        out_specs=(in_vmem,) * (out_count + 1),
        scratch_shapes=[
            pltpu.VMEM((levels + 2 * HALO,) + fields.shape[1:], jnp.float32),
            scratch,
            scratch,
            pltpu.VMEM((2, together, 16, ROWS, LANES), jnp.float32),
        ],
        compiler_params=pltpu.CompilerParams(vmem_limit_bytes=16 * 1024 * 1024),
        cost_estimate=pl.CostEstimate(
            flops=count * 500, bytes_accessed=count * 40, transcendentals=0
        ),
    )(base, fields, points, *nears, *extra)


def swap_levels(send):
    if lax.axis_size("lev") == 2:
        return (lax.ppermute(send[0], "lev", [(0, 1), (1, 0)]),)
    up = [(i, i + 1) for i in range(lax.axis_size("lev") - 1)]
    down = [(j, i) for i, j in up]
    return lax.ppermute(send[1], "lev", up), lax.ppermute(send[0], "lev", down)


def up_to(value, step):
    return -(-value // step) * step


TALL = ROWS + 2 * HALO
PAIRED = TALL // 2
HALF = LANES // 2


def codes_kernel(numbers_ref, out_ref):
    out_ref[...] = numbers_ref[...]


def legendre_kernel(numbers_ref, codes_ref, spectra_ref, *others):
    table_count = (len(others) - 8) // 2
    sources, others = (spectra_ref,) + others[:table_count], others[table_count:]
    out_ref, done_ref, sums, table_tail, column_tail, order_ref = others[:6]
    targets, arrivals = others[6:-1], others[-1]
    spectra_here, tables = targets[0], targets[1:]
    _, pairs, level_fields, degrees = spectra_ref.shape
    group = table_tail.shape[0]
    bands, block, _ = out_ref.shape
    full = degrees // LANES * LANES
    at_top = numbers_ref[0] == 0
    step = pl.program_id(0)

    def copies(number):
        here = pl.ds(number * group, group)
        return [
            pltpu.make_async_copy(source.at[:, here], target.at[:, here], arrivals.at[n, number])
            for n, (source, target) in enumerate(zip(sources, targets))
        ]

    @pl.when(step == 0)
    def _():
        for number in range(pairs // group):
            for copy in copies(number):
                copy.start()
        sums[...] = jnp.zeros(sums.shape, jnp.float32)
        done_ref[...] = jnp.zeros(done_ref.shape, jnp.float32)
        table_tail[...] = jnp.zeros(table_tail.shape, jnp.float32)
        column_tail[...] = jnp.zeros(column_tail.shape, jnp.float32)
        order_ref[...] = column_order(level_fields)
        codes = codes_ref[...]
        code_row = up_to(pl.num_programs(0) * group * PAIRED, ROWS)
        for band in range(bands):
            first = band * block + code_row
            sums[pl.ds(first, 1), :] = jnp.right_shift(codes, 4).astype(jnp.float32)
            sums[pl.ds(first + 1, 1), :] = (codes & 15).astype(jnp.float32)

    for copy in copies(step):
        copy.wait()
    band_row = lax.broadcasted_iota(jnp.int32, (bands, LANES), 0)
    first_half = lax.broadcasted_iota(jnp.int32, (bands, LANES), 1) < HALF
    nothing = jnp.zeros((bands, LANES), jnp.float32)
    for p in range(group):
        slot = step * group + p
        edge = degrees - 1 - numbers_ref[1 + slot]
        left = []
        for number, table_ref in enumerate(tables):
            for row in range(table_ref.shape[0]):
                piece = table_ref[row, slot]
                left.append(piece[:, :full])
                first = (number * table_ref.shape[0] + row) * bands
                table_tail[p, first : first + bands, : degrees - full] = piece[:, full:].astype(
                    jnp.float32
                )
        left = jnp.concatenate(left, axis=0)
        left = jnp.concatenate([left, table_tail[p].astype(jnp.bfloat16)], axis=1)
        halves = ([], [])
        for part in range(2):
            piece = spectra_here[part, slot]
            whole = piece[:, :full].astype(jnp.float32)
            lane = lax.broadcasted_iota(jnp.int32, whole.shape, 1)
            zero = jnp.zeros_like(whole)
            halves[0].append(jnp.where(lane < edge, whole, zero).astype(jnp.bfloat16))
            halves[1].append(jnp.where(lane < edge, zero, whole).astype(jnp.bfloat16))
            first = part * level_fields
            column_tail[p, first : first + level_fields, : degrees - full] = piece[
                :, full:
            ].astype(jnp.float32)
        tail = column_tail[p].astype(jnp.bfloat16)
        right = jnp.concatenate(
            [
                jnp.concatenate([jnp.concatenate(halves[0], axis=0), jnp.zeros_like(tail)], axis=1),
                jnp.concatenate([jnp.concatenate(halves[1], axis=0), tail], axis=1),
            ],
            axis=0,
        )
        found = lax.dot_general(
            left, right, (((1,), (1,)), ((), ())), preferred_element_type=jnp.float32
        )
        found = jnp.dot(
            found.astype(jnp.bfloat16), order_ref[...], preferred_element_type=jnp.float32
        )
        found = [found[i * bands : (i + 1) * bands] for i in range(ROWS)]
        if len(tables) == 2:
            low, high = found[: ROWS // 2], found[ROWS // 2 :]
            found = [jnp.where(at_top, x, y) for x, y in zip(low, high)]
            found += [jnp.where(at_top, y, x) for x, y in zip(low, high)]
        above = [
            jnp.where(band_row == 0, nothing, pltpu.roll(x, 1, 0)) for x in found[ROWS - HALO :]
        ]
        below = [
            jnp.where(band_row == bands - 1, nothing, pltpu.roll(x, bands - 1, 0))
            for x in found[:HALO]
        ]
        rows = above + found + below
        for i in range(PAIRED):
            low, high = rows[i], rows[PAIRED + i]
            place = slot * PAIRED + i
            pairs_of = (
                jnp.where(first_half, low, pltpu.roll(high, HALF, 1)),
                jnp.where(first_half, pltpu.roll(low, HALF, 1), high),
            )
            for number, value in enumerate(pairs_of):
                sums[pl.ds(number * (block // 2) + place, bands, stride=block), :] = value

    @pl.when(step == pl.num_programs(0) - 1)
    def _():
        out_ref[...] = sums[...].astype(jnp.bfloat16).reshape(out_ref.shape)


def column_order(level_fields):
    shift = level_fields.bit_length() - 1
    shape = (4 * level_fields, LANES)
    column = lax.broadcasted_iota(jnp.int32, shape, 0)
    part = jnp.right_shift(column, shift)
    rest = column & (level_fields - 1)
    target = jnp.right_shift(rest & 3, 1) * HALF + part * (level_fields // 2)
    target = target + 2 * jnp.right_shift(rest, 2) + (rest & 1)
    here = lax.broadcasted_iota(jnp.int32, shape, 1) == target
    return jnp.where(here, 1.0, 0.0).astype(jnp.bfloat16)


def block_rows(pairs):
    return up_to(up_to(pairs * PAIRED, ROWS) + 2, 16)


def legendre_call(pairing, spectra, tables):
    _, pairs, level_fields, degrees = spectra.shape
    bands = tables[0].shape[2]
    block = 2 * block_rows(pairs)
    group = next(n for n in (4, 5, 2, 1) if pairs % n == 0)
    numbers = jnp.concatenate([lax.axis_index("lev").astype(jnp.int32)[None], pairing])
    codes = pl.pallas_call(
        codes_kernel,
        out_shape=jax.ShapeDtypeStruct((1, LANES), jnp.int32),
        in_specs=[pl.BlockSpec(memory_space=pltpu.VMEM)],
        out_specs=pl.BlockSpec(memory_space=pltpu.VMEM),
        compiler_params=pltpu.CompilerParams(vmem_limit_bytes=60 * 1024 * 1024),
        cost_estimate=pl.CostEstimate(flops=0, bytes_accessed=4_000_000, transcendentals=0),
    )(jnp.pad(pairing, (0, LANES - pairs))[None, :])
    shape = jax.ShapeDtypeStruct((bands, block, LANES), jnp.bfloat16)
    whole = pl.BlockSpec((bands, block, LANES), lambda i: (0, 0, 0))
    in_vmem = pl.BlockSpec(memory_space=pltpu.VMEM)
    in_hbm = pl.BlockSpec(memory_space=pl.ANY)
    return pl.pallas_call(
        legendre_kernel,
        grid=(pairs // group,),
        out_shape=(shape, jax.ShapeDtypeStruct((ROWS, LANES), jnp.float32)),
        in_specs=[
            pl.BlockSpec(memory_space=pltpu.SMEM),
            pl.BlockSpec((1, LANES), lambda i: (0, 0)),
            in_hbm,
        ]
        + [in_hbm] * len(tables),
        out_specs=(whole, in_vmem),
        scratch_shapes=[
            pltpu.VMEM((bands * block, LANES), jnp.float32),
            pltpu.VMEM((group, ROWS * bands, LANES), jnp.float32),
            pltpu.VMEM((group, 2 * level_fields, LANES), jnp.float32),
            pltpu.VMEM((4 * level_fields, LANES), jnp.bfloat16),
        ]
        + [pltpu.VMEM(x.shape, x.dtype) for x in (spectra,) + tables]
        + [pltpu.SemaphoreType.DMA((1 + len(tables), pairs // group))],
        compiler_params=pltpu.CompilerParams(vmem_limit_bytes=60 * 1024 * 1024),
        cost_estimate=pl.CostEstimate(
            flops=2 * ROWS * bands * 4 * level_fields * pairs * degrees,
            bytes_accessed=8_000_000,
            transcendentals=0,
        ),
    )(numbers, codes, spectra, *tables)


def fourier_table(pair_total, padded, lon_total):
    order_total = 2 * pair_total
    half = pair_total // 2
    low = 2 * np.arange(half)
    high = low + 1
    even = np.concatenate([low, order_total - 1 - high])
    odd = np.concatenate([order_total - 1 - low, high])
    lon = np.arange(lon_total // 2)
    table = np.zeros((4, 2, padded, lon_total // 2), np.float32)
    for parity, orders in enumerate((even, odd)):
        phase = (orders[:, None] * lon[None, :]) % lon_total * (2.0 * math.pi / lon_total)
        weight = np.where(orders == 0, 1.0, 2.0)[:, None]
        table[parity, 0, :pair_total] = weight * np.cos(phase)
        table[parity, 1, :pair_total] = -weight * np.sin(phase)
    return table.reshape(4, 2 * padded, lon_total // 2).astype(jnp.bfloat16)


def owner_tables(bands, pairs):
    slots = np.arange(bands * pairs)
    owner = slots[:, None] // pairs == np.arange(LANES)[None, :]
    lane = slots[:, None] % pairs == np.arange(LANES)[None, :]
    return owner.astype(jnp.bfloat16), lane.astype(np.float32)


def pair_places(flat, owner_ref, lane_ref, codes, bands, block, code_row, padded):
    pair_total = owner_ref.shape[0]
    codes[...] = jnp.zeros(codes.shape, jnp.float32)
    numbers = []
    for part in range(2):
        codes[part, :bands, :] = flat[pl.ds(code_row + part, bands, stride=block), :]
        numbers.append(
            jnp.dot(
                owner_ref[...],
                codes[part].astype(jnp.bfloat16),
                preferred_element_type=jnp.float32,
            )
        )
    pair_id = jnp.sum(
        (16.0 * numbers[0] + numbers[1]) * lane_ref[...], axis=1, keepdims=True
    ).astype(jnp.int32)
    place = jnp.right_shift(pair_id, 1) + (pair_id & 1) * (pair_total // 2)
    columns = lax.broadcasted_iota(jnp.int32, (pair_total, padded), 1)
    place = jnp.where(columns == place, 1.0, 0.0)
    if padded > pair_total:
        place = jnp.concatenate(
            [place, jnp.zeros((padded - pair_total, padded), jnp.float32)], axis=0
        )
    return place.astype(jnp.bfloat16)


def fourier_kernel(
    pairs, levels, base_ref, after_ref, sums_ref, owner_ref, lane_ref, table_source, *others
):
    field_refs, send_ref, others = others[:2], others[2], others[3:]
    codes, flat, gathered, lhs, table_ref, arrival_sem = others
    copy = pltpu.make_async_copy(table_source.at[:2], table_ref, arrival_sem)
    copy.start()
    bands, block, width = sums_ref.shape
    pair_total = bands * pairs
    padded = gathered.shape[0]
    blocks = padded // LANES
    fields = 2 * levels
    flat[...] = sums_ref[...].astype(jnp.float32).reshape(bands * block, width)
    gathered[pair_total:, :] = jnp.zeros((padded - pair_total, width), jnp.float32)
    code_row = up_to(pairs * PAIRED, ROWS)
    place = pair_places(flat, owner_ref, lane_ref, codes, bands, block, code_row, padded)
    low = lax.broadcasted_iota(jnp.int32, (fields, padded), 1) < pair_total // 2
    middle = fields * ROWS
    for number in range(2):
        for i in range(PAIRED):
            for band in range(bands):
                first = band * block + number * (block // 2) + i
                gathered[band * pairs : (band + 1) * pairs, :] = flat[
                    pl.ds(first, pairs, stride=PAIRED), :
                ]
            ordered = jnp.dot(
                gathered[...].T.astype(jnp.bfloat16), place, preferred_element_type=jnp.float32
            )
            for side in range(2):
                row = side * PAIRED + i
                if HALO <= row < HALO + ROWS:
                    first, stride = row - HALO, ROWS
                else:
                    first, stride = middle + (row - HALO - ROWS) % TALL, 2 * HALO
                for part in range(2):
                    start = side * HALF + part * fields
                    straight = ordered[start : start + fields]
                    start = start + 2 * fields
                    crossed = ordered[start : start + fields]
                    both = (jnp.where(low, straight, crossed), jnp.where(low, crossed, straight))
                    for parity in range(2):
                        for t in range(blocks):
                            lhs[
                                number,
                                parity,
                                part * blocks + t,
                                pl.ds(first, fields, stride=stride),
                                :,
                            ] = both[parity][:, t * LANES : (t + 1) * LANES]
    copy.wait()
    half = table_ref.shape[2]

    def transform(number, first, count):
        found = []
        for parity in range(2):
            left = jnp.concatenate(
                [
                    lhs[number, parity, t, first : first + count, :].astype(jnp.bfloat16)
                    for t in range(2 * blocks)
                ],
                axis=1,
            )
            found.append(jnp.dot(left, table_ref[parity], preferred_element_type=jnp.float32))
        pieces = (found[0] + found[1], found[0] - found[1])
        return [piece.astype(jnp.bfloat16).astype(jnp.float32) for piece in pieces]

    group = next(n for n in (4, 2, 1) if levels % n == 0)
    for number, field_ref in enumerate(field_refs):
        for level in range(0, levels, group):
            pieces = transform(number, level * 2 * ROWS, group * 2 * ROWS)
            for part, value in enumerate(pieces):
                value = value.reshape(group, 2 * ROWS, half)
                lanes = slice(part * half, (part + 1) * half)
                field_ref[level : level + group, : 2 * ROWS, lanes] = value
        for part, value in enumerate(transform(number, middle, fields * 2 * HALO)):
            value = value.reshape(levels, 4 * HALO, half)
            field_ref[:, 2 * ROWS :, part * half : (part + 1) * half] = value
        if send_ref.shape[0] == 1:
            start = jnp.where(base_ref[0] == 0, levels - HALO, 0)
            send_ref[0, number] = field_ref[pl.ds(start, HALO)].astype(jnp.bfloat16)
        else:
            send_ref[0, number] = field_ref[:HALO].astype(jnp.bfloat16)
            send_ref[1, number] = field_ref[levels - HALO :].astype(jnp.bfloat16)


def fourier_call(base, after, sums, table, pairs, levels, lon_total):
    bands, block, width = sums.shape
    padded = up_to(bands * pairs, LANES)
    extra = [jnp.asarray(x) for x in owner_tables(bands, pairs)]
    sends = 1 if lax.axis_size("lev") == 2 else 2
    field_shape = (levels, 3 * ROWS, lon_total)
    field = jax.ShapeDtypeStruct(field_shape, jnp.float32)
    send = jax.ShapeDtypeStruct((sends, 2, HALO) + field_shape[1:], jnp.bfloat16)
    in_vmem = pl.BlockSpec(memory_space=pltpu.VMEM)
    return pl.pallas_call(
        functools.partial(fourier_kernel, pairs, levels),
        out_shape=(field, field, send),
        in_specs=[pl.BlockSpec(memory_space=pltpu.SMEM)]
        + [in_vmem] * 4
        + [pl.BlockSpec(memory_space=pl.ANY)],
        out_specs=(in_vmem,) * 3,
        scratch_shapes=[
            pltpu.VMEM((2, LANES, LANES), jnp.float32),
            pltpu.VMEM((bands * block, width), jnp.float32),
            pltpu.VMEM((padded, width), jnp.float32),
            pltpu.VMEM((2, 2, 2 * padded // LANES, 2 * levels * TALL, LANES), jnp.float32),
            pltpu.VMEM((2,) + table.shape[1:], table.dtype),
            pltpu.SemaphoreType.DMA,
        ],
        compiler_params=pltpu.CompilerParams(vmem_limit_bytes=44 * 1024 * 1024),
        cost_estimate=pl.CostEstimate(
            flops=8_000_000_000, bytes_accessed=8_000_000, transcendentals=0
        ),
    )(base, after, sums, *extra, table)


def exchange(sums):
    return lax.all_to_all(sums, "band", split_axis=0, concat_axis=0, tiled=True)


def per_device(spectra, legendre, pairing, eta_shift, cells):
    levels, rows, lon_total = eta_shift.shape
    pairs = pairing.shape[0]
    spectra = jnp.transpose(spectra, (0, 2, 1, 3))
    table = jnp.transpose(legendre, (0, 2, 1, 3))
    if lax.axis_size("lev") == 2:
        tables = (table, lax.ppermute(table, "lev", [(0, 1), (1, 0)]))
    else:
        tables = (lax.all_gather(table, "lev", axis=0, tiled=True),)
    base = jnp.stack([lax.axis_index("lev") * levels, lax.axis_index("band") * rows])
    base = base.astype(jnp.int32)
    sums, done = legendre_call(pairing, spectra, tables)
    sums = exchange(sums)
    points, done = prepare_call(base, done, eta_shift, cells)
    pair_total = pairs * lax.axis_size("band")
    twiddles = jnp.asarray(fourier_table(pair_total, up_to(pair_total, LANES), lon_total))
    winds, tracers, send = fourier_call(base, done, sums, twiddles, pairs, levels, lon_total)
    nears = swap_levels(send)
    displacement, moved, _ = interpolation_call(
        wind_levels, base, 0, winds, points, nears, (), jnp.float32, 2
    )
    advected, _ = interpolation_call(
        tracer_levels, base, 1, tracers, points, nears, (moved,), jnp.bfloat16, 1
    )
    return advected, displacement


def solution(mesh):
    return jax.shard_map(
        per_device,
        mesh=mesh,
        in_specs=(
            P(None, "lev", "band", None),
            P("lev", None, "band", None),
            P("band"),
            P("lev", "band", None),
            P(None, "lev", "band", None),
        ),
        out_specs=(P(None, "lev", "band", None), P(None, "lev", "band", None)),
        check_vma=False,
    )
```

```python
import functools
import math

import jax
import jax.numpy as jnp
import numpy as np
from jax import lax
from jax.experimental import pallas as pl
from jax.experimental.pallas import tpu as pltpu
from jax.sharding import PartitionSpec as P

ITERS = 2


COURANT = 0.8
HALO = 2
LANES = 128
ROWS = 8
SLOTS = (-1, 0, 1, 2)


def slot_weights(place, here, low, high, sixth):
    z = jnp.minimum(jnp.maximum(place, low), high)
    square = z * z
    less = square - 1.0
    outer = less * z * sixth
    triple = 3.0 * outer
    half = 0.5 * z
    half_square = 0.5 * square
    return (
        half_square - half - jnp.where(here, outer, triple),
        triple - less,
        half_square + half - jnp.where(here, triple, outer),
        outer,
    )


def bounds(here):
    return (
        jnp.where(here, -0.5, -1.5),
        jnp.where(here, 1.5, 0.5),
        jnp.where(here, 1.0 / 6.0, -1.0 / 6.0),
    )


def weighted(weights, values):
    return (weights[0] * values[0] + weights[1] * values[1]) + (
        weights[2] * values[2] + weights[3] * values[3]
    )


def shifted_lanes(before, here, after, lane):
    return (
        pltpu.roll(jnp.where(lane < LANES - 2, here, before), 2, 1),
        pltpu.roll(jnp.where(lane < LANES - 1, here, before), 1, 1),
        here,
        pltpu.roll(jnp.where(lane < 1, after, here), LANES - 1, 1),
        pltpu.roll(jnp.where(lane < 2, after, here), LANES - 2, 1),
    )


STACK = 5 * ROWS
FIELD_ROW = (ROWS, 3 * ROWS)


def fill_units(slab, chunk, chunk_total, source, scratch):
    field_ref, row = source
    before = jnp.where(chunk == 0, chunk_total - 1, chunk - 1)
    after = jnp.where(chunk == chunk_total - 1, 0, chunk + 1)
    starts = [pl.multiple_of(c * LANES, LANES) for c in (before, chunk, after)]
    lane = lax.broadcasted_iota(jnp.int32, (ROWS, LANES), 1)
    first = slab * (5 * STACK)

    def edge_start():
        moved = shifted_lanes(
            *[field_ref[row, 2 * ROWS : 3 * ROWS, pl.ds(s, LANES)] for s in starts], lane
        )
        return [(value, pltpu.roll(value, ROWS // 2, 0)) for value in moved]

    def edge_finish(values):
        for step, (between, outside) in enumerate(values):
            for offset, value in ((0, outside), (2 * ROWS, between), (4 * ROWS, outside)):
                scratch[pl.ds(first + step * STACK + offset, ROWS), :] = value

    def center_unit(field):
        def start():
            rows = slice(field * ROWS, (field + 1) * ROWS)
            blocks = [field_ref[row, rows, pl.ds(s, LANES)] for s in starts]
            return shifted_lanes(*blocks, lane)

        def finish(values):
            for step, moved in enumerate(values):
                scratch[pl.ds(first + step * STACK + FIELD_ROW[field], ROWS), :] = moved

        return start, finish

    return [(edge_start, edge_finish)] + [center_unit(field) for field in range(2)]


class Interleave:
    def __init__(self, units, ticks):
        self.units = list(units)
        self.every = max(1, ticks // max(1, len(self.units)))
        self.count = 0
        self.pending = None

    def advance(self):
        if self.pending is not None:
            self.pending[0](self.pending[1])
            self.pending = None
        if self.units:
            start, finish = self.units.pop(0)
            self.pending = (finish, start())

    def tick(self):
        if self.count % self.every == 0:
            self.advance()
        self.count += 1

    def flush(self):
        while self.units or self.pending is not None:
            self.advance()


def level_sums(scratch, field, base, slot, points):
    loaded = {}

    def load(a, b, c):
        offset = ((a + HALO) * 5 + c + HALO) * STACK + FIELD_ROW[field] + b
        if slot == (2, 2):
            return scratch[pl.ds(base + offset, ROWS), :]
        if (a, b, c) not in loaded:
            loaded[a, b, c] = scratch[pl.ds(base + offset, ROWS), :]
        return loaded[a, b, c]

    def one(step, weights, level_here, row_here, lon_here):
        def pick_lon(a, b):
            if slot[1] == 2:
                return jnp.where(lon_here, load(a + step, b, 2), load(a + step, b, -2))
            return load(a + step, b, slot[1])

        def pick(a):
            if slot[0] == 2:
                return jnp.where(row_here, pick_lon(a, 2), pick_lon(a, -2))
            return pick_lon(a, slot[0])

        total = weights[0] * pick(-1) + weights[1] * pick(0)
        total = total + weights[2] * pick(1)
        return total + weights[3] * jnp.where(level_here, pick(2), pick(-2))

    return [one(step, *point) for step, point in enumerate(points)]


def across(scratch, field, base, points, row_weights, lon_weights, filling, keep=None):
    columns = [[None] * 4 for _ in points]
    for b, row_slot in enumerate(SLOTS):
        for c, lon_slot in enumerate(SLOTS):
            filling.tick()
            found = level_sums(scratch, field, base, (row_slot, lon_slot), points)
            for step, value in enumerate(found):
                if keep is not None:
                    keep[field, step, 4 * b + c] = value
                term = row_weights[step][b] * value
                columns[step][c] = term if b == 0 else columns[step][c] + term
    return [weighted(weights, column) for weights, column in zip(lon_weights, columns)]


def across_kept(keep, field, step, row_weights, lon_weights):
    return weighted(
        lon_weights,
        [
            weighted(row_weights, [keep[field, step, 4 * b + c] for b in range(4)])
            for c in range(4)
        ],
    )


def prepare_kernel(base_ref, after_ref, eta_ref, cells_ref, points_ref, done_ref):
    done_ref[...] = after_ref[...]
    levels, rows, lon_total = eta_ref.shape
    shape = (rows, LANES)
    row_here = base_ref[1] + lax.broadcasted_iota(jnp.int32, shape, 0)
    lane = lax.broadcasted_iota(jnp.int32, shape, 1)

    def chunk_step(chunk, carry):
        lanes = pl.ds(pl.multiple_of(chunk * LANES, LANES), LANES)
        for k in range(levels):
            level_here = cells_ref[2, k, :, lanes] == base_ref[0] + k
            weights = slot_weights(
                -eta_ref[k, :, lanes].astype(jnp.float32), level_here, *bounds(level_here)
            )
            here = (
                level_here,
                cells_ref[0, k, :, lanes] == row_here,
                cells_ref[1, k, :, lanes] == chunk * LANES + lane,
            )
            for n, value in enumerate(weights + tuple(bounds(x)[0] for x in here)):
                points_ref[n, k, :, lanes] = value
        return carry

    lax.fori_loop(0, lon_total // LANES, chunk_step, 0)


def prepare_call(base, after, eta_shift, cells):
    in_vmem = pl.BlockSpec(memory_space=pltpu.VMEM)
    return pl.pallas_call(
        prepare_kernel,
        out_shape=(
            jax.ShapeDtypeStruct((7,) + eta_shift.shape, jnp.float32),
            jax.ShapeDtypeStruct(after.shape, after.dtype),
        ),
        in_specs=[pl.BlockSpec(memory_space=pltpu.SMEM)] + [in_vmem] * 3,
        out_specs=(in_vmem, in_vmem),
        compiler_params=pltpu.CompilerParams(vmem_limit_bytes=16 * 1024 * 1024),
        cost_estimate=pl.CostEstimate(
            flops=40 * eta_shift.size, bytes_accessed=20_000_000, transcendentals=0
        ),
    )(base, after, eta_shift, cells)


def arrival(points_ref, k, lanes):
    here = [points_ref[n, k, :, lanes] > -1.0 for n in range(4, 7)]
    return tuple(points_ref[n, k, :, lanes] for n in range(4)), *here


def both_weights(shift_row, shift_lon, point):
    _, _, row_here, lon_here = point
    return (
        slot_weights(-shift_row, row_here, *bounds(row_here)),
        slot_weights(-shift_lon, lon_here, *bounds(lon_here)),
    )


def wind_levels(base, lanes, k, points, scratch, keep, filling, *out_refs):
    def arrival_wind(field, step):
        middle = (HALO * 5 + HALO) * STACK + step * (5 * STACK) + FIELD_ROW[field]
        return scratch[pl.ds(base + middle, ROWS), :]

    count = range(len(points))
    weights = [
        both_weights(
            COURANT * arrival_wind(1, step), COURANT * arrival_wind(0, step), points[step]
        )
        for step in count
    ]
    row_weights, lon_weights = zip(*weights)
    found = [
        across(scratch, field, base, points, row_weights, lon_weights, filling, keep)
        for field in range(2)
    ]
    for step in count:
        east, north = arrival_wind(0, step), arrival_wind(1, step)
        east_found, north_found = found[0][step], found[1][step]
        for sweep in range(ITERS):
            shift_row = 0.5 * COURANT * (north + north_found)
            shift_lon = 0.5 * COURANT * (east + east_found)
            if sweep < ITERS - 1:
                weights = both_weights(shift_row, shift_lon, points[step])
                east_found = across_kept(keep, 0, step, *weights)
                north_found = across_kept(keep, 1, step, *weights)
        for out_ref in out_refs:
            out_ref[0, k + step, :, lanes] = shift_row
            out_ref[1, k + step, :, lanes] = shift_lon


def tracer_levels(shift_ref, base, lanes, k, points, scratch, keep, filling, out_ref):
    weights = [
        both_weights(
            shift_ref[0, k + step, :, lanes], shift_ref[1, k + step, :, lanes], points[step]
        )
        for step in range(len(points))
    ]
    row_weights, lon_weights = zip(*weights)
    found = [
        across(scratch, field, base, points, row_weights, lon_weights, filling)
        for field in range(2)
    ]
    for field in range(2):
        for step, total in enumerate(found[field]):
            out_ref[field, k + step, :, lanes] = total.astype(out_ref.dtype)


def interpolation_kernel(
    levels_body, together, number, near_count, out_count, base_ref, field_ref, points_ref, *others
):
    nears, others = others[:near_count], others[near_count:]
    around, even_scratch, odd_scratch, keep = others[-4:]
    extra, out_refs, done_ref = others[: -5 - out_count], others[-5 - out_count : -5], others[-5]
    done_ref[...] = jnp.zeros(done_ref.shape, done_ref.dtype)
    _, levels, rows, lon_total = points_ref.shape
    chunk_total = lon_total // LANES
    if near_count == 1:
        found = jnp.where(base_ref[0] == 0, HALO, 0)
        around[pl.ds(found, HALO)] = nears[0][number].astype(jnp.float32)
        around[pl.ds(HALO - found, HALO)] = jnp.zeros((HALO,) + around.shape[1:], jnp.float32)
    else:
        around[:HALO] = nears[0][number].astype(jnp.float32)
        around[HALO:] = nears[1][number].astype(jnp.float32)
    sources = [(around, n) for n in range(HALO)]
    sources += [(field_ref, n) for n in range(levels)]
    sources += [(around, HALO + n) for n in range(HALO)]

    def all_units(chunk, scratch):
        units = []
        for slab, source in enumerate(sources):
            units += fill_units(slab, chunk, chunk_total, source, scratch)
        return units

    for start, finish in all_units(0, even_scratch):
        finish(start())

    def one_chunk(chunk, scratch, other):
        lanes = pl.ds(pl.multiple_of(chunk * LANES, LANES), LANES)
        following = jnp.where(chunk == chunk_total - 1, 0, chunk + 1)
        filling = Interleave(all_units(following, other), 32 * (levels // together))
        for k in range(0, levels, together):
            points = [arrival(points_ref, k + n, lanes) for n in range(together)]
            base = k * (5 * STACK)
            levels_body(*extra, base, lanes, k, points, scratch, keep, filling, *out_refs)
        filling.flush()

    def chunk_pair(pair, carry):
        one_chunk(2 * pair, even_scratch, odd_scratch)
        one_chunk(2 * pair + 1, odd_scratch, even_scratch)
        return carry

    lax.fori_loop(0, chunk_total // 2, chunk_pair, 0)


def interpolation_call(
    levels_body, base, number, fields, points, nears, extra, out_dtype, out_count
):
    _, levels, rows, lon_total = points.shape
    count = levels * rows * lon_total
    together = next(n for n in (4, 2, 1) if levels % n == 0)
    scratch = pltpu.VMEM(((levels + 2 * HALO) * 5 * STACK, LANES), jnp.float32)
    in_vmem = pl.BlockSpec(memory_space=pltpu.VMEM)
    out = jax.ShapeDtypeStruct((2, levels, rows, lon_total), out_dtype)
    done = jax.ShapeDtypeStruct((ROWS, LANES), jnp.float32)
    return pl.pallas_call(
        functools.partial(
            interpolation_kernel, levels_body, together, number, len(nears), out_count
        ),
        out_shape=(out,) * out_count + (done,),
        in_specs=[pl.BlockSpec(memory_space=pltpu.SMEM)]
        + [in_vmem] * (2 + len(nears) + len(extra)),
        out_specs=(in_vmem,) * (out_count + 1),
        scratch_shapes=[
            pltpu.VMEM((2 * HALO,) + fields.shape[1:], jnp.float32),
            scratch,
            scratch,
            pltpu.VMEM((2, together, 16, ROWS, LANES), jnp.float32),
        ],
        compiler_params=pltpu.CompilerParams(vmem_limit_bytes=16 * 1024 * 1024),
        cost_estimate=pl.CostEstimate(
            flops=count * 500, bytes_accessed=count * 40, transcendentals=0
        ),
    )(base, fields, points, *nears, *extra)


def swap_levels(send):
    if lax.axis_size("lev") == 2:
        return (lax.ppermute(send[0], "lev", [(0, 1), (1, 0)]),)
    up = [(i, i + 1) for i in range(lax.axis_size("lev") - 1)]
    down = [(j, i) for i, j in up]
    return lax.ppermute(send[1], "lev", up), lax.ppermute(send[0], "lev", down)


def up_to(value, step):
    return -(-value // step) * step


TALL = ROWS + 2 * HALO
PAIRED = TALL // 2
HALF = LANES // 2


def codes_kernel(numbers_ref, out_ref):
    out_ref[...] = numbers_ref[...]


def legendre_kernel(numbers_ref, codes_ref, spectra_ref, *others):
    table_count = (len(others) - 8) // 2
    sources, others = (spectra_ref,) + others[:table_count], others[table_count:]
    out_ref, done_ref, sums, table_tail, column_tail, order_ref = others[:6]
    targets, arrivals = others[6:-1], others[-1]
    spectra_here, tables = targets[0], targets[1:]
    _, pairs, level_fields, degrees = spectra_ref.shape
    group = table_tail.shape[0]
    bands, block, _ = out_ref.shape
    full = degrees // LANES * LANES
    at_top = numbers_ref[0] == 0
    step = pl.program_id(0)

    def copies(number):
        here = pl.ds(number * group, group)
        return [
            pltpu.make_async_copy(source.at[:, here], target.at[:, here], arrivals.at[n, number])
            for n, (source, target) in enumerate(zip(sources, targets))
        ]

    @pl.when(step == 0)
    def _():
        for copy in copies(0):
            copy.start()
        sums[...] = jnp.zeros(sums.shape, jnp.float32)
        done_ref[...] = jnp.zeros(done_ref.shape, jnp.float32)
        table_tail[...] = jnp.zeros(table_tail.shape, jnp.float32)
        column_tail[...] = jnp.zeros(column_tail.shape, jnp.float32)
        order_ref[...] = column_order(level_fields)
        codes = codes_ref[...]
        code_row = up_to(pl.num_programs(0) * group * PAIRED, ROWS)
        for band in range(bands):
            first = band * block + code_row
            sums[pl.ds(first, 1), :] = jnp.right_shift(codes, 4).astype(jnp.float32)
            sums[pl.ds(first + 1, 1), :] = (codes & 15).astype(jnp.float32)

    @pl.when(step + 1 < pairs // group)
    def _():
        for copy in copies(step + 1):
            copy.start()

    for copy in copies(step):
        copy.wait()
    band_row = lax.broadcasted_iota(jnp.int32, (bands, LANES), 0)
    first_half = lax.broadcasted_iota(jnp.int32, (bands, LANES), 1) < HALF
    nothing = jnp.zeros((bands, LANES), jnp.float32)
    for p in range(group):
        slot = step * group + p
        edge = degrees - 1 - numbers_ref[1 + slot]
        left = []
        for number, table_ref in enumerate(tables):
            for row in range(table_ref.shape[0]):
                piece = table_ref[row, slot]
                left.append(piece[:, :full])
                first = (number * table_ref.shape[0] + row) * bands
                table_tail[p, first : first + bands, : degrees - full] = piece[:, full:].astype(
                    jnp.float32
                )
        left = jnp.concatenate(left, axis=0)
        left = jnp.concatenate([left, table_tail[p].astype(jnp.bfloat16)], axis=1)
        halves = ([], [])
        for part in range(2):
            piece = spectra_here[part, slot]
            whole = piece[:, :full].astype(jnp.float32)
            lane = lax.broadcasted_iota(jnp.int32, whole.shape, 1)
            zero = jnp.zeros_like(whole)
            halves[0].append(jnp.where(lane < edge, whole, zero).astype(jnp.bfloat16))
            halves[1].append(jnp.where(lane < edge, zero, whole).astype(jnp.bfloat16))
            first = part * level_fields
            column_tail[p, first : first + level_fields, : degrees - full] = piece[
                :, full:
            ].astype(jnp.float32)
        tail = column_tail[p].astype(jnp.bfloat16)
        right = jnp.concatenate(
            [
                jnp.concatenate([jnp.concatenate(halves[0], axis=0), jnp.zeros_like(tail)], axis=1),
                jnp.concatenate([jnp.concatenate(halves[1], axis=0), tail], axis=1),
            ],
            axis=0,
        )
        found = lax.dot_general(
            left, right, (((1,), (1,)), ((), ())), preferred_element_type=jnp.float32
        )
        found = jnp.dot(
            found.astype(jnp.bfloat16), order_ref[...], preferred_element_type=jnp.float32
        )
        found = [found[i * bands : (i + 1) * bands] for i in range(ROWS)]
        if len(tables) == 2:
            low, high = found[: ROWS // 2], found[ROWS // 2 :]
            found = [jnp.where(at_top, x, y) for x, y in zip(low, high)]
            found += [jnp.where(at_top, y, x) for x, y in zip(low, high)]
        above = [
            jnp.where(band_row == 0, nothing, pltpu.roll(x, 1, 0)) for x in found[ROWS - HALO :]
        ]
        below = [
            jnp.where(band_row == bands - 1, nothing, pltpu.roll(x, bands - 1, 0))
            for x in found[:HALO]
        ]
        rows = above + found + below
        for i in range(PAIRED):
            low, high = rows[i], rows[PAIRED + i]
            place = slot * PAIRED + i
            pairs_of = (
                jnp.where(first_half, low, pltpu.roll(high, HALF, 1)),
                jnp.where(first_half, pltpu.roll(low, HALF, 1), high),
            )
            for number, value in enumerate(pairs_of):
                sums[pl.ds(number * (block // 2) + place, bands, stride=block), :] = value

    @pl.when(step == pl.num_programs(0) - 1)
    def _():
        out_ref[...] = sums[...].astype(jnp.bfloat16).reshape(out_ref.shape)


def column_order(level_fields):
    shift = level_fields.bit_length() - 1
    shape = (4 * level_fields, LANES)
    column = lax.broadcasted_iota(jnp.int32, shape, 0)
    part = jnp.right_shift(column, shift)
    rest = column & (level_fields - 1)
    target = jnp.right_shift(rest & 3, 1) * HALF + part * (level_fields // 2)
    target = target + 2 * jnp.right_shift(rest, 2) + (rest & 1)
    here = lax.broadcasted_iota(jnp.int32, shape, 1) == target
    return jnp.where(here, 1.0, 0.0).astype(jnp.bfloat16)


def block_rows(pairs):
    return up_to(up_to(pairs * PAIRED, ROWS) + 2, 16)


def legendre_call(pairing, spectra, tables):
    _, pairs, level_fields, degrees = spectra.shape
    bands = tables[0].shape[2]
    block = 2 * block_rows(pairs)
    group = next(n for n in (4, 5, 2, 1) if pairs % n == 0)
    numbers = jnp.concatenate([lax.axis_index("lev").astype(jnp.int32)[None], pairing])
    codes = pl.pallas_call(
        codes_kernel,
        out_shape=jax.ShapeDtypeStruct((1, LANES), jnp.int32),
        in_specs=[pl.BlockSpec(memory_space=pltpu.VMEM)],
        out_specs=pl.BlockSpec(memory_space=pltpu.VMEM),
        compiler_params=pltpu.CompilerParams(vmem_limit_bytes=60 * 1024 * 1024),
        cost_estimate=pl.CostEstimate(flops=0, bytes_accessed=4_000_000, transcendentals=0),
    )(jnp.pad(pairing, (0, LANES - pairs))[None, :])
    shape = jax.ShapeDtypeStruct((bands, block, LANES), jnp.bfloat16)
    whole = pl.BlockSpec((bands, block, LANES), lambda i: (0, 0, 0))
    in_vmem = pl.BlockSpec(memory_space=pltpu.VMEM)
    in_hbm = pl.BlockSpec(memory_space=pl.ANY)
    return pl.pallas_call(
        legendre_kernel,
        grid=(pairs // group,),
        out_shape=(shape, jax.ShapeDtypeStruct((ROWS, LANES), jnp.float32)),
        in_specs=[
            pl.BlockSpec(memory_space=pltpu.SMEM),
            pl.BlockSpec((1, LANES), lambda i: (0, 0)),
            in_hbm,
        ]
        + [in_hbm] * len(tables),
        out_specs=(whole, in_vmem),
        scratch_shapes=[
            pltpu.VMEM((bands * block, LANES), jnp.float32),
            pltpu.VMEM((group, ROWS * bands, LANES), jnp.float32),
            pltpu.VMEM((group, 2 * level_fields, LANES), jnp.float32),
            pltpu.VMEM((4 * level_fields, LANES), jnp.bfloat16),
        ]
        + [pltpu.VMEM(x.shape, x.dtype) for x in (spectra,) + tables]
        + [pltpu.SemaphoreType.DMA((1 + len(tables), pairs // group))],
        compiler_params=pltpu.CompilerParams(vmem_limit_bytes=60 * 1024 * 1024),
        cost_estimate=pl.CostEstimate(
            flops=2 * ROWS * bands * 4 * level_fields * pairs * degrees,
            bytes_accessed=8_000_000,
            transcendentals=0,
        ),
    )(numbers, codes, spectra, *tables)


def fourier_table(pair_total, padded, lon_total):
    order_total = 2 * pair_total
    half = pair_total // 2
    low = 2 * np.arange(half)
    high = low + 1
    even = np.concatenate([low, order_total - 1 - high])
    odd = np.concatenate([order_total - 1 - low, high])
    lon = np.arange(lon_total // 2)
    table = np.zeros((4, 2, padded, lon_total // 2), np.float32)
    for parity, orders in enumerate((even, odd)):
        phase = (orders[:, None] * lon[None, :]) % lon_total * (2.0 * math.pi / lon_total)
        weight = np.where(orders == 0, 1.0, 2.0)[:, None]
        table[parity, 0, :pair_total] = weight * np.cos(phase)
        table[parity, 1, :pair_total] = -weight * np.sin(phase)
    return table.reshape(4, 2 * padded, lon_total // 2).astype(jnp.bfloat16)


def owner_tables(bands, pairs):
    slots = np.arange(bands * pairs)
    owner = slots[:, None] // pairs == np.arange(LANES)[None, :]
    lane = slots[:, None] % pairs == np.arange(LANES)[None, :]
    return owner.astype(jnp.bfloat16), lane.astype(np.float32)


def pair_places(flat, owner_ref, lane_ref, codes, bands, block, code_row, padded):
    pair_total = owner_ref.shape[0]
    codes[...] = jnp.zeros(codes.shape, jnp.float32)
    numbers = []
    for part in range(2):
        codes[part, :bands, :] = flat[pl.ds(code_row + part, bands, stride=block), :]
        numbers.append(
            jnp.dot(
                owner_ref[...],
                codes[part].astype(jnp.bfloat16),
                preferred_element_type=jnp.float32,
            )
        )
    pair_id = jnp.sum(
        (16.0 * numbers[0] + numbers[1]) * lane_ref[...], axis=1, keepdims=True
    ).astype(jnp.int32)
    place = jnp.right_shift(pair_id, 1) + (pair_id & 1) * (pair_total // 2)
    columns = lax.broadcasted_iota(jnp.int32, (pair_total, padded), 1)
    place = jnp.where(columns == place, 1.0, 0.0)
    if padded > pair_total:
        place = jnp.concatenate(
            [place, jnp.zeros((padded - pair_total, padded), jnp.float32)], axis=0
        )
    return place.astype(jnp.bfloat16)


def fourier_kernel(
    pairs, levels, base_ref, after_ref, sums_ref, owner_ref, lane_ref, table_source, *others
):
    field_refs, send_ref, others = others[:2], others[2], others[3:]
    codes, flat, gathered, lhs, table_ref, arrival_sem = others
    copy = pltpu.make_async_copy(table_source.at[:2], table_ref, arrival_sem)
    copy.start()
    bands, block, width = sums_ref.shape
    pair_total = bands * pairs
    padded = gathered.shape[0]
    blocks = padded // LANES
    fields = 2 * levels
    flat[...] = sums_ref[...].astype(jnp.float32).reshape(bands * block, width)
    gathered[pair_total:, :] = jnp.zeros((padded - pair_total, width), jnp.float32)
    code_row = up_to(pairs * PAIRED, ROWS)
    place = pair_places(flat, owner_ref, lane_ref, codes, bands, block, code_row, padded)
    low = lax.broadcasted_iota(jnp.int32, (fields, padded), 1) < pair_total // 2
    middle = fields * ROWS
    for number in range(2):
        for i in range(PAIRED):
            for band in range(bands):
                first = band * block + number * (block // 2) + i
                gathered[band * pairs : (band + 1) * pairs, :] = flat[
                    pl.ds(first, pairs, stride=PAIRED), :
                ]
            ordered = jnp.dot(
                gathered[...].T.astype(jnp.bfloat16), place, preferred_element_type=jnp.float32
            )
            for side in range(2):
                row = side * PAIRED + i
                if HALO <= row < HALO + ROWS:
                    first, stride = row - HALO, ROWS
                else:
                    first, stride = middle + (row - HALO - ROWS) % TALL, 2 * HALO
                for part in range(2):
                    start = side * HALF + part * fields
                    straight = ordered[start : start + fields]
                    start = start + 2 * fields
                    crossed = ordered[start : start + fields]
                    both = (jnp.where(low, straight, crossed), jnp.where(low, crossed, straight))
                    for parity in range(2):
                        for t in range(blocks):
                            lhs[
                                number,
                                parity,
                                part * blocks + t,
                                pl.ds(first, fields, stride=stride),
                                :,
                            ] = both[parity][:, t * LANES : (t + 1) * LANES]
    copy.wait()
    half = table_ref.shape[2]

    def transform(number, first, count):
        found = []
        for parity in range(2):
            left = jnp.concatenate(
                [
                    lhs[number, parity, t, first : first + count, :].astype(jnp.bfloat16)
                    for t in range(2 * blocks)
                ],
                axis=1,
            )
            found.append(jnp.dot(left, table_ref[parity], preferred_element_type=jnp.float32))
        pieces = (found[0] + found[1], found[0] - found[1])
        return [piece.astype(jnp.bfloat16).astype(jnp.float32) for piece in pieces]

    group = next(n for n in (4, 2, 1) if levels % n == 0)
    for number, field_ref in enumerate(field_refs):
        for level in range(0, levels, group):
            pieces = transform(number, level * 2 * ROWS, group * 2 * ROWS)
            for part, value in enumerate(pieces):
                value = value.reshape(group, 2 * ROWS, half)
                lanes = slice(part * half, (part + 1) * half)
                field_ref[level : level + group, : 2 * ROWS, lanes] = value
        for part, value in enumerate(transform(number, middle, fields * 2 * HALO)):
            value = value.reshape(levels, 4 * HALO, half)
            field_ref[:, 2 * ROWS :, part * half : (part + 1) * half] = value
        if send_ref.shape[0] == 1:
            start = jnp.where(base_ref[0] == 0, levels - HALO, 0)
            send_ref[0, number] = field_ref[pl.ds(start, HALO)].astype(jnp.bfloat16)
        else:
            send_ref[0, number] = field_ref[:HALO].astype(jnp.bfloat16)
            send_ref[1, number] = field_ref[levels - HALO :].astype(jnp.bfloat16)


def fourier_call(base, after, sums, table, pairs, levels, lon_total):
    bands, block, width = sums.shape
    padded = up_to(bands * pairs, LANES)
    extra = [jnp.asarray(x) for x in owner_tables(bands, pairs)]
    sends = 1 if lax.axis_size("lev") == 2 else 2
    field_shape = (levels, 3 * ROWS, lon_total)
    field = jax.ShapeDtypeStruct(field_shape, jnp.float32)
    send = jax.ShapeDtypeStruct((sends, 2, HALO) + field_shape[1:], jnp.bfloat16)
    in_vmem = pl.BlockSpec(memory_space=pltpu.VMEM)
    return pl.pallas_call(
        functools.partial(fourier_kernel, pairs, levels),
        out_shape=(field, field, send),
        in_specs=[pl.BlockSpec(memory_space=pltpu.SMEM)]
        + [in_vmem] * 4
        + [pl.BlockSpec(memory_space=pl.ANY)],
        out_specs=(in_vmem,) * 3,
        scratch_shapes=[
            pltpu.VMEM((2, LANES, LANES), jnp.float32),
            pltpu.VMEM((bands * block, width), jnp.float32),
            pltpu.VMEM((padded, width), jnp.float32),
            pltpu.VMEM((2, 2, 2 * padded // LANES, 2 * levels * TALL, LANES), jnp.float32),
            pltpu.VMEM((2,) + table.shape[1:], table.dtype),
            pltpu.SemaphoreType.DMA,
        ],
        compiler_params=pltpu.CompilerParams(vmem_limit_bytes=44 * 1024 * 1024),
        cost_estimate=pl.CostEstimate(
            flops=8_000_000_000, bytes_accessed=8_000_000, transcendentals=0
        ),
    )(base, after, sums, *extra, table)


def exchange(sums):
    return lax.all_to_all(sums, "band", split_axis=0, concat_axis=0, tiled=True)


def per_device(spectra, legendre, pairing, eta_shift, cells):
    levels, rows, lon_total = eta_shift.shape
    pairs = pairing.shape[0]
    spectra = jnp.transpose(spectra, (0, 2, 1, 3))
    table = jnp.transpose(legendre, (0, 2, 1, 3))
    if lax.axis_size("lev") == 2:
        tables = (table, lax.ppermute(table, "lev", [(0, 1), (1, 0)]))
    else:
        tables = (lax.all_gather(table, "lev", axis=0, tiled=True),)
    base = jnp.stack([lax.axis_index("lev") * levels, lax.axis_index("band") * rows])
    base = base.astype(jnp.int32)
    sums, done = legendre_call(pairing, spectra, tables)
    sums = exchange(sums)
    points, done = prepare_call(base, done, eta_shift, cells)
    pair_total = pairs * lax.axis_size("band")
    twiddles = jnp.asarray(fourier_table(pair_total, up_to(pair_total, LANES), lon_total))
    winds, tracers, send = fourier_call(base, done, sums, twiddles, pairs, levels, lon_total)
    nears = swap_levels(send)
    displacement, moved, _ = interpolation_call(
        wind_levels, base, 0, winds, points, nears, (), jnp.float32, 2
    )
    advected, _ = interpolation_call(
        tracer_levels, base, 1, tracers, points, nears, (moved,), jnp.bfloat16, 1
    )
    return advected, displacement


def solution(mesh):
    return jax.shard_map(
        per_device,
        mesh=mesh,
        in_specs=(
            P(None, "lev", "band", None),
            P("lev", None, "band", None),
            P("band"),
            P("lev", "band", None),
            P(None, "lev", "band", None),
        ),
        out_specs=(P(None, "lev", "band", None), P(None, "lev", "band", None)),
        check_vma=False,
    )
```

```python
import functools
import math

import jax
import jax.numpy as jnp
import numpy as np
from jax import lax
from jax.experimental import pallas as pl
from jax.experimental.pallas import tpu as pltpu
from jax.sharding import PartitionSpec as P

ITERS = 2


COURANT = 0.8
HALO = 2
LANES = 128
ROWS = 8
SLOTS = (-1, 0, 1, 2)


def slot_weights(place, here, low, high, sixth):
    z = jnp.minimum(jnp.maximum(place, low), high)
    square = z * z
    less = square - 1.0
    outer = less * z * sixth
    triple = 3.0 * outer
    half = 0.5 * z
    half_square = 0.5 * square
    return (
        half_square - half - jnp.where(here, outer, triple),
        triple - less,
        half_square + half - jnp.where(here, triple, outer),
        outer,
    )


def bounds(here):
    return (
        jnp.where(here, -0.5, -1.5),
        jnp.where(here, 1.5, 0.5),
        jnp.where(here, 1.0 / 6.0, -1.0 / 6.0),
    )


def weighted(weights, values):
    return (weights[0] * values[0] + weights[1] * values[1]) + (
        weights[2] * values[2] + weights[3] * values[3]
    )


def shifted_lanes(before, here, after, lane):
    return (
        pltpu.roll(jnp.where(lane < LANES - 2, here, before), 2, 1),
        pltpu.roll(jnp.where(lane < LANES - 1, here, before), 1, 1),
        here,
        pltpu.roll(jnp.where(lane < 1, after, here), LANES - 1, 1),
        pltpu.roll(jnp.where(lane < 2, after, here), LANES - 2, 1),
    )


STACK = 5 * ROWS
FIELD_ROW = (ROWS, 3 * ROWS)


def fill_units(slab, chunk, chunk_total, source, scratch):
    field_ref, row = source
    before = jnp.where(chunk == 0, chunk_total - 1, chunk - 1)
    after = jnp.where(chunk == chunk_total - 1, 0, chunk + 1)
    starts = [pl.multiple_of(c * LANES, LANES) for c in (before, chunk, after)]
    lane = lax.broadcasted_iota(jnp.int32, (ROWS, LANES), 1)
    first = slab * (5 * STACK)

    def edge_start():
        moved = shifted_lanes(
            *[field_ref[row, 2 * ROWS : 3 * ROWS, pl.ds(s, LANES)] for s in starts], lane
        )
        return [(value, pltpu.roll(value, ROWS // 2, 0)) for value in moved]

    def edge_finish(values):
        for step, (between, outside) in enumerate(values):
            for offset, value in ((0, outside), (2 * ROWS, between), (4 * ROWS, outside)):
                scratch[pl.ds(first + step * STACK + offset, ROWS), :] = value

    def center_unit(field):
        def start():
            rows = slice(field * ROWS, (field + 1) * ROWS)
            blocks = [field_ref[row, rows, pl.ds(s, LANES)] for s in starts]
            return shifted_lanes(*blocks, lane)

        def finish(values):
            for step, moved in enumerate(values):
                scratch[pl.ds(first + step * STACK + FIELD_ROW[field], ROWS), :] = moved

        return start, finish

    return [(edge_start, edge_finish)] + [center_unit(field) for field in range(2)]


class Interleave:
    def __init__(self, units, ticks, later):
        self.units = list(units)
        self.every = max(1, ticks // max(1, len(self.units)))
        self.count = 0
        self.pending = None
        self.later = later

    def advance(self):
        if self.pending is not None:
            self.pending[0](self.pending[1])
            self.pending = None
        if self.units:
            start, finish = self.units.pop(0)
            self.pending = (finish, start())

    def tick(self):
        if self.count % self.every == 0:
            self.advance()
        self.count += 1
        if self.later and self.count % 3 == 0:
            self.later.pop(0)()

    def flush(self):
        while self.units or self.pending is not None:
            self.advance()

    def finish_later(self):
        while self.later:
            self.later.pop(0)()


def level_sums(scratch, field, base, slot, points):
    loaded = {}

    def load(a, b, c):
        offset = ((a + HALO) * 5 + c + HALO) * STACK + FIELD_ROW[field] + b
        if slot == (2, 2):
            return scratch[pl.ds(base + offset, ROWS), :]
        if (a, b, c) not in loaded:
            loaded[a, b, c] = scratch[pl.ds(base + offset, ROWS), :]
        return loaded[a, b, c]

    def one(step, weights, level_here, row_here, lon_here):
        def pick_lon(a, b):
            if slot[1] == 2:
                return jnp.where(lon_here, load(a + step, b, 2), load(a + step, b, -2))
            return load(a + step, b, slot[1])

        def pick(a):
            if slot[0] == 2:
                return jnp.where(row_here, pick_lon(a, 2), pick_lon(a, -2))
            return pick_lon(a, slot[0])

        total = weights[0] * pick(-1) + weights[1] * pick(0)
        total = total + weights[2] * pick(1)
        return total + weights[3] * jnp.where(level_here, pick(2), pick(-2))

    return [one(step, *point) for step, point in enumerate(points)]


def across(scratch, field, base, points, row_weights, lon_weights, filling, keep=None):
    columns = [[None] * 4 for _ in points]
    for b, row_slot in enumerate(SLOTS):
        for c, lon_slot in enumerate(SLOTS):
            filling.tick()
            found = level_sums(scratch, field, base, (row_slot, lon_slot), points)
            for step, value in enumerate(found):
                if keep is not None:
                    keep[field, step, 4 * b + c] = value
                term = row_weights[step][b] * value
                columns[step][c] = term if b == 0 else columns[step][c] + term
    return [weighted(weights, column) for weights, column in zip(lon_weights, columns)]


def across_kept(keep, field, step, row_weights, lon_weights):
    return weighted(
        lon_weights,
        [
            weighted(row_weights, [keep[field, step, 4 * b + c] for b in range(4)])
            for c in range(4)
        ],
    )


def prepare_kernel(base_ref, after_ref, eta_ref, cells_ref, points_ref, done_ref):
    done_ref[...] = after_ref[...]
    levels, rows, lon_total = eta_ref.shape
    shape = (rows, LANES)
    row_here = base_ref[1] + lax.broadcasted_iota(jnp.int32, shape, 0)
    lane = lax.broadcasted_iota(jnp.int32, shape, 1)

    def chunk_step(chunk, carry):
        lanes = pl.ds(pl.multiple_of(chunk * LANES, LANES), LANES)
        for k in range(levels):
            level_here = cells_ref[2, k, :, lanes] == base_ref[0] + k
            weights = slot_weights(
                -eta_ref[k, :, lanes].astype(jnp.float32), level_here, *bounds(level_here)
            )
            here = (
                level_here,
                cells_ref[0, k, :, lanes] == row_here,
                cells_ref[1, k, :, lanes] == chunk * LANES + lane,
            )
            for n, value in enumerate(weights + tuple(bounds(x)[0] for x in here)):
                points_ref[n, k, :, lanes] = value
        return carry

    lax.fori_loop(0, lon_total // LANES, chunk_step, 0)


def prepare_call(base, after, eta_shift, cells):
    in_vmem = pl.BlockSpec(memory_space=pltpu.VMEM)
    return pl.pallas_call(
        prepare_kernel,
        out_shape=(
            jax.ShapeDtypeStruct((7,) + eta_shift.shape, jnp.float32),
            jax.ShapeDtypeStruct(after.shape, after.dtype),
        ),
        in_specs=[pl.BlockSpec(memory_space=pltpu.SMEM)] + [in_vmem] * 3,
        out_specs=(in_vmem, in_vmem),
        compiler_params=pltpu.CompilerParams(vmem_limit_bytes=16 * 1024 * 1024),
        cost_estimate=pl.CostEstimate(
            flops=40 * eta_shift.size, bytes_accessed=20_000_000, transcendentals=0
        ),
    )(base, after, eta_shift, cells)


def arrival(points_ref, k, lanes):
    here = [points_ref[n, k, :, lanes] > -1.0 for n in range(4, 7)]
    return tuple(points_ref[n, k, :, lanes] for n in range(4)), *here


def both_weights(shift_row, shift_lon, point):
    _, _, row_here, lon_here = point
    return (
        slot_weights(-shift_row, row_here, *bounds(row_here)),
        slot_weights(-shift_lon, lon_here, *bounds(lon_here)),
    )


def wind_levels(base, lanes, k, points, scratch, keep, filling, *out_refs):
    def arrival_wind(field, step):
        middle = (HALO * 5 + HALO) * STACK + step * (5 * STACK) + FIELD_ROW[field]
        return scratch[pl.ds(base + middle, ROWS), :]

    weights = []
    for step, point in enumerate(points):
        east, north = arrival_wind(0, step), arrival_wind(1, step)
        keep[0, step, 16], keep[1, step, 16] = east, north
        weights.append(both_weights(COURANT * north, COURANT * east, point))
    row_weights, lon_weights = zip(*weights)
    found = [
        across(scratch, field, base, points, row_weights, lon_weights, filling, keep)
        for field in range(2)
    ]
    filling.finish_later()

    def tail(step, east_found, north_found):
        def finish():
            east, north = keep[0, step, 16], keep[1, step, 16]
            here = (east_found, north_found)
            for sweep in range(ITERS):
                shift_row = 0.5 * COURANT * (north + here[1])
                shift_lon = 0.5 * COURANT * (east + here[0])
                if sweep < ITERS - 1:
                    weights = both_weights(shift_row, shift_lon, points[step])
                    here = [across_kept(keep, field, step, *weights) for field in range(2)]
            for out_ref in out_refs:
                out_ref[0, k + step, :, lanes] = shift_row
                out_ref[1, k + step, :, lanes] = shift_lon

        return finish

    filling.later += [tail(step, found[0][step], found[1][step]) for step in range(len(points))]


def tracer_levels(shift_ref, base, lanes, k, points, scratch, keep, filling, out_ref):
    weights = [
        both_weights(
            shift_ref[0, k + step, :, lanes], shift_ref[1, k + step, :, lanes], points[step]
        )
        for step in range(len(points))
    ]
    row_weights, lon_weights = zip(*weights)
    found = [
        across(scratch, field, base, points, row_weights, lon_weights, filling)
        for field in range(2)
    ]
    for field in range(2):
        for step, total in enumerate(found[field]):
            out_ref[field, k + step, :, lanes] = total.astype(out_ref.dtype)


def interpolation_kernel(
    levels_body, together, number, near_count, out_count, base_ref, field_ref, points_ref, *others
):
    nears, others = others[:near_count], others[near_count:]
    around, even_scratch, odd_scratch, keep = others[-4:]
    extra, out_refs, done_ref = others[: -5 - out_count], others[-5 - out_count : -5], others[-5]
    done_ref[...] = jnp.zeros(done_ref.shape, done_ref.dtype)
    _, levels, rows, lon_total = points_ref.shape
    chunk_total = lon_total // LANES
    if near_count == 1:
        found = jnp.where(base_ref[0] == 0, HALO, 0)
        around[pl.ds(found, HALO)] = nears[0][number].astype(jnp.float32)
        around[pl.ds(HALO - found, HALO)] = jnp.zeros((HALO,) + around.shape[1:], jnp.float32)
    else:
        around[:HALO] = nears[0][number].astype(jnp.float32)
        around[HALO:] = nears[1][number].astype(jnp.float32)
    sources = [(around, n) for n in range(HALO)]
    sources += [(field_ref, n) for n in range(levels)]
    sources += [(around, HALO + n) for n in range(HALO)]

    def all_units(chunk, scratch):
        units = []
        for slab, source in enumerate(sources):
            units += fill_units(slab, chunk, chunk_total, source, scratch)
        return units

    for start, finish in all_units(0, even_scratch):
        finish(start())

    def one_chunk(chunk, scratch, other, later):
        lanes = pl.ds(pl.multiple_of(chunk * LANES, LANES), LANES)
        following = jnp.where(chunk == chunk_total - 1, 0, chunk + 1)
        filling = Interleave(all_units(following, other), 32 * (levels // together), later)
        for k in range(0, levels, together):
            points = [arrival(points_ref, k + n, lanes) for n in range(together)]
            base = k * (5 * STACK)
            keep_here = keep.at[k // together % 2]
            levels_body(*extra, base, lanes, k, points, scratch, keep_here, filling, *out_refs)
        filling.flush()
        if levels // together % 2:
            filling.finish_later()

    def chunk_pair(pair, carry):
        later = []
        one_chunk(2 * pair, even_scratch, odd_scratch, later)
        one_chunk(2 * pair + 1, odd_scratch, even_scratch, later)
        for finish in later:
            finish()
        return carry

    lax.fori_loop(0, chunk_total // 2, chunk_pair, 0)


def interpolation_call(
    levels_body, base, number, fields, points, nears, extra, out_dtype, out_count
):
    _, levels, rows, lon_total = points.shape
    count = levels * rows * lon_total
    together = next(n for n in (4, 2, 1) if levels % n == 0)
    scratch = pltpu.VMEM(((levels + 2 * HALO) * 5 * STACK, LANES), jnp.float32)
    in_vmem = pl.BlockSpec(memory_space=pltpu.VMEM)
    out = jax.ShapeDtypeStruct((2, levels, rows, lon_total), out_dtype)
    done = jax.ShapeDtypeStruct((ROWS, LANES), jnp.float32)
    return pl.pallas_call(
        functools.partial(
            interpolation_kernel, levels_body, together, number, len(nears), out_count
        ),
        out_shape=(out,) * out_count + (done,),
        in_specs=[pl.BlockSpec(memory_space=pltpu.SMEM)]
        + [in_vmem] * (2 + len(nears) + len(extra)),
        out_specs=(in_vmem,) * (out_count + 1),
        scratch_shapes=[
            pltpu.VMEM((2 * HALO,) + fields.shape[1:], jnp.float32),
            scratch,
            scratch,
            pltpu.VMEM((2, 2, together, 17, ROWS, LANES), jnp.float32),
        ],
        compiler_params=pltpu.CompilerParams(vmem_limit_bytes=16 * 1024 * 1024),
        cost_estimate=pl.CostEstimate(
            flops=count * 500, bytes_accessed=count * 40, transcendentals=0
        ),
    )(base, fields, points, *nears, *extra)


def swap_levels(send):
    if lax.axis_size("lev") == 2:
        return (lax.ppermute(send[0], "lev", [(0, 1), (1, 0)]),)
    up = [(i, i + 1) for i in range(lax.axis_size("lev") - 1)]
    down = [(j, i) for i, j in up]
    return lax.ppermute(send[1], "lev", up), lax.ppermute(send[0], "lev", down)


def up_to(value, step):
    return -(-value // step) * step


TALL = ROWS + 2 * HALO


def codes_kernel(numbers_ref, out_ref):
    out_ref[...] = numbers_ref[...]


def legendre_kernel(numbers_ref, codes_ref, spectra_ref, *others):
    table_count = (len(others) - 7) // 2
    sources, others = (spectra_ref,) + others[:table_count], others[table_count:]
    out_ref, done_ref, sums, table_tail, column_tail = others[:5]
    targets, arrivals = others[5:-1], others[-1]
    spectra_here, tables = targets[0], targets[1:]
    _, pairs, level_fields, degrees = spectra_ref.shape
    group = table_tail.shape[0]
    bands, block, _ = out_ref.shape
    full = degrees // LANES * LANES
    at_top = numbers_ref[0] == 0
    step = pl.program_id(0)

    def copies(number):
        here = pl.ds(number * group, group)
        return [
            pltpu.make_async_copy(source.at[:, here], target.at[:, here], arrivals.at[n, number])
            for n, (source, target) in enumerate(zip(sources, targets))
        ]

    @pl.when(step == 0)
    def _():
        for copy in copies(0):
            copy.start()
        sums[...] = jnp.zeros(sums.shape, jnp.float32)
        done_ref[...] = jnp.zeros(done_ref.shape, jnp.float32)
        table_tail[...] = jnp.zeros(table_tail.shape, jnp.float32)
        column_tail[...] = jnp.zeros(column_tail.shape, jnp.float32)
        codes = codes_ref[...]
        code_row = up_to(pl.num_programs(0) * group * TALL, ROWS)
        for band in range(bands):
            first = band * block + code_row
            sums[pl.ds(first, 1), :] = jnp.right_shift(codes, 4).astype(jnp.float32)
            sums[pl.ds(first + 1, 1), :] = (codes & 15).astype(jnp.float32)

    @pl.when(step + 1 < pairs // group)
    def _():
        for copy in copies(step + 1):
            copy.start()

    for copy in copies(step):
        copy.wait()
    band_row = lax.broadcasted_iota(jnp.int32, (bands, 4 * level_fields), 0)
    count = 2 * level_fields
    nothing = jnp.zeros((bands, 2 * count), jnp.float32)
    for p in range(group):
        slot = step * group + p
        edge = degrees - 1 - numbers_ref[1 + slot]
        left = []
        for number, table_ref in enumerate(tables):
            for row in range(table_ref.shape[0]):
                piece = table_ref[row, slot]
                left.append(piece[:, :full])
                first = (number * table_ref.shape[0] + row) * bands
                table_tail[p, first : first + bands, : degrees - full] = piece[:, full:].astype(
                    jnp.float32
                )
        left = jnp.concatenate(left, axis=0)
        left = jnp.concatenate([left, table_tail[p].astype(jnp.bfloat16)], axis=1)
        halves = ([], [])
        for part in range(2):
            piece = spectra_here[part, slot]
            whole = piece[:, :full].astype(jnp.float32)
            lane = lax.broadcasted_iota(jnp.int32, whole.shape, 1)
            zero = jnp.zeros_like(whole)
            halves[0].append(jnp.where(lane < edge, whole, zero).astype(jnp.bfloat16))
            halves[1].append(jnp.where(lane < edge, zero, whole).astype(jnp.bfloat16))
            first = part * level_fields
            column_tail[p, first : first + level_fields, : degrees - full] = piece[
                :, full:
            ].astype(jnp.float32)
        tail = column_tail[p].astype(jnp.bfloat16)
        right = jnp.concatenate(
            [
                jnp.concatenate([jnp.concatenate(halves[0], axis=0), jnp.zeros_like(tail)], axis=1),
                jnp.concatenate([jnp.concatenate(halves[1], axis=0), tail], axis=1),
            ],
            axis=0,
        )
        found = lax.dot_general(
            left, right, (((1,), (1,)), ((), ())), preferred_element_type=jnp.float32
        )
        found = [found[i * bands : (i + 1) * bands] for i in range(ROWS)]
        if len(tables) == 2:
            low, high = found[: ROWS // 2], found[ROWS // 2 :]
            found = [jnp.where(at_top, x, y) for x, y in zip(low, high)]
            found += [jnp.where(at_top, y, x) for x, y in zip(low, high)]
        above = [
            jnp.where(band_row == 0, nothing, pltpu.roll(x, 1, 0)) for x in found[ROWS - HALO :]
        ]
        below = [
            jnp.where(band_row == bands - 1, nothing, pltpu.roll(x, bands - 1, 0))
            for x in found[:HALO]
        ]
        rows = above + found + below
        for i, value in enumerate(rows):
            place = pl.ds(slot * TALL + i, bands, stride=block)
            sums[place, : 2 * count] = value

    @pl.when(step == pl.num_programs(0) - 1)
    def _():
        out_ref[...] = sums[...].astype(jnp.bfloat16).reshape(out_ref.shape)


def block_rows(pairs):
    return up_to(up_to(pairs * TALL, ROWS) + 2, 16)


def legendre_call(pairing, spectra, tables):
    _, pairs, level_fields, degrees = spectra.shape
    bands = tables[0].shape[2]
    block = block_rows(pairs)
    group = next(n for n in (4, 5, 2, 1) if pairs % n == 0)
    numbers = jnp.concatenate([lax.axis_index("lev").astype(jnp.int32)[None], pairing])
    codes = pl.pallas_call(
        codes_kernel,
        out_shape=jax.ShapeDtypeStruct((1, LANES), jnp.int32),
        in_specs=[pl.BlockSpec(memory_space=pltpu.VMEM)],
        out_specs=pl.BlockSpec(memory_space=pltpu.VMEM),
        compiler_params=pltpu.CompilerParams(vmem_limit_bytes=60 * 1024 * 1024),
        cost_estimate=pl.CostEstimate(flops=0, bytes_accessed=4_000_000, transcendentals=0),
    )(jnp.pad(pairing, (0, LANES - pairs))[None, :])
    shape = jax.ShapeDtypeStruct((bands, block, LANES), jnp.bfloat16)
    whole = pl.BlockSpec((bands, block, LANES), lambda i: (0, 0, 0))
    in_vmem = pl.BlockSpec(memory_space=pltpu.VMEM)
    in_hbm = pl.BlockSpec(memory_space=pl.ANY)
    return pl.pallas_call(
        legendre_kernel,
        grid=(pairs // group,),
        out_shape=(shape, jax.ShapeDtypeStruct((ROWS, LANES), jnp.float32)),
        in_specs=[
            pl.BlockSpec(memory_space=pltpu.SMEM),
            pl.BlockSpec((1, LANES), lambda i: (0, 0)),
            in_hbm,
        ]
        + [in_hbm] * len(tables),
        out_specs=(whole, in_vmem),
        scratch_shapes=[
            pltpu.VMEM((bands * block, LANES), jnp.float32),
            pltpu.VMEM((group, ROWS * bands, LANES), jnp.float32),
            pltpu.VMEM((group, 2 * level_fields, LANES), jnp.float32),
        ]
        + [pltpu.VMEM(x.shape, x.dtype) for x in (spectra,) + tables]
        + [pltpu.SemaphoreType.DMA((1 + len(tables), pairs // group))],
        compiler_params=pltpu.CompilerParams(vmem_limit_bytes=60 * 1024 * 1024),
        cost_estimate=pl.CostEstimate(
            flops=2 * ROWS * bands * 4 * level_fields * pairs * degrees,
            bytes_accessed=8_000_000,
            transcendentals=0,
        ),
    )(numbers, codes, spectra, *tables)


def fourier_table(pair_total, padded, lon_total):
    order_total = 2 * pair_total
    half = pair_total // 2
    low = 2 * np.arange(half)
    high = low + 1
    even = np.concatenate([low, order_total - 1 - high])
    odd = np.concatenate([order_total - 1 - low, high])
    lon = np.arange(lon_total // 2)
    table = np.zeros((4, 2, padded, lon_total // 2), np.float32)
    for parity, orders in enumerate((even, odd)):
        phase = (orders[:, None] * lon[None, :]) % lon_total * (2.0 * math.pi / lon_total)
        weight = np.where(orders == 0, 1.0, 2.0)[:, None]
        table[parity, 0, :pair_total] = weight * np.cos(phase)
        table[parity, 1, :pair_total] = -weight * np.sin(phase)
    return table.reshape(4, 2 * padded, lon_total // 2).astype(jnp.bfloat16)


def owner_tables(bands, pairs):
    room = up_to(pairs, ROWS)
    slots = np.arange(up_to(bands * room, LANES))
    owner = slots[:, None] // room == np.arange(LANES)[None, :]
    lane = slots[:, None] % room == np.arange(LANES)[None, :]
    return owner.astype(jnp.bfloat16), lane.astype(np.float32)


def pair_places(flat, owner_ref, lane_ref, codes, bands, block, code_row, pair_total, padded):
    codes[...] = jnp.zeros(codes.shape, jnp.float32)
    numbers = []
    for part in range(2):
        codes[part, :bands, :] = flat[pl.ds(code_row + part, bands, stride=block), :]
        numbers.append(
            jnp.dot(
                owner_ref[...],
                codes[part].astype(jnp.bfloat16),
                preferred_element_type=jnp.float32,
            )
        )
    pair_id = jnp.sum(
        (16.0 * numbers[0] + numbers[1]) * lane_ref[...], axis=1, keepdims=True
    ).astype(jnp.int32)
    place = jnp.right_shift(pair_id, 1) + (pair_id & 1) * (pair_total // 2)
    columns = lax.broadcasted_iota(jnp.int32, (owner_ref.shape[0], padded), 1)
    return jnp.where(columns == place, 1.0, 0.0).astype(jnp.bfloat16)


def fourier_kernel(
    pairs, levels, base_ref, after_ref, sums_ref, owner_ref, lane_ref, table_source, *others
):
    field_refs, send_ref, others = others[:2], others[2], others[3:]
    codes, flat, gathered, lhs, table_ref, arrival_sem = others
    copy = pltpu.make_async_copy(table_source.at[:2], table_ref, arrival_sem)
    copy.start()
    bands, block, width = sums_ref.shape
    pair_total = bands * pairs
    padded = up_to(pair_total, LANES)
    blocks = padded // LANES
    fields = 4 * levels
    room = up_to(pairs, ROWS)
    flat[...] = sums_ref[...].astype(jnp.float32).reshape(bands * block, width)
    gathered[...] = jnp.zeros(gathered.shape, jnp.float32)
    code_row = up_to(pairs * TALL, ROWS)
    place = pair_places(
        flat, owner_ref, lane_ref, codes, bands, block, code_row, pair_total, padded
    )
    low = lax.broadcasted_iota(jnp.int32, (fields, padded), 1) < pair_total // 2
    middle = fields * ROWS
    for row in range(TALL):
        here = gathered.at[row % 2]
        for band in range(bands):
            here[band * room : band * room + pairs, :] = flat[
                pl.ds(band * block + row, pairs, stride=TALL), :
            ]
        ordered = jnp.dot(
            here[...].T.astype(jnp.bfloat16), place, preferred_element_type=jnp.float32
        )
        if HALO <= row < HALO + ROWS:
            first, stride = row - HALO, ROWS
        else:
            first, stride = middle + (row - HALO - ROWS) % TALL, 2 * HALO
        for part in range(2):
            start = part * fields
            straight = ordered[start : start + fields]
            start = start + 2 * fields
            crossed = ordered[start : start + fields]
            both = (jnp.where(low, straight, crossed), jnp.where(low, crossed, straight))
            for parity in range(2):
                for t in range(blocks):
                    lhs[parity, part * blocks + t, pl.ds(first, fields, stride=stride), :] = both[
                        parity
                    ][:, t * LANES : (t + 1) * LANES]
    copy.wait()
    half = table_ref.shape[2]

    def transform(first, count):
        found = []
        for parity in range(2):
            left = jnp.concatenate(
                [
                    lhs[parity, t, first : first + count, :].astype(jnp.bfloat16)
                    for t in range(2 * blocks)
                ],
                axis=1,
            )
            found.append(jnp.dot(left, table_ref[parity], preferred_element_type=jnp.float32))
        pieces = (found[0] + found[1], found[0] - found[1])
        return [piece.astype(jnp.bfloat16).astype(jnp.float32) for piece in pieces]

    group = next(n for n in (4, 2, 1) if levels % n == 0)
    for level in range(0, levels, group):
        for part, value in enumerate(transform(level * 4 * ROWS, group * 4 * ROWS)):
            value = value.reshape(group, 4 * ROWS, half)
            lanes = slice(part * half, (part + 1) * half)
            for number, field_ref in enumerate(field_refs):
                field_ref[level : level + group, : 2 * ROWS, lanes] = value[
                    :, 2 * ROWS * number : 2 * ROWS * (number + 1)
                ]
    for part, value in enumerate(transform(middle, fields * 2 * HALO)):
        value = value.reshape(levels, 8 * HALO, half)
        lanes = slice(part * half, (part + 1) * half)
        for number, field_ref in enumerate(field_refs):
            field_ref[:, 2 * ROWS :, lanes] = value[:, 4 * HALO * number : 4 * HALO * (number + 1)]
    for number, field_ref in enumerate(field_refs):
        if send_ref.shape[0] == 1:
            start = jnp.where(base_ref[0] == 0, levels - HALO, 0)
            send_ref[0, number] = field_ref[pl.ds(start, HALO)].astype(jnp.bfloat16)
        else:
            send_ref[0, number] = field_ref[:HALO].astype(jnp.bfloat16)
            send_ref[1, number] = field_ref[levels - HALO :].astype(jnp.bfloat16)


def fourier_call(base, after, sums, table, pairs, levels, lon_total):
    bands, block, width = sums.shape
    padded = up_to(bands * pairs, LANES)
    extra = [jnp.asarray(x) for x in owner_tables(bands, pairs)]
    sends = 1 if lax.axis_size("lev") == 2 else 2
    field_shape = (levels, 3 * ROWS, lon_total)
    field = jax.ShapeDtypeStruct(field_shape, jnp.float32)
    send = jax.ShapeDtypeStruct((sends, 2, HALO) + field_shape[1:], jnp.bfloat16)
    in_vmem = pl.BlockSpec(memory_space=pltpu.VMEM)
    return pl.pallas_call(
        functools.partial(fourier_kernel, pairs, levels),
        out_shape=(field, field, send),
        in_specs=[pl.BlockSpec(memory_space=pltpu.SMEM)]
        + [in_vmem] * 4
        + [pl.BlockSpec(memory_space=pl.ANY)],
        out_specs=(in_vmem,) * 3,
        scratch_shapes=[
            pltpu.VMEM((2, LANES, LANES), jnp.float32),
            pltpu.VMEM((bands * block, width), jnp.float32),
            pltpu.VMEM((2, extra[0].shape[0], width), jnp.float32),
            pltpu.VMEM((2, 2 * padded // LANES, 4 * levels * TALL, LANES), jnp.float32),
            pltpu.VMEM((2,) + table.shape[1:], table.dtype),
            pltpu.SemaphoreType.DMA,
        ],
        compiler_params=pltpu.CompilerParams(vmem_limit_bytes=44 * 1024 * 1024),
        cost_estimate=pl.CostEstimate(
            flops=8_000_000_000, bytes_accessed=8_000_000, transcendentals=0
        ),
    )(base, after, sums, *extra, table)


def exchange(sums):
    return lax.all_to_all(sums, "band", split_axis=0, concat_axis=0, tiled=True)


def per_device(spectra, legendre, pairing, eta_shift, cells):
    levels, rows, lon_total = eta_shift.shape
    pairs = pairing.shape[0]
    spectra = jnp.transpose(spectra, (0, 2, 1, 3))
    table = jnp.transpose(legendre, (0, 2, 1, 3))
    if lax.axis_size("lev") == 2:
        tables = (table, lax.ppermute(table, "lev", [(0, 1), (1, 0)]))
    else:
        tables = (lax.all_gather(table, "lev", axis=0, tiled=True),)
    base = jnp.stack([lax.axis_index("lev") * levels, lax.axis_index("band") * rows])
    base = base.astype(jnp.int32)
    sums, done = legendre_call(pairing, spectra, tables)
    sums = exchange(sums)
    points, done = prepare_call(base, done, eta_shift, cells)
    pair_total = pairs * lax.axis_size("band")
    twiddles = jnp.asarray(fourier_table(pair_total, up_to(pair_total, LANES), lon_total))
    winds, tracers, send = fourier_call(base, done, sums, twiddles, pairs, levels, lon_total)
    nears = swap_levels(send)
    displacement, moved, _ = interpolation_call(
        wind_levels, base, 0, winds, points, nears, (), jnp.float32, 2
    )
    advected, _ = interpolation_call(
        tracer_levels, base, 1, tracers, points, nears, (moved,), jnp.bfloat16, 1
    )
    return advected, displacement


def solution(mesh):
    return jax.shard_map(
        per_device,
        mesh=mesh,
        in_specs=(
            P(None, "lev", "band", None),
            P("lev", None, "band", None),
            P("band"),
            P("lev", "band", None),
            P(None, "lev", "band", None),
        ),
        out_specs=(P(None, "lev", "band", None), P(None, "lev", "band", None)),
        check_vma=False,
    )
```

```python
import functools
import math

import jax
import jax.numpy as jnp
import numpy as np
from jax import lax
from jax.experimental import pallas as pl
from jax.experimental.pallas import tpu as pltpu
from jax.sharding import PartitionSpec as P

ITERS = 2


COURANT = 0.8
HALO = 2
LANES = 128
ROWS = 8
SLOTS = (-1, 0, 1, 2)


def slot_weights(place, here, low, high, sixth):
    z = jnp.minimum(jnp.maximum(place, low), high)
    square = z * z
    less = square - 1.0
    outer = less * z * sixth
    triple = 3.0 * outer
    half = 0.5 * z
    half_square = 0.5 * square
    return (
        half_square - half - jnp.where(here, outer, triple),
        triple - less,
        half_square + half - jnp.where(here, triple, outer),
        outer,
    )


def bounds(here):
    return (
        jnp.where(here, -0.5, -1.5),
        jnp.where(here, 1.5, 0.5),
        jnp.where(here, 1.0 / 6.0, -1.0 / 6.0),
    )


def weighted(weights, values):
    return (weights[0] * values[0] + weights[1] * values[1]) + (
        weights[2] * values[2] + weights[3] * values[3]
    )


def shifted_lanes(before, here, after, lane):
    return (
        pltpu.roll(jnp.where(lane < LANES - 2, here, before), 2, 1),
        pltpu.roll(jnp.where(lane < LANES - 1, here, before), 1, 1),
        here,
        pltpu.roll(jnp.where(lane < 1, after, here), LANES - 1, 1),
        pltpu.roll(jnp.where(lane < 2, after, here), LANES - 2, 1),
    )


STACK = 5 * ROWS
FIELD_ROW = (ROWS, 3 * ROWS)


def fill_units(slab, chunk, chunk_total, source, scratch):
    field_ref, row = source
    before = jnp.where(chunk == 0, chunk_total - 1, chunk - 1)
    after = jnp.where(chunk == chunk_total - 1, 0, chunk + 1)
    starts = [pl.multiple_of(c * LANES, LANES) for c in (before, chunk, after)]
    lane = lax.broadcasted_iota(jnp.int32, (ROWS, LANES), 1)
    first = slab * (5 * STACK)

    def edge_start():
        moved = shifted_lanes(
            *[field_ref[row, 2 * ROWS : 3 * ROWS, pl.ds(s, LANES)] for s in starts], lane
        )
        return [(value, pltpu.roll(value, ROWS // 2, 0)) for value in moved]

    def edge_finish(values):
        for step, (between, outside) in enumerate(values):
            for offset, value in ((0, outside), (2 * ROWS, between), (4 * ROWS, outside)):
                scratch[pl.ds(first + step * STACK + offset, ROWS), :] = value

    def center_unit(field):
        def start():
            rows = slice(field * ROWS, (field + 1) * ROWS)
            blocks = [field_ref[row, rows, pl.ds(s, LANES)] for s in starts]
            return shifted_lanes(*blocks, lane)

        def finish(values):
            for step, moved in enumerate(values):
                scratch[pl.ds(first + step * STACK + FIELD_ROW[field], ROWS), :] = moved

        return start, finish

    return [(edge_start, edge_finish)] + [center_unit(field) for field in range(2)]


class Interleave:
    def __init__(self, units, ticks, later):
        self.units = list(units)
        self.every = max(1, ticks // max(1, len(self.units)))
        self.count = 0
        self.pending = None
        self.later = later

    def advance(self):
        if self.pending is not None:
            self.pending[0](self.pending[1])
            self.pending = None
        if self.units:
            start, finish = self.units.pop(0)
            self.pending = (finish, start())

    def tick(self):
        if self.count % self.every == 0:
            self.advance()
        self.count += 1
        if self.later and self.count % 3 == 0:
            self.later.pop(0)()

    def flush(self):
        while self.units or self.pending is not None:
            self.advance()

    def finish_later(self):
        while self.later:
            self.later.pop(0)()


def level_sums(scratch, field, base, slot, points):
    loaded = {}

    def load(a, b, c):
        offset = ((a + HALO) * 5 + c + HALO) * STACK + FIELD_ROW[field] + b
        if (a, b, c) not in loaded:
            loaded[a, b, c] = scratch[pl.ds(base + offset, ROWS), :]
        return loaded[a, b, c]

    def one(step, weights, level_here, row_here, lon_here):
        def pick_lon(a, b):
            if slot[1] == 2:
                return jnp.where(lon_here, load(a + step, b, 2), load(a + step, b, -2))
            return load(a + step, b, slot[1])

        def pick(a):
            if slot[0] == 2:
                return jnp.where(row_here, pick_lon(a, 2), pick_lon(a, -2))
            return pick_lon(a, slot[0])

        total = weights[0] * pick(-1) + weights[1] * pick(0)
        total = total + weights[2] * pick(1)
        return total + weights[3] * jnp.where(level_here, pick(2), pick(-2))

    return [one(step, *point) for step, point in enumerate(points)]


def across(scratch, field, base, points, row_weights, lon_weights, filling, keep=None):
    columns = [[None] * 4 for _ in points]
    for b, row_slot in enumerate(SLOTS):
        for c, lon_slot in enumerate(SLOTS):
            filling.tick()
            found = level_sums(scratch, field, base, (row_slot, lon_slot), points)
            for step, value in enumerate(found):
                if keep is not None:
                    keep[field, step, 4 * b + c] = value
                term = row_weights[step][b] * value
                columns[step][c] = term if b == 0 else columns[step][c] + term
    return [weighted(weights, column) for weights, column in zip(lon_weights, columns)]


def across_kept(keep, field, step, row_weights, lon_weights):
    return weighted(
        lon_weights,
        [
            weighted(row_weights, [keep[field, step, 4 * b + c] for b in range(4)])
            for c in range(4)
        ],
    )


def prepare_kernel(base_ref, after_ref, eta_ref, cells_ref, points_ref, done_ref):
    done_ref[...] = after_ref[...]
    levels, rows, lon_total = eta_ref.shape
    shape = (rows, LANES)
    row_here = base_ref[1] + lax.broadcasted_iota(jnp.int32, shape, 0)
    lane = lax.broadcasted_iota(jnp.int32, shape, 1)

    def chunk_step(chunk, carry):
        lanes = pl.ds(pl.multiple_of(chunk * LANES, LANES), LANES)
        for k in range(levels):
            level_here = cells_ref[2, k, :, lanes] == base_ref[0] + k
            weights = slot_weights(
                -eta_ref[k, :, lanes].astype(jnp.float32), level_here, *bounds(level_here)
            )
            here = (
                level_here,
                cells_ref[0, k, :, lanes] == row_here,
                cells_ref[1, k, :, lanes] == chunk * LANES + lane,
            )
            for n, value in enumerate(weights + tuple(bounds(x)[0] for x in here)):
                points_ref[n, k, :, lanes] = value
        return carry

    lax.fori_loop(0, lon_total // LANES, chunk_step, 0)


def prepare_call(base, after, eta_shift, cells):
    in_vmem = pl.BlockSpec(memory_space=pltpu.VMEM)
    return pl.pallas_call(
        prepare_kernel,
        out_shape=(
            jax.ShapeDtypeStruct((7,) + eta_shift.shape, jnp.float32),
            jax.ShapeDtypeStruct(after.shape, after.dtype),
        ),
        in_specs=[pl.BlockSpec(memory_space=pltpu.SMEM)] + [in_vmem] * 3,
        out_specs=(in_vmem, in_vmem),
        compiler_params=pltpu.CompilerParams(vmem_limit_bytes=16 * 1024 * 1024),
        cost_estimate=pl.CostEstimate(
            flops=40 * eta_shift.size, bytes_accessed=20_000_000, transcendentals=0
        ),
    )(base, after, eta_shift, cells)


def arrival(points_ref, k, lanes):
    here = [points_ref[n, k, :, lanes] > -1.0 for n in range(4, 7)]
    return tuple(points_ref[n, k, :, lanes] for n in range(4)), *here


def both_weights(shift_row, shift_lon, point):
    _, _, row_here, lon_here = point
    return (
        slot_weights(-shift_row, row_here, *bounds(row_here)),
        slot_weights(-shift_lon, lon_here, *bounds(lon_here)),
    )


def wind_levels(base, lanes, k, points, scratch, keep, filling, out_ref):
    def arrival_wind(field, step):
        middle = (HALO * 5 + HALO) * STACK + step * (5 * STACK) + FIELD_ROW[field]
        return scratch[pl.ds(base + middle, ROWS), :]

    weights = []
    for step, point in enumerate(points):
        east, north = arrival_wind(0, step), arrival_wind(1, step)
        keep[0, step, 16], keep[1, step, 16] = east, north
        weights.append(both_weights(COURANT * north, COURANT * east, point))
    row_weights, lon_weights = zip(*weights)
    found = [
        across(scratch, field, base, points, row_weights, lon_weights, filling, keep)
        for field in range(2)
    ]
    filling.finish_later()

    def tail(step, east_found, north_found):
        def finish():
            east, north = keep[0, step, 16], keep[1, step, 16]
            here = (east_found, north_found)
            for sweep in range(ITERS):
                shift_row = 0.5 * COURANT * (north + here[1])
                shift_lon = 0.5 * COURANT * (east + here[0])
                if sweep < ITERS - 1:
                    weights = both_weights(shift_row, shift_lon, points[step])
                    here = [across_kept(keep, field, step, *weights) for field in range(2)]
            out_ref[0, k + step, :, lanes] = shift_row
            out_ref[1, k + step, :, lanes] = shift_lon

        return finish

    filling.later += [tail(step, found[0][step], found[1][step]) for step in range(len(points))]


def tracer_levels(shift_ref, base, lanes, k, points, scratch, keep, filling, out_ref):
    weights = [
        both_weights(
            shift_ref[0, k + step, :, lanes], shift_ref[1, k + step, :, lanes], points[step]
        )
        for step in range(len(points))
    ]
    row_weights, lon_weights = zip(*weights)
    found = [
        across(scratch, field, base, points, row_weights, lon_weights, filling)
        for field in range(2)
    ]
    for field in range(2):
        for step, total in enumerate(found[field]):
            out_ref[field, k + step, :, lanes] = total.astype(out_ref.dtype)


def interpolation_kernel(
    levels_body, together, number, near_count, base_ref, field_ref, points_ref, *others
):
    nears, others = others[:near_count], others[near_count:]
    extra = ()
    if number == 1:
        shift_ref, out_ref, shift_out, around, even_scratch, odd_scratch, keep, sem = others
        extra = (shift_ref,)
        copy = pltpu.make_async_copy(shift_ref, shift_out, sem)
        copy.start()
    else:
        out_ref, around, even_scratch, odd_scratch, keep = others
    _, levels, rows, lon_total = points_ref.shape
    chunk_total = lon_total // LANES
    if near_count == 1:
        found = jnp.where(base_ref[0] == 0, HALO, 0)
        around[pl.ds(found, HALO)] = nears[0][number].astype(jnp.float32)
        around[pl.ds(HALO - found, HALO)] = jnp.zeros((HALO,) + around.shape[1:], jnp.float32)
    else:
        around[:HALO] = nears[0][number].astype(jnp.float32)
        around[HALO:] = nears[1][number].astype(jnp.float32)
    sources = [(around, n) for n in range(HALO)]
    sources += [(field_ref, n) for n in range(levels)]
    sources += [(around, HALO + n) for n in range(HALO)]

    def all_units(chunk, scratch):
        units = []
        for slab, source in enumerate(sources):
            units += fill_units(slab, chunk, chunk_total, source, scratch)
        return units

    for start, finish in all_units(0, even_scratch):
        finish(start())

    def one_chunk(chunk, scratch, other, later):
        lanes = pl.ds(pl.multiple_of(chunk * LANES, LANES), LANES)
        following = jnp.where(chunk == chunk_total - 1, 0, chunk + 1)
        filling = Interleave(all_units(following, other), 32 * (levels // together), later)
        for k in range(0, levels, together):
            points = [arrival(points_ref, k + n, lanes) for n in range(together)]
            base = k * (5 * STACK)
            keep_here = keep.at[k // together % 2]
            levels_body(*extra, base, lanes, k, points, scratch, keep_here, filling, out_ref)
        filling.flush()
        if levels // together % 2:
            filling.finish_later()

    def chunk_pair(pair, carry):
        later = []
        one_chunk(2 * pair, even_scratch, odd_scratch, later)
        one_chunk(2 * pair + 1, odd_scratch, even_scratch, later)
        for finish in later:
            finish()
        return carry

    lax.fori_loop(0, chunk_total // 2, chunk_pair, 0)
    if number == 1:
        copy.wait()


def interpolation_call(levels_body, base, number, fields, points, nears, extra, out_dtype):
    _, levels, rows, lon_total = points.shape
    count = levels * rows * lon_total
    together = next(n for n in (4, 2, 1) if levels % n == 0)
    scratch = pltpu.VMEM(((levels + 2 * HALO) * 5 * STACK, LANES), jnp.float32)
    in_vmem = pl.BlockSpec(memory_space=pltpu.VMEM)
    return pl.pallas_call(
        functools.partial(interpolation_kernel, levels_body, together, number, len(nears)),
        out_shape=(jax.ShapeDtypeStruct((2, levels, rows, lon_total), out_dtype),)
        + tuple(jax.ShapeDtypeStruct(x.shape, x.dtype) for x in extra),
        in_specs=[pl.BlockSpec(memory_space=pltpu.SMEM)]
        + [in_vmem] * (2 + len(nears) + len(extra)),
        out_specs=(in_vmem,) + (pl.BlockSpec(memory_space=pl.ANY),) * len(extra),
        scratch_shapes=[
            pltpu.VMEM((2 * HALO,) + fields.shape[1:], jnp.float32),
            scratch,
            scratch,
            pltpu.VMEM((2, 2, together, 17, ROWS, LANES), jnp.float32),
        ]
        + [pltpu.SemaphoreType.DMA] * len(extra),
        compiler_params=pltpu.CompilerParams(vmem_limit_bytes=16 * 1024 * 1024),
        cost_estimate=pl.CostEstimate(
            flops=count * 500, bytes_accessed=count * 40, transcendentals=0
        ),
    )(base, fields, points, *nears, *extra)


def swap_levels(send):
    if lax.axis_size("lev") == 2:
        return (lax.ppermute(send[0], "lev", [(0, 1), (1, 0)]),)
    up = [(i, i + 1) for i in range(lax.axis_size("lev") - 1)]
    down = [(j, i) for i, j in up]
    return lax.ppermute(send[1], "lev", up), lax.ppermute(send[0], "lev", down)


def up_to(value, step):
    return -(-value // step) * step


TALL = ROWS + 2 * HALO


def codes_kernel(numbers_ref, out_ref):
    out_ref[...] = numbers_ref[...]


def legendre_kernel(numbers_ref, codes_ref, spectra_ref, *others):
    table_count = (len(others) - 9) // 2
    sources, others = (spectra_ref,) + others[:table_count], others[table_count:]
    out_ref, done_ref, sums, table_tail, column_tail, staged = others[:6]
    targets, arrivals, departures = others[6:-2], others[-2], others[-1]
    spectra_here, tables = targets[0], targets[1:]
    _, pairs, level_fields, degrees = spectra_ref.shape
    group = table_tail.shape[0]
    bands, block, _ = out_ref.shape
    full = degrees // LANES * LANES
    at_top = numbers_ref[0] == 0
    step = pl.program_id(0)

    def copies(number):
        here = pl.ds(number * group, group)
        return [
            pltpu.make_async_copy(source.at[:, here], target.at[:, here], arrivals.at[n, number])
            for n, (source, target) in enumerate(zip(sources, targets))
        ]

    @pl.when(step == 0)
    def _():
        for copy in copies(0):
            copy.start()
        sums[...] = jnp.zeros(sums.shape, jnp.float32)
        done_ref[...] = jnp.zeros(done_ref.shape, jnp.float32)
        table_tail[...] = jnp.zeros(table_tail.shape, jnp.float32)
        column_tail[...] = jnp.zeros(column_tail.shape, jnp.float32)
        codes = codes_ref[...]
        code_row = up_to(pl.num_programs(0) * group * TALL, ROWS)
        for band in range(bands):
            first = band * block + code_row
            sums[pl.ds(first, 1), :] = jnp.right_shift(codes, 4).astype(jnp.float32)
            sums[pl.ds(first + 1, 1), :] = (codes & 15).astype(jnp.float32)

    @pl.when(step + 1 < pairs // group)
    def _():
        for copy in copies(step + 1):
            copy.start()

    for copy in copies(step):
        copy.wait()
    band_row = lax.broadcasted_iota(jnp.int32, (bands, 4 * level_fields), 0)
    count = 2 * level_fields
    nothing = jnp.zeros((bands, 2 * count), jnp.float32)
    for p in range(group):
        slot = step * group + p
        edge = degrees - 1 - numbers_ref[1 + slot]
        left = []
        for number, table_ref in enumerate(tables):
            for row in range(table_ref.shape[0]):
                piece = table_ref[row, slot]
                left.append(piece[:, :full])
                first = (number * table_ref.shape[0] + row) * bands
                table_tail[p, first : first + bands, : degrees - full] = piece[:, full:].astype(
                    jnp.float32
                )
        left = jnp.concatenate(left, axis=0)
        left = jnp.concatenate([left, table_tail[p].astype(jnp.bfloat16)], axis=1)
        halves = ([], [])
        for part in range(2):
            piece = spectra_here[part, slot]
            whole = piece[:, :full].astype(jnp.float32)
            lane = lax.broadcasted_iota(jnp.int32, whole.shape, 1)
            zero = jnp.zeros_like(whole)
            halves[0].append(jnp.where(lane < edge, whole, zero).astype(jnp.bfloat16))
            halves[1].append(jnp.where(lane < edge, zero, whole).astype(jnp.bfloat16))
            first = part * level_fields
            column_tail[p, first : first + level_fields, : degrees - full] = piece[
                :, full:
            ].astype(jnp.float32)
        tail = column_tail[p].astype(jnp.bfloat16)
        right = jnp.concatenate(
            [
                jnp.concatenate([jnp.concatenate(halves[0], axis=0), jnp.zeros_like(tail)], axis=1),
                jnp.concatenate([jnp.concatenate(halves[1], axis=0), tail], axis=1),
            ],
            axis=0,
        )
        found = lax.dot_general(
            left, right, (((1,), (1,)), ((), ())), preferred_element_type=jnp.float32
        )
        found = [found[i * bands : (i + 1) * bands] for i in range(ROWS)]
        if len(tables) == 2:
            low, high = found[: ROWS // 2], found[ROWS // 2 :]
            found = [jnp.where(at_top, x, y) for x, y in zip(low, high)]
            found += [jnp.where(at_top, y, x) for x, y in zip(low, high)]
        above = [
            jnp.where(band_row == 0, nothing, pltpu.roll(x, 1, 0)) for x in found[ROWS - HALO :]
        ]
        below = [
            jnp.where(band_row == bands - 1, nothing, pltpu.roll(x, bands - 1, 0))
            for x in found[:HALO]
        ]
        rows = above + found + below
        for i, value in enumerate(rows):
            place = pl.ds(slot * TALL + i, bands, stride=block)
            sums[place, : 2 * count] = value

    @pl.when(step == pl.num_programs(0) - 1)
    def _():
        leaving = []
        for band in range(bands):
            staged[band] = sums[band * block : (band + 1) * block, :].astype(jnp.bfloat16)
            leaving.append(
                pltpu.make_async_copy(staged.at[band], out_ref.at[band], departures.at[band])
            )
            leaving[-1].start()
        for copy in leaving:
            copy.wait()


def block_rows(pairs):
    return up_to(up_to(pairs * TALL, ROWS) + 2, 16)


def legendre_call(pairing, spectra, tables):
    _, pairs, level_fields, degrees = spectra.shape
    bands = tables[0].shape[2]
    block = block_rows(pairs)
    group = next(n for n in (4, 5, 2, 1) if pairs % n == 0)
    numbers = jnp.concatenate([lax.axis_index("lev").astype(jnp.int32)[None], pairing])
    codes = pl.pallas_call(
        codes_kernel,
        out_shape=jax.ShapeDtypeStruct((1, LANES), jnp.int32),
        in_specs=[pl.BlockSpec(memory_space=pltpu.VMEM)],
        out_specs=pl.BlockSpec(memory_space=pltpu.VMEM),
        compiler_params=pltpu.CompilerParams(vmem_limit_bytes=60 * 1024 * 1024),
        cost_estimate=pl.CostEstimate(flops=0, bytes_accessed=4_000_000, transcendentals=0),
    )(jnp.pad(pairing, (0, LANES - pairs))[None, :])
    shape = jax.ShapeDtypeStruct((bands, block, LANES), jnp.bfloat16)
    in_vmem = pl.BlockSpec(memory_space=pltpu.VMEM)
    in_hbm = pl.BlockSpec(memory_space=pl.ANY)
    return pl.pallas_call(
        legendre_kernel,
        grid=(pairs // group,),
        out_shape=(shape, jax.ShapeDtypeStruct((ROWS, LANES), jnp.float32)),
        in_specs=[
            pl.BlockSpec(memory_space=pltpu.SMEM),
            pl.BlockSpec((1, LANES), lambda i: (0, 0)),
            in_hbm,
        ]
        + [in_hbm] * len(tables),
        out_specs=(in_hbm, in_vmem),
        scratch_shapes=[
            pltpu.VMEM((bands * block, LANES), jnp.float32),
            pltpu.VMEM((group, ROWS * bands, LANES), jnp.float32),
            pltpu.VMEM((group, 2 * level_fields, LANES), jnp.float32),
            pltpu.VMEM(shape.shape, shape.dtype),
        ]
        + [pltpu.VMEM(x.shape, x.dtype) for x in (spectra,) + tables]
        + [pltpu.SemaphoreType.DMA((1 + len(tables), pairs // group))]
        + [pltpu.SemaphoreType.DMA((bands,))],
        compiler_params=pltpu.CompilerParams(vmem_limit_bytes=60 * 1024 * 1024),
        cost_estimate=pl.CostEstimate(
            flops=2 * ROWS * bands * 4 * level_fields * pairs * degrees,
            bytes_accessed=8_000_000,
            transcendentals=0,
        ),
    )(numbers, codes, spectra, *tables)


def fourier_table(pair_total, padded, lon_total):
    order_total = 2 * pair_total
    half = pair_total // 2
    low = 2 * np.arange(half)
    high = low + 1
    even = np.concatenate([low, order_total - 1 - high])
    odd = np.concatenate([order_total - 1 - low, high])
    lon = np.arange(lon_total // 2)
    table = np.zeros((4, 2, padded, lon_total // 2), np.float32)
    for parity, orders in enumerate((even, odd)):
        phase = (orders[:, None] * lon[None, :]) % lon_total * (2.0 * math.pi / lon_total)
        weight = np.where(orders == 0, 1.0, 2.0)[:, None]
        table[parity, 0, :pair_total] = weight * np.cos(phase)
        table[parity, 1, :pair_total] = -weight * np.sin(phase)
    return table.reshape(4, 2 * padded, lon_total // 2).astype(jnp.bfloat16)


def owner_tables(bands, pairs):
    room = up_to(pairs, ROWS)
    slots = np.arange(up_to(bands * room, LANES))
    owner = slots[:, None] // room == np.arange(LANES)[None, :]
    lane = slots[:, None] % room == np.arange(LANES)[None, :]
    return owner.astype(jnp.bfloat16), lane.astype(np.float32)


def pair_places(flat, owner_ref, lane_ref, codes, bands, block, code_row, pair_total, padded):
    codes[...] = jnp.zeros(codes.shape, jnp.float32)
    numbers = []
    for part in range(2):
        codes[part, :bands, :] = flat[pl.ds(code_row + part, bands, stride=block), :]
        numbers.append(
            jnp.dot(
                owner_ref[...],
                codes[part].astype(jnp.bfloat16),
                preferred_element_type=jnp.float32,
            )
        )
    pair_id = jnp.sum(
        (16.0 * numbers[0] + numbers[1]) * lane_ref[...], axis=1, keepdims=True
    ).astype(jnp.int32)
    place = jnp.right_shift(pair_id, 1) + (pair_id & 1) * (pair_total // 2)
    columns = lax.broadcasted_iota(jnp.int32, (owner_ref.shape[0], padded), 1)
    return jnp.where(columns == place, 1.0, 0.0).astype(jnp.bfloat16)


def fourier_kernel(
    pairs, levels, base_ref, after_ref, sums_ref, owner_ref, lane_ref, table_source, *others
):
    field_refs, send_ref, others = others[:2], others[2], others[3:]
    codes, flat, gathered, lhs, table_ref, arrival_sem = others
    copy = pltpu.make_async_copy(table_source.at[:2], table_ref, arrival_sem)
    copy.start()
    bands, block, width = sums_ref.shape
    pair_total = bands * pairs
    padded = up_to(pair_total, LANES)
    blocks = padded // LANES
    fields = 4 * levels
    room = up_to(pairs, ROWS)
    flat[...] = sums_ref[...].astype(jnp.float32).reshape(bands * block, width)
    gathered[...] = jnp.zeros(gathered.shape, jnp.float32)
    code_row = up_to(pairs * TALL, ROWS)
    place = pair_places(
        flat, owner_ref, lane_ref, codes, bands, block, code_row, pair_total, padded
    )
    low = lax.broadcasted_iota(jnp.int32, (fields, padded), 1) < pair_total // 2
    middle = fields * ROWS
    for row in range(TALL):
        here = gathered.at[row % 2]
        for band in range(bands):
            here[band * room : band * room + pairs, :] = flat[
                pl.ds(band * block + row, pairs, stride=TALL), :
            ]
        ordered = jnp.dot(
            here[...].T.astype(jnp.bfloat16), place, preferred_element_type=jnp.float32
        )
        if HALO <= row < HALO + ROWS:
            first, stride = row - HALO, ROWS
        else:
            first, stride = middle + (row - HALO - ROWS) % TALL, 2 * HALO
        for part in range(2):
            start = part * fields
            straight = ordered[start : start + fields]
            start = start + 2 * fields
            crossed = ordered[start : start + fields]
            both = (jnp.where(low, straight, crossed), jnp.where(low, crossed, straight))
            for parity in range(2):
                for t in range(blocks):
                    lhs[parity, part * blocks + t, pl.ds(first, fields, stride=stride), :] = both[
                        parity
                    ][:, t * LANES : (t + 1) * LANES]
    copy.wait()
    half = table_ref.shape[2]

    def transform(first, count):
        found = []
        for parity in range(2):
            left = jnp.concatenate(
                [
                    lhs[parity, t, first : first + count, :].astype(jnp.bfloat16)
                    for t in range(2 * blocks)
                ],
                axis=1,
            )
            found.append(jnp.dot(left, table_ref[parity], preferred_element_type=jnp.float32))
        pieces = (found[0] + found[1], found[0] - found[1])
        return [piece.astype(jnp.bfloat16).astype(jnp.float32) for piece in pieces]

    group = next(n for n in (4, 2, 1) if levels % n == 0)
    for level in range(0, levels, group):
        for part, value in enumerate(transform(level * 4 * ROWS, group * 4 * ROWS)):
            value = value.reshape(group, 4 * ROWS, half)
            lanes = slice(part * half, (part + 1) * half)
            for number, field_ref in enumerate(field_refs):
                field_ref[level : level + group, : 2 * ROWS, lanes] = value[
                    :, 2 * ROWS * number : 2 * ROWS * (number + 1)
                ]
    for part, value in enumerate(transform(middle, fields * 2 * HALO)):
        value = value.reshape(levels, 8 * HALO, half)
        lanes = slice(part * half, (part + 1) * half)
        for number, field_ref in enumerate(field_refs):
            field_ref[:, 2 * ROWS :, lanes] = value[:, 4 * HALO * number : 4 * HALO * (number + 1)]
    for number, field_ref in enumerate(field_refs):
        if send_ref.shape[0] == 1:
            start = jnp.where(base_ref[0] == 0, levels - HALO, 0)
            send_ref[0, number] = field_ref[pl.ds(start, HALO)].astype(jnp.bfloat16)
        else:
            send_ref[0, number] = field_ref[:HALO].astype(jnp.bfloat16)
            send_ref[1, number] = field_ref[levels - HALO :].astype(jnp.bfloat16)


def fourier_call(base, after, sums, table, pairs, levels, lon_total):
    bands, block, width = sums.shape
    padded = up_to(bands * pairs, LANES)
    extra = [jnp.asarray(x) for x in owner_tables(bands, pairs)]
    sends = 1 if lax.axis_size("lev") == 2 else 2
    field_shape = (levels, 3 * ROWS, lon_total)
    field = jax.ShapeDtypeStruct(field_shape, jnp.float32)
    send = jax.ShapeDtypeStruct((sends, 2, HALO) + field_shape[1:], jnp.bfloat16)
    in_vmem = pl.BlockSpec(memory_space=pltpu.VMEM)
    return pl.pallas_call(
        functools.partial(fourier_kernel, pairs, levels),
        out_shape=(field, field, send),
        in_specs=[pl.BlockSpec(memory_space=pltpu.SMEM)]
        + [in_vmem] * 4
        + [pl.BlockSpec(memory_space=pl.ANY)],
        out_specs=(in_vmem,) * 3,
        scratch_shapes=[
            pltpu.VMEM((2, LANES, LANES), jnp.float32),
            pltpu.VMEM((bands * block, width), jnp.float32),
            pltpu.VMEM((2, extra[0].shape[0], width), jnp.float32),
            pltpu.VMEM((2, 2 * padded // LANES, 4 * levels * TALL, LANES), jnp.float32),
            pltpu.VMEM((2,) + table.shape[1:], table.dtype),
            pltpu.SemaphoreType.DMA,
        ],
        compiler_params=pltpu.CompilerParams(vmem_limit_bytes=44 * 1024 * 1024),
        cost_estimate=pl.CostEstimate(
            flops=8_000_000_000, bytes_accessed=8_000_000, transcendentals=0
        ),
    )(base, after, sums, *extra, table)


def exchange(sums):
    return lax.all_to_all(sums, "band", split_axis=0, concat_axis=0, tiled=True)


def per_device(spectra, legendre, pairing, eta_shift, cells):
    levels, rows, lon_total = eta_shift.shape
    pairs = pairing.shape[0]
    spectra = jnp.transpose(spectra, (0, 2, 1, 3))
    table = jnp.transpose(legendre, (0, 2, 1, 3))
    if lax.axis_size("lev") == 2:
        tables = (table, lax.ppermute(table, "lev", [(0, 1), (1, 0)]))
    else:
        tables = (lax.all_gather(table, "lev", axis=0, tiled=True),)
    base = jnp.stack([lax.axis_index("lev") * levels, lax.axis_index("band") * rows])
    base = base.astype(jnp.int32)
    sums, done = legendre_call(pairing, spectra, tables)
    sums = exchange(sums)
    points, done = prepare_call(base, done, eta_shift, cells)
    pair_total = pairs * lax.axis_size("band")
    twiddles = jnp.asarray(fourier_table(pair_total, up_to(pair_total, LANES), lon_total))
    winds, tracers, send = fourier_call(base, done, sums, twiddles, pairs, levels, lon_total)
    nears = swap_levels(send)
    (moved,) = interpolation_call(
        wind_levels, base, 0, winds, points, nears, (), jnp.float32
    )
    advected, displacement = interpolation_call(
        tracer_levels, base, 1, tracers, points, nears, (moved,), jnp.bfloat16
    )
    return advected, displacement


def solution(mesh):
    return jax.shard_map(
        per_device,
        mesh=mesh,
        in_specs=(
            P(None, "lev", "band", None),
            P("lev", None, "band", None),
            P("band"),
            P("lev", "band", None),
            P(None, "lev", "band", None),
        ),
        out_specs=(P(None, "lev", "band", None), P(None, "lev", "band", None)),
        check_vma=False,
    )
```

```python
import functools
import math

import jax
import jax.numpy as jnp
import numpy as np
from jax import lax
from jax.experimental import pallas as pl
from jax.experimental.pallas import tpu as pltpu
from jax.sharding import PartitionSpec as P

ITERS = 2


COURANT = 0.8
HALO = 2
LANES = 128
ROWS = 8
SLOTS = (-1, 0, 1, 2)


def slot_weights(place, here, low, high, sixth):
    z = jnp.minimum(jnp.maximum(place, low), high)
    square = z * z
    less = square - 1.0
    outer = less * z * sixth
    triple = 3.0 * outer
    half = 0.5 * z
    half_square = 0.5 * square
    return (
        half_square - half - jnp.where(here, outer, triple),
        triple - less,
        half_square + half - jnp.where(here, triple, outer),
        outer,
    )


def bounds(here):
    return (
        jnp.where(here, -0.5, -1.5),
        jnp.where(here, 1.5, 0.5),
        jnp.where(here, 1.0 / 6.0, -1.0 / 6.0),
    )


def weighted(weights, values):
    return (weights[0] * values[0] + weights[1] * values[1]) + (
        weights[2] * values[2] + weights[3] * values[3]
    )


def shifted_lanes(before, here, after, lane):
    return (
        pltpu.roll(jnp.where(lane < LANES - 2, here, before), 2, 1),
        pltpu.roll(jnp.where(lane < LANES - 1, here, before), 1, 1),
        here,
        pltpu.roll(jnp.where(lane < 1, after, here), LANES - 1, 1),
        pltpu.roll(jnp.where(lane < 2, after, here), LANES - 2, 1),
    )


STACK = 5 * ROWS
FIELD_ROW = (ROWS, 3 * ROWS)


def fill_units(slab, chunk, chunk_total, source, scratch):
    field_ref, row = source
    before = jnp.where(chunk == 0, chunk_total - 1, chunk - 1)
    after = jnp.where(chunk == chunk_total - 1, 0, chunk + 1)
    starts = [pl.multiple_of(c * LANES, LANES) for c in (before, chunk, after)]
    lane = lax.broadcasted_iota(jnp.int32, (ROWS, LANES), 1)
    first = slab * (5 * STACK)

    def edge_start():
        moved = shifted_lanes(
            *[field_ref[row, 2 * ROWS : 3 * ROWS, pl.ds(s, LANES)] for s in starts], lane
        )
        return [(value, pltpu.roll(value, ROWS // 2, 0)) for value in moved]

    def edge_finish(values):
        for step, (between, outside) in enumerate(values):
            for offset, value in ((0, outside), (2 * ROWS, between), (4 * ROWS, outside)):
                scratch[pl.ds(first + step * STACK + offset, ROWS), :] = value

    def center_unit(field):
        def start():
            rows = slice(field * ROWS, (field + 1) * ROWS)
            blocks = [field_ref[row, rows, pl.ds(s, LANES)] for s in starts]
            return shifted_lanes(*blocks, lane)

        def finish(values):
            for step, moved in enumerate(values):
                scratch[pl.ds(first + step * STACK + FIELD_ROW[field], ROWS), :] = moved

        return start, finish

    return [(edge_start, edge_finish)] + [center_unit(field) for field in range(2)]


class Interleave:
    def __init__(self, units, ticks, later):
        self.units = list(units)
        self.every = max(1, ticks // max(1, len(self.units)))
        self.count = 0
        self.pending = None
        self.later = later

    def advance(self):
        if self.pending is not None:
            self.pending[0](self.pending[1])
            self.pending = None
        if self.units:
            start, finish = self.units.pop(0)
            self.pending = (finish, start())

    def tick(self):
        if self.count % self.every == 0:
            self.advance()
        self.count += 1
        if self.later and self.count % 3 == 0:
            self.later.pop(0)()

    def flush(self):
        while self.units or self.pending is not None:
            self.advance()

    def finish_later(self):
        while self.later:
            self.later.pop(0)()


def level_sums(scratch, field, base, slot, points):
    loaded = {}

    def load(a, b, c):
        offset = ((a + HALO) * 5 + c + HALO) * STACK + FIELD_ROW[field] + b
        if (a, b, c) not in loaded:
            loaded[a, b, c] = scratch[pl.ds(base + offset, ROWS), :]
        return loaded[a, b, c]

    def one(step, weights, level_here, row_here, lon_here):
        def pick_lon(a, b):
            if slot[1] == 2:
                return jnp.where(lon_here, load(a + step, b, 2), load(a + step, b, -2))
            return load(a + step, b, slot[1])

        def pick(a):
            if slot[0] == 2:
                return jnp.where(row_here, pick_lon(a, 2), pick_lon(a, -2))
            return pick_lon(a, slot[0])

        total = weights[0] * pick(-1) + weights[1] * pick(0)
        total = total + weights[2] * pick(1)
        return total + weights[3] * jnp.where(level_here, pick(2), pick(-2))

    return [one(step, *point) for step, point in enumerate(points)]


def across(scratch, field, base, points, row_weights, lon_weights, filling, keep=None):
    columns = [[None] * 4 for _ in points]
    for b, row_slot in enumerate(SLOTS):
        for c, lon_slot in enumerate(SLOTS):
            filling.tick()
            found = level_sums(scratch, field, base, (row_slot, lon_slot), points)
            for step, value in enumerate(found):
                if keep is not None:
                    keep[field, step, 4 * b + c] = value
                term = row_weights[step][b] * value
                columns[step][c] = term if b == 0 else columns[step][c] + term
    return [weighted(weights, column) for weights, column in zip(lon_weights, columns)]


def across_kept(keep, field, step, row_weights, lon_weights):
    return weighted(
        lon_weights,
        [
            weighted(row_weights, [keep[field, step, 4 * b + c] for b in range(4)])
            for c in range(4)
        ],
    )


def prepare_kernel(base_ref, after_ref, eta_ref, cells_ref, points_ref, done_ref):
    done_ref[...] = after_ref[...]
    levels, rows, lon_total = eta_ref.shape
    shape = (rows, LANES)
    row_here = base_ref[1] + lax.broadcasted_iota(jnp.int32, shape, 0)
    lane = lax.broadcasted_iota(jnp.int32, shape, 1)

    def chunk_step(chunk, carry):
        lanes = pl.ds(pl.multiple_of(chunk * LANES, LANES), LANES)
        for k in range(levels):
            level_here = cells_ref[2, k, :, lanes] == base_ref[0] + k
            weights = slot_weights(
                -eta_ref[k, :, lanes].astype(jnp.float32), level_here, *bounds(level_here)
            )
            here = (
                level_here,
                cells_ref[0, k, :, lanes] == row_here,
                cells_ref[1, k, :, lanes] == chunk * LANES + lane,
            )
            for n, value in enumerate(weights + tuple(bounds(x)[0] for x in here)):
                points_ref[n, k, :, lanes] = value
        return carry

    lax.fori_loop(0, lon_total // LANES, chunk_step, 0)


def prepare_call(base, after, eta_shift, cells):
    in_vmem = pl.BlockSpec(memory_space=pltpu.VMEM)
    return pl.pallas_call(
        prepare_kernel,
        out_shape=(
            jax.ShapeDtypeStruct((7,) + eta_shift.shape, jnp.float32),
            jax.ShapeDtypeStruct(after.shape, after.dtype),
        ),
        in_specs=[pl.BlockSpec(memory_space=pltpu.SMEM)] + [in_vmem] * 3,
        out_specs=(in_vmem, in_vmem),
        compiler_params=pltpu.CompilerParams(vmem_limit_bytes=16 * 1024 * 1024),
        cost_estimate=pl.CostEstimate(
            flops=40 * eta_shift.size, bytes_accessed=20_000_000, transcendentals=0
        ),
    )(base, after, eta_shift, cells)


def arrival(points_ref, k, lanes):
    here = [points_ref[n, k, :, lanes] > -1.0 for n in range(4, 7)]
    return tuple(points_ref[n, k, :, lanes] for n in range(4)), *here


def both_weights(shift_row, shift_lon, point):
    _, _, row_here, lon_here = point
    return (
        slot_weights(-shift_row, row_here, *bounds(row_here)),
        slot_weights(-shift_lon, lon_here, *bounds(lon_here)),
    )


def wind_levels(base, lanes, k, points, scratch, keep, filling, out_ref):
    def arrival_wind(field, step):
        middle = (HALO * 5 + HALO) * STACK + step * (5 * STACK) + FIELD_ROW[field]
        return scratch[pl.ds(base + middle, ROWS), :]

    weights = []
    for step, point in enumerate(points):
        east, north = arrival_wind(0, step), arrival_wind(1, step)
        keep[0, step, 16], keep[1, step, 16] = east, north
        weights.append(both_weights(COURANT * north, COURANT * east, point))
    row_weights, lon_weights = zip(*weights)
    found = [
        across(scratch, field, base, points, row_weights, lon_weights, filling, keep)
        for field in range(2)
    ]
    filling.finish_later()

    def tail(step, east_found, north_found):
        def finish():
            east, north = keep[0, step, 16], keep[1, step, 16]
            here = (east_found, north_found)
            for sweep in range(ITERS):
                shift_row = 0.5 * COURANT * (north + here[1])
                shift_lon = 0.5 * COURANT * (east + here[0])
                if sweep < ITERS - 1:
                    weights = both_weights(shift_row, shift_lon, points[step])
                    here = [across_kept(keep, field, step, *weights) for field in range(2)]
            out_ref[0, k + step, :, lanes] = shift_row
            out_ref[1, k + step, :, lanes] = shift_lon

        return finish

    filling.later += [tail(step, found[0][step], found[1][step]) for step in range(len(points))]


def tracer_levels(shift_ref, base, lanes, k, points, scratch, keep, filling, out_ref):
    weights = [
        both_weights(
            shift_ref[0, k + step, :, lanes], shift_ref[1, k + step, :, lanes], points[step]
        )
        for step in range(len(points))
    ]
    row_weights, lon_weights = zip(*weights)
    found = [
        across(scratch, field, base, points, row_weights, lon_weights, filling)
        for field in range(2)
    ]
    for field in range(2):
        for step, total in enumerate(found[field]):
            out_ref[field, k + step, :, lanes] = total.astype(out_ref.dtype)


def interpolation_kernel(
    levels_body, together, number, near_count, base_ref, field_ref, points_ref, *others
):
    nears, others = others[:near_count], others[near_count:]
    extra = ()
    if number == 1:
        shift_ref, out_ref, shift_out, around, even_scratch, odd_scratch, keep, sem = others
        extra = (shift_ref,)
        copy = pltpu.make_async_copy(shift_ref, shift_out, sem)
        copy.start()
    else:
        out_ref, around, even_scratch, odd_scratch, keep = others
    _, levels, rows, lon_total = points_ref.shape
    chunk_total = lon_total // LANES
    if near_count == 1:
        found = jnp.where(base_ref[0] == 0, HALO, 0)
        around[pl.ds(found, HALO)] = nears[0][number].astype(jnp.float32)
        around[pl.ds(HALO - found, HALO)] = jnp.zeros((HALO,) + around.shape[1:], jnp.float32)
    else:
        around[:HALO] = nears[0][number].astype(jnp.float32)
        around[HALO:] = nears[1][number].astype(jnp.float32)
    sources = [(around, n) for n in range(HALO)]
    sources += [(field_ref, n) for n in range(levels)]
    sources += [(around, HALO + n) for n in range(HALO)]

    def all_units(chunk, scratch):
        units = []
        for slab, source in enumerate(sources):
            units += fill_units(slab, chunk, chunk_total, source, scratch)
        return units

    for start, finish in all_units(0, even_scratch):
        finish(start())

    def one_chunk(chunk, scratch, other, later):
        lanes = pl.ds(pl.multiple_of(chunk * LANES, LANES), LANES)
        following = jnp.where(chunk == chunk_total - 1, 0, chunk + 1)
        filling = Interleave(all_units(following, other), 32 * (levels // together), later)
        for k in range(0, levels, together):
            points = [arrival(points_ref, k + n, lanes) for n in range(together)]
            base = k * (5 * STACK)
            keep_here = keep.at[k // together % 2]
            levels_body(*extra, base, lanes, k, points, scratch, keep_here, filling, out_ref)
        filling.flush()
        if levels // together % 2:
            filling.finish_later()

    def chunk_pair(pair, carry):
        later = []
        one_chunk(2 * pair, even_scratch, odd_scratch, later)
        one_chunk(2 * pair + 1, odd_scratch, even_scratch, later)
        for finish in later:
            finish()
        return carry

    lax.fori_loop(0, chunk_total // 2, chunk_pair, 0)
    if number == 1:
        copy.wait()


def interpolation_call(levels_body, base, number, fields, points, nears, extra, out_dtype):
    _, levels, rows, lon_total = points.shape
    count = levels * rows * lon_total
    together = 2 if levels % 2 == 0 else 1
    scratch = pltpu.VMEM(((levels + 2 * HALO) * 5 * STACK, LANES), jnp.float32)
    in_vmem = pl.BlockSpec(memory_space=pltpu.VMEM)
    return pl.pallas_call(
        functools.partial(interpolation_kernel, levels_body, together, number, len(nears)),
        out_shape=(jax.ShapeDtypeStruct((2, levels, rows, lon_total), out_dtype),)
        + tuple(jax.ShapeDtypeStruct(x.shape, x.dtype) for x in extra),
        in_specs=[pl.BlockSpec(memory_space=pltpu.SMEM)]
        + [in_vmem] * (2 + len(nears) + len(extra)),
        out_specs=(in_vmem,) + (pl.BlockSpec(memory_space=pl.ANY),) * len(extra),
        scratch_shapes=[
            pltpu.VMEM((2 * HALO,) + fields.shape[1:], jnp.float32),
            scratch,
            scratch,
            pltpu.VMEM((2, 2, together, 17, ROWS, LANES), jnp.float32),
        ]
        + [pltpu.SemaphoreType.DMA] * len(extra),
        compiler_params=pltpu.CompilerParams(vmem_limit_bytes=16 * 1024 * 1024),
        cost_estimate=pl.CostEstimate(
            flops=count * 500, bytes_accessed=count * 40, transcendentals=0
        ),
    )(base, fields, points, *nears, *extra)


def swap_levels(send):
    if lax.axis_size("lev") == 2:
        return (lax.ppermute(send[0], "lev", [(0, 1), (1, 0)]),)
    up = [(i, i + 1) for i in range(lax.axis_size("lev") - 1)]
    down = [(j, i) for i, j in up]
    return lax.ppermute(send[1], "lev", up), lax.ppermute(send[0], "lev", down)


def up_to(value, step):
    return -(-value // step) * step


TALL = ROWS + 2 * HALO


def codes_kernel(numbers_ref, out_ref):
    out_ref[...] = numbers_ref[...]


def legendre_kernel(numbers_ref, codes_ref, spectra_ref, *others):
    table_count = (len(others) - 7) // 2
    sources, others = (spectra_ref,) + others[:table_count], others[table_count:]
    out_ref, done_ref, sums, table_tail, column_tail = others[:5]
    targets, arrivals = others[5:-1], others[-1]
    spectra_here, tables = targets[0], targets[1:]
    _, pairs, level_fields, degrees = spectra_ref.shape
    group = table_tail.shape[0]
    bands, block, _ = out_ref.shape
    full = degrees // LANES * LANES
    at_top = numbers_ref[0] == 0
    step = pl.program_id(0)

    def copies(number):
        here = pl.ds(number * group, group)
        return [
            pltpu.make_async_copy(source.at[:, here], target.at[:, here], arrivals.at[n, number])
            for n, (source, target) in enumerate(zip(sources, targets))
        ]

    @pl.when(step == 0)
    def _():
        for copy in copies(0):
            copy.start()
        sums[...] = jnp.zeros(sums.shape, jnp.float32)
        done_ref[...] = jnp.zeros(done_ref.shape, jnp.float32)
        table_tail[...] = jnp.zeros(table_tail.shape, jnp.float32)
        column_tail[...] = jnp.zeros(column_tail.shape, jnp.float32)
        codes = codes_ref[...]
        code_row = up_to(pl.num_programs(0) * group * TALL, ROWS)
        for band in range(bands):
            first = band * block + code_row
            sums[pl.ds(first, 1), :] = jnp.right_shift(codes, 4).astype(jnp.float32)
            sums[pl.ds(first + 1, 1), :] = (codes & 15).astype(jnp.float32)

    @pl.when(step + 1 < pairs // group)
    def _():
        for copy in copies(step + 1):
            copy.start()

    for copy in copies(step):
        copy.wait()
    band_row = lax.broadcasted_iota(jnp.int32, (bands, 4 * level_fields), 0)
    count = 2 * level_fields
    nothing = jnp.zeros((bands, 2 * count), jnp.float32)
    for p in range(group):
        slot = step * group + p
        edge = degrees - 1 - numbers_ref[1 + slot]
        left = []
        for number, table_ref in enumerate(tables):
            for row in range(table_ref.shape[0]):
                piece = table_ref[row, slot]
                left.append(piece[:, :full])
                first = (number * table_ref.shape[0] + row) * bands
                table_tail[p, first : first + bands, : degrees - full] = piece[:, full:].astype(
                    jnp.float32
                )
        left = jnp.concatenate(left, axis=0)
        left = jnp.concatenate([left, table_tail[p].astype(jnp.bfloat16)], axis=1)
        halves = ([], [])
        for part in range(2):
            piece = spectra_here[part, slot]
            whole = piece[:, :full].astype(jnp.float32)
            lane = lax.broadcasted_iota(jnp.int32, whole.shape, 1)
            zero = jnp.zeros_like(whole)
            halves[0].append(jnp.where(lane < edge, whole, zero).astype(jnp.bfloat16))
            halves[1].append(jnp.where(lane < edge, zero, whole).astype(jnp.bfloat16))
            first = part * level_fields
            column_tail[p, first : first + level_fields, : degrees - full] = piece[
                :, full:
            ].astype(jnp.float32)
        tail = column_tail[p].astype(jnp.bfloat16)
        right = jnp.concatenate(
            [
                jnp.concatenate([jnp.concatenate(halves[0], axis=0), jnp.zeros_like(tail)], axis=1),
                jnp.concatenate([jnp.concatenate(halves[1], axis=0), tail], axis=1),
            ],
            axis=0,
        )
        found = lax.dot_general(
            left, right, (((1,), (1,)), ((), ())), preferred_element_type=jnp.float32
        )
        found = [found[i * bands : (i + 1) * bands] for i in range(ROWS)]
        if len(tables) == 2:
            low, high = found[: ROWS // 2], found[ROWS // 2 :]
            found = [jnp.where(at_top, x, y) for x, y in zip(low, high)]
            found += [jnp.where(at_top, y, x) for x, y in zip(low, high)]
        above = [
            jnp.where(band_row == 0, nothing, pltpu.roll(x, 1, 0)) for x in found[ROWS - HALO :]
        ]
        below = [
            jnp.where(band_row == bands - 1, nothing, pltpu.roll(x, bands - 1, 0))
            for x in found[:HALO]
        ]
        rows = above + found + below
        for i, value in enumerate(rows):
            place = pl.ds(slot * TALL + i, bands, stride=block)
            sums[place, : 2 * count] = value

    @pl.when(step == pl.num_programs(0) - 1)
    def _():
        out_ref[...] = sums[...].astype(jnp.bfloat16).reshape(out_ref.shape)


def block_rows(pairs):
    return up_to(up_to(pairs * TALL, ROWS) + 2, 16)


def legendre_call(pairing, spectra, tables):
    _, pairs, level_fields, degrees = spectra.shape
    bands = tables[0].shape[2]
    block = block_rows(pairs)
    group = next(n for n in (4, 5, 2, 1) if pairs % n == 0)
    numbers = jnp.concatenate([lax.axis_index("lev").astype(jnp.int32)[None], pairing])
    codes = pl.pallas_call(
        codes_kernel,
        out_shape=jax.ShapeDtypeStruct((1, LANES), jnp.int32),
        in_specs=[pl.BlockSpec(memory_space=pltpu.VMEM)],
        out_specs=pl.BlockSpec(memory_space=pltpu.VMEM),
        compiler_params=pltpu.CompilerParams(vmem_limit_bytes=60 * 1024 * 1024),
        cost_estimate=pl.CostEstimate(flops=0, bytes_accessed=4_000_000, transcendentals=0),
    )(jnp.pad(pairing, (0, LANES - pairs))[None, :])
    shape = jax.ShapeDtypeStruct((bands, block, LANES), jnp.bfloat16)
    in_vmem = pl.BlockSpec(memory_space=pltpu.VMEM)
    in_hbm = pl.BlockSpec(memory_space=pl.ANY)
    return pl.pallas_call(
        legendre_kernel,
        grid=(pairs // group,),
        out_shape=(shape, jax.ShapeDtypeStruct((ROWS, LANES), jnp.float32)),
        in_specs=[
            pl.BlockSpec(memory_space=pltpu.SMEM),
            pl.BlockSpec((1, LANES), lambda i: (0, 0)),
            in_hbm,
        ]
        + [in_hbm] * len(tables),
        out_specs=(in_vmem, in_vmem),
        scratch_shapes=[
            pltpu.VMEM((bands * block, LANES), jnp.float32),
            pltpu.VMEM((group, ROWS * bands, LANES), jnp.float32),
            pltpu.VMEM((group, 2 * level_fields, LANES), jnp.float32),
        ]
        + [pltpu.VMEM(x.shape, x.dtype) for x in (spectra,) + tables]
        + [pltpu.SemaphoreType.DMA((1 + len(tables), pairs // group))],
        compiler_params=pltpu.CompilerParams(vmem_limit_bytes=60 * 1024 * 1024),
        cost_estimate=pl.CostEstimate(
            flops=2 * ROWS * bands * 4 * level_fields * pairs * degrees,
            bytes_accessed=8_000_000,
            transcendentals=0,
        ),
    )(numbers, codes, spectra, *tables)


def fourier_table(pair_total, padded, lon_total):
    order_total = 2 * pair_total
    half = pair_total // 2
    low = 2 * np.arange(half)
    high = low + 1
    even = np.concatenate([low, order_total - 1 - high])
    odd = np.concatenate([order_total - 1 - low, high])
    lon = np.arange(lon_total // 2)
    table = np.zeros((4, 2, padded, lon_total // 2), np.float32)
    for parity, orders in enumerate((even, odd)):
        phase = (orders[:, None] * lon[None, :]) % lon_total * (2.0 * math.pi / lon_total)
        weight = np.where(orders == 0, 1.0, 2.0)[:, None]
        table[parity, 0, :pair_total] = weight * np.cos(phase)
        table[parity, 1, :pair_total] = -weight * np.sin(phase)
    return table.reshape(4, 2 * padded, lon_total // 2).astype(jnp.bfloat16)


def owner_tables(bands, pairs):
    room = up_to(pairs, ROWS)
    slots = np.arange(up_to(bands * room, LANES))
    owner = slots[:, None] // room == np.arange(LANES)[None, :]
    lane = slots[:, None] % room == np.arange(LANES)[None, :]
    return owner.astype(jnp.bfloat16), lane.astype(np.float32)


def pair_places(flat, owner_ref, lane_ref, codes, bands, block, code_row, pair_total, padded):
    codes[...] = jnp.zeros(codes.shape, jnp.float32)
    numbers = []
    for part in range(2):
        codes[part, :bands, :] = flat[pl.ds(code_row + part, bands, stride=block), :]
        numbers.append(
            jnp.dot(
                owner_ref[...],
                codes[part].astype(jnp.bfloat16),
                preferred_element_type=jnp.float32,
            )
        )
    pair_id = jnp.sum(
        (16.0 * numbers[0] + numbers[1]) * lane_ref[...], axis=1, keepdims=True
    ).astype(jnp.int32)
    place = jnp.right_shift(pair_id, 1) + (pair_id & 1) * (pair_total // 2)
    columns = lax.broadcasted_iota(jnp.int32, (owner_ref.shape[0], padded), 1)
    return jnp.where(columns == place, 1.0, 0.0).astype(jnp.bfloat16)


def fourier_kernel(
    pairs, levels, base_ref, after_ref, sums_ref, owner_ref, lane_ref, table_source, *others
):
    field_refs, send_ref, others = others[:2], others[2], others[3:]
    codes, flat, gathered, lhs, table_ref, arrival_sem = others
    copy = pltpu.make_async_copy(table_source.at[:2], table_ref, arrival_sem)
    copy.start()
    bands, block, width = sums_ref.shape
    pair_total = bands * pairs
    padded = up_to(pair_total, LANES)
    blocks = padded // LANES
    fields = 4 * levels
    room = up_to(pairs, ROWS)
    flat[...] = sums_ref[...].astype(jnp.float32).reshape(bands * block, width)
    gathered[...] = jnp.zeros(gathered.shape, jnp.float32)
    code_row = up_to(pairs * TALL, ROWS)
    place = pair_places(
        flat, owner_ref, lane_ref, codes, bands, block, code_row, pair_total, padded
    )
    low = lax.broadcasted_iota(jnp.int32, (fields, padded), 1) < pair_total // 2
    middle = fields * ROWS
    for row in range(TALL):
        here = gathered.at[row % 2]
        for band in range(bands):
            here[band * room : band * room + pairs, :] = flat[
                pl.ds(band * block + row, pairs, stride=TALL), :
            ]
        ordered = jnp.dot(
            here[...].T.astype(jnp.bfloat16), place, preferred_element_type=jnp.float32
        )
        if HALO <= row < HALO + ROWS:
            first, stride = row - HALO, ROWS
        else:
            first, stride = middle + (row - HALO - ROWS) % TALL, 2 * HALO
        for part in range(2):
            start = part * fields
            straight = ordered[start : start + fields]
            start = start + 2 * fields
            crossed = ordered[start : start + fields]
            both = (jnp.where(low, straight, crossed), jnp.where(low, crossed, straight))
            for parity in range(2):
                for t in range(blocks):
                    lhs[parity, part * blocks + t, pl.ds(first, fields, stride=stride), :] = both[
                        parity
                    ][:, t * LANES : (t + 1) * LANES]
    copy.wait()
    half = table_ref.shape[2]

    def transform(first, count):
        found = []
        for parity in range(2):
            left = jnp.concatenate(
                [
                    lhs[parity, t, first : first + count, :].astype(jnp.bfloat16)
                    for t in range(2 * blocks)
                ],
                axis=1,
            )
            found.append(jnp.dot(left, table_ref[parity], preferred_element_type=jnp.float32))
        pieces = (found[0] + found[1], found[0] - found[1])
        return [piece.astype(jnp.bfloat16).astype(jnp.float32) for piece in pieces]

    group = next(n for n in (4, 2, 1) if levels % n == 0)
    for level in range(0, levels, group):
        for part, value in enumerate(transform(level * 4 * ROWS, group * 4 * ROWS)):
            value = value.reshape(group, 4 * ROWS, half)
            lanes = slice(part * half, (part + 1) * half)
            for number, field_ref in enumerate(field_refs):
                field_ref[level : level + group, : 2 * ROWS, lanes] = value[
                    :, 2 * ROWS * number : 2 * ROWS * (number + 1)
                ]
    for part, value in enumerate(transform(middle, fields * 2 * HALO)):
        value = value.reshape(levels, 8 * HALO, half)
        lanes = slice(part * half, (part + 1) * half)
        for number, field_ref in enumerate(field_refs):
            field_ref[:, 2 * ROWS :, lanes] = value[:, 4 * HALO * number : 4 * HALO * (number + 1)]
    for number, field_ref in enumerate(field_refs):
        if send_ref.shape[0] == 1:
            start = jnp.where(base_ref[0] == 0, levels - HALO, 0)
            send_ref[0, number] = field_ref[pl.ds(start, HALO)].astype(jnp.bfloat16)
        else:
            send_ref[0, number] = field_ref[:HALO].astype(jnp.bfloat16)
            send_ref[1, number] = field_ref[levels - HALO :].astype(jnp.bfloat16)


def fourier_call(base, after, sums, table, pairs, levels, lon_total):
    bands, block, width = sums.shape
    padded = up_to(bands * pairs, LANES)
    extra = [jnp.asarray(x) for x in owner_tables(bands, pairs)]
    sends = 1 if lax.axis_size("lev") == 2 else 2
    field_shape = (levels, 3 * ROWS, lon_total)
    field = jax.ShapeDtypeStruct(field_shape, jnp.float32)
    send = jax.ShapeDtypeStruct((sends, 2, HALO) + field_shape[1:], jnp.bfloat16)
    in_vmem = pl.BlockSpec(memory_space=pltpu.VMEM)
    return pl.pallas_call(
        functools.partial(fourier_kernel, pairs, levels),
        out_shape=(field, field, send),
        in_specs=[pl.BlockSpec(memory_space=pltpu.SMEM)]
        + [in_vmem] * 4
        + [pl.BlockSpec(memory_space=pl.ANY)],
        out_specs=(in_vmem,) * 3,
        scratch_shapes=[
            pltpu.VMEM((2, LANES, LANES), jnp.float32),
            pltpu.VMEM((bands * block, width), jnp.float32),
            pltpu.VMEM((2, extra[0].shape[0], width), jnp.float32),
            pltpu.VMEM((2, 2 * padded // LANES, 4 * levels * TALL, LANES), jnp.float32),
            pltpu.VMEM((2,) + table.shape[1:], table.dtype),
            pltpu.SemaphoreType.DMA,
        ],
        compiler_params=pltpu.CompilerParams(vmem_limit_bytes=44 * 1024 * 1024),
        cost_estimate=pl.CostEstimate(
            flops=8_000_000_000, bytes_accessed=8_000_000, transcendentals=0
        ),
    )(base, after, sums, *extra, table)


def exchange(sums):
    return lax.all_to_all(sums, "band", split_axis=0, concat_axis=0, tiled=True)


def per_device(spectra, legendre, pairing, eta_shift, cells):
    levels, rows, lon_total = eta_shift.shape
    pairs = pairing.shape[0]
    spectra = jnp.transpose(spectra, (0, 2, 1, 3))
    table = jnp.transpose(legendre, (0, 2, 1, 3))
    if lax.axis_size("lev") == 2:
        tables = (table, lax.ppermute(table, "lev", [(0, 1), (1, 0)]))
    else:
        tables = (lax.all_gather(table, "lev", axis=0, tiled=True),)
    base = jnp.stack([lax.axis_index("lev") * levels, lax.axis_index("band") * rows])
    base = base.astype(jnp.int32)
    sums, done = legendre_call(pairing, spectra, tables)
    sums = exchange(sums)
    points, done = prepare_call(base, done, eta_shift, cells)
    pair_total = pairs * lax.axis_size("band")
    twiddles = jnp.asarray(fourier_table(pair_total, up_to(pair_total, LANES), lon_total))
    winds, tracers, send = fourier_call(base, done, sums, twiddles, pairs, levels, lon_total)
    nears = swap_levels(send)
    (moved,) = interpolation_call(
        wind_levels, base, 0, winds, points, nears, (), jnp.float32
    )
    advected, displacement = interpolation_call(
        tracer_levels, base, 1, tracers, points, nears, (moved,), jnp.bfloat16
    )
    return advected, displacement


def solution(mesh):
    return jax.shard_map(
        per_device,
        mesh=mesh,
        in_specs=(
            P(None, "lev", "band", None),
            P("lev", None, "band", None),
            P("band"),
            P("lev", "band", None),
            P(None, "lev", "band", None),
        ),
        out_specs=(P(None, "lev", "band", None), P(None, "lev", "band", None)),
        check_vma=False,
    )
```

```python
import functools
import math

import jax
import jax.numpy as jnp
import numpy as np
from jax import lax
from jax.experimental import pallas as pl
from jax.experimental.pallas import tpu as pltpu
from jax.sharding import PartitionSpec as P

ITERS = 2


COURANT = 0.8
HALO = 2
LANES = 128
ROWS = 8
SLOTS = (-1, 0, 1, 2)


def slot_weights(place, here, low, high, sixth):
    z = jnp.minimum(jnp.maximum(place, low), high)
    square = z * z
    less = square - 1.0
    outer = less * z * sixth
    triple = 3.0 * outer
    half = 0.5 * z
    half_square = 0.5 * square
    return (
        half_square - half - jnp.where(here, outer, triple),
        triple - less,
        half_square + half - jnp.where(here, triple, outer),
        outer,
    )


def bounds(here):
    return (
        jnp.where(here, -0.5, -1.5),
        jnp.where(here, 1.5, 0.5),
        jnp.where(here, 1.0 / 6.0, -1.0 / 6.0),
    )


def weighted(weights, values):
    return (weights[0] * values[0] + weights[1] * values[1]) + (
        weights[2] * values[2] + weights[3] * values[3]
    )


def shifted_lanes(before, here, after, lane):
    return (
        pltpu.roll(jnp.where(lane < LANES - 2, here, before), 2, 1),
        pltpu.roll(jnp.where(lane < LANES - 1, here, before), 1, 1),
        here,
        pltpu.roll(jnp.where(lane < 1, after, here), LANES - 1, 1),
        pltpu.roll(jnp.where(lane < 2, after, here), LANES - 2, 1),
    )


STACK = 5 * ROWS
FIELD_ROW = (ROWS, 3 * ROWS)


def fill_units(slab, chunk, chunk_total, source, scratch):
    field_ref, row = source
    before = jnp.where(chunk == 0, chunk_total - 1, chunk - 1)
    after = jnp.where(chunk == chunk_total - 1, 0, chunk + 1)
    starts = [pl.multiple_of(c * LANES, LANES) for c in (before, chunk, after)]
    lane = lax.broadcasted_iota(jnp.int32, (ROWS, LANES), 1)
    first = slab * (5 * STACK)

    def edge_start():
        moved = shifted_lanes(
            *[field_ref[row, 2 * ROWS : 3 * ROWS, pl.ds(s, LANES)] for s in starts], lane
        )
        return [(value, pltpu.roll(value, ROWS // 2, 0)) for value in moved]

    def edge_finish(values):
        for step, (between, outside) in enumerate(values):
            for offset, value in ((0, outside), (2 * ROWS, between), (4 * ROWS, outside)):
                scratch[pl.ds(first + step * STACK + offset, ROWS), :] = value

    def center_unit(field):
        def start():
            rows = slice(field * ROWS, (field + 1) * ROWS)
            blocks = [field_ref[row, rows, pl.ds(s, LANES)] for s in starts]
            return shifted_lanes(*blocks, lane)

        def finish(values):
            for step, moved in enumerate(values):
                scratch[pl.ds(first + step * STACK + FIELD_ROW[field], ROWS), :] = moved

        return start, finish

    return [(edge_start, edge_finish)] + [center_unit(field) for field in range(2)]


class Interleave:
    def __init__(self, units, ticks, later):
        self.units = list(units)
        self.every = max(1, ticks // max(1, len(self.units)))
        self.count = 0
        self.pending = None
        self.later = later

    def advance(self):
        if self.pending is not None:
            self.pending[0](self.pending[1])
            self.pending = None
        if self.units:
            start, finish = self.units.pop(0)
            self.pending = (finish, start())

    def tick(self):
        if self.count % self.every == 0:
            self.advance()
        self.count += 1
        if self.later and self.count % 3 == 0:
            self.later.pop(0)()

    def flush(self):
        while self.units or self.pending is not None:
            self.advance()

    def finish_later(self):
        while self.later:
            self.later.pop(0)()


def level_sums(scratch, field, base, slot, points):
    loaded = {}

    def load(a, b, c):
        offset = ((a + HALO) * 5 + c + HALO) * STACK + FIELD_ROW[field] + b
        if (a, b, c) not in loaded:
            loaded[a, b, c] = scratch[pl.ds(base + offset, ROWS), :]
        return loaded[a, b, c]

    def one(step, weights, level_here, row_here, lon_here):
        def pick_lon(a, b):
            if slot[1] == 2:
                return jnp.where(lon_here, load(a + step, b, 2), load(a + step, b, -2))
            return load(a + step, b, slot[1])

        def pick(a):
            if slot[0] == 2:
                return jnp.where(row_here, pick_lon(a, 2), pick_lon(a, -2))
            return pick_lon(a, slot[0])

        total = weights[0] * pick(-1) + weights[1] * pick(0)
        total = total + weights[2] * pick(1)
        return total + weights[3] * jnp.where(level_here, pick(2), pick(-2))

    return [one(step, *point) for step, point in enumerate(points)]


def across(scratch, field, base, points, row_weights, lon_weights, filling, keep=None):
    columns = [[None] * 4 for _ in points]
    for b, row_slot in enumerate(SLOTS):
        for c, lon_slot in enumerate(SLOTS):
            filling.tick()
            found = level_sums(scratch, field, base, (row_slot, lon_slot), points)
            for step, value in enumerate(found):
                if keep is not None:
                    keep[field, step, 4 * b + c] = value
                term = row_weights[step][b] * value
                columns[step][c] = term if b == 0 else columns[step][c] + term
    return [weighted(weights, column) for weights, column in zip(lon_weights, columns)]


def across_kept(keep, field, step, row_weights, lon_weights):
    return weighted(
        lon_weights,
        [
            weighted(row_weights, [keep[field, step, 4 * b + c] for b in range(4)])
            for c in range(4)
        ],
    )


def prepare_kernel(base_ref, after_ref, eta_ref, cells_ref, points_ref, done_ref):
    done_ref[...] = after_ref[...]
    levels, rows, lon_total = eta_ref.shape
    shape = (rows, LANES)
    row_here = base_ref[1] + lax.broadcasted_iota(jnp.int32, shape, 0)
    lane = lax.broadcasted_iota(jnp.int32, shape, 1)

    def chunk_step(chunk, carry):
        lanes = pl.ds(pl.multiple_of(chunk * LANES, LANES), LANES)
        for k in range(levels):
            level_here = cells_ref[2, k, :, lanes] == base_ref[0] + k
            weights = slot_weights(
                -eta_ref[k, :, lanes].astype(jnp.float32), level_here, *bounds(level_here)
            )
            here = (
                level_here,
                cells_ref[0, k, :, lanes] == row_here,
                cells_ref[1, k, :, lanes] == chunk * LANES + lane,
            )
            for n, value in enumerate(weights + tuple(bounds(x)[0] for x in here)):
                points_ref[n, k, :, lanes] = value
        return carry

    lax.fori_loop(0, lon_total // LANES, chunk_step, 0)


def prepare_call(base, after, eta_shift, cells):
    in_vmem = pl.BlockSpec(memory_space=pltpu.VMEM)
    return pl.pallas_call(
        prepare_kernel,
        out_shape=(
            jax.ShapeDtypeStruct((7,) + eta_shift.shape, jnp.float32),
            jax.ShapeDtypeStruct(after.shape, after.dtype),
        ),
        in_specs=[pl.BlockSpec(memory_space=pltpu.SMEM)] + [in_vmem] * 3,
        out_specs=(in_vmem, in_vmem),
        compiler_params=pltpu.CompilerParams(vmem_limit_bytes=16 * 1024 * 1024),
        cost_estimate=pl.CostEstimate(
            flops=40 * eta_shift.size, bytes_accessed=20_000_000, transcendentals=0
        ),
    )(base, after, eta_shift, cells)


def arrival(points_ref, k, lanes):
    here = [points_ref[n, k, :, lanes] > -1.0 for n in range(4, 7)]
    return tuple(points_ref[n, k, :, lanes] for n in range(4)), *here


def both_weights(shift_row, shift_lon, point):
    _, _, row_here, lon_here = point
    return (
        slot_weights(-shift_row, row_here, *bounds(row_here)),
        slot_weights(-shift_lon, lon_here, *bounds(lon_here)),
    )


def wind_levels(base, lanes, k, points, scratch, keep, filling, out_ref):
    def arrival_wind(field, step):
        middle = (HALO * 5 + HALO) * STACK + step * (5 * STACK) + FIELD_ROW[field]
        return scratch[pl.ds(base + middle, ROWS), :]

    weights = []
    for step, point in enumerate(points):
        east, north = arrival_wind(0, step), arrival_wind(1, step)
        keep[0, step, 16], keep[1, step, 16] = east, north
        weights.append(both_weights(COURANT * north, COURANT * east, point))
    row_weights, lon_weights = zip(*weights)
    found = [
        across(scratch, field, base, points, row_weights, lon_weights, filling, keep)
        for field in range(2)
    ]
    filling.finish_later()

    def tail(step, east_found, north_found):
        def finish():
            east, north = keep[0, step, 16], keep[1, step, 16]
            here = (east_found, north_found)
            for sweep in range(ITERS):
                shift_row = 0.5 * COURANT * (north + here[1])
                shift_lon = 0.5 * COURANT * (east + here[0])
                if sweep < ITERS - 1:
                    weights = both_weights(shift_row, shift_lon, points[step])
                    here = [across_kept(keep, field, step, *weights) for field in range(2)]
            out_ref[0, k + step, :, lanes] = shift_row
            out_ref[1, k + step, :, lanes] = shift_lon

        return finish

    filling.later += [tail(step, found[0][step], found[1][step]) for step in range(len(points))]


def tracer_levels(shift_ref, base, lanes, k, points, scratch, keep, filling, out_ref):
    weights = [
        both_weights(
            shift_ref[0, k + step, :, lanes], shift_ref[1, k + step, :, lanes], points[step]
        )
        for step in range(len(points))
    ]
    row_weights, lon_weights = zip(*weights)
    found = [
        across(scratch, field, base, points, row_weights, lon_weights, filling)
        for field in range(2)
    ]
    for field in range(2):
        for step, total in enumerate(found[field]):
            out_ref[field, k + step, :, lanes] = total.astype(out_ref.dtype)


def interpolation_kernel(
    levels_body, together, number, near_count, base_ref, field_ref, points_ref, *others
):
    nears, others = others[:near_count], others[near_count:]
    extra = ()
    if number == 1:
        shift_ref, out_ref, shift_out, around, even_scratch, odd_scratch, keep, sem = others
        extra = (shift_ref,)
        copy = pltpu.make_async_copy(shift_ref, shift_out, sem)
        copy.start()
    else:
        out_ref, around, even_scratch, odd_scratch, keep = others
    _, levels, rows, lon_total = points_ref.shape
    chunk_total = lon_total // LANES
    if near_count == 1:
        found = jnp.where(base_ref[0] == 0, HALO, 0)
        around[pl.ds(found, HALO)] = nears[0][number].astype(jnp.float32)
        around[pl.ds(HALO - found, HALO)] = jnp.zeros((HALO,) + around.shape[1:], jnp.float32)
    else:
        around[:HALO] = nears[0][number].astype(jnp.float32)
        around[HALO:] = nears[1][number].astype(jnp.float32)
    sources = [(around, n) for n in range(HALO)]
    sources += [(field_ref, n) for n in range(levels)]
    sources += [(around, HALO + n) for n in range(HALO)]

    def all_units(chunk, scratch):
        units = []
        for slab, source in enumerate(sources):
            units += fill_units(slab, chunk, chunk_total, source, scratch)
        return units

    for start, finish in all_units(0, even_scratch):
        finish(start())

    def one_chunk(chunk, scratch, other, later):
        lanes = pl.ds(pl.multiple_of(chunk * LANES, LANES), LANES)
        following = jnp.where(chunk == chunk_total - 1, 0, chunk + 1)
        filling = Interleave(all_units(following, other), 32 * (levels // together), later)
        for k in range(0, levels, together):
            points = [arrival(points_ref, k + n, lanes) for n in range(together)]
            base = k * (5 * STACK)
            keep_here = keep.at[k // together % 2]
            levels_body(*extra, base, lanes, k, points, scratch, keep_here, filling, out_ref)
        filling.flush()
        if levels // together % 2:
            filling.finish_later()

    def chunk_pair(pair, carry):
        later = []
        one_chunk(2 * pair, even_scratch, odd_scratch, later)
        one_chunk(2 * pair + 1, odd_scratch, even_scratch, later)
        for finish in later:
            finish()
        return carry

    lax.fori_loop(0, chunk_total // 2, chunk_pair, 0)
    if number == 1:
        copy.wait()


def interpolation_call(levels_body, base, number, fields, points, nears, extra, out_dtype):
    _, levels, rows, lon_total = points.shape
    count = levels * rows * lon_total
    together = 1
    scratch = pltpu.VMEM(((levels + 2 * HALO) * 5 * STACK, LANES), jnp.float32)
    in_vmem = pl.BlockSpec(memory_space=pltpu.VMEM)
    return pl.pallas_call(
        functools.partial(interpolation_kernel, levels_body, together, number, len(nears)),
        out_shape=(jax.ShapeDtypeStruct((2, levels, rows, lon_total), out_dtype),)
        + tuple(jax.ShapeDtypeStruct(x.shape, x.dtype) for x in extra),
        in_specs=[pl.BlockSpec(memory_space=pltpu.SMEM)]
        + [in_vmem] * (2 + len(nears) + len(extra)),
        out_specs=(in_vmem,) + (pl.BlockSpec(memory_space=pl.ANY),) * len(extra),
        scratch_shapes=[
            pltpu.VMEM((2 * HALO,) + fields.shape[1:], jnp.float32),
            scratch,
            scratch,
            pltpu.VMEM((2, 2, together, 17, ROWS, LANES), jnp.float32),
        ]
        + [pltpu.SemaphoreType.DMA] * len(extra),
        compiler_params=pltpu.CompilerParams(vmem_limit_bytes=16 * 1024 * 1024),
        cost_estimate=pl.CostEstimate(
            flops=count * 500, bytes_accessed=count * 40, transcendentals=0
        ),
    )(base, fields, points, *nears, *extra)


def swap_levels(send):
    if lax.axis_size("lev") == 2:
        return (lax.ppermute(send[0], "lev", [(0, 1), (1, 0)]),)
    up = [(i, i + 1) for i in range(lax.axis_size("lev") - 1)]
    down = [(j, i) for i, j in up]
    return lax.ppermute(send[1], "lev", up), lax.ppermute(send[0], "lev", down)


def up_to(value, step):
    return -(-value // step) * step


TALL = ROWS + 2 * HALO


def codes_kernel(numbers_ref, out_ref):
    out_ref[...] = numbers_ref[...]


def legendre_kernel(numbers_ref, codes_ref, spectra_ref, *others):
    table_count = (len(others) - 7) // 2
    sources, others = (spectra_ref,) + others[:table_count], others[table_count:]
    out_ref, done_ref, sums, table_tail, column_tail = others[:5]
    targets, arrivals = others[5:-1], others[-1]
    spectra_here, tables = targets[0], targets[1:]
    _, pairs, level_fields, degrees = spectra_ref.shape
    group = table_tail.shape[0]
    bands, block, _ = out_ref.shape
    full = degrees // LANES * LANES
    at_top = numbers_ref[0] == 0
    step = pl.program_id(0)

    def copies(number):
        here = pl.ds(number * group, group)
        return [
            pltpu.make_async_copy(source.at[:, here], target.at[:, here], arrivals.at[n, number])
            for n, (source, target) in enumerate(zip(sources, targets))
        ]

    @pl.when(step == 0)
    def _():
        for copy in copies(0):
            copy.start()
        sums[...] = jnp.zeros(sums.shape, jnp.float32)
        done_ref[...] = jnp.zeros(done_ref.shape, jnp.float32)
        table_tail[...] = jnp.zeros(table_tail.shape, jnp.float32)
        column_tail[...] = jnp.zeros(column_tail.shape, jnp.float32)
        codes = codes_ref[...]
        code_row = up_to(pl.num_programs(0) * group * TALL, ROWS)
        for band in range(bands):
            first = band * block + code_row
            sums[pl.ds(first, 1), :] = jnp.right_shift(codes, 4).astype(jnp.float32)
            sums[pl.ds(first + 1, 1), :] = (codes & 15).astype(jnp.float32)

    @pl.when(step + 1 < pairs // group)
    def _():
        for copy in copies(step + 1):
            copy.start()

    for copy in copies(step):
        copy.wait()
    band_row = lax.broadcasted_iota(jnp.int32, (bands, 4 * level_fields), 0)
    count = 2 * level_fields
    nothing = jnp.zeros((bands, 2 * count), jnp.float32)
    for p in range(group):
        slot = step * group + p
        edge = degrees - 1 - numbers_ref[1 + slot]
        left = []
        for number, table_ref in enumerate(tables):
            for row in range(table_ref.shape[0]):
                piece = table_ref[row, slot]
                left.append(piece[:, :full])
                first = (number * table_ref.shape[0] + row) * bands
                table_tail[p, first : first + bands, : degrees - full] = piece[:, full:].astype(
                    jnp.float32
                )
        left = jnp.concatenate(left, axis=0)
        left = jnp.concatenate([left, table_tail[p].astype(jnp.bfloat16)], axis=1)
        halves = ([], [])
        for part in range(2):
            piece = spectra_here[part, slot]
            whole = piece[:, :full].astype(jnp.float32)
            lane = lax.broadcasted_iota(jnp.int32, whole.shape, 1)
            zero = jnp.zeros_like(whole)
            halves[0].append(jnp.where(lane < edge, whole, zero).astype(jnp.bfloat16))
            halves[1].append(jnp.where(lane < edge, zero, whole).astype(jnp.bfloat16))
            first = part * level_fields
            column_tail[p, first : first + level_fields, : degrees - full] = piece[
                :, full:
            ].astype(jnp.float32)
        tail = column_tail[p].astype(jnp.bfloat16)
        right = jnp.concatenate(
            [
                jnp.concatenate([jnp.concatenate(halves[0], axis=0), jnp.zeros_like(tail)], axis=1),
                jnp.concatenate([jnp.concatenate(halves[1], axis=0), tail], axis=1),
            ],
            axis=0,
        )
        found = lax.dot_general(
            left, right, (((1,), (1,)), ((), ())), preferred_element_type=jnp.float32
        )
        found = [found[i * bands : (i + 1) * bands] for i in range(ROWS)]
        if len(tables) == 2:
            low, high = found[: ROWS // 2], found[ROWS // 2 :]
            found = [jnp.where(at_top, x, y) for x, y in zip(low, high)]
            found += [jnp.where(at_top, y, x) for x, y in zip(low, high)]
        above = [
            jnp.where(band_row == 0, nothing, pltpu.roll(x, 1, 0)) for x in found[ROWS - HALO :]
        ]
        below = [
            jnp.where(band_row == bands - 1, nothing, pltpu.roll(x, bands - 1, 0))
            for x in found[:HALO]
        ]
        rows = above + found + below
        for i, value in enumerate(rows):
            place = pl.ds(slot * TALL + i, bands, stride=block)
            sums[place, : 2 * count] = value

    @pl.when(step == pl.num_programs(0) - 1)
    def _():
        for band in range(bands):
            out_ref[band] = sums[band * block : (band + 1) * block, :].astype(jnp.bfloat16)


def block_rows(pairs):
    return up_to(up_to(pairs * TALL, ROWS) + 2, ROWS)


def legendre_call(pairing, spectra, tables):
    _, pairs, level_fields, degrees = spectra.shape
    bands = tables[0].shape[2]
    block = block_rows(pairs)
    group = next(n for n in (4, 5, 2, 1) if pairs % n == 0)
    numbers = jnp.concatenate([lax.axis_index("lev").astype(jnp.int32)[None], pairing])
    codes = pl.pallas_call(
        codes_kernel,
        out_shape=jax.ShapeDtypeStruct((1, LANES), jnp.int32),
        in_specs=[pl.BlockSpec(memory_space=pltpu.VMEM)],
        out_specs=pl.BlockSpec(memory_space=pltpu.VMEM),
        compiler_params=pltpu.CompilerParams(vmem_limit_bytes=60 * 1024 * 1024),
        cost_estimate=pl.CostEstimate(flops=0, bytes_accessed=4_000_000, transcendentals=0),
    )(jnp.pad(pairing, (0, LANES - pairs))[None, :])
    shape = jax.ShapeDtypeStruct((bands, block, LANES), jnp.bfloat16)
    in_vmem = pl.BlockSpec(memory_space=pltpu.VMEM)
    in_hbm = pl.BlockSpec(memory_space=pl.ANY)
    return pl.pallas_call(
        legendre_kernel,
        grid=(pairs // group,),
        out_shape=(shape, jax.ShapeDtypeStruct((ROWS, LANES), jnp.float32)),
        in_specs=[
            pl.BlockSpec(memory_space=pltpu.SMEM),
            pl.BlockSpec((1, LANES), lambda i: (0, 0)),
            in_hbm,
        ]
        + [in_hbm] * len(tables),
        out_specs=(in_vmem, in_vmem),
        scratch_shapes=[
            pltpu.VMEM((bands * block, LANES), jnp.float32),
            pltpu.VMEM((group, ROWS * bands, LANES), jnp.float32),
            pltpu.VMEM((group, 2 * level_fields, LANES), jnp.float32),
        ]
        + [pltpu.VMEM(x.shape, x.dtype) for x in (spectra,) + tables]
        + [pltpu.SemaphoreType.DMA((1 + len(tables), pairs // group))],
        compiler_params=pltpu.CompilerParams(vmem_limit_bytes=60 * 1024 * 1024),
        cost_estimate=pl.CostEstimate(
            flops=2 * ROWS * bands * 4 * level_fields * pairs * degrees,
            bytes_accessed=8_000_000,
            transcendentals=0,
        ),
    )(numbers, codes, spectra, *tables)


def fourier_table(pair_total, padded, lon_total):
    order_total = 2 * pair_total
    half = pair_total // 2
    low = 2 * np.arange(half)
    high = low + 1
    even = np.concatenate([low, order_total - 1 - high])
    odd = np.concatenate([order_total - 1 - low, high])
    lon = np.arange(lon_total // 2)
    table = np.zeros((4, 2, padded, lon_total // 2), np.float32)
    for parity, orders in enumerate((even, odd)):
        phase = (orders[:, None] * lon[None, :]) % lon_total * (2.0 * math.pi / lon_total)
        weight = np.where(orders == 0, 1.0, 2.0)[:, None]
        table[parity, 0, :pair_total] = weight * np.cos(phase)
        table[parity, 1, :pair_total] = -weight * np.sin(phase)
    return table.reshape(4, 2 * padded, lon_total // 2).astype(jnp.bfloat16)


def owner_tables(bands, pairs):
    room = up_to(pairs, ROWS)
    slots = np.arange(up_to(bands * room, LANES))
    owner = slots[:, None] // room == np.arange(LANES)[None, :]
    lane = slots[:, None] % room == np.arange(LANES)[None, :]
    return owner.astype(jnp.bfloat16), lane.astype(np.float32)


def pair_places(flat, owner_ref, lane_ref, codes, bands, block, code_row, pair_total, padded):
    codes[...] = jnp.zeros(codes.shape, jnp.float32)
    numbers = []
    for part in range(2):
        codes[part, :bands, :] = flat[pl.ds(code_row + part, bands, stride=block), :]
        numbers.append(
            jnp.dot(
                owner_ref[...],
                codes[part].astype(jnp.bfloat16),
                preferred_element_type=jnp.float32,
            )
        )
    pair_id = jnp.sum(
        (16.0 * numbers[0] + numbers[1]) * lane_ref[...], axis=1, keepdims=True
    ).astype(jnp.int32)
    place = jnp.right_shift(pair_id, 1) + (pair_id & 1) * (pair_total // 2)
    columns = lax.broadcasted_iota(jnp.int32, (owner_ref.shape[0], padded), 1)
    return jnp.where(columns == place, 1.0, 0.0).astype(jnp.bfloat16)


def fourier_kernel(
    pairs, levels, base_ref, after_ref, sums_ref, owner_ref, lane_ref, table_source, *others
):
    field_refs, send_ref, others = others[:2], others[2], others[3:]
    codes, flat, gathered, lhs, table_ref, arrival_sem = others
    copy = pltpu.make_async_copy(table_source.at[:2], table_ref, arrival_sem)
    copy.start()
    bands, block, width = sums_ref.shape
    pair_total = bands * pairs
    padded = up_to(pair_total, LANES)
    blocks = padded // LANES
    fields = 4 * levels
    room = up_to(pairs, ROWS)
    for band in range(bands):
        flat[band * block : (band + 1) * block, :] = sums_ref[band].astype(jnp.float32)
    gathered[...] = jnp.zeros(gathered.shape, jnp.float32)
    code_row = up_to(pairs * TALL, ROWS)
    place = pair_places(
        flat, owner_ref, lane_ref, codes, bands, block, code_row, pair_total, padded
    )
    low = lax.broadcasted_iota(jnp.int32, (fields, padded), 1) < pair_total // 2
    middle = fields * ROWS
    for row in range(TALL):
        here = gathered.at[row % 2]
        for band in range(bands):
            here[band * room : band * room + pairs, :] = flat[
                pl.ds(band * block + row, pairs, stride=TALL), :
            ]
        ordered = jnp.dot(
            here[...].T.astype(jnp.bfloat16), place, preferred_element_type=jnp.float32
        )
        if HALO <= row < HALO + ROWS:
            first, stride = row - HALO, ROWS
        else:
            first, stride = middle + (row - HALO - ROWS) % TALL, 2 * HALO
        for part in range(2):
            start = part * fields
            straight = ordered[start : start + fields]
            start = start + 2 * fields
            crossed = ordered[start : start + fields]
            both = (jnp.where(low, straight, crossed), jnp.where(low, crossed, straight))
            for parity in range(2):
                for t in range(blocks):
                    lhs[parity, part * blocks + t, pl.ds(first, fields, stride=stride), :] = both[
                        parity
                    ][:, t * LANES : (t + 1) * LANES]
    copy.wait()
    half = table_ref.shape[2]

    def transform(first, count):
        found = []
        for parity in range(2):
            left = jnp.concatenate(
                [
                    lhs[parity, t, first : first + count, :].astype(jnp.bfloat16)
                    for t in range(2 * blocks)
                ],
                axis=1,
            )
            found.append(jnp.dot(left, table_ref[parity], preferred_element_type=jnp.float32))
        pieces = (found[0] + found[1], found[0] - found[1])
        return [piece.astype(jnp.bfloat16).astype(jnp.float32) for piece in pieces]

    group = next(n for n in (4, 2, 1) if levels % n == 0)
    for level in range(0, levels, group):
        for part, value in enumerate(transform(level * 4 * ROWS, group * 4 * ROWS)):
            value = value.reshape(group, 4 * ROWS, half)
            lanes = slice(part * half, (part + 1) * half)
            for number, field_ref in enumerate(field_refs):
                field_ref[level : level + group, : 2 * ROWS, lanes] = value[
                    :, 2 * ROWS * number : 2 * ROWS * (number + 1)
                ]
    for part, value in enumerate(transform(middle, fields * 2 * HALO)):
        value = value.reshape(levels, 8 * HALO, half)
        lanes = slice(part * half, (part + 1) * half)
        for number, field_ref in enumerate(field_refs):
            field_ref[:, 2 * ROWS :, lanes] = value[:, 4 * HALO * number : 4 * HALO * (number + 1)]
    for number, field_ref in enumerate(field_refs):
        if send_ref.shape[0] == 1:
            start = jnp.where(base_ref[0] == 0, levels - HALO, 0)
            send_ref[0, number] = field_ref[pl.ds(start, HALO)].astype(jnp.bfloat16)
        else:
            send_ref[0, number] = field_ref[:HALO].astype(jnp.bfloat16)
            send_ref[1, number] = field_ref[levels - HALO :].astype(jnp.bfloat16)


def fourier_call(base, after, sums, table, pairs, levels, lon_total):
    bands, block, width = sums.shape
    padded = up_to(bands * pairs, LANES)
    extra = [jnp.asarray(x) for x in owner_tables(bands, pairs)]
    sends = 1 if lax.axis_size("lev") == 2 else 2
    field_shape = (levels, 3 * ROWS, lon_total)
    field = jax.ShapeDtypeStruct(field_shape, jnp.float32)
    send = jax.ShapeDtypeStruct((sends, 2, HALO) + field_shape[1:], jnp.bfloat16)
    in_vmem = pl.BlockSpec(memory_space=pltpu.VMEM)
    return pl.pallas_call(
        functools.partial(fourier_kernel, pairs, levels),
        out_shape=(field, field, send),
        in_specs=[pl.BlockSpec(memory_space=pltpu.SMEM)]
        + [in_vmem] * 4
        + [pl.BlockSpec(memory_space=pl.ANY)],
        out_specs=(in_vmem,) * 3,
        scratch_shapes=[
            pltpu.VMEM((2, LANES, LANES), jnp.float32),
            pltpu.VMEM((bands * block, width), jnp.float32),
            pltpu.VMEM((2, extra[0].shape[0], width), jnp.float32),
            pltpu.VMEM((2, 2 * padded // LANES, 4 * levels * TALL, LANES), jnp.float32),
            pltpu.VMEM((2,) + table.shape[1:], table.dtype),
            pltpu.SemaphoreType.DMA,
        ],
        compiler_params=pltpu.CompilerParams(vmem_limit_bytes=44 * 1024 * 1024),
        cost_estimate=pl.CostEstimate(
            flops=8_000_000_000, bytes_accessed=8_000_000, transcendentals=0
        ),
    )(base, after, sums, *extra, table)


def exchange(sums):
    return lax.all_to_all(sums, "band", split_axis=0, concat_axis=0, tiled=True)


def per_device(spectra, legendre, pairing, eta_shift, cells):
    levels, rows, lon_total = eta_shift.shape
    pairs = pairing.shape[0]
    spectra = jnp.transpose(spectra, (0, 2, 1, 3))
    table = jnp.transpose(legendre, (0, 2, 1, 3))
    if lax.axis_size("lev") == 2:
        tables = (table, lax.ppermute(table, "lev", [(0, 1), (1, 0)]))
    else:
        tables = (lax.all_gather(table, "lev", axis=0, tiled=True),)
    base = jnp.stack([lax.axis_index("lev") * levels, lax.axis_index("band") * rows])
    base = base.astype(jnp.int32)
    sums, done = legendre_call(pairing, spectra, tables)
    sums = exchange(sums)
    points, done = prepare_call(base, done, eta_shift, cells)
    pair_total = pairs * lax.axis_size("band")
    twiddles = jnp.asarray(fourier_table(pair_total, up_to(pair_total, LANES), lon_total))
    winds, tracers, send = fourier_call(base, done, sums, twiddles, pairs, levels, lon_total)
    nears = swap_levels(send)
    (moved,) = interpolation_call(
        wind_levels, base, 0, winds, points, nears, (), jnp.float32
    )
    advected, displacement = interpolation_call(
        tracer_levels, base, 1, tracers, points, nears, (moved,), jnp.bfloat16
    )
    return advected, displacement


def solution(mesh):
    return jax.shard_map(
        per_device,
        mesh=mesh,
        in_specs=(
            P(None, "lev", "band", None),
            P("lev", None, "band", None),
            P("band"),
            P("lev", "band", None),
            P(None, "lev", "band", None),
        ),
        out_specs=(P(None, "lev", "band", None), P(None, "lev", "band", None)),
        check_vma=False,
    )
```

```python
import functools
import math

import jax
import jax.numpy as jnp
import numpy as np
from jax import lax
from jax.experimental import pallas as pl
from jax.experimental.pallas import tpu as pltpu
from jax.sharding import PartitionSpec as P

ITERS = 2


COURANT = 0.8
HALO = 2
LANES = 128
ROWS = 8
SLOTS = (-1, 0, 1, 2)


def slot_weights(place, here, low, high, sixth):
    z = jnp.minimum(jnp.maximum(place, low), high)
    square = z * z
    less = square - 1.0
    outer = less * z * sixth
    triple = 3.0 * outer
    half = 0.5 * z
    half_square = 0.5 * square
    return (
        half_square - half - jnp.where(here, outer, triple),
        triple - less,
        half_square + half - jnp.where(here, triple, outer),
        outer,
    )


def bounds(here):
    return (
        jnp.where(here, -0.5, -1.5),
        jnp.where(here, 1.5, 0.5),
        jnp.where(here, 1.0 / 6.0, -1.0 / 6.0),
    )


def weighted(weights, values):
    return (weights[0] * values[0] + weights[1] * values[1]) + (
        weights[2] * values[2] + weights[3] * values[3]
    )


def shifted_lanes(before, here, after, lane):
    return (
        pltpu.roll(jnp.where(lane < LANES - 2, here, before), 2, 1),
        pltpu.roll(jnp.where(lane < LANES - 1, here, before), 1, 1),
        here,
        pltpu.roll(jnp.where(lane < 1, after, here), LANES - 1, 1),
        pltpu.roll(jnp.where(lane < 2, after, here), LANES - 2, 1),
    )


STACK = 5 * ROWS
FIELD_ROW = (ROWS, 3 * ROWS)


def fill_units(slab, chunk, chunk_total, source, scratch):
    field_ref, row = source
    before = jnp.where(chunk == 0, chunk_total - 1, chunk - 1)
    after = jnp.where(chunk == chunk_total - 1, 0, chunk + 1)
    starts = [pl.multiple_of(c * LANES, LANES) for c in (before, chunk, after)]
    lane = lax.broadcasted_iota(jnp.int32, (ROWS, LANES), 1)
    first = slab * (5 * STACK)

    def edge_start():
        moved = shifted_lanes(
            *[field_ref[row, 2 * ROWS : 3 * ROWS, pl.ds(s, LANES)] for s in starts], lane
        )
        return [(value, pltpu.roll(value, ROWS // 2, 0)) for value in moved]

    def edge_finish(values):
        for step, (between, outside) in enumerate(values):
            for offset, value in ((0, outside), (2 * ROWS, between), (4 * ROWS, outside)):
                scratch[pl.ds(first + step * STACK + offset, ROWS), :] = value

    def center_unit(field):
        def start():
            rows = slice(field * ROWS, (field + 1) * ROWS)
            blocks = [field_ref[row, rows, pl.ds(s, LANES)] for s in starts]
            return shifted_lanes(*blocks, lane)

        def finish(values):
            for step, moved in enumerate(values):
                scratch[pl.ds(first + step * STACK + FIELD_ROW[field], ROWS), :] = moved

        return start, finish

    return [(edge_start, edge_finish)] + [center_unit(field) for field in range(2)]


class Interleave:
    def __init__(self, units, ticks, later):
        self.units = list(units)
        self.every = max(1, ticks // max(1, len(self.units)))
        self.count = 0
        self.pending = None
        self.later = later

    def advance(self):
        if self.pending is not None:
            self.pending[0](self.pending[1])
            self.pending = None
        if self.units:
            start, finish = self.units.pop(0)
            self.pending = (finish, start())

    def tick(self):
        if self.count % self.every == 0:
            self.advance()
        self.count += 1
        if self.later and self.count % 3 == 0:
            self.later.pop(0)()

    def flush(self):
        while self.units or self.pending is not None:
            self.advance()

    def finish_later(self):
        while self.later:
            self.later.pop(0)()


def level_sums(scratch, field, base, slot, points):
    loaded = {}

    def load(a, b, c):
        offset = ((a + HALO) * 5 + c + HALO) * STACK + FIELD_ROW[field] + b
        if (a, b, c) not in loaded:
            loaded[a, b, c] = scratch[pl.ds(base + offset, ROWS), :]
        return loaded[a, b, c]

    def one(step, weights, level_here, row_here, lon_here):
        def pick_lon(a, b):
            if slot[1] == 2:
                return jnp.where(lon_here, load(a + step, b, 2), load(a + step, b, -2))
            return load(a + step, b, slot[1])

        def pick(a):
            if slot[0] == 2:
                return jnp.where(row_here, pick_lon(a, 2), pick_lon(a, -2))
            return pick_lon(a, slot[0])

        total = weights[0] * pick(-1) + weights[1] * pick(0)
        total = total + weights[2] * pick(1)
        return total + weights[3] * jnp.where(level_here, pick(2), pick(-2))

    return [one(step, *point) for step, point in enumerate(points)]


def across(scratch, field, base, points, row_weights, lon_weights, filling, keep=None):
    columns = [[None] * 4 for _ in points]
    for b, row_slot in enumerate(SLOTS):
        for c, lon_slot in enumerate(SLOTS):
            filling.tick()
            found = level_sums(scratch, field, base, (row_slot, lon_slot), points)
            for step, value in enumerate(found):
                if keep is not None:
                    keep[field, step, 4 * b + c] = value
                term = row_weights[step][b] * value
                columns[step][c] = term if b == 0 else columns[step][c] + term
    return [weighted(weights, column) for weights, column in zip(lon_weights, columns)]


def across_kept(keep, field, step, row_weights, lon_weights):
    return weighted(
        lon_weights,
        [
            weighted(row_weights, [keep[field, step, 4 * b + c] for b in range(4)])
            for c in range(4)
        ],
    )


def prepare_kernel(base_ref, after_ref, eta_ref, cells_ref, points_ref, done_ref):
    done_ref[...] = after_ref[...]
    levels, rows, lon_total = eta_ref.shape
    shape = (rows, LANES)
    row_here = base_ref[1] + lax.broadcasted_iota(jnp.int32, shape, 0)
    lane = lax.broadcasted_iota(jnp.int32, shape, 1)

    def chunk_step(chunk, carry):
        lanes = pl.ds(pl.multiple_of(chunk * LANES, LANES), LANES)
        for k in range(levels):
            level_here = cells_ref[2, k, :, lanes] == base_ref[0] + k
            weights = slot_weights(
                -eta_ref[k, :, lanes].astype(jnp.float32), level_here, *bounds(level_here)
            )
            here = (
                level_here,
                cells_ref[0, k, :, lanes] == row_here,
                cells_ref[1, k, :, lanes] == chunk * LANES + lane,
            )
            for n, value in enumerate(weights + tuple(bounds(x)[0] for x in here)):
                points_ref[n, k, :, lanes] = value
        return carry

    lax.fori_loop(0, lon_total // LANES, chunk_step, 0)


def prepare_call(base, after, eta_shift, cells):
    in_vmem = pl.BlockSpec(memory_space=pltpu.VMEM)
    return pl.pallas_call(
        prepare_kernel,
        out_shape=(
            jax.ShapeDtypeStruct((7,) + eta_shift.shape, jnp.float32),
            jax.ShapeDtypeStruct(after.shape, after.dtype),
        ),
        in_specs=[pl.BlockSpec(memory_space=pltpu.SMEM)] + [in_vmem] * 3,
        out_specs=(in_vmem, in_vmem),
        compiler_params=pltpu.CompilerParams(vmem_limit_bytes=16 * 1024 * 1024),
        cost_estimate=pl.CostEstimate(
            flops=40 * eta_shift.size, bytes_accessed=20_000_000, transcendentals=0
        ),
    )(base, after, eta_shift, cells)


def arrival(points_ref, k, lanes):
    here = [points_ref[n, k, :, lanes] > -1.0 for n in range(4, 7)]
    return tuple(points_ref[n, k, :, lanes] for n in range(4)), *here


def both_weights(shift_row, shift_lon, point):
    _, _, row_here, lon_here = point
    return (
        slot_weights(-shift_row, row_here, *bounds(row_here)),
        slot_weights(-shift_lon, lon_here, *bounds(lon_here)),
    )


def wind_levels(base, lanes, k, points, scratch, keep, filling, out_ref):
    def arrival_wind(field, step):
        middle = (HALO * 5 + HALO) * STACK + step * (5 * STACK) + FIELD_ROW[field]
        return scratch[pl.ds(base + middle, ROWS), :]

    weights = []
    for step, point in enumerate(points):
        east, north = arrival_wind(0, step), arrival_wind(1, step)
        keep[0, step, 16], keep[1, step, 16] = east, north
        weights.append(both_weights(COURANT * north, COURANT * east, point))
    row_weights, lon_weights = zip(*weights)
    found = [
        across(scratch, field, base, points, row_weights, lon_weights, filling, keep)
        for field in range(2)
    ]
    filling.finish_later()

    def tail(step, east_found, north_found):
        def finish():
            east, north = keep[0, step, 16], keep[1, step, 16]
            here = (east_found, north_found)
            for sweep in range(ITERS):
                shift_row = 0.5 * COURANT * (north + here[1])
                shift_lon = 0.5 * COURANT * (east + here[0])
                if sweep < ITERS - 1:
                    weights = both_weights(shift_row, shift_lon, points[step])
                    here = [across_kept(keep, field, step, *weights) for field in range(2)]
            out_ref[0, k + step, :, lanes] = shift_row
            out_ref[1, k + step, :, lanes] = shift_lon

        return finish

    filling.later += [tail(step, found[0][step], found[1][step]) for step in range(len(points))]


def tracer_levels(shift_ref, base, lanes, k, points, scratch, keep, filling, out_ref):
    weights = [
        both_weights(
            shift_ref[0, k + step, :, lanes], shift_ref[1, k + step, :, lanes], points[step]
        )
        for step in range(len(points))
    ]
    row_weights, lon_weights = zip(*weights)
    found = [
        across(scratch, field, base, points, row_weights, lon_weights, filling)
        for field in range(2)
    ]
    for field in range(2):
        for step, total in enumerate(found[field]):
            out_ref[field, k + step, :, lanes] = total.astype(out_ref.dtype)


def interpolation_kernel(
    levels_body, together, number, near_count, base_ref, field_ref, points_ref, *others
):
    nears, others = others[:near_count], others[near_count:]
    extra = ()
    if number == 1:
        shift_ref, out_ref, shift_out, around, even_scratch, odd_scratch, keep, sem = others
        extra = (shift_ref,)
        copy = pltpu.make_async_copy(shift_ref, shift_out, sem)
        copy.start()
    else:
        out_ref, around, even_scratch, odd_scratch, keep = others
    _, levels, rows, lon_total = points_ref.shape
    chunk_total = lon_total // LANES
    if near_count == 1:
        found = jnp.where(base_ref[0] == 0, HALO, 0)
        around[pl.ds(found, HALO)] = nears[0][number].astype(jnp.float32)
        around[pl.ds(HALO - found, HALO)] = jnp.zeros((HALO,) + around.shape[1:], jnp.float32)
    else:
        around[:HALO] = nears[0][number].astype(jnp.float32)
        around[HALO:] = nears[1][number].astype(jnp.float32)
    sources = [(around, n) for n in range(HALO)]
    sources += [(field_ref, n) for n in range(levels)]
    sources += [(around, HALO + n) for n in range(HALO)]

    def all_units(chunk, scratch):
        units = []
        for slab, source in enumerate(sources):
            units += fill_units(slab, chunk, chunk_total, source, scratch)
        return units

    for start, finish in all_units(0, even_scratch):
        finish(start())

    def one_chunk(chunk, scratch, other, later):
        lanes = pl.ds(pl.multiple_of(chunk * LANES, LANES), LANES)
        following = jnp.where(chunk == chunk_total - 1, 0, chunk + 1)
        filling = Interleave(all_units(following, other), 32 * (levels // together), later)
        for k in range(0, levels, together):
            points = [arrival(points_ref, k + n, lanes) for n in range(together)]
            base = k * (5 * STACK)
            keep_here = keep.at[k // together % 2]
            levels_body(*extra, base, lanes, k, points, scratch, keep_here, filling, out_ref)
        filling.flush()
        if levels // together % 2:
            filling.finish_later()

    def chunk_pair(pair, carry):
        later = []
        one_chunk(2 * pair, even_scratch, odd_scratch, later)
        one_chunk(2 * pair + 1, odd_scratch, even_scratch, later)
        for finish in later:
            finish()
        return carry

    lax.fori_loop(0, chunk_total // 2, chunk_pair, 0)
    if number == 1:
        copy.wait()


def interpolation_call(levels_body, base, number, fields, points, nears, extra, out_dtype):
    _, levels, rows, lon_total = points.shape
    count = levels * rows * lon_total
    together = 2 if levels % 2 == 0 else 1
    scratch = pltpu.VMEM(((levels + 2 * HALO) * 5 * STACK, LANES), jnp.float32)
    in_vmem = pl.BlockSpec(memory_space=pltpu.VMEM)
    return pl.pallas_call(
        functools.partial(interpolation_kernel, levels_body, together, number, len(nears)),
        out_shape=(jax.ShapeDtypeStruct((2, levels, rows, lon_total), out_dtype),)
        + tuple(jax.ShapeDtypeStruct(x.shape, x.dtype) for x in extra),
        in_specs=[pl.BlockSpec(memory_space=pltpu.SMEM)]
        + [in_vmem] * (2 + len(nears) + len(extra)),
        out_specs=(in_vmem,) + (pl.BlockSpec(memory_space=pl.ANY),) * len(extra),
        scratch_shapes=[
            pltpu.VMEM((2 * HALO,) + fields.shape[1:], jnp.float32),
            scratch,
            scratch,
            pltpu.VMEM((2, 2, together, 17, ROWS, LANES), jnp.float32),
        ]
        + [pltpu.SemaphoreType.DMA] * len(extra),
        compiler_params=pltpu.CompilerParams(vmem_limit_bytes=16 * 1024 * 1024),
        cost_estimate=pl.CostEstimate(
            flops=count * 500, bytes_accessed=count * 40, transcendentals=0
        ),
    )(base, fields, points, *nears, *extra)


def swap_levels(send):
    if lax.axis_size("lev") == 2:
        return (lax.ppermute(send[0], "lev", [(0, 1), (1, 0)]),)
    up = [(i, i + 1) for i in range(lax.axis_size("lev") - 1)]
    down = [(j, i) for i, j in up]
    return lax.ppermute(send[1], "lev", up), lax.ppermute(send[0], "lev", down)


def up_to(value, step):
    return -(-value // step) * step


TALL = ROWS + 2 * HALO


def codes_kernel(numbers_ref, out_ref):
    out_ref[...] = numbers_ref[...]


def legendre_kernel(numbers_ref, codes_ref, spectra_ref, *others):
    table_count = (len(others) - 7) // 2
    sources, others = (spectra_ref,) + others[:table_count], others[table_count:]
    out_ref, done_ref, sums, table_tail, column_tail = others[:5]
    targets, arrivals = others[5:-1], others[-1]
    spectra_here, tables = targets[0], targets[1:]
    _, pairs, level_fields, degrees = spectra_ref.shape
    group = table_tail.shape[0]
    bands, block, _ = out_ref.shape
    full = degrees // LANES * LANES
    at_top = numbers_ref[0] == 0
    step = pl.program_id(0)

    def copies(number):
        here = pl.ds(number * group, group)
        return [
            pltpu.make_async_copy(source.at[:, here], target.at[:, here], arrivals.at[n, number])
            for n, (source, target) in enumerate(zip(sources, targets))
        ]

    @pl.when(step == 0)
    def _():
        for copy in copies(0):
            copy.start()
        sums[...] = jnp.zeros(sums.shape, jnp.float32)
        done_ref[...] = jnp.zeros(done_ref.shape, jnp.float32)
        table_tail[...] = jnp.zeros(table_tail.shape, jnp.float32)
        column_tail[...] = jnp.zeros(column_tail.shape, jnp.float32)
        codes = codes_ref[...]
        code_row = up_to(pl.num_programs(0) * group * TALL, ROWS)
        for band in range(bands):
            first = band * block + code_row
            sums[pl.ds(first, 1), :] = jnp.right_shift(codes, 4).astype(jnp.float32)
            sums[pl.ds(first + 1, 1), :] = (codes & 15).astype(jnp.float32)

    @pl.when(step + 1 < pairs // group)
    def _():
        for copy in copies(step + 1):
            copy.start()

    for copy in copies(step):
        copy.wait()
    band_row = lax.broadcasted_iota(jnp.int32, (bands, 4 * level_fields), 0)
    count = 2 * level_fields
    nothing = jnp.zeros((bands, 2 * count), jnp.float32)
    for p in range(group):
        slot = step * group + p
        edge = degrees - 1 - numbers_ref[1 + slot]
        left = []
        for number, table_ref in enumerate(tables):
            for row in range(table_ref.shape[0]):
                piece = table_ref[row, slot]
                left.append(piece[:, :full])
                first = (number * table_ref.shape[0] + row) * bands
                table_tail[p, first : first + bands, : degrees - full] = piece[:, full:].astype(
                    jnp.float32
                )
        left = jnp.concatenate(left, axis=0)
        left = jnp.concatenate([left, table_tail[p].astype(jnp.bfloat16)], axis=1)
        halves = ([], [])
        for part in range(2):
            piece = spectra_here[part, slot]
            whole = piece[:, :full].astype(jnp.float32)
            lane = lax.broadcasted_iota(jnp.int32, whole.shape, 1)
            zero = jnp.zeros_like(whole)
            halves[0].append(jnp.where(lane < edge, whole, zero).astype(jnp.bfloat16))
            halves[1].append(jnp.where(lane < edge, zero, whole).astype(jnp.bfloat16))
            first = part * level_fields
            column_tail[p, first : first + level_fields, : degrees - full] = piece[
                :, full:
            ].astype(jnp.float32)
        tail = column_tail[p].astype(jnp.bfloat16)
        right = jnp.concatenate(
            [
                jnp.concatenate([jnp.concatenate(halves[0], axis=0), jnp.zeros_like(tail)], axis=1),
                jnp.concatenate([jnp.concatenate(halves[1], axis=0), tail], axis=1),
            ],
            axis=0,
        )
        found = lax.dot_general(
            left, right, (((1,), (1,)), ((), ())), preferred_element_type=jnp.float32
        )
        found = [found[i * bands : (i + 1) * bands] for i in range(ROWS)]
        if len(tables) == 2:
            low, high = found[: ROWS // 2], found[ROWS // 2 :]
            found = [jnp.where(at_top, x, y) for x, y in zip(low, high)]
            found += [jnp.where(at_top, y, x) for x, y in zip(low, high)]
        above = [
            jnp.where(band_row == 0, nothing, pltpu.roll(x, 1, 0)) for x in found[ROWS - HALO :]
        ]
        below = [
            jnp.where(band_row == bands - 1, nothing, pltpu.roll(x, bands - 1, 0))
            for x in found[:HALO]
        ]
        rows = above + found + below
        for i, value in enumerate(rows):
            place = pl.ds(slot * TALL + i, bands, stride=block)
            sums[place, : 2 * count] = value

    @pl.when(step == pl.num_programs(0) - 1)
    def _():
        for band in range(bands):
            out_ref[band] = sums[band * block : (band + 1) * block, :].astype(jnp.bfloat16)


def block_rows(pairs):
    return up_to(up_to(pairs * TALL, ROWS) + 2, ROWS)


def legendre_call(pairing, spectra, tables):
    _, pairs, level_fields, degrees = spectra.shape
    bands = tables[0].shape[2]
    block = block_rows(pairs)
    group = next(n for n in (4, 5, 2, 1) if pairs % n == 0)
    numbers = jnp.concatenate([lax.axis_index("lev").astype(jnp.int32)[None], pairing])
    codes = pl.pallas_call(
        codes_kernel,
        out_shape=jax.ShapeDtypeStruct((1, LANES), jnp.int32),
        in_specs=[pl.BlockSpec(memory_space=pltpu.VMEM)],
        out_specs=pl.BlockSpec(memory_space=pltpu.VMEM),
        compiler_params=pltpu.CompilerParams(vmem_limit_bytes=60 * 1024 * 1024),
        cost_estimate=pl.CostEstimate(flops=0, bytes_accessed=4_000_000, transcendentals=0),
    )(jnp.pad(pairing, (0, LANES - pairs))[None, :])
    shape = jax.ShapeDtypeStruct((bands, block, LANES), jnp.bfloat16)
    in_vmem = pl.BlockSpec(memory_space=pltpu.VMEM)
    in_hbm = pl.BlockSpec(memory_space=pl.ANY)
    return pl.pallas_call(
        legendre_kernel,
        grid=(pairs // group,),
        out_shape=(shape, jax.ShapeDtypeStruct((ROWS, LANES), jnp.float32)),
        in_specs=[
            pl.BlockSpec(memory_space=pltpu.SMEM),
            pl.BlockSpec((1, LANES), lambda i: (0, 0)),
            in_hbm,
        ]
        + [in_hbm] * len(tables),
        out_specs=(in_vmem, in_vmem),
        scratch_shapes=[
            pltpu.VMEM((bands * block, LANES), jnp.float32),
            pltpu.VMEM((group, ROWS * bands, LANES), jnp.float32),
            pltpu.VMEM((group, 2 * level_fields, LANES), jnp.float32),
        ]
        + [pltpu.VMEM(x.shape, x.dtype) for x in (spectra,) + tables]
        + [pltpu.SemaphoreType.DMA((1 + len(tables), pairs // group))],
        compiler_params=pltpu.CompilerParams(vmem_limit_bytes=60 * 1024 * 1024),
        cost_estimate=pl.CostEstimate(
            flops=2 * ROWS * bands * 4 * level_fields * pairs * degrees,
            bytes_accessed=8_000_000,
            transcendentals=0,
        ),
    )(numbers, codes, spectra, *tables)


def fourier_table(pair_total, padded, lon_total):
    order_total = 2 * pair_total
    half = pair_total // 2
    low = 2 * np.arange(half)
    high = low + 1
    even = np.concatenate([low, order_total - 1 - high])
    odd = np.concatenate([order_total - 1 - low, high])
    lon = np.arange(lon_total // 2)
    table = np.zeros((4, 2, padded, lon_total // 2), np.float32)
    for parity, orders in enumerate((even, odd)):
        phase = (orders[:, None] * lon[None, :]) % lon_total * (2.0 * math.pi / lon_total)
        weight = np.where(orders == 0, 1.0, 2.0)[:, None]
        table[parity, 0, :pair_total] = weight * np.cos(phase)
        table[parity, 1, :pair_total] = -weight * np.sin(phase)
    return table.reshape(4, 2 * padded, lon_total // 2).astype(jnp.bfloat16)


def owner_tables(slots, pairs):
    room = up_to(pairs, ROWS)
    slot = lax.broadcasted_iota(jnp.int32, (slots, LANES), 0)
    lane = lax.broadcasted_iota(jnp.int32, (slots, LANES), 1)
    owner = ((slot.astype(jnp.float32) + 0.5) * (1.0 / room)).astype(jnp.int32)
    return (
        jnp.where(owner == lane, 1.0, 0.0).astype(jnp.bfloat16),
        jnp.where(slot - room * owner == lane, 1.0, 0.0),
    )


def pair_places(flat, codes, bands, block, code_row, pairs, slots, padded):
    pair_total = bands * pairs
    owner, own_lane = owner_tables(slots, pairs)
    codes[...] = jnp.zeros(codes.shape, jnp.float32)
    numbers = []
    for part in range(2):
        codes[part, :bands, :] = flat[pl.ds(code_row + part, bands, stride=block), :]
        numbers.append(
            jnp.dot(
                owner,
                codes[part].astype(jnp.bfloat16),
                preferred_element_type=jnp.float32,
            )
        )
    pair_id = jnp.sum(
        (16.0 * numbers[0] + numbers[1]) * own_lane, axis=1, keepdims=True
    ).astype(jnp.int32)
    place = jnp.right_shift(pair_id, 1) + (pair_id & 1) * (pair_total // 2)
    columns = lax.broadcasted_iota(jnp.int32, (slots, padded), 1)
    return jnp.where(columns == place, 1.0, 0.0).astype(jnp.bfloat16)


def fourier_kernel(
    pairs, levels, base_ref, after_ref, sums_ref, table_source, *others
):
    field_refs, send_ref, others = others[:2], others[2], others[3:]
    codes, flat, gathered, lhs, table_ref, arrival_sem = others
    copy = pltpu.make_async_copy(table_source.at[:2], table_ref, arrival_sem)
    copy.start()
    bands, block, width = sums_ref.shape
    pair_total = bands * pairs
    padded = up_to(pair_total, LANES)
    blocks = padded // LANES
    fields = 4 * levels
    room = up_to(pairs, ROWS)
    for band in range(bands):
        flat[band * block : (band + 1) * block, :] = sums_ref[band].astype(jnp.float32)
    gathered[...] = jnp.zeros(gathered.shape, jnp.float32)
    code_row = up_to(pairs * TALL, ROWS)
    place = pair_places(flat, codes, bands, block, code_row, pairs, gathered.shape[1], padded)
    low = lax.broadcasted_iota(jnp.int32, (fields, padded), 1) < pair_total // 2
    middle = fields * ROWS
    for row in range(TALL):
        here = gathered.at[row % 2]
        for band in range(bands):
            here[band * room : band * room + pairs, :] = flat[
                pl.ds(band * block + row, pairs, stride=TALL), :
            ]
        ordered = jnp.dot(
            here[...].T.astype(jnp.bfloat16), place, preferred_element_type=jnp.float32
        )
        if HALO <= row < HALO + ROWS:
            first, stride = row - HALO, ROWS
        else:
            first, stride = middle + (row - HALO - ROWS) % TALL, 2 * HALO
        for part in range(2):
            start = part * fields
            straight = ordered[start : start + fields]
            start = start + 2 * fields
            crossed = ordered[start : start + fields]
            both = (jnp.where(low, straight, crossed), jnp.where(low, crossed, straight))
            for parity in range(2):
                for t in range(blocks):
                    lhs[parity, part * blocks + t, pl.ds(first, fields, stride=stride), :] = both[
                        parity
                    ][:, t * LANES : (t + 1) * LANES]
    copy.wait()
    half = table_ref.shape[2]

    def transform(first, count):
        found = []
        for parity in range(2):
            left = jnp.concatenate(
                [
                    lhs[parity, t, first : first + count, :].astype(jnp.bfloat16)
                    for t in range(2 * blocks)
                ],
                axis=1,
            )
            found.append(jnp.dot(left, table_ref[parity], preferred_element_type=jnp.float32))
        pieces = (found[0] + found[1], found[0] - found[1])
        return [piece.astype(jnp.bfloat16).astype(jnp.float32) for piece in pieces]

    group = next(n for n in (4, 2, 1) if levels % n == 0)
    for level in range(0, levels, group):
        for part, value in enumerate(transform(level * 4 * ROWS, group * 4 * ROWS)):
            value = value.reshape(group, 4 * ROWS, half)
            lanes = slice(part * half, (part + 1) * half)
            for number, field_ref in enumerate(field_refs):
                field_ref[level : level + group, : 2 * ROWS, lanes] = value[
                    :, 2 * ROWS * number : 2 * ROWS * (number + 1)
                ]
    for part, value in enumerate(transform(middle, fields * 2 * HALO)):
        value = value.reshape(levels, 8 * HALO, half)
        lanes = slice(part * half, (part + 1) * half)
        for number, field_ref in enumerate(field_refs):
            field_ref[:, 2 * ROWS :, lanes] = value[:, 4 * HALO * number : 4 * HALO * (number + 1)]
    for number, field_ref in enumerate(field_refs):
        if send_ref.shape[0] == 1:
            start = jnp.where(base_ref[0] == 0, levels - HALO, 0)
            send_ref[0, number] = field_ref[pl.ds(start, HALO)].astype(jnp.bfloat16)
        else:
            send_ref[0, number] = field_ref[:HALO].astype(jnp.bfloat16)
            send_ref[1, number] = field_ref[levels - HALO :].astype(jnp.bfloat16)


def fourier_call(base, after, sums, table, pairs, levels, lon_total):
    bands, block, width = sums.shape
    padded = up_to(bands * pairs, LANES)
    slots = up_to(bands * up_to(pairs, ROWS), LANES)
    sends = 1 if lax.axis_size("lev") == 2 else 2
    field_shape = (levels, 3 * ROWS, lon_total)
    field = jax.ShapeDtypeStruct(field_shape, jnp.float32)
    send = jax.ShapeDtypeStruct((sends, 2, HALO) + field_shape[1:], jnp.bfloat16)
    in_vmem = pl.BlockSpec(memory_space=pltpu.VMEM)
    return pl.pallas_call(
        functools.partial(fourier_kernel, pairs, levels),
        out_shape=(field, field, send),
        in_specs=[pl.BlockSpec(memory_space=pltpu.SMEM)]
        + [in_vmem] * 2
        + [pl.BlockSpec(memory_space=pl.ANY)],
        out_specs=(in_vmem,) * 3,
        scratch_shapes=[
            pltpu.VMEM((2, LANES, LANES), jnp.float32),
            pltpu.VMEM((bands * block, width), jnp.float32),
            pltpu.VMEM((2, slots, width), jnp.float32),
            pltpu.VMEM((2, 2 * padded // LANES, 4 * levels * TALL, LANES), jnp.float32),
            pltpu.VMEM((2,) + table.shape[1:], table.dtype),
            pltpu.SemaphoreType.DMA,
        ],
        compiler_params=pltpu.CompilerParams(vmem_limit_bytes=44 * 1024 * 1024),
        cost_estimate=pl.CostEstimate(
            flops=8_000_000_000, bytes_accessed=8_000_000, transcendentals=0
        ),
    )(base, after, sums, table)


def exchange(sums):
    return lax.all_to_all(sums, "band", split_axis=0, concat_axis=0, tiled=True)


def per_device(spectra, legendre, pairing, eta_shift, cells):
    levels, rows, lon_total = eta_shift.shape
    pairs = pairing.shape[0]
    spectra = jnp.transpose(spectra, (0, 2, 1, 3))
    table = jnp.transpose(legendre, (0, 2, 1, 3))
    if lax.axis_size("lev") == 2:
        tables = (table, lax.ppermute(table, "lev", [(0, 1), (1, 0)]))
    else:
        tables = (lax.all_gather(table, "lev", axis=0, tiled=True),)
    base = jnp.stack([lax.axis_index("lev") * levels, lax.axis_index("band") * rows])
    base = base.astype(jnp.int32)
    sums, done = legendre_call(pairing, spectra, tables)
    sums = exchange(sums)
    points, done = prepare_call(base, done, eta_shift, cells)
    pair_total = pairs * lax.axis_size("band")
    twiddles = jnp.asarray(fourier_table(pair_total, up_to(pair_total, LANES), lon_total))
    winds, tracers, send = fourier_call(base, done, sums, twiddles, pairs, levels, lon_total)
    nears = swap_levels(send)
    (moved,) = interpolation_call(
        wind_levels, base, 0, winds, points, nears, (), jnp.float32
    )
    advected, displacement = interpolation_call(
        tracer_levels, base, 1, tracers, points, nears, (moved,), jnp.bfloat16
    )
    return advected, displacement


def solution(mesh):
    return jax.shard_map(
        per_device,
        mesh=mesh,
        in_specs=(
            P(None, "lev", "band", None),
            P("lev", None, "band", None),
            P("band"),
            P("lev", "band", None),
            P(None, "lev", "band", None),
        ),
        out_specs=(P(None, "lev", "band", None), P(None, "lev", "band", None)),
        check_vma=False,
    )
```

```python
import functools
import math

import jax
import jax.numpy as jnp
import numpy as np
from jax import lax
from jax.experimental import pallas as pl
from jax.experimental.pallas import tpu as pltpu
from jax.sharding import PartitionSpec as P

ITERS = 2


COURANT = 0.8
HALO = 2
LANES = 128
ROWS = 8
SLOTS = (-1, 0, 1, 2)


def slot_weights(place, here, low, high, sixth):
    z = jnp.minimum(jnp.maximum(place, low), high)
    square = z * z
    less = square - 1.0
    outer = less * z * sixth
    triple = 3.0 * outer
    half = 0.5 * z
    half_square = 0.5 * square
    return (
        half_square - half - jnp.where(here, outer, triple),
        triple - less,
        half_square + half - jnp.where(here, triple, outer),
        outer,
    )


def bounds(here):
    return (
        jnp.where(here, -0.5, -1.5),
        jnp.where(here, 1.5, 0.5),
        jnp.where(here, 1.0 / 6.0, -1.0 / 6.0),
    )


def weighted(weights, values):
    return (weights[0] * values[0] + weights[1] * values[1]) + (
        weights[2] * values[2] + weights[3] * values[3]
    )


def shifted_lanes(before, here, after, lane):
    return (
        pltpu.roll(jnp.where(lane < LANES - 2, here, before), 2, 1),
        pltpu.roll(jnp.where(lane < LANES - 1, here, before), 1, 1),
        here,
        pltpu.roll(jnp.where(lane < 1, after, here), LANES - 1, 1),
        pltpu.roll(jnp.where(lane < 2, after, here), LANES - 2, 1),
    )


STACK = 5 * ROWS
FIELD_ROW = (ROWS, 3 * ROWS)


def fill_units(slab, chunk, chunk_total, source, scratch):
    field_ref, row = source
    before = jnp.where(chunk == 0, chunk_total - 1, chunk - 1)
    after = jnp.where(chunk == chunk_total - 1, 0, chunk + 1)
    starts = [pl.multiple_of(c * LANES, LANES) for c in (before, chunk, after)]
    lane = lax.broadcasted_iota(jnp.int32, (ROWS, LANES), 1)
    first = slab * (5 * STACK)

    def edge_start():
        moved = shifted_lanes(
            *[field_ref[row, 2 * ROWS : 3 * ROWS, pl.ds(s, LANES)] for s in starts], lane
        )
        return [(value, pltpu.roll(value, ROWS // 2, 0)) for value in moved]

    def edge_finish(values):
        for step, (between, outside) in enumerate(values):
            for offset, value in ((0, outside), (2 * ROWS, between), (4 * ROWS, outside)):
                scratch[pl.ds(first + step * STACK + offset, ROWS), :] = value

    def center_unit(field):
        def start():
            rows = slice(field * ROWS, (field + 1) * ROWS)
            blocks = [field_ref[row, rows, pl.ds(s, LANES)] for s in starts]
            return shifted_lanes(*blocks, lane)

        def finish(values):
            for step, moved in enumerate(values):
                scratch[pl.ds(first + step * STACK + FIELD_ROW[field], ROWS), :] = moved

        return start, finish

    return [(edge_start, edge_finish)] + [center_unit(field) for field in range(2)]


class Interleave:
    def __init__(self, units, ticks, later):
        self.units = list(units)
        self.every = max(1, ticks // max(1, len(self.units)))
        self.count = 0
        self.pending = None
        self.later = later

    def advance(self):
        if self.pending is not None:
            self.pending[0](self.pending[1])
            self.pending = None
        if self.units:
            start, finish = self.units.pop(0)
            self.pending = (finish, start())

    def tick(self):
        if self.count % self.every == 0:
            self.advance()
        self.count += 1
        if self.later and self.count % 3 == 0:
            self.later.pop(0)()

    def flush(self):
        while self.units or self.pending is not None:
            self.advance()

    def finish_later(self):
        while self.later:
            self.later.pop(0)()


def level_sums(scratch, field, base, slot, points):
    loaded = {}

    def load(a, b, c):
        offset = ((a + HALO) * 5 + c + HALO) * STACK + FIELD_ROW[field] + b
        if (a, b, c) not in loaded:
            loaded[a, b, c] = scratch[pl.ds(base + offset, ROWS), :]
        return loaded[a, b, c]

    def one(step, weights, level_here, row_here, lon_here):
        def pick_lon(a, b):
            if slot[1] == 2:
                return jnp.where(lon_here, load(a + step, b, 2), load(a + step, b, -2))
            return load(a + step, b, slot[1])

        def pick(a):
            if slot[0] == 2:
                return jnp.where(row_here, pick_lon(a, 2), pick_lon(a, -2))
            return pick_lon(a, slot[0])

        total = weights[0] * pick(-1) + weights[1] * pick(0)
        total = total + weights[2] * pick(1)
        return total + weights[3] * jnp.where(level_here, pick(2), pick(-2))

    return [one(step, *point) for step, point in enumerate(points)]


def across(scratch, field, base, points, row_weights, lon_weights, filling, keep=None):
    columns = [[None] * 4 for _ in points]
    for b, row_slot in enumerate(SLOTS):
        for c, lon_slot in enumerate(SLOTS):
            filling.tick()
            found = level_sums(scratch, field, base, (row_slot, lon_slot), points)
            for step, value in enumerate(found):
                if keep is not None:
                    keep[field, step, 4 * b + c] = value
                term = row_weights[step][b] * value
                columns[step][c] = term if b == 0 else columns[step][c] + term
    return [weighted(weights, column) for weights, column in zip(lon_weights, columns)]


def across_kept(keep, field, step, row_weights, lon_weights):
    return weighted(
        lon_weights,
        [
            weighted(row_weights, [keep[field, step, 4 * b + c] for b in range(4)])
            for c in range(4)
        ],
    )


def prepare_kernel(base_ref, after_ref, eta_ref, cells_ref, points_ref, done_ref):
    done_ref[...] = after_ref[...]
    levels, rows, lon_total = eta_ref.shape
    shape = (rows, LANES)
    row_here = base_ref[1] + lax.broadcasted_iota(jnp.int32, shape, 0)
    lane = lax.broadcasted_iota(jnp.int32, shape, 1)

    def chunk_step(chunk, carry):
        lanes = pl.ds(pl.multiple_of(chunk * LANES, LANES), LANES)
        for k in range(levels):
            level_here = cells_ref[2, k, :, lanes] == base_ref[0] + k
            weights = slot_weights(
                -eta_ref[k, :, lanes].astype(jnp.float32), level_here, *bounds(level_here)
            )
            here = (
                level_here,
                cells_ref[0, k, :, lanes] == row_here,
                cells_ref[1, k, :, lanes] == chunk * LANES + lane,
            )
            for n, value in enumerate(weights + tuple(bounds(x)[0] for x in here)):
                points_ref[n, k, :, lanes] = value
        return carry

    lax.fori_loop(0, lon_total // LANES, chunk_step, 0)


def prepare_call(base, after, eta_shift, cells):
    in_vmem = pl.BlockSpec(memory_space=pltpu.VMEM)
    return pl.pallas_call(
        prepare_kernel,
        out_shape=(
            jax.ShapeDtypeStruct((7,) + eta_shift.shape, jnp.float32),
            jax.ShapeDtypeStruct(after.shape, after.dtype),
        ),
        in_specs=[pl.BlockSpec(memory_space=pltpu.SMEM)] + [in_vmem] * 3,
        out_specs=(in_vmem, in_vmem),
        compiler_params=pltpu.CompilerParams(vmem_limit_bytes=16 * 1024 * 1024),
        cost_estimate=pl.CostEstimate(
            flops=40 * eta_shift.size, bytes_accessed=20_000_000, transcendentals=0
        ),
    )(base, after, eta_shift, cells)


def arrival(points_ref, k, lanes):
    here = [points_ref[n, k, :, lanes] > -1.0 for n in range(4, 7)]
    return tuple(points_ref[n, k, :, lanes] for n in range(4)), *here


def both_weights(shift_row, shift_lon, point):
    _, _, row_here, lon_here = point
    return (
        slot_weights(-shift_row, row_here, *bounds(row_here)),
        slot_weights(-shift_lon, lon_here, *bounds(lon_here)),
    )


def wind_levels(base, lanes, k, points, scratch, keep, filling, out_ref):
    def arrival_wind(field, step):
        middle = (HALO * 5 + HALO) * STACK + step * (5 * STACK) + FIELD_ROW[field]
        return scratch[pl.ds(base + middle, ROWS), :]

    weights = []
    for step, point in enumerate(points):
        east, north = arrival_wind(0, step), arrival_wind(1, step)
        keep[0, step, 16], keep[1, step, 16] = east, north
        weights.append(both_weights(COURANT * north, COURANT * east, point))
    row_weights, lon_weights = zip(*weights)
    found = [
        across(scratch, field, base, points, row_weights, lon_weights, filling, keep)
        for field in range(2)
    ]
    filling.finish_later()

    def tail(step, east_found, north_found):
        def finish():
            east, north = keep[0, step, 16], keep[1, step, 16]
            here = (east_found, north_found)
            for sweep in range(ITERS):
                shift_row = 0.5 * COURANT * (north + here[1])
                shift_lon = 0.5 * COURANT * (east + here[0])
                if sweep < ITERS - 1:
                    weights = both_weights(shift_row, shift_lon, points[step])
                    here = [across_kept(keep, field, step, *weights) for field in range(2)]
            out_ref[0, k + step, :, lanes] = shift_row
            out_ref[1, k + step, :, lanes] = shift_lon

        return finish

    filling.later += [tail(step, found[0][step], found[1][step]) for step in range(len(points))]


def tracer_levels(shift_ref, base, lanes, k, points, scratch, keep, filling, out_ref):
    weights = [
        both_weights(
            shift_ref[0, k + step, :, lanes], shift_ref[1, k + step, :, lanes], points[step]
        )
        for step in range(len(points))
    ]
    row_weights, lon_weights = zip(*weights)
    found = [
        across(scratch, field, base, points, row_weights, lon_weights, filling)
        for field in range(2)
    ]
    for field in range(2):
        for step, total in enumerate(found[field]):
            out_ref[field, k + step, :, lanes] = total.astype(out_ref.dtype)


def interpolation_kernel(
    levels_body, together, number, near_count, base_ref, field_ref, points_ref, *others
):
    nears, others = others[:near_count], others[near_count:]
    extra = ()
    if number == 1:
        shift_ref, out_ref, shift_out, around, even_scratch, odd_scratch, keep, sem = others
        extra = (shift_ref,)
        copy = pltpu.make_async_copy(shift_ref, shift_out, sem)
        copy.start()
    else:
        out_ref, around, even_scratch, odd_scratch, keep = others
    _, levels, rows, lon_total = points_ref.shape
    chunk_total = lon_total // LANES
    if near_count == 1:
        found = jnp.where(base_ref[0] == 0, HALO, 0)
        around[pl.ds(found, HALO)] = nears[0][number].astype(jnp.float32)
        around[pl.ds(HALO - found, HALO)] = jnp.zeros((HALO,) + around.shape[1:], jnp.float32)
    else:
        around[:HALO] = nears[0][number].astype(jnp.float32)
        around[HALO:] = nears[1][number].astype(jnp.float32)
    sources = [(around, n) for n in range(HALO)]
    sources += [(field_ref, n) for n in range(levels)]
    sources += [(around, HALO + n) for n in range(HALO)]

    def all_units(chunk, scratch):
        units = []
        for slab, source in enumerate(sources):
            units += fill_units(slab, chunk, chunk_total, source, scratch)
        return units

    for start, finish in all_units(0, even_scratch):
        finish(start())

    def one_chunk(chunk, scratch, other, later):
        lanes = pl.ds(pl.multiple_of(chunk * LANES, LANES), LANES)
        following = jnp.where(chunk == chunk_total - 1, 0, chunk + 1)
        filling = Interleave(all_units(following, other), 32 * (levels // together), later)
        for k in range(0, levels, together):
            points = [arrival(points_ref, k + n, lanes) for n in range(together)]
            base = k * (5 * STACK)
            keep_here = keep.at[k // together % 2]
            levels_body(*extra, base, lanes, k, points, scratch, keep_here, filling, out_ref)
        filling.flush()
        if levels // together % 2:
            filling.finish_later()

    def chunk_pair(pair, carry):
        later = []
        one_chunk(2 * pair, even_scratch, odd_scratch, later)
        one_chunk(2 * pair + 1, odd_scratch, even_scratch, later)
        for finish in later:
            finish()
        return carry

    lax.fori_loop(0, chunk_total // 2, chunk_pair, 0)
    if number == 1:
        copy.wait()


def interpolation_call(levels_body, base, number, fields, points, nears, extra, out_dtype):
    _, levels, rows, lon_total = points.shape
    count = levels * rows * lon_total
    together = 2 if levels % 2 == 0 else 1
    scratch = pltpu.VMEM(((levels + 2 * HALO) * 5 * STACK, LANES), jnp.float32)
    in_vmem = pl.BlockSpec(memory_space=pltpu.VMEM)
    return pl.pallas_call(
        functools.partial(interpolation_kernel, levels_body, together, number, len(nears)),
        out_shape=(jax.ShapeDtypeStruct((2, levels, rows, lon_total), out_dtype),)
        + tuple(jax.ShapeDtypeStruct(x.shape, x.dtype) for x in extra),
        in_specs=[pl.BlockSpec(memory_space=pltpu.SMEM)]
        + [in_vmem] * (2 + len(nears) + len(extra)),
        out_specs=(in_vmem,) + (pl.BlockSpec(memory_space=pl.ANY),) * len(extra),
        scratch_shapes=[
            pltpu.VMEM((2 * HALO,) + fields.shape[1:], jnp.float32),
            scratch,
            scratch,
            pltpu.VMEM((2, 2, together, 17, ROWS, LANES), jnp.float32),
        ]
        + [pltpu.SemaphoreType.DMA] * len(extra),
        compiler_params=pltpu.CompilerParams(vmem_limit_bytes=16 * 1024 * 1024),
        cost_estimate=pl.CostEstimate(
            flops=count * 500, bytes_accessed=count * 40, transcendentals=0
        ),
    )(base, fields, points, *nears, *extra)


def swap_levels(send):
    if lax.axis_size("lev") == 2:
        return (lax.ppermute(send[0], "lev", [(0, 1), (1, 0)]),)
    up = [(i, i + 1) for i in range(lax.axis_size("lev") - 1)]
    down = [(j, i) for i, j in up]
    return lax.ppermute(send[1], "lev", up), lax.ppermute(send[0], "lev", down)


def up_to(value, step):
    return -(-value // step) * step


TALL = ROWS + 2 * HALO


def codes_kernel(numbers_ref, out_ref):
    out_ref[...] = numbers_ref[...]


def legendre_kernel(numbers_ref, codes_ref, spectra_ref, *others):
    table_count = (len(others) - 7) // 2
    sources, others = (spectra_ref,) + others[:table_count], others[table_count:]
    out_ref, done_ref, sums, table_tail, column_tail = others[:5]
    targets, arrivals = others[5:-1], others[-1]
    spectra_here, tables = targets[0], targets[1:]
    _, pairs, level_fields, degrees = spectra_ref.shape
    group = table_tail.shape[0]
    bands, block, _ = out_ref.shape
    full = degrees // LANES * LANES
    at_top = numbers_ref[0] == 0
    step = pl.program_id(0)

    def copies(number):
        here = pl.ds(number * group, group)
        return [
            pltpu.make_async_copy(source.at[:, here], target.at[:, here], arrivals.at[n, number])
            for n, (source, target) in enumerate(zip(sources, targets))
        ]

    @pl.when(step == 0)
    def _():
        for copy in copies(0):
            copy.start()
        sums[...] = jnp.zeros(sums.shape, jnp.float32)
        done_ref[...] = jnp.zeros(done_ref.shape, jnp.float32)
        table_tail[...] = jnp.zeros(table_tail.shape, jnp.float32)
        column_tail[...] = jnp.zeros(column_tail.shape, jnp.float32)
        codes = codes_ref[...]
        code_row = up_to(pl.num_programs(0) * group * TALL, ROWS)
        for band in range(bands):
            first = band * block + code_row
            sums[pl.ds(first, 1), :] = jnp.right_shift(codes, 4).astype(jnp.float32)
            sums[pl.ds(first + 1, 1), :] = (codes & 15).astype(jnp.float32)

    @pl.when(step + 1 < pairs // group)
    def _():
        for copy in copies(step + 1):
            copy.start()

    for copy in copies(step):
        copy.wait()
    band_row = lax.broadcasted_iota(jnp.int32, (bands, 4 * level_fields), 0)
    count = 2 * level_fields
    nothing = jnp.zeros((bands, 2 * count), jnp.float32)
    for p in range(group):
        slot = step * group + p
        edge = degrees - 1 - numbers_ref[1 + slot]
        left = []
        for number, table_ref in enumerate(tables):
            for row in range(table_ref.shape[0]):
                piece = table_ref[row, slot]
                left.append(piece[:, :full])
                first = (number * table_ref.shape[0] + row) * bands
                table_tail[p, first : first + bands, : degrees - full] = piece[:, full:].astype(
                    jnp.float32
                )
        left = jnp.concatenate(left, axis=0)
        left = jnp.concatenate([left, table_tail[p].astype(jnp.bfloat16)], axis=1)
        halves = ([], [])
        for part in range(2):
            piece = spectra_here[part, slot]
            whole = piece[:, :full].astype(jnp.float32)
            lane = lax.broadcasted_iota(jnp.int32, whole.shape, 1)
            zero = jnp.zeros_like(whole)
            halves[0].append(jnp.where(lane < edge, whole, zero).astype(jnp.bfloat16))
            halves[1].append(jnp.where(lane < edge, zero, whole).astype(jnp.bfloat16))
            first = part * level_fields
            column_tail[p, first : first + level_fields, : degrees - full] = piece[
                :, full:
            ].astype(jnp.float32)
        tail = column_tail[p].astype(jnp.bfloat16)
        right = jnp.concatenate(
            [
                jnp.concatenate([jnp.concatenate(halves[0], axis=0), jnp.zeros_like(tail)], axis=1),
                jnp.concatenate([jnp.concatenate(halves[1], axis=0), tail], axis=1),
            ],
            axis=0,
        )
        found = lax.dot_general(
            left, right, (((1,), (1,)), ((), ())), preferred_element_type=jnp.float32
        )
        found = [found[i * bands : (i + 1) * bands] for i in range(ROWS)]
        if len(tables) == 2:
            low, high = found[: ROWS // 2], found[ROWS // 2 :]
            found = [jnp.where(at_top, x, y) for x, y in zip(low, high)]
            found += [jnp.where(at_top, y, x) for x, y in zip(low, high)]
        above = [
            jnp.where(band_row == 0, nothing, pltpu.roll(x, 1, 0)) for x in found[ROWS - HALO :]
        ]
        below = [
            jnp.where(band_row == bands - 1, nothing, pltpu.roll(x, bands - 1, 0))
            for x in found[:HALO]
        ]
        rows = above + found + below
        for i, value in enumerate(rows):
            place = pl.ds(slot * TALL + i, bands, stride=block)
            sums[place, : 2 * count] = value

    @pl.when(step == pl.num_programs(0) - 1)
    def _():
        for band in range(bands):
            out_ref[band] = sums[band * block : (band + 1) * block, :].astype(jnp.bfloat16)


def block_rows(pairs):
    return up_to(up_to(pairs * TALL, ROWS) + 2, ROWS)


def legendre_call(pairing, spectra, tables):
    _, pairs, level_fields, degrees = spectra.shape
    bands = tables[0].shape[2]
    block = block_rows(pairs)
    group = next(n for n in (4, 5, 2, 1) if pairs % n == 0)
    numbers = jnp.concatenate([lax.axis_index("lev").astype(jnp.int32)[None], pairing])
    codes = pl.pallas_call(
        codes_kernel,
        out_shape=jax.ShapeDtypeStruct((1, LANES), jnp.int32),
        in_specs=[pl.BlockSpec(memory_space=pltpu.VMEM)],
        out_specs=pl.BlockSpec(memory_space=pltpu.VMEM),
        cost_estimate=pl.CostEstimate(flops=0, bytes_accessed=4_000_000, transcendentals=0),
    )(jnp.pad(pairing, (0, LANES - pairs))[None, :])
    shape = jax.ShapeDtypeStruct((bands, block, LANES), jnp.bfloat16)
    in_vmem = pl.BlockSpec(memory_space=pltpu.VMEM)
    in_hbm = pl.BlockSpec(memory_space=pl.ANY)
    return pl.pallas_call(
        legendre_kernel,
        grid=(pairs // group,),
        out_shape=(shape, jax.ShapeDtypeStruct((ROWS, LANES), jnp.float32)),
        in_specs=[
            pl.BlockSpec(memory_space=pltpu.SMEM),
            pl.BlockSpec((1, LANES), lambda i: (0, 0)),
            in_hbm,
        ]
        + [in_hbm] * len(tables),
        out_specs=(in_vmem, in_vmem),
        scratch_shapes=[
            pltpu.VMEM((bands * block, LANES), jnp.float32),
            pltpu.VMEM((group, ROWS * bands, LANES), jnp.float32),
            pltpu.VMEM((group, 2 * level_fields, LANES), jnp.float32),
        ]
        + [pltpu.VMEM(x.shape, x.dtype) for x in (spectra,) + tables]
        + [pltpu.SemaphoreType.DMA((1 + len(tables), pairs // group))],
        compiler_params=pltpu.CompilerParams(vmem_limit_bytes=60 * 1024 * 1024),
        cost_estimate=pl.CostEstimate(
            flops=2 * ROWS * bands * 4 * level_fields * pairs * degrees,
            bytes_accessed=8_000_000,
            transcendentals=0,
        ),
    )(numbers, codes, spectra, *tables)


def fourier_table(pair_total, padded, lon_total):
    order_total = 2 * pair_total
    half = pair_total // 2
    low = 2 * np.arange(half)
    high = low + 1
    even = np.concatenate([low, order_total - 1 - high])
    odd = np.concatenate([order_total - 1 - low, high])
    lon = np.arange(lon_total // 2)
    table = np.zeros((4, 2, padded, lon_total // 2), np.float32)
    for parity, orders in enumerate((even, odd)):
        phase = (orders[:, None] * lon[None, :]) % lon_total * (2.0 * math.pi / lon_total)
        weight = np.where(orders == 0, 1.0, 2.0)[:, None]
        table[parity, 0, :pair_total] = weight * np.cos(phase)
        table[parity, 1, :pair_total] = -weight * np.sin(phase)
    return table.reshape(4, 2 * padded, lon_total // 2).astype(jnp.bfloat16)


def owner_tables(slots, pairs):
    room = up_to(pairs, ROWS)
    slot = lax.broadcasted_iota(jnp.int32, (slots, LANES), 0)
    lane = lax.broadcasted_iota(jnp.int32, (slots, LANES), 1)
    owner = ((slot.astype(jnp.float32) + 0.5) * (1.0 / room)).astype(jnp.int32)
    return (
        jnp.where(owner == lane, 1.0, 0.0).astype(jnp.bfloat16),
        jnp.where(slot - room * owner == lane, 1.0, 0.0),
    )


def pair_places(flat, codes, bands, block, code_row, pairs, slots, padded):
    pair_total = bands * pairs
    owner, own_lane = owner_tables(slots, pairs)
    codes[...] = jnp.zeros(codes.shape, jnp.float32)
    numbers = []
    for part in range(2):
        codes[part, :bands, :] = flat[pl.ds(code_row + part, bands, stride=block), :]
        numbers.append(
            jnp.dot(
                owner,
                codes[part].astype(jnp.bfloat16),
                preferred_element_type=jnp.float32,
            )
        )
    pair_id = jnp.sum(
        (16.0 * numbers[0] + numbers[1]) * own_lane, axis=1, keepdims=True
    ).astype(jnp.int32)
    place = jnp.right_shift(pair_id, 1) + (pair_id & 1) * (pair_total // 2)
    columns = lax.broadcasted_iota(jnp.int32, (slots, padded), 1)
    return jnp.where(columns == place, 1.0, 0.0).astype(jnp.bfloat16)


def fourier_kernel(
    pairs, levels, base_ref, after_ref, sums_ref, table_source, *others
):
    field_refs, send_ref, others = others[:2], others[2], others[3:]
    codes, flat, gathered, lhs, table_ref, arrival_sem = others
    copy = pltpu.make_async_copy(table_source.at[:2], table_ref, arrival_sem)
    copy.start()
    bands, block, width = sums_ref.shape
    pair_total = bands * pairs
    padded = up_to(pair_total, LANES)
    blocks = padded // LANES
    fields = 4 * levels
    room = up_to(pairs, ROWS)
    for band in range(bands):
        flat[band * block : (band + 1) * block, :] = sums_ref[band].astype(jnp.float32)
    gathered[...] = jnp.zeros(gathered.shape, jnp.float32)
    code_row = up_to(pairs * TALL, ROWS)
    place = pair_places(flat, codes, bands, block, code_row, pairs, gathered.shape[1], padded)
    low = lax.broadcasted_iota(jnp.int32, (fields, padded), 1) < pair_total // 2
    middle = fields * ROWS
    for row in range(TALL):
        here = gathered.at[row % 2]
        for band in range(bands):
            here[band * room : band * room + pairs, :] = flat[
                pl.ds(band * block + row, pairs, stride=TALL), :
            ]
        ordered = jnp.dot(
            here[...].T.astype(jnp.bfloat16), place, preferred_element_type=jnp.float32
        )
        if HALO <= row < HALO + ROWS:
            first, stride = row - HALO, ROWS
        else:
            first, stride = middle + (row - HALO - ROWS) % TALL, 2 * HALO
        for part in range(2):
            start = part * fields
            straight = ordered[start : start + fields]
            start = start + 2 * fields
            crossed = ordered[start : start + fields]
            both = (jnp.where(low, straight, crossed), jnp.where(low, crossed, straight))
            for parity in range(2):
                for t in range(blocks):
                    lhs[parity, part * blocks + t, pl.ds(first, fields, stride=stride), :] = both[
                        parity
                    ][:, t * LANES : (t + 1) * LANES]
    copy.wait()
    half = table_ref.shape[2]

    def transform(first, count):
        found = []
        for parity in range(2):
            left = jnp.concatenate(
                [
                    lhs[parity, t, first : first + count, :].astype(jnp.bfloat16)
                    for t in range(2 * blocks)
                ],
                axis=1,
            )
            found.append(jnp.dot(left, table_ref[parity], preferred_element_type=jnp.float32))
        pieces = (found[0] + found[1], found[0] - found[1])
        return [piece.astype(jnp.bfloat16).astype(jnp.float32) for piece in pieces]

    group = next(n for n in (4, 2, 1) if levels % n == 0)
    for level in range(0, levels, group):
        for part, value in enumerate(transform(level * 4 * ROWS, group * 4 * ROWS)):
            value = value.reshape(group, 4 * ROWS, half)
            lanes = slice(part * half, (part + 1) * half)
            for number, field_ref in enumerate(field_refs):
                field_ref[level : level + group, : 2 * ROWS, lanes] = value[
                    :, 2 * ROWS * number : 2 * ROWS * (number + 1)
                ]
    for part, value in enumerate(transform(middle, fields * 2 * HALO)):
        value = value.reshape(levels, 8 * HALO, half)
        lanes = slice(part * half, (part + 1) * half)
        for number, field_ref in enumerate(field_refs):
            field_ref[:, 2 * ROWS :, lanes] = value[:, 4 * HALO * number : 4 * HALO * (number + 1)]
    for number, field_ref in enumerate(field_refs):
        if send_ref.shape[0] == 1:
            start = jnp.where(base_ref[0] == 0, levels - HALO, 0)
            send_ref[0, number] = field_ref[pl.ds(start, HALO)].astype(jnp.bfloat16)
        else:
            send_ref[0, number] = field_ref[:HALO].astype(jnp.bfloat16)
            send_ref[1, number] = field_ref[levels - HALO :].astype(jnp.bfloat16)


def fourier_call(base, after, sums, table, pairs, levels, lon_total):
    bands, block, width = sums.shape
    padded = up_to(bands * pairs, LANES)
    slots = up_to(bands * up_to(pairs, ROWS), LANES)
    sends = 1 if lax.axis_size("lev") == 2 else 2
    field_shape = (levels, 3 * ROWS, lon_total)
    field = jax.ShapeDtypeStruct(field_shape, jnp.float32)
    send = jax.ShapeDtypeStruct((sends, 2, HALO) + field_shape[1:], jnp.bfloat16)
    in_vmem = pl.BlockSpec(memory_space=pltpu.VMEM)
    return pl.pallas_call(
        functools.partial(fourier_kernel, pairs, levels),
        out_shape=(field, field, send),
        in_specs=[pl.BlockSpec(memory_space=pltpu.SMEM)]
        + [in_vmem] * 2
        + [pl.BlockSpec(memory_space=pl.ANY)],
        out_specs=(in_vmem,) * 3,
        scratch_shapes=[
            pltpu.VMEM((2, LANES, LANES), jnp.float32),
            pltpu.VMEM((bands * block, width), jnp.float32),
            pltpu.VMEM((2, slots, width), jnp.float32),
            pltpu.VMEM((2, 2 * padded // LANES, 4 * levels * TALL, LANES), jnp.float32),
            pltpu.VMEM((2,) + table.shape[1:], table.dtype),
            pltpu.SemaphoreType.DMA,
        ],
        compiler_params=pltpu.CompilerParams(vmem_limit_bytes=44 * 1024 * 1024),
        cost_estimate=pl.CostEstimate(
            flops=8_000_000_000, bytes_accessed=8_000_000, transcendentals=0
        ),
    )(base, after, sums, table)


def exchange(sums):
    return lax.all_to_all(sums, "band", split_axis=0, concat_axis=0, tiled=True)


def per_device(spectra, legendre, pairing, eta_shift, cells):
    levels, rows, lon_total = eta_shift.shape
    pairs = pairing.shape[0]
    spectra = jnp.transpose(spectra, (0, 2, 1, 3))
    table = jnp.transpose(legendre, (0, 2, 1, 3))
    if lax.axis_size("lev") == 2:
        tables = (table, lax.ppermute(table, "lev", [(0, 1), (1, 0)]))
    else:
        tables = (lax.all_gather(table, "lev", axis=0, tiled=True),)
    base = jnp.stack([lax.axis_index("lev") * levels, lax.axis_index("band") * rows])
    base = base.astype(jnp.int32)
    sums, done = legendre_call(pairing, spectra, tables)
    sums = exchange(sums)
    points, done = prepare_call(base, done, eta_shift, cells)
    pair_total = pairs * lax.axis_size("band")
    twiddles = jnp.asarray(fourier_table(pair_total, up_to(pair_total, LANES), lon_total))
    winds, tracers, send = fourier_call(base, done, sums, twiddles, pairs, levels, lon_total)
    nears = swap_levels(send)
    (moved,) = interpolation_call(
        wind_levels, base, 0, winds, points, nears, (), jnp.float32
    )
    advected, displacement = interpolation_call(
        tracer_levels, base, 1, tracers, points, nears, (moved,), jnp.bfloat16
    )
    return advected, displacement


def solution(mesh):
    return jax.shard_map(
        per_device,
        mesh=mesh,
        in_specs=(
            P(None, "lev", "band", None),
            P("lev", None, "band", None),
            P("band"),
            P("lev", "band", None),
            P(None, "lev", "band", None),
        ),
        out_specs=(P(None, "lev", "band", None), P(None, "lev", "band", None)),
        check_vma=False,
    )
```
